32 devices in a mesh: batch: 4 (over y, x), seq: 8 (over z, core).
Axes of the slice: x: 2, y: 2, z: 4, core: 2. Of those that a mesh axis runs over, the one named last changes fastest.
Arguments:
- inputs: bfloat16 [4, 16384, 512], P('batch', 'seq'), may hold values from -6 to 6
- out_grad: bfloat16 [4, 16384, 512], P('batch', 'seq'), may hold values from -6 to 6
- lengths: int32 [4], P('batch'), may hold values from 128 to 16384, as said below
- qkv_weight: float32 [512, 1536], P(('batch', 'seq')), may hold values from -0.125 to 0.125
- proj_weight: float32 [512, 512], P(('batch', 'seq')), may hold values from -3 to 3
- up_weight: float32 [512, 2048], P(('batch', 'seq')), may hold values from -0.125 to 0.125
- down_weight: float32 [2048, 512], P(('batch', 'seq')), may hold values from -0.125 to 0.125
- norm_params: float32 [4, 512], P(None, ('batch', 'seq'))
- qkv_mean: float32 [512, 1536], P(('batch', 'seq')), may hold values from -0.0034179688 to 0.0034179688
- proj_mean: float32 [512, 512], P(('batch', 'seq')), may hold values from -0.0007324219 to 0.0007324219
- up_mean: float32 [512, 2048], P(('batch', 'seq')), may hold values from -0.0007324219 to 0.0007324219
- down_mean: float32 [2048, 512], P(('batch', 'seq')), may hold values from -0.0004272461 to 0.0004272461
- norm_mean: float32 [4, 512], P(None, ('batch', 'seq')), may hold values from -0.009765625 to 0.009765625
- qkv_second: float32 [512, 1536], P(('batch', 'seq')), may hold values from 3.1768462e-07 to 1.2707385e-06
- proj_second: float32 [512, 512], P(('batch', 'seq')), may hold values from 1.588423e-08 to 6.353692e-08
- up_second: float32 [512, 2048], P(('batch', 'seq')), may hold values from 1.588423e-08 to 6.353692e-08
- down_second: float32 [2048, 512], P(('batch', 'seq')), may hold values from 4.9638222e-09 to 1.9855289e-08
- norm_second: float32 [4, 512], P(None, ('batch', 'seq')), may hold values from 2.8591614e-06 to 1.1436646e-05
Outputs:
- outputs: bfloat16 [4, 16384, 512], P('batch', 'seq')
- input_grad: float32 [4, 16384, 512], P('batch', 'seq')
- grad_norm: float32 [], replicated
- qkv_moment: float32 [512, 1536], P(('batch', 'seq'))
- proj_moment: float32 [512, 512], P(('batch', 'seq'))
- up_moment: float32 [512, 2048], P(('batch', 'seq'))
- down_moment: float32 [2048, 512], P(('batch', 'seq'))
- norm_moment: float32 [4, 512], P(None, ('batch', 'seq'))
- qkv_square: float32 [512, 1536], P(('batch', 'seq'))
- proj_square: float32 [512, 512], P(('batch', 'seq'))
- up_square: float32 [512, 2048], P(('batch', 'seq'))
- down_square: float32 [2048, 512], P(('batch', 'seq'))
- norm_square: float32 [4, 512], P(None, ('batch', 'seq'))
- qkv_master: float32 [512, 1536], P(('batch', 'seq'))
- proj_master: float32 [512, 512], P(('batch', 'seq'))
- up_master: float32 [512, 2048], P(('batch', 'seq'))
- down_master: float32 [2048, 512], P(('batch', 'seq'))
- norm_master: float32 [4, 512], P(None, ('batch', 'seq'))
- shift_clipped: float32 [512], P(('batch', 'seq'))
The draws below stay inside these ranges and needn't reach their ends.
Inputs may be any that keep to these rules, and one draw needn't show every extreme that they name: `lengths`: one of the 4 sequences in every draw has all 16384 tokens.
All inputs are finite; a program needn't handle non-finite values.
Results may differ from the reference program's by a relative error of at most 0.012.
The reference program's roundings to bfloat16 on the way count: a program that leaves them out, or rounds other values in their place, can miss the bound.
Values may be sent and summed in bfloat16 or wider, within the bound.
A program may use at most 384 MiB of HBM per device.

```python
import math
import jax
import jax.numpy as jnp
from jax import lax

D = 512
HEADS = 8
HD = 64
FF = 2048
SPAN = 128
STEP = 10
TOK_DEV = 2048
SEQS = 4
SEQLEN = 16384
SPANS = 128
NPARAMS = 3147776


def draw_lengths(key, part):
    key = jax.random.fold_in(key, 11)
    first_key, second_key = jax.random.split(key)
    drawn = jax.random.randint(first_key, (SEQS,), SPAN, SEQLEN + 1)
    longest = jax.random.randint(second_key, (), 0, SEQS)
    return jnp.where(jnp.arange(SEQS) == longest, SEQLEN, drawn).astype(jnp.int32)


def draw_norm_params(key, part):
    key = jax.random.fold_in(key, 23)
    keys = jax.random.split(key, 4)
    ramp = jnp.arange(D, dtype=jnp.float32) / (D - 1)
    base = 1.0 + 2.0 * ramp
    gain_one = base * jax.random.uniform(keys[0], (D,), jnp.float32, 0.8, 1.2)
    shift_one = 0.3 * jax.random.normal(keys[1], (D,), jnp.float32)
    gain_two = base * jax.random.uniform(keys[2], (D,), jnp.float32, 0.8, 1.2)
    shift_two = 0.3 * jax.random.normal(keys[3], (D,), jnp.float32)
    return jnp.stack([gain_one, shift_one, gain_two, shift_two]).astype(jnp.float32)


def levels(own_key, shape, cuts, least, top_value):
    level = 1.0
    for dim, blocks in cuts:
        steps = jax.random.uniform(jax.random.fold_in(jax.random.fold_in(own_key, 6), dim), (blocks,), jnp.float32, least / len(cuts), top_value / len(cuts))
        level = level * jnp.repeat(jnp.exp(steps), shape[dim] // blocks).reshape((-1,) + (1,) * (len(shape) - 1 - dim))
    return level


def bell_draw(key, extent, scale, limit, pieces=(), kind=jnp.bfloat16):
    values = jax.random.normal(key, extent, jnp.float32) * scale
    if len(pieces) > 0:
        values = levels(key, extent, pieces, -0.22, 0.18) * values
    return jnp.clip(values, min=-limit, max=limit).astype(kind)


def setup_inputs(seed: int = 0) -> dict:
    seeds = jax.random.split(jax.random.key(seed), 19)
    return {
        "inputs": bell_draw(seeds[0], (SEQS, SEQLEN, D), 1.0, 6.0, ((0, 4), (1, 8))),
        "out_grad": bell_draw(seeds[1], (SEQS, SEQLEN, D), 1.0, 6.0, ((0, 4), (1, 8))),
        "lengths": draw_lengths(jax.random.fold_in(seeds[18], 71), 0),
        "qkv_weight": bell_draw(seeds[3], (D, 3 * D), (4 * D) ** -0.5, 0.125, ((0, 32),), jnp.float32),
        "proj_weight": bell_draw(seeds[4], (D, D), (max(D // SPAN, 1)) ** -0.5, 3.0, ((0, 32),), jnp.float32),
        "up_weight": bell_draw(seeds[5], (D, FF), (4 * D) ** -0.5, 0.125, ((0, 32),), jnp.float32),
        "down_weight": bell_draw(seeds[6], (FF, D), FF ** -0.5, 0.125, ((0, 32),), jnp.float32),
        "norm_params": draw_norm_params(jax.random.fold_in(seeds[18], 71), 0),
        "qkv_mean": bell_draw(seeds[8], (D, 3 * D), NPARAMS ** -0.5, 0.0034179688, ((0, 32),), jnp.float32),
        "proj_mean": bell_draw(seeds[9], (D, D), (20 * NPARAMS) ** -0.5, 0.0007324219, ((0, 32),), jnp.float32),
        "up_mean": bell_draw(seeds[10], (D, FF), (20 * NPARAMS) ** -0.5, 0.0007324219, ((0, 32),), jnp.float32),
        "down_mean": bell_draw(seeds[11], (FF, D), (64 * NPARAMS) ** -0.5, 0.0004272461, ((0, 32),), jnp.float32),
        "norm_mean": bell_draw(seeds[12], (4, D), (NPARAMS // 9) ** -0.5, 0.009765625, ((1, 32),), jnp.float32),
        "qkv_second": jnp.clip(jnp.exp(math.log(1.2707384939858457e-06) - 1.3862944 * jax.random.uniform(seeds[13], (D, 3 * D), jnp.float32) ** levels(seeds[13], (D, 3 * D), ((0, 32),), -0.2, 0.2)), 3.1768462349646143e-07, 1.2707384939858457e-06),
        "proj_second": jnp.clip(jnp.exp(math.log(6.353692327820681e-08) - 1.3862944 * jax.random.uniform(seeds[14], (D, D), jnp.float32) ** levels(seeds[14], (D, D), ((0, 32),), -0.2, 0.2)), 1.5884230819551703e-08, 6.353692327820681e-08),
        "up_second": jnp.clip(jnp.exp(math.log(6.353692327820681e-08) - 1.3862944 * jax.random.uniform(seeds[15], (D, FF), jnp.float32) ** levels(seeds[15], (D, FF), ((0, 32),), -0.2, 0.2)), 1.5884230819551703e-08, 6.353692327820681e-08),
        "down_second": jnp.clip(jnp.exp(math.log(1.985528896852884e-08) - 1.3862944 * jax.random.uniform(seeds[16], (FF, D), jnp.float32) ** levels(seeds[16], (FF, D), ((0, 32),), -0.2, 0.2)), 4.96382224213221e-09, 1.985528896852884e-08),
        "norm_second": jnp.clip(jnp.exp(math.log(1.1436645763751585e-05) - 1.3862944 * jax.random.uniform(seeds[17], (4, D), jnp.float32) ** levels(seeds[17], (4, D), ((1, 32),), -0.2, 0.2)), 2.8591614409378963e-06, 1.1436645763751585e-05),
    }


@jax.custom_vjp
def low(v):
    return lax.optimization_barrier(v.astype(jnp.bfloat16)).astype(jnp.float32)

@jax.custom_vjp
def low_back(v):
    return v

def low_keep(v):
    return (low(v), None)

def low_pass(kept, grad):
    return (grad,)

def back_keep(v):
    return (v, None)

def back_low(kept, grad):
    return (low(grad),)
low.defvjp(low_keep, low_pass)
low_back.defvjp(back_keep, back_low)
HIGH = lax.Precision.HIGHEST
LN_EPS = 1e-05
NEG_FILL = -1e+30
CLIP = 1.0
BETA = 0.5
ADAM_EPS = 1e-08
DECAY = 0.1
RATES = (0.02, 0.3, 0.02, 0.02, 0.5)

def layer_norm(vector, gain, shift):
    centre = lax.optimization_barrier(jnp.mean(vector, axis=-1, keepdims=True))
    centred = vector - centre
    spread = lax.optimization_barrier(jnp.mean(centred * centred, axis=-1, keepdims=True))
    return centred * lax.rsqrt(spread + LN_EPS) * gain + shift

def attend(query, keys, values, key_ok, summ_keys, summ_values, summ_ok, first_span):
    block_rows = query.shape[0]
    spans = block_rows // SPAN
    shape = (spans, SPAN, HEADS, HD)
    query_s = query.reshape(shape)
    keys_s = keys.reshape(shape)
    values_s = values.reshape(shape)
    near = jnp.einsum('sqhd,skhd->shqk', query_s, keys_s, precision=HIGH) * 0.125
    far = jnp.einsum('sqhd,nhd->shqn', query_s, summ_keys, precision=HIGH) * 0.125
    scores = low_back(jnp.concatenate([near, far], axis=-1))
    causal = jnp.arange(SPAN)[:, None] >= jnp.arange(SPAN)[None, :]
    near_ok = causal[None, None] & key_ok.reshape(spans, SPAN)[:, None, None, :]
    span_index = first_span + jnp.arange(spans, dtype=jnp.int32)
    far_ok = (jnp.arange(SPANS, dtype=jnp.int32)[None, :] < span_index[:, None]) & summ_ok[None, :]
    allowed = jnp.concatenate([jnp.broadcast_to(near_ok, (spans, HEADS, SPAN, SPAN)), jnp.broadcast_to(far_ok[:, None, None, :], (spans, HEADS, SPAN, SPANS))], axis=-1)
    scores = jnp.where(allowed, scores, NEG_FILL)
    peak = lax.optimization_barrier(jnp.max(scores, axis=-1, keepdims=True))
    expo = jnp.exp(scores - peak)
    probs = low(expo / lax.optimization_barrier(jnp.sum(expo, axis=-1, keepdims=True)))
    mixed = jnp.einsum('shqk,skhd->sqhd', probs[..., :SPAN], values_s, precision=HIGH)
    mixed = mixed + jnp.einsum('shqn,nhd->sqhd', probs[..., SPAN:], summ_values, precision=HIGH)
    return mixed.reshape(block_rows, HEADS * HD)

def sequence_forward(params, seq_in, length):
    qkv_w, proj_w, up_w, down_w, norms = params
    key_valid = jnp.arange(SEQLEN, dtype=jnp.int32) < length
    valid_f = key_valid.astype(jnp.float32)
    counts = lax.optimization_barrier(jnp.sum(valid_f.reshape(SPANS, SPAN), axis=1))
    summ_scale = lax.rsqrt(jnp.maximum(counts, 1.0))
    summ_ok = counts > 0.5
    normed_one = low(layer_norm(seq_in, norms[0], norms[1]))
    mixed = low(low_back(jnp.dot(normed_one, qkv_w, precision=HIGH)))
    query = mixed[:, :D].reshape(SEQLEN, HEADS, HD)
    keys = mixed[:, D:2 * D].reshape(SEQLEN, HEADS, HD)
    values = mixed[:, 2 * D:].reshape(SEQLEN, HEADS, HD)
    masked_keys = (keys * valid_f[:, None, None]).reshape(SPANS, SPAN, HEADS, HD)
    masked_values = (values * valid_f[:, None, None]).reshape(SPANS, SPAN, HEADS, HD)
    summ_keys = low(lax.optimization_barrier(jnp.sum(masked_keys, axis=1)) * summ_scale[:, None, None])
    summ_values = low(lax.optimization_barrier(jnp.sum(masked_values, axis=1)) * summ_scale[:, None, None])
    block_rows = min(512, TOK_DEV)

    def one_block(block_index):
        begin = block_index * block_rows
        query_b = lax.dynamic_slice_in_dim(query, begin, block_rows, 0)
        keys_b = lax.dynamic_slice_in_dim(keys, begin, block_rows, 0)
        values_b = lax.dynamic_slice_in_dim(values, begin, block_rows, 0)
        okay_b = lax.dynamic_slice_in_dim(key_valid, begin, block_rows, 0)
        return attend(query_b, keys_b, values_b, okay_b, summ_keys, summ_values, summ_ok, begin // SPAN)
    attn = lax.map(jax.checkpoint(one_block), jnp.arange(SEQLEN // block_rows, dtype=jnp.int32))
    attn_out = low(low_back(attn.reshape(SEQLEN, D)))
    resid = seq_in + low_back(jnp.dot(attn_out, proj_w, precision=HIGH))
    normed_two = low(layer_norm(resid, norms[2], norms[3]))
    pre_act = low_back(jnp.dot(normed_two, up_w, precision=HIGH))
    activ = low(jax.nn.gelu(pre_act, approximate=True))
    return resid + jnp.dot(activ, down_w, precision=HIGH)

def reference(inputs, out_grad, lengths, qkv_weight, proj_weight, up_weight, down_weight, norm_params, qkv_mean, proj_mean, up_mean, down_mean, norm_mean, qkv_second, proj_second, up_second, down_second, norm_second):
    masters = (qkv_weight, proj_weight, up_weight, down_weight, norm_params)
    copies = tuple((low(master) for master in masters))

    def forward(params, seq_inputs):

        def per_sequence(item):
            return sequence_forward(params, item[0], item[1])
        return lax.map(jax.checkpoint(per_sequence), (seq_inputs, lengths))
    outputs, pullback = jax.vjp(forward, copies, inputs.astype(jnp.float32))
    grads, input_grad = pullback(out_grad.astype(jnp.float32))
    total = sum((jnp.sum(grad * grad) for grad in grads))
    grad_norm = jnp.sqrt(total)
    factor = jnp.minimum(1.0, CLIP / (grad_norm + 1e-06))
    fix = 1.0 - BETA ** STEP
    firsts = (qkv_mean, proj_mean, up_mean, down_mean, norm_mean)
    seconds = (qkv_second, proj_second, up_second, down_second, norm_second)
    moments, squares, fresh = ([], [], [])
    for grad, master, first, second, rate in zip(grads, masters, firsts, seconds, RATES):
        clipped = grad * factor
        moment = BETA * first + (1.0 - BETA) * clipped
        square = BETA * second + (1.0 - BETA) * clipped * clipped
        update = moment / fix / (jnp.sqrt(square / fix) + ADAM_EPS)
        moments.append(moment)
        squares.append(square)
        fresh.append(master - rate * (update + DECAY * master))
    shift_clipped = grads[4][3] * factor
    return (outputs.astype(jnp.bfloat16), input_grad, grad_norm, moments[0], moments[1], moments[2], moments[3], moments[4], squares[0], squares[1], squares[2], squares[3], squares[4], fresh[0], fresh[1], fresh[2], fresh[3], fresh[4], shift_clipped)
```

```python
import functools
import jax
import jax.numpy as jnp
from jax import lax
from jax.experimental import pallas as pl
from jax.experimental.pallas import tpu as pltpu
from jax.sharding import PartitionSpec as P

HEADS = 8
HD = 64
SPAN = 128
STEP = 10
LN_EPS = 1e-05
NEG_FILL = -1e30
CLIP = 1.0
BETA = 0.5
ADAM_EPS = 1e-08
DECAY = 0.1
RATES = (0.02, 0.3, 0.02, 0.02, 0.5)
BF = jnp.bfloat16
F32 = jnp.float32
LANES = 128
VMEM_LIMIT = 56 * 1024 * 1024


def dot(a, b, dims=((1,), (0,))):
    return lax.dot_general(a, b, (dims, ((), ())), preferred_element_type=F32)


def dot_nt(a, b):
    return dot(a, b, ((1,), (1,)))


def normalize(x):
    inv = 1.0 / x.shape[-1]
    centred = x - jnp.sum(x, axis=-1, keepdims=True) * inv
    spread = jnp.sum(centred * centred, axis=-1, keepdims=True) * inv
    rstd = lax.rsqrt(spread + LN_EPS)
    return centred * rstd, rstd


def norm_back(grad, gain, xhat, rstd):
    inv = 1.0 / grad.shape[-1]
    e = grad * gain
    mean_e = jnp.sum(e, axis=-1, keepdims=True) * inv
    mean_ex = jnp.sum(e * xhat, axis=-1, keepdims=True) * inv
    return rstd * (e - mean_e - xhat * mean_ex)


def qkv_tile(x, norms_ref, weight_ref):
    xhat, _ = normalize(x.astype(F32))
    normed = (xhat * norms_ref[0:1, :] + norms_ref[1:2, :]).astype(BF)
    return dot(normed, weight_ref[...]).astype(BF)


def span_scale(length, begin, shape):
    count = jnp.clip(length - begin, 1, SPAN)
    return lax.rsqrt(jnp.full(shape, count, jnp.int32).astype(F32))


def span_sum(kv, length, begin):
    row = lax.broadcasted_iota(jnp.int32, kv.shape, 0)
    kept = jnp.where(row < length - begin, kv.astype(F32), 0.0)
    total = jnp.sum(kept, axis=0, keepdims=True)
    return total * span_scale(length, begin, total.shape)


def stack_heads(pair):
    lane = lax.broadcasted_iota(jnp.int32, pair.shape, 1)
    zero = jnp.zeros_like(pair)
    return jnp.concatenate(
        [jnp.where(lane < HD, pair, zero), jnp.where(lane >= HD, pair, zero)], axis=0
    )


def fold_heads(both):
    picked = jnp.concatenate([both[:HD, :SPAN], both[HD:, SPAN:]], axis=0)
    return picked.T


def masked_scores(keys, query2, near_cap, far_cap):
    raw = dot_nt(keys, query2)
    far = raw.shape[0] - SPAN
    key_pos = lax.broadcasted_iota(jnp.int32, (SPAN, 2 * SPAN), 0)
    near = jnp.where(key_pos <= near_cap, raw[:SPAN], NEG_FILL)
    summ_pos = lax.broadcasted_iota(jnp.int32, (far, 2 * SPAN), 0)
    far = jnp.where(summ_pos < far_cap, raw[SPAN:], NEG_FILL)
    return jnp.concatenate([near, far], axis=0)


def span_caps(length, span):
    query_pos = lax.broadcasted_iota(jnp.int32, (1, 2 * SPAN), 1) & (SPAN - 1)
    near_cap = jnp.minimum(query_pos, length - span * SPAN - 1)
    far_cap = jnp.minimum(span, (length + SPAN - 1) // SPAN)
    return near_cap, far_cap


def attend_span(mixed_ref, row, width, summ_ref, summ_vt_ref, caps, out_ref, out_row, lse_store):
    near_cap, far_cap = caps
    rows = pl.ds(row, SPAN)
    for pair in range(width // LANES):
        at = pair * LANES
        query2 = stack_heads(mixed_ref[rows, at : at + LANES] * BF(0.125))
        keys = jnp.concatenate(
            [mixed_ref[rows, width + at : width + at + LANES], summ_ref[:, at : at + LANES]], axis=0
        )
        values_t = jnp.concatenate(
            [
                mixed_ref[rows, 2 * width + at : 2 * width + at + LANES].T,
                summ_vt_ref[at : at + LANES, :],
            ],
            axis=1,
        )
        scores = masked_scores(keys, query2, near_cap, far_cap)
        peak = jnp.max(scores, axis=0, keepdims=True)
        expo = jnp.exp(scores - peak)
        total = jnp.sum(expo, axis=0, keepdims=True)
        out_t = dot(values_t, expo.astype(BF)) * (1.0 / total)
        out_ref[pl.ds(out_row, SPAN), at : at + LANES] = fold_heads(out_t).astype(BF)
        lse_store(pair, peak + jnp.log(total))


def attend_back_span(
    mixed_ref, grad_ref, row, width, summ_ref, summ_kt_ref, caps, lse_load, dq_ref, dkv_ref, out_row, dsumm_ref
):
    near_cap, far_cap = caps
    rows = pl.ds(row, SPAN)
    for pair in range(width // LANES):
        at = pair * LANES
        query2 = stack_heads(mixed_ref[rows, at : at + LANES] * BF(0.125))
        grad2 = stack_heads(grad_ref[rows, at : at + LANES])
        near_k = mixed_ref[rows, width + at : width + at + LANES]
        keys = jnp.concatenate([near_k, summ_ref[:, at : at + LANES]], axis=0)
        keys_t = jnp.concatenate([near_k.T, summ_kt_ref[at : at + LANES, :]], axis=1)
        values = jnp.concatenate(
            [
                mixed_ref[rows, 2 * width + at : 2 * width + at + LANES],
                summ_ref[:, width + at : width + at + LANES],
            ],
            axis=0,
        )
        scores = masked_scores(keys, query2, near_cap, far_cap)
        probs = jnp.exp(scores - lse_load(pair))
        dprob = dot_nt(values, grad2)
        delta = jnp.sum(probs * dprob, axis=0, keepdims=True)
        dscore = (probs * (dprob - delta)).astype(BF)
        dq = fold_heads(dot(keys_t, dscore)) * 0.125
        dk = dot(dscore, query2)
        dv = dot(probs.astype(BF), grad2)
        out = pl.ds(out_row, SPAN)
        dq_ref[out, at : at + LANES] = dq.astype(dq_ref.dtype)
        dkv_ref[out, at : at + LANES] = dk[:SPAN]
        dkv_ref[out, width + at : width + at + LANES] = dv[:SPAN]
        dsumm_ref[:, at : at + LANES] += dk[SPAN:]
        dsumm_ref[:, width + at : width + at + LANES] += dv[SPAN:]


GELU_A = 0.7978845608
GELU_B = 0.044715


def gelu_parts(t):
    sq = t * t
    th = jnp.tanh(t * (GELU_A + (GELU_A * GELU_B) * sq))
    half = 0.5 * th + 0.5
    slope = half + (2.0 * t) * (half * (1.0 - half)) * (GELU_A + (3.0 * GELU_A * GELU_B) * sq)
    return t * half, slope


def qkv_kernel(info_ref, x_ref, norms_ref, weight_ref, mixed_ref, summ_ref, sum_scr):
    step = pl.program_id(0)
    tile, width = x_ref.shape
    length, first_span = info_ref[0], info_ref[1]
    mixed = qkv_tile(x_ref[...], norms_ref, weight_ref)
    mixed_ref[...] = mixed
    per = tile // SPAN
    for part in range(per):
        span = step * per + part
        sum_scr[pl.ds(span, 1), :] = span_sum(
            mixed[part * SPAN : (part + 1) * SPAN, width:], length, (first_span + span) * SPAN
        )

    @pl.when(step == pl.num_programs(0) - 1)
    def _():
        summ_ref[...] = sum_scr[...].astype(BF)


def attend_kernel(info_ref, mixed_ref, summ_ref, out_ref, lse_ref, vt_scr):
    step = pl.program_id(0)
    width = out_ref.shape[1]

    @pl.when(step == 0)
    def _():
        vt_scr[...] = summ_ref[:, width:].T

    caps = span_caps(info_ref[0], info_ref[1] + step)

    def keep(pair, value):
        lse_ref[0, pair : pair + 1, :] = value

    attend_span(mixed_ref, 0, width, summ_ref, vt_scr, caps, out_ref, 0, keep)


def attend_back_kernel(info_ref, mixed_ref, grad_ref, lse_ref, summ_ref, dq_ref, dkv_ref, dsumm_ref, kt_scr):
    step = pl.program_id(0)
    width = dq_ref.shape[1]

    @pl.when(step == 0)
    def _():
        kt_scr[...] = summ_ref[:, :width].T
        dsumm_ref[...] = jnp.zeros_like(dsumm_ref)

    caps = span_caps(info_ref[0], info_ref[1] + step)
    attend_back_span(
        mixed_ref, grad_ref, 0, width, summ_ref, kt_scr, caps,
        lambda pair: lse_ref[0, pair : pair + 1, :], dq_ref, dkv_ref, 0, dsumm_ref,
    )


def mlp_kernel(
    x_ref, attn_ref, og_ref, norms_ref, proj_ref, up_ref, down_ref,
    out_ref, resid_grad_ref, attn_grad_ref, proj_grad_ref, up_grad_ref, down_grad_ref, norm_grad_ref,
    activ_scr, pre_grad_scr, n2t_scr, attnt_scr, ogt_scr, pig_scr, norm_scr,
):
    step = pl.program_id(0)
    tile, width = x_ref.shape
    hidden = up_ref.shape[1]
    rows = pl.ds(pl.multiple_of(step * tile, tile), tile)
    chunk = 512
    attn = attn_ref[...]
    grad = og_ref[...]
    resid = x_ref[...].astype(F32) + dot(attn, proj_ref[...])
    xhat, rstd = normalize(resid)
    gain = norms_ref[2:3, :]
    normed = (xhat * gain + norms_ref[3:4, :]).astype(BF)
    attnt_scr[:, rows] = attn.T
    n2t_scr[:, rows] = normed.T
    ogt_scr[:, rows] = grad.T
    acc = resid
    back = jnp.zeros_like(resid)
    for at in range(0, hidden, chunk):
        pre = dot(normed, up_ref[:, at : at + chunk])
        act_grad = dot_nt(grad, down_ref[at : at + chunk, :])
        value, slope = gelu_parts(pre)
        activ = value.astype(BF)
        pre_grad = (act_grad * slope).astype(BF)
        activ_scr[rows, at : at + chunk] = activ
        pre_grad_scr[rows, at : at + chunk] = pre_grad
        acc = acc + dot(activ, down_ref[at : at + chunk, :])
        back = back + dot_nt(pre_grad, up_ref[:, at : at + chunk])
    out_ref[...] = acc.astype(BF)
    resid_grad = grad.astype(F32) + norm_back(back, gain, xhat, rstd)
    resid_grad_ref[...] = resid_grad
    pig = resid_grad.astype(BF)
    pig_scr[rows, :] = pig
    attn_grad_ref[...] = dot_nt(pig, proj_ref[...]).astype(BF)
    gain_part = jnp.sum(back * xhat, axis=0, keepdims=True)
    shift_part = jnp.sum(back, axis=0, keepdims=True)
    part = jnp.concatenate([gain_part, shift_part], axis=0)

    @pl.when(step == 0)
    def _():
        norm_scr[...] = part

    @pl.when(step > 0)
    def _():
        norm_scr[...] += part

    @pl.when(step == pl.num_programs(0) - 1)
    def _():
        norm_grad_ref[...] = norm_scr[...]
        proj_grad_ref[...] = dot(attnt_scr[...], pig_scr[...])
        cols = 256

        def one(index, carry):
            c = pl.ds(pl.multiple_of(index * cols, cols), cols)
            up_grad_ref[:, c] = dot(n2t_scr[...], pre_grad_scr[:, c])
            down_grad_ref[c, :] = dot(ogt_scr[...], activ_scr[:, c]).T
            return carry

        lax.fori_loop(0, hidden // cols, one, 0)


def final_kernel(
    info_ref, x_ref, dq_ref, dkv_ref, extra_ref, resid_grad_ref, norms_ref, weight_ref,
    input_grad_ref, qkv_grad_ref, norm_grad_ref, mg_scr, n1t_scr, norm_scr,
):
    step = pl.program_id(0)
    tile, width = x_ref.shape
    rows = pl.ds(pl.multiple_of(step * tile, tile), tile)
    length, first_span = info_ref[0], info_ref[1]
    xhat, rstd = normalize(x_ref[...].astype(F32))
    gain = norms_ref[0:1, :]
    normed = (xhat * gain + norms_ref[1:2, :]).astype(BF)
    n1t_scr[:, rows] = normed.T
    per = tile // SPAN
    parts = []
    for part in range(per):
        span = step * per + part
        begin = (first_span + span) * SPAN
        extra = extra_ref[pl.ds(span, 1), :]
        extra = extra * span_scale(length, begin, extra.shape)
        local = dkv_ref[part * SPAN : (part + 1) * SPAN, :]
        pos = lax.broadcasted_iota(jnp.int32, local.shape, 0)
        parts.append(local + jnp.where(pos < length - begin, extra, 0.0))
    mg = jnp.concatenate([dq_ref[...], jnp.concatenate(parts, axis=0).astype(BF)], axis=1)
    mg_scr[rows, :] = mg
    back = dot_nt(mg, weight_ref[...])
    input_grad_ref[...] = resid_grad_ref[...] + norm_back(back, gain, xhat, rstd)
    gain_part = jnp.sum(back * xhat, axis=0, keepdims=True)
    shift_part = jnp.sum(back, axis=0, keepdims=True)
    part = jnp.concatenate([gain_part, shift_part], axis=0)

    @pl.when(step == 0)
    def _():
        norm_scr[...] = part

    @pl.when(step > 0)
    def _():
        norm_scr[...] += part

    @pl.when(step == pl.num_programs(0) - 1)
    def _():
        norm_grad_ref[...] = norm_scr[...]
        cols = 256

        def one(index, carry):
            c = pl.ds(pl.multiple_of(index * cols, cols), cols)
            qkv_grad_ref[:, c] = dot(n1t_scr[...], mg_scr[:, c])
            return carry

        lax.fori_loop(0, qkv_grad_ref.shape[1] // cols, one, 0)


def whole(shape):
    return pl.BlockSpec(shape, lambda i: (0,) * len(shape))


def by_rows(tile, width):
    return pl.BlockSpec((tile, width), lambda i: (i, 0))


SCALARS = pl.BlockSpec(memory_space=pltpu.SMEM)
PARAMS = pltpu.CompilerParams(vmem_limit_bytes=VMEM_LIMIT)


def regroup(grad, dim, outer, inner):
    shape = grad.shape
    piece = shape[dim] // (outer * inner)
    split = grad.reshape(shape[:dim] + (outer, inner, piece) + shape[dim + 1 :])
    return jnp.swapaxes(split, dim, dim + 1).reshape(shape)


def body(
    inputs, out_grad, lengths, qkv_weight, proj_weight, up_weight, down_weight, norm_params,
    qkv_mean, proj_mean, up_mean, down_mean, norm_mean,
    qkv_second, proj_second, up_second, down_second, norm_second,
):
    both = ("batch", "seq")
    gather = lambda w, axis: lax.all_gather(w.astype(BF), both, axis=axis, tiled=True)
    qkv_full = gather(qkv_weight, 0)
    proj_full = gather(proj_weight, 0)
    up_full = gather(up_weight, 0)
    down_full = gather(down_weight, 0)
    norms = gather(norm_params, 1).astype(F32)
    rows, width = inputs.shape[1], inputs.shape[2]
    hidden = up_full.shape[1]
    local = rows // SPAN
    spans = local * lax.axis_size("seq")
    first_span = lax.axis_index("seq") * local
    length = lengths[0]
    info = jnp.stack([length, first_span.astype(jnp.int32)])
    x, grad_rows = inputs[0], out_grad[0]
    tile = 256
    steps = rows // tile
    sds = jax.ShapeDtypeStruct
    mixed, own_summ = pl.pallas_call(
        qkv_kernel,
        grid=(steps,),
        in_specs=[SCALARS, by_rows(tile, width), whole(norms.shape), whole(qkv_full.shape)],
        out_specs=[by_rows(tile, 3 * width), whole((local, 2 * width))],
        out_shape=[sds((rows, 3 * width), BF), sds((local, 2 * width), BF)],
        scratch_shapes=[pltpu.VMEM((local, 2 * width), F32)],
        compiler_params=PARAMS,
        name="qkv",
    )(info, x, norms, qkv_full)
    summ = lax.all_gather(own_summ, "seq", axis=0, tiled=True)
    pairs = width // LANES
    lse_spec = pl.BlockSpec((1, pairs, 2 * SPAN), lambda i: (i, 0, 0))
    attn_out, lse = pl.pallas_call(
        attend_kernel,
        grid=(local,),
        in_specs=[SCALARS, by_rows(SPAN, 3 * width), whole(summ.shape)],
        out_specs=[by_rows(SPAN, width), lse_spec],
        out_shape=[sds((rows, width), BF), sds((local, pairs, 2 * SPAN), F32)],
        scratch_shapes=[pltpu.VMEM((width, spans), BF)],
        compiler_params=PARAMS,
        name="attend",
    )(info, mixed, summ)
    outputs, resid_grad, attn_grad, proj_grad, up_grad, down_grad, norm_two = pl.pallas_call(
        mlp_kernel,
        grid=(steps,),
        in_specs=[by_rows(tile, width)] * 3
        + [whole(norms.shape), whole(proj_full.shape), whole(up_full.shape), whole(down_full.shape)],
        out_specs=[by_rows(tile, width)] * 3
        + [whole(proj_full.shape), whole(up_full.shape), whole(down_full.shape), whole((2, width))],
        out_shape=[
            sds((rows, width), BF), sds((rows, width), F32), sds((rows, width), BF),
            sds(proj_full.shape, F32), sds(up_full.shape, F32), sds(down_full.shape, F32),
            sds((2, width), F32),
        ],
        scratch_shapes=[
            pltpu.VMEM((rows, hidden), BF), pltpu.VMEM((rows, hidden), BF),
            pltpu.VMEM((width, rows), BF), pltpu.VMEM((width, rows), BF), pltpu.VMEM((width, rows), BF),
            pltpu.VMEM((rows, width), BF), pltpu.VMEM((2, width), F32),
        ],
        compiler_params=PARAMS,
        name="mlp",
    )(x, attn_out, grad_rows, norms, proj_full, up_full, down_full)
    dq, dkv, dsumm = pl.pallas_call(
        attend_back_kernel,
        grid=(local,),
        in_specs=[SCALARS, by_rows(SPAN, 3 * width), by_rows(SPAN, width), lse_spec, whole(summ.shape)],
        out_specs=[by_rows(SPAN, width), by_rows(SPAN, 2 * width), whole((spans, 2 * width))],
        out_shape=[sds((rows, width), BF), sds((rows, 2 * width), F32), sds((spans, 2 * width), F32)],
        scratch_shapes=[pltpu.VMEM((width, spans), BF)],
        compiler_params=PARAMS,
        name="attend_back",
    )(info, mixed, attn_grad, lse, summ)
    extra = lax.psum_scatter(dsumm, "seq", scatter_dimension=0, tiled=True)
    input_grad, qkv_grad, norm_one = pl.pallas_call(
        final_kernel,
        grid=(steps,),
        in_specs=[
            SCALARS, by_rows(tile, width), by_rows(tile, width), by_rows(tile, 2 * width),
            whole(extra.shape), by_rows(tile, width), whole(norms.shape), whole(qkv_full.shape),
        ],
        out_specs=[by_rows(tile, width), whole(qkv_full.shape), whole((2, width))],
        out_shape=[sds((rows, width), F32), sds(qkv_full.shape, F32), sds((2, width), F32)],
        scratch_shapes=[
            pltpu.VMEM((rows, 3 * width), BF), pltpu.VMEM((width, rows), BF), pltpu.VMEM((2, width), F32),
        ],
        compiler_params=PARAMS,
        name="final",
    )(info, x, dq, dkv, extra, resid_grad, norms, qkv_full)
    norm_grad = jnp.concatenate([norm_one, norm_two], axis=0)
    groups = lax.axis_size("batch")
    seq_count = lax.axis_size("seq")
    reduced = []
    for grad, dim in ((qkv_grad, 0), (proj_grad, 0), (up_grad, 0), (down_grad, 0), (norm_grad, 1)):
        part = lax.psum_scatter(
            regroup(grad, dim, groups, seq_count), "seq", scatter_dimension=dim, tiled=True
        )
        reduced.append(lax.psum_scatter(part, "batch", scatter_dimension=dim, tiled=True))
    local_squares = sum((jnp.sum(grad * grad) for grad in reduced))
    grad_norm = jnp.sqrt(lax.psum(local_squares, both))
    factor = jnp.minimum(1.0, CLIP / (grad_norm + 1e-06))
    fix = 1.0 - BETA**STEP
    masters = (qkv_weight, proj_weight, up_weight, down_weight, norm_params)
    firsts = (qkv_mean, proj_mean, up_mean, down_mean, norm_mean)
    seconds = (qkv_second, proj_second, up_second, down_second, norm_second)
    moments, squares, fresh = ([], [], [])
    for grad, master, first, second, rate in zip(reduced, masters, firsts, seconds, RATES):
        clipped = grad * factor
        moment = BETA * first + (1.0 - BETA) * clipped
        square = BETA * second + (1.0 - BETA) * clipped * clipped
        update = moment / fix / (jnp.sqrt(square / fix) + ADAM_EPS)
        moments.append(moment)
        squares.append(square)
        fresh.append(master - rate * (update + DECAY * master))
    shift_clipped = reduced[4][3] * factor
    return (
        outputs[None], input_grad[None], grad_norm, *moments, *squares, *fresh, shift_clipped,
    )


def solution(mesh):
    tokens = P("batch", "seq", None)
    owned = P(("batch", "seq"), None)
    columns = P(None, ("batch", "seq"))
    state = (owned, owned, owned, owned, columns)
    return jax.shard_map(
        body,
        mesh=mesh,
        in_specs=(tokens, tokens, P("batch")) + state * 3,
        out_specs=(tokens, tokens, P()) + state * 3 + (P(("batch", "seq")),),
        check_vma=False,
    )
```

```python
import functools
import jax
import jax.numpy as jnp
from jax import lax
from jax.experimental import pallas as pl
from jax.experimental.pallas import tpu as pltpu
from jax.sharding import PartitionSpec as P

HEADS = 8
HD = 64
SPAN = 128
STEP = 10
LN_EPS = 1e-05
NEG_FILL = -1e30
CLIP = 1.0
BETA = 0.5
ADAM_EPS = 1e-08
DECAY = 0.1
RATES = (0.02, 0.3, 0.02, 0.02, 0.5)
BF = jnp.bfloat16
F32 = jnp.float32
LANES = 128
VMEM_LIMIT = 56 * 1024 * 1024


def dot(a, b, dims=((1,), (0,))):
    return lax.dot_general(a, b, (dims, ((), ())), preferred_element_type=F32)


def dot_nt(a, b):
    return dot(a, b, ((1,), (1,)))


def normalize(x):
    inv = 1.0 / x.shape[-1]
    centred = x - jnp.sum(x, axis=-1, keepdims=True) * inv
    spread = jnp.sum(centred * centred, axis=-1, keepdims=True) * inv
    rstd = lax.rsqrt(spread + LN_EPS)
    return centred * rstd, rstd


def norm_back(grad, gain, xhat, rstd):
    inv = 1.0 / grad.shape[-1]
    e = grad * gain
    mean_e = jnp.sum(e, axis=-1, keepdims=True) * inv
    mean_ex = jnp.sum(e * xhat, axis=-1, keepdims=True) * inv
    return rstd * (e - mean_e - xhat * mean_ex)


def qkv_tile(x, norms_ref, weight_ref):
    xhat, _ = normalize(x.astype(F32))
    normed = (xhat * norms_ref[0:1, :] + norms_ref[1:2, :]).astype(BF)
    return dot(normed, weight_ref[...]).astype(BF)


def span_scale(length, begin, shape):
    count = jnp.clip(length - begin, 1, SPAN)
    return lax.rsqrt(jnp.full(shape, count, jnp.int32).astype(F32))


def span_sum(kv, length, begin):
    row = lax.broadcasted_iota(jnp.int32, kv.shape, 0)
    kept = jnp.where(row < length - begin, kv.astype(F32), 0.0)
    total = jnp.sum(kept, axis=0, keepdims=True)
    return total * span_scale(length, begin, total.shape)


def stack_heads(pair):
    lane = lax.broadcasted_iota(jnp.int32, pair.shape, 1)
    zero = jnp.zeros_like(pair)
    return jnp.concatenate(
        [jnp.where(lane < HD, pair, zero), jnp.where(lane >= HD, pair, zero)], axis=0
    )


def fold_heads(both):
    picked = jnp.concatenate([both[:HD, :SPAN], both[HD:, SPAN:]], axis=0)
    return picked.T


def masked_scores(keys, query2, near_cap, far_cap):
    raw = dot_nt(keys, query2)
    far = raw.shape[0] - SPAN
    key_pos = lax.broadcasted_iota(jnp.int32, (SPAN, 2 * SPAN), 0)
    near = jnp.where(key_pos <= near_cap, raw[:SPAN], NEG_FILL)
    summ_pos = lax.broadcasted_iota(jnp.int32, (far, 2 * SPAN), 0)
    far = jnp.where(summ_pos < far_cap, raw[SPAN:], NEG_FILL)
    return jnp.concatenate([near, far], axis=0)


def span_caps(length, span):
    query_pos = lax.broadcasted_iota(jnp.int32, (1, 2 * SPAN), 1) & (SPAN - 1)
    near_cap = jnp.minimum(query_pos, length - span * SPAN - 1)
    far_cap = jnp.minimum(span, (length + SPAN - 1) // SPAN)
    return near_cap, far_cap


def attend_span(mixed_ref, row, width, summ_ref, summ_vt_ref, caps, out_ref, out_row, lse_store):
    near_cap, far_cap = caps
    rows = pl.ds(row, SPAN)
    for pair in range(width // LANES):
        at = pair * LANES
        query2 = stack_heads(mixed_ref[rows, at : at + LANES] * BF(0.125))
        keys = jnp.concatenate(
            [mixed_ref[rows, width + at : width + at + LANES], summ_ref[:, at : at + LANES]], axis=0
        )
        values_t = jnp.concatenate(
            [
                mixed_ref[rows, 2 * width + at : 2 * width + at + LANES].T,
                summ_vt_ref[at : at + LANES, :],
            ],
            axis=1,
        )
        scores = masked_scores(keys, query2, near_cap, far_cap)
        peak = jnp.max(scores, axis=0, keepdims=True)
        expo = jnp.exp(scores - peak)
        total = jnp.sum(expo, axis=0, keepdims=True)
        out_t = dot(values_t, expo.astype(BF)) * (1.0 / total)
        out_ref[pl.ds(out_row, SPAN), at : at + LANES] = fold_heads(out_t).astype(BF)
        lse_store(pair, peak + jnp.log(total))


def attend_back_span(
    mixed_ref, grad_ref, row, width, summ_ref, summ_kt_ref, caps, lse_load, dq_ref, dkv_ref, out_row, dsumm_ref
):
    near_cap, far_cap = caps
    rows = pl.ds(row, SPAN)
    for pair in range(width // LANES):
        at = pair * LANES
        query2 = stack_heads(mixed_ref[rows, at : at + LANES] * BF(0.125))
        grad2 = stack_heads(grad_ref[rows, at : at + LANES])
        near_k = mixed_ref[rows, width + at : width + at + LANES]
        keys = jnp.concatenate([near_k, summ_ref[:, at : at + LANES]], axis=0)
        keys_t = jnp.concatenate([near_k.T, summ_kt_ref[at : at + LANES, :]], axis=1)
        values = jnp.concatenate(
            [
                mixed_ref[rows, 2 * width + at : 2 * width + at + LANES],
                summ_ref[:, width + at : width + at + LANES],
            ],
            axis=0,
        )
        scores = masked_scores(keys, query2, near_cap, far_cap)
        probs = jnp.exp(scores - lse_load(pair))
        dprob = dot_nt(values, grad2)
        delta = jnp.sum(probs * dprob, axis=0, keepdims=True)
        dscore = (probs * (dprob - delta)).astype(BF)
        dq = fold_heads(dot(keys_t, dscore)) * 0.125
        dk = dot(dscore, query2)
        dv = dot(probs.astype(BF), grad2)
        out = pl.ds(out_row, SPAN)
        dq_ref[out, at : at + LANES] = dq.astype(dq_ref.dtype)
        dkv_ref[out, at : at + LANES] = dk[:SPAN]
        dkv_ref[out, width + at : width + at + LANES] = dv[:SPAN]
        dsumm_ref[:, at : at + LANES] += dk[SPAN:]
        dsumm_ref[:, width + at : width + at + LANES] += dv[SPAN:]


GELU_A = 0.7978845608
GELU_B = 0.044715


def gelu_parts(t):
    sq = t * t
    th = jnp.tanh(t * (GELU_A + (GELU_A * GELU_B) * sq))
    half = 0.5 * th + 0.5
    slope = half + (2.0 * t) * (half * (1.0 - half)) * (GELU_A + (3.0 * GELU_A * GELU_B) * sq)
    return t * half, slope


MESH = pl.DeviceIdType.MESH


class Place:
    def __init__(self, groups, seqs):
        self.groups, self.chips = groups, seqs // 2
        self.b = lax.axis_index("batch")
        seq = lax.axis_index("seq")
        self.z, self.c = seq // 2, seq % 2
        self.other = 1 - self.c
        self.b1 = self.b + 1 - 2 * (self.b % 2)
        self.b2 = (self.b + 2) % 4
        self.b3 = self.b1 + 2 - 4 * (self.b1 // 2)

    def at(self, b, z, c):
        return (b, 2 * z + c)

    def sibling(self):
        return self.at(self.b, self.z, self.other)

    def along(self, step):
        return (self.z + step) % self.chips


def meet(place):
    barrier = pltpu.get_barrier_semaphore()
    partners = [place.sibling(), place.at(place.b1, place.z, place.c), place.at(place.b2, place.z, place.c)]
    partners += [place.at(place.b, place.along(k), place.c) for k in range(1, place.chips)]
    for partner in partners:
        pl.semaphore_signal(barrier, inc=1, device_id=partner, device_id_type=MESH)
    pl.semaphore_wait(barrier, len(partners))


class Copies:
    def __init__(self, send_sems, recv_sems):
        self.send, self.recv, self.made = send_sems, recv_sems, []

    def start(self, src, dst, device):
        at = len(self.made)
        assert at < self.send.shape[0]
        copy = pltpu.make_async_remote_copy(
            src_ref=src, dst_ref=dst, send_sem=self.send.at[at], recv_sem=self.recv.at[at],
            device_id=device, device_id_type=MESH,
        )
        copy.start()
        self.made.append(copy)
        return copy

    def finish(self):
        for copy in self.made:
            copy.wait_send()


def gather_steps(place, copies, full):
    p, half = place, place.chips // 2
    low, high = pl.ds(0, half), pl.ds(half, place.chips - half)
    own = full.at[p.b, p.z, p.c]
    along = [copies.start(own, own, p.at(p.b, p.along(k), p.c)) for k in range(1, p.chips)]
    yield
    for copy in along:
        copy.wait_recv()
    column = full.at[p.b, :, p.c]
    to_x = copies.start(column, column, p.at(p.b1, p.z, p.c))
    to_y = copies.start(column, column, p.at(p.b2, p.z, p.c))
    sib = [copies.start(column, column, p.sibling())]
    yield
    to_x.wait_recv()
    block = full.at[p.b1, low, p.c]
    on_y = copies.start(block, block, p.at(p.b2, p.z, p.c))
    to_y.wait_recv()
    block = full.at[p.b2, high, p.c]
    on_x = copies.start(block, block, p.at(p.b1, p.z, p.c))
    for b in (p.b1, p.b2):
        column = full.at[b, :, p.c]
        sib.append(copies.start(column, column, p.sibling()))
    yield
    for copy, part in ((on_y, low), (on_x, high)):
        copy.wait_recv()
        block = full.at[p.b3, part, p.c]
        sib.append(copies.start(block, block, p.sibling()))
    yield
    for copy in sib:
        copy.wait_recv()


GATHER_COPIES = 12


def add_into(acc, index, other, part=None):
    acc[index] = (acc[index].astype(F32) + other.astype(F32)).astype(acc.dtype)


def scatter_steps(place, copies, grad, acc, got, near, far, last, result):
    p, half = place, place.chips // 2
    low, high = pl.ds(0, half), pl.ds(half, place.chips - half)
    groups, chips = p.groups, p.chips
    swap = copies.start(grad.at[:, :, p.other], got, p.sibling())
    yield
    swap.wait_recv()

    def add_one(i, carry):
        b, z = i // chips, i % chips
        acc[b, z] = (grad[b, z, p.c].astype(F32) + got[b, z].astype(F32)).astype(BF)
        return carry

    lax.fori_loop(0, groups * chips, add_one, 0)
    on_y = copies.start(acc.at[p.b3, low], far.at[0], p.at(p.b2, p.z, p.c))
    on_x = copies.start(acc.at[p.b3, high], far.at[1], p.at(p.b1, p.z, p.c))
    early_x = copies.start(acc.at[p.b1, high], near.at[0, high], p.at(p.b1, p.z, p.c))
    early_y = copies.start(acc.at[p.b2, low], near.at[1, low], p.at(p.b2, p.z, p.c))
    yield
    on_y.wait_recv()
    for z in range(half):
        acc[p.b1, z] = (acc[p.b1, z].astype(F32) + far[0, z].astype(F32)).astype(BF)
    late_x = copies.start(acc.at[p.b1, low], near.at[0, low], p.at(p.b1, p.z, p.c))
    on_x.wait_recv()
    for z in range(half, chips):
        acc[p.b2, z] = (acc[p.b2, z].astype(F32) + far[1, z - half].astype(F32)).astype(BF)
    late_y = copies.start(acc.at[p.b2, high], near.at[1, high], p.at(p.b2, p.z, p.c))
    yield
    for copy in (early_x, early_y, late_x, late_y):
        copy.wait_recv()
    for z in range(chips):
        acc[p.b, z] = (acc[p.b, z].astype(F32) + near[0, z].astype(F32) + near[1, z].astype(F32)).astype(BF)
    along = []
    for k in range(1, chips):
        to = p.along(k)
        along.append(copies.start(acc.at[p.b, to], last.at[k - 1], p.at(p.b, to, p.c)))
    yield
    total = acc[p.b, p.z].astype(F32)
    for k, copy in enumerate(along):
        copy.wait_recv()
        total = total + last[k].astype(F32)
    result[...] = total


SCATTER_COPIES = 10


def scatter_scratch(groups, chips, rows, cols):
    half = chips // 2
    return [
        pltpu.VMEM((groups, chips, rows, cols), BF),
        pltpu.VMEM((groups, chips, rows, cols), BF),
        pltpu.VMEM((2, chips, rows, cols), BF),
        pltpu.VMEM((2, half, rows, cols), BF),
        pltpu.VMEM((chips - 1, rows, cols), BF),
    ]


def share_sum_steps(place, copies, mine, slots, column, result):
    p = place
    stage = mine[...]
    partners = (p.sibling(), p.at(p.b1, p.z, p.c), p.at(p.b2, p.z, p.c))
    for at, device in enumerate(partners):
        slots[3 + at] = stage
        copy = copies.start(slots.at[3 + at], slots.at[at], device)
        yield
        copy.wait_recv()
        stage = stage + slots[at]
    column[p.z] = stage
    own = column.at[p.z]
    along = [copies.start(own, own, p.at(p.b, p.along(k), p.c)) for k in range(1, p.chips)]
    yield
    for copy in along:
        copy.wait_recv()
    total = column[0]
    for z in range(1, p.chips):
        total = total + column[z]
    result[...] = total


SHARE_COPIES = 6


def run_all(*steps):
    live = list(steps)
    while live:
        for step in list(live):
            try:
                next(step)
            except StopIteration:
                live.remove(step)


def gather_kernel(
    groups, seqs, qkv_ref, proj_ref, up_ref, down_ref, norm_ref,
    qkv_full, pu_full, down_full, norms_out, norm_full, send_sems, recv_sems,
):
    p = Place(groups, seqs)
    width = proj_ref.shape[1]
    b, z, c = p.b, p.z, p.c
    index = b * seqs + 2 * z + c
    qkv_full[b, z, c] = qkv_ref[...].astype(BF)
    pu_full[b, z, c, :, :width] = proj_ref[...].astype(BF)
    pu_full[b, z, c, :, width:] = up_ref[...].astype(BF)
    down_full[b, z, c] = down_ref[...].astype(BF)
    rows, piece = norm_ref.shape
    per = LANES // piece
    tiled = jnp.concatenate([norm_ref[...].astype(BF).astype(F32)] * per, axis=1)
    lane = lax.broadcasted_iota(jnp.int32, tiled.shape, 1)
    norm_full[b, z, c] = jnp.where(lane // piece == index % per, tiled, 0.0)
    meet(p)
    copies = Copies(send_sems, recv_sems)
    run_all(*(gather_steps(p, copies, full) for full in (norm_full, qkv_full, pu_full, down_full)))
    for block in range(norms_out.shape[1] // LANES):
        total = None
        for device in range(block * per, (block + 1) * per):
            one = norm_full[device // seqs, device % seqs // 2, device % 2]
            total = one if total is None else total + one
        norms_out[:, block * LANES : (block + 1) * LANES] = total
    copies.finish()


def summary_gather_kernel(groups, seqs, own_ref, full_ref, send_sems, recv_sems):
    p = Place(groups, seqs)
    full_ref[p.z, p.c] = own_ref[...]
    meet(p)
    copies = Copies(send_sems, recv_sems)
    own = full_ref.at[p.z, p.c]
    along = [copies.start(own, own, p.at(p.b, p.along(k), p.c)) for k in range(1, p.chips)]
    sib = [copies.start(own, own, p.sibling())]
    for k, copy in enumerate(along):
        copy.wait_recv()
        block = full_ref.at[(p.z + p.chips - 1 - k) % p.chips, p.c]
        sib.append(copies.start(block, block, p.sibling()))
    for copy in sib:
        copy.wait_recv()
    copies.finish()


def summary_scatter_kernel(groups, seqs, grad_ref, out_ref, got, low, last, send_sems, recv_sems):
    p = Place(groups, seqs)
    meet(p)
    copies = Copies(send_sems, recv_sems)
    swap = copies.start(grad_ref.at[:, p.other], got, p.sibling())
    swap.wait_recv()
    along = []
    for k in range(1, p.chips):
        to = p.along(k)
        low[k - 1] = (grad_ref[to, p.c] + got[to]).astype(BF)
        along.append(copies.start(low.at[k - 1], last.at[k - 1], p.at(p.b, to, p.c)))
    total = grad_ref[p.z, p.c] + got[p.z]
    for k, copy in enumerate(along):
        copy.wait_recv()
        total = total + last[k].astype(F32)
    out_ref[...] = total
    copies.finish()


def reduce_kernel(
    groups, seqs, qkv_ref, pu_ref, down_ref, norm_ref, qkv_out, pu_out, down_out, norm_out, total_out, *scratch
):
    *buffers, slots, column, sq_mine, sq_slots, sq_column, send_sems, recv_sems = scratch
    p = Place(groups, seqs)
    meet(p)
    copies = Copies(send_sems, recv_sems)
    steps = [share_sum_steps(p, copies, norm_ref, slots, column, norm_out)]
    for at, (grad, out) in enumerate(((down_ref, down_out), (pu_ref, pu_out), (qkv_ref, qkv_out))):
        steps.append(scatter_steps(p, copies, grad, *buffers[5 * at : 5 * at + 5], out))
    run_all(*steps)
    local = sum(jnp.sum(jnp.square(out[...]), keepdims=True) for out in (qkv_out, pu_out, down_out))
    sq_mine[...] = jnp.broadcast_to(local, sq_mine.shape)
    run_all(share_sum_steps(p, copies, sq_mine, sq_slots, sq_column, total_out))
    total_out[...] = total_out[...] + jnp.sum(jnp.square(norm_out[...]), keepdims=True)
    copies.finish()


def adam(grad, master, first, second, rate, moment_out, square_out, fresh_out):
    fix = 1.0 - BETA**STEP
    moment = BETA * first + (1.0 - BETA) * grad
    square = BETA * second + (1.0 - BETA) * grad * grad
    update = moment / fix / (jnp.sqrt(square / fix) + ADAM_EPS)
    moment_out[...] = moment
    square_out[...] = square
    fresh_out[...] = master - rate * (update + DECAY * master)


def update_kernel(index_ref, total_ref, qkv_grad, pu_grad, down_grad, norm_grad, *refs):
    state, outs = refs[:15], refs[15:]
    norm_out, moments, squares, fresh = outs[0], outs[1:6], outs[6:11], outs[11:16]
    grad_norm = jnp.sqrt(total_ref[0:1, 0:1])
    norm_out[...] = grad_norm
    factor = jnp.minimum(1.0, CLIP / (grad_norm + 1e-06))
    width = state[1].shape[1]
    piece = state[4].shape[1]
    per = LANES // piece
    index = index_ref[0]
    block = norm_grad[:, pl.ds(pl.multiple_of(index // per * LANES, LANES), LANES)]
    own = pltpu.roll(block, (LANES - index % per * piece) % LANES, 1)[:, :piece]
    grads = (qkv_grad[...], pu_grad[:, :width], pu_grad[:, width:], down_grad[...], own)
    for at, (grad, rate) in enumerate(zip(grads, RATES)):
        adam(
            grad * factor, state[at][...], state[5 + at][...], state[10 + at][...], rate,
            moments[at], squares[at], fresh[at],
        )
    outs[16][...] = own[3:4] * factor


def qkv_kernel(info_ref, x_ref, norms_ref, weight_ref, mixed_ref, summ_ref, sum_scr):
    step = pl.program_id(0)
    tile, width = x_ref.shape
    length, first_span = info_ref[0], info_ref[1]
    mixed = qkv_tile(x_ref[...], norms_ref, weight_ref)
    mixed_ref[...] = mixed
    per = tile // SPAN
    for part in range(per):
        span = step * per + part
        sum_scr[pl.ds(span, 1), :] = span_sum(
            mixed[part * SPAN : (part + 1) * SPAN, width:], length, (first_span + span) * SPAN
        )

    @pl.when(step == pl.num_programs(0) - 1)
    def _():
        summ_ref[...] = sum_scr[...].astype(BF)


def attend_kernel(info_ref, mixed_ref, summ_ref, out_ref, lse_ref, vt_scr):
    step = pl.program_id(0)
    width = out_ref.shape[1]

    @pl.when(step == 0)
    def _():
        vt_scr[...] = summ_ref[:, width:].T

    caps = span_caps(info_ref[0], info_ref[1] + step)

    def keep(pair, value):
        lse_ref[0, pair : pair + 1, :] = value

    attend_span(mixed_ref, 0, width, summ_ref, vt_scr, caps, out_ref, 0, keep)


def attend_back_kernel(info_ref, mixed_ref, grad_ref, lse_ref, summ_ref, dq_ref, dkv_ref, dsumm_ref, kt_scr):
    step = pl.program_id(0)
    width = dq_ref.shape[1]

    @pl.when(step == 0)
    def _():
        kt_scr[...] = summ_ref[:, :width].T
        dsumm_ref[...] = jnp.zeros_like(dsumm_ref)

    caps = span_caps(info_ref[0], info_ref[1] + step)
    attend_back_span(
        mixed_ref, grad_ref, 0, width, summ_ref, kt_scr, caps,
        lambda pair: lse_ref[0, pair : pair + 1, :], dq_ref, dkv_ref, 0, dsumm_ref,
    )


def mlp_kernel(
    x_ref, attn_ref, og_ref, norms_ref, pu_ref, down_ref,
    out_ref, resid_grad_ref, attn_grad_ref, pu_grad_ref, down_grad_ref, norm_grad_ref,
    activ_scr, pre_grad_scr, n2t_scr, attnt_scr, ogt_scr, pig_scr, norm_scr,
):
    step = pl.program_id(0)
    tile, width = x_ref.shape
    hidden = down_ref.shape[0]
    rows = pl.ds(pl.multiple_of(step * tile, tile), tile)
    chunk = 512
    attn = attn_ref[...]
    grad = og_ref[...]
    resid = x_ref[...].astype(F32) + dot(attn, pu_ref[:, :width])
    xhat, rstd = normalize(resid)
    gain = norms_ref[2:3, :]
    normed = (xhat * gain + norms_ref[3:4, :]).astype(BF)
    attnt_scr[:, rows] = attn.T
    n2t_scr[:, rows] = normed.T
    ogt_scr[:, rows] = grad.T
    acc = resid
    back = jnp.zeros_like(resid)
    for at in range(0, hidden, chunk):
        pre = dot(normed, pu_ref[:, width + at : width + at + chunk])
        act_grad = dot_nt(grad, down_ref[at : at + chunk, :])
        value, slope = gelu_parts(pre)
        activ = value.astype(BF)
        pre_grad = (act_grad * slope).astype(BF)
        activ_scr[rows, at : at + chunk] = activ
        pre_grad_scr[rows, at : at + chunk] = pre_grad
        acc = acc + dot(activ, down_ref[at : at + chunk, :])
        back = back + dot_nt(pre_grad, pu_ref[:, width + at : width + at + chunk])
    out_ref[...] = acc.astype(BF)
    resid_grad = grad.astype(F32) + norm_back(back, gain, xhat, rstd)
    resid_grad_ref[...] = resid_grad
    pig = resid_grad.astype(BF)
    pig_scr[rows, :] = pig
    attn_grad_ref[...] = dot_nt(pig, pu_ref[:, :width]).astype(BF)
    gain_part = jnp.sum(back * xhat, axis=0, keepdims=True)
    shift_part = jnp.sum(back, axis=0, keepdims=True)
    part = jnp.concatenate([gain_part, shift_part], axis=0)

    @pl.when(step == 0)
    def _():
        norm_scr[...] = part

    @pl.when(step > 0)
    def _():
        norm_scr[...] += part

    @pl.when(step == pl.num_programs(0) - 1)
    def _():
        norm_grad_ref[...] = norm_scr[...]
        pu_grad_ref[:, :width] = dot(attnt_scr[...], pig_scr[...]).astype(BF)
        cols = 256

        def one(index, carry):
            c = pl.ds(pl.multiple_of(index * cols, cols), cols)
            out = pl.ds(pl.multiple_of(width + index * cols, cols), cols)
            pu_grad_ref[:, out] = dot(n2t_scr[...], pre_grad_scr[:, c]).astype(BF)
            down_grad_ref[c, :] = dot(ogt_scr[...], activ_scr[:, c]).T.astype(BF)
            return carry

        lax.fori_loop(0, hidden // cols, one, 0)


def final_kernel(
    info_ref, x_ref, dq_ref, dkv_ref, extra_ref, resid_grad_ref, norms_ref, weight_ref,
    input_grad_ref, qkv_grad_ref, norm_grad_ref, mg_scr, n1t_scr, norm_scr,
):
    step = pl.program_id(0)
    tile, width = x_ref.shape
    rows = pl.ds(pl.multiple_of(step * tile, tile), tile)
    length, first_span = info_ref[0], info_ref[1]
    xhat, rstd = normalize(x_ref[...].astype(F32))
    gain = norms_ref[0:1, :]
    normed = (xhat * gain + norms_ref[1:2, :]).astype(BF)
    n1t_scr[:, rows] = normed.T
    per = tile // SPAN
    parts = []
    for part in range(per):
        span = step * per + part
        begin = (first_span + span) * SPAN
        extra = extra_ref[pl.ds(span, 1), :]
        extra = extra * span_scale(length, begin, extra.shape)
        local = dkv_ref[part * SPAN : (part + 1) * SPAN, :]
        pos = lax.broadcasted_iota(jnp.int32, local.shape, 0)
        parts.append(local + jnp.where(pos < length - begin, extra, 0.0))
    mg = jnp.concatenate([dq_ref[...], jnp.concatenate(parts, axis=0).astype(BF)], axis=1)
    mg_scr[rows, :] = mg
    back = dot_nt(mg, weight_ref[...])
    input_grad_ref[...] = resid_grad_ref[...] + norm_back(back, gain, xhat, rstd)
    gain_part = jnp.sum(back * xhat, axis=0, keepdims=True)
    shift_part = jnp.sum(back, axis=0, keepdims=True)
    part = jnp.concatenate([gain_part, shift_part], axis=0)

    @pl.when(step == 0)
    def _():
        norm_scr[...] = part

    @pl.when(step > 0)
    def _():
        norm_scr[...] += part

    @pl.when(step == pl.num_programs(0) - 1)
    def _():
        norm_grad_ref[...] = norm_scr[...]
        cols = 256

        def one(index, carry):
            c = pl.ds(pl.multiple_of(index * cols, cols), cols)
            qkv_grad_ref[:, c] = dot(n1t_scr[...], mg_scr[:, c]).astype(BF)
            return carry

        lax.fori_loop(0, qkv_grad_ref.shape[1] // cols, one, 0)


def whole(shape):
    return pl.BlockSpec(shape, lambda i: (0,) * len(shape))


def by_rows(tile, width):
    return pl.BlockSpec((tile, width), lambda i: (i, 0))


SCALARS = pl.BlockSpec(memory_space=pltpu.SMEM)
PARAMS = pltpu.CompilerParams(vmem_limit_bytes=VMEM_LIMIT)


def remote_call(kernel, groups, seqs, name, collective_id, out_shape, scratch, copies):
    return pl.pallas_call(
        functools.partial(kernel, groups, seqs),
        out_shape=out_shape,
        scratch_shapes=list(scratch)
        + [pltpu.SemaphoreType.DMA((copies,)), pltpu.SemaphoreType.DMA((copies,))],
        compiler_params=pltpu.CompilerParams(
            vmem_limit_bytes=VMEM_LIMIT, collective_id=collective_id, has_side_effects=True
        ),
        name=name,
    )


def regroup(grad, dim, outer, inner):
    shape = grad.shape
    piece = shape[dim] // (outer * inner)
    split = grad.reshape(shape[:dim] + (outer, inner, piece) + shape[dim + 1 :])
    return jnp.swapaxes(split, dim, dim + 1).reshape(shape)


def gather_plain(state):
    both = ("batch", "seq")
    qkv, proj, up, down = (lax.all_gather(w.astype(BF), both, axis=0, tiled=True) for w in state[:4])
    norms = lax.all_gather(state[4].astype(BF), both, axis=1, tiled=True).astype(F32)
    return qkv, jnp.concatenate([proj, up], axis=1), down, norms


def reduce_plain(qkv_grad, pu_grad, down_grad, norm_grad):
    groups, seqs = lax.axis_size("batch"), lax.axis_size("seq")
    reduced = []
    for grad, dim in ((qkv_grad, 0), (pu_grad, 0), (down_grad, 0)):
        part = lax.psum_scatter(
            regroup(grad.astype(F32), dim, groups, seqs), "seq", scatter_dimension=dim, tiled=True
        )
        reduced.append(lax.psum_scatter(part, "batch", scatter_dimension=dim, tiled=True))
    norm_total = lax.psum(norm_grad, ("batch", "seq"))
    squares = lax.psum(sum(jnp.sum(grad * grad) for grad in reduced), ("batch", "seq"))
    squares = squares + jnp.sum(norm_total * norm_total)
    return (*reduced, norm_total, jnp.broadcast_to(squares, (8, LANES)))


def body(groups, seqs, inputs, out_grad, lengths, *state):
    sds = jax.ShapeDtypeStruct
    rows, width = inputs.shape[1], inputs.shape[2]
    own_rows, down_rows = state[0].shape[0], state[3].shape[0]
    hidden = state[2].shape[1]
    chips = seqs // 2
    direct = groups == 4 and seqs % 4 == 0 and own_rows % 16 == 0
    grid3 = (groups, chips, 2)
    if direct:
        qkv_full, pu_full, down_full, norms = remote_call(
            gather_kernel, groups, seqs, "gather", 0,
            [
                sds((*grid3, own_rows, 3 * width), BF), sds((*grid3, own_rows, width + hidden), BF),
                sds((*grid3, down_rows, width), BF), sds((4, width), F32),
            ],
            [pltpu.VMEM((*grid3, 4, LANES), F32)], 4 * GATHER_COPIES,
        )(*state[:5])
        qkv_full = qkv_full.reshape(width, 3 * width)
        pu_full = pu_full.reshape(width, width + hidden)
        down_full = down_full.reshape(hidden, width)
    else:
        qkv_full, pu_full, down_full, norms = gather_plain(state[:5])
    local = rows // SPAN
    spans = local * seqs
    first_span = lax.axis_index("seq") * local
    length = lengths[0]
    info = jnp.stack([length, first_span.astype(jnp.int32)])
    x, grad_rows = inputs[0], out_grad[0]
    tile = 256
    steps = rows // tile
    mixed, own_summ = pl.pallas_call(
        qkv_kernel,
        grid=(steps,),
        in_specs=[SCALARS, by_rows(tile, width), whole(norms.shape), whole(qkv_full.shape)],
        out_specs=[by_rows(tile, 3 * width), whole((local, 2 * width))],
        out_shape=[sds((rows, 3 * width), BF), sds((local, 2 * width), BF)],
        scratch_shapes=[pltpu.VMEM((local, 2 * width), F32)],
        compiler_params=PARAMS,
        name="qkv",
    )(info, x, norms, qkv_full)
    if direct:
        summ = remote_call(
            summary_gather_kernel, groups, seqs, "summary_gather", 1,
            sds((chips, 2, local, 2 * width), BF), [], 2 * chips,
        )(own_summ).reshape(spans, 2 * width)
    else:
        summ = lax.all_gather(own_summ, "seq", axis=0, tiled=True)
    pairs = width // LANES
    lse_spec = pl.BlockSpec((1, pairs, 2 * SPAN), lambda i: (i, 0, 0))
    attn_out, lse = pl.pallas_call(
        attend_kernel,
        grid=(local,),
        in_specs=[SCALARS, by_rows(SPAN, 3 * width), whole(summ.shape)],
        out_specs=[by_rows(SPAN, width), lse_spec],
        out_shape=[sds((rows, width), BF), sds((local, pairs, 2 * SPAN), F32)],
        scratch_shapes=[pltpu.VMEM((width, spans), BF)],
        compiler_params=PARAMS,
        name="attend",
    )(info, mixed, summ)
    outputs, resid_grad, attn_grad, pu_grad, down_grad, norm_two = pl.pallas_call(
        mlp_kernel,
        grid=(steps,),
        in_specs=[by_rows(tile, width)] * 3
        + [whole(norms.shape), whole(pu_full.shape), whole(down_full.shape)],
        out_specs=[by_rows(tile, width)] * 3
        + [whole(pu_full.shape), whole(down_full.shape), whole((2, width))],
        out_shape=[
            sds((rows, width), BF), sds((rows, width), F32), sds((rows, width), BF),
            sds(pu_full.shape, BF), sds(down_full.shape, BF), sds((2, width), F32),
        ],
        scratch_shapes=[
            pltpu.VMEM((rows, hidden), BF), pltpu.VMEM((rows, hidden), BF),
            pltpu.VMEM((width, rows), BF), pltpu.VMEM((width, rows), BF), pltpu.VMEM((width, rows), BF),
            pltpu.VMEM((rows, width), BF), pltpu.VMEM((2, width), F32),
        ],
        compiler_params=PARAMS,
        name="mlp",
    )(x, attn_out, grad_rows, norms, pu_full, down_full)
    dq, dkv, dsumm = pl.pallas_call(
        attend_back_kernel,
        grid=(local,),
        in_specs=[SCALARS, by_rows(SPAN, 3 * width), by_rows(SPAN, width), lse_spec, whole(summ.shape)],
        out_specs=[by_rows(SPAN, width), by_rows(SPAN, 2 * width), whole((spans, 2 * width))],
        out_shape=[sds((rows, width), BF), sds((rows, 2 * width), F32), sds((spans, 2 * width), F32)],
        scratch_shapes=[pltpu.VMEM((width, spans), BF)],
        compiler_params=PARAMS,
        name="attend_back",
    )(info, mixed, attn_grad, lse, summ)
    if direct:
        block = (local, 2 * width)
        extra = remote_call(
            summary_scatter_kernel, groups, seqs, "summary_scatter", 2, sds(block, F32),
            [
                pltpu.VMEM((chips, *block), F32), pltpu.VMEM((chips - 1, *block), BF),
                pltpu.VMEM((chips - 1, *block), BF),
            ],
            chips,
        )(dsumm.reshape(chips, 2, *block))
    else:
        extra = lax.psum_scatter(dsumm, "seq", scatter_dimension=0, tiled=True)
    input_grad, qkv_grad, norm_one = pl.pallas_call(
        final_kernel,
        grid=(steps,),
        in_specs=[
            SCALARS, by_rows(tile, width), by_rows(tile, width), by_rows(tile, 2 * width),
            whole(extra.shape), by_rows(tile, width), whole(norms.shape), whole(qkv_full.shape),
        ],
        out_specs=[by_rows(tile, width), whole(qkv_full.shape), whole((2, width))],
        out_shape=[sds((rows, width), F32), sds(qkv_full.shape, BF), sds((2, width), F32)],
        scratch_shapes=[
            pltpu.VMEM((rows, 3 * width), BF), pltpu.VMEM((width, rows), BF), pltpu.VMEM((2, width), F32),
        ],
        compiler_params=PARAMS,
        name="final",
    )(info, x, dq, dkv, extra, resid_grad, norms, qkv_full)
    norm_grad = jnp.concatenate([norm_one, norm_two], axis=0)
    if direct:
        shapes = ((down_rows, width), (own_rows, width + hidden), (own_rows, 3 * width))
        scratch = [buffer for shape in shapes for buffer in scatter_scratch(groups, chips, *shape)]
        scratch += [
            pltpu.VMEM((6, 4, width), F32), pltpu.VMEM((chips, 4, width), F32),
            pltpu.VMEM((8, LANES), F32), pltpu.VMEM((6, 8, LANES), F32), pltpu.VMEM((chips, 8, LANES), F32),
        ]
        reduced = remote_call(
            reduce_kernel, groups, seqs, "reduce", 3,
            [sds(shape, F32) for shape in (*reversed(shapes), (4, width), (8, LANES))],
            scratch, 3 * SCATTER_COPIES + 2 * SHARE_COPIES,
        )(
            qkv_grad.reshape(*grid3, own_rows, 3 * width),
            pu_grad.reshape(*grid3, own_rows, width + hidden),
            down_grad.reshape(*grid3, down_rows, width), norm_grad,
        )
    else:
        reduced = reduce_plain(qkv_grad, pu_grad, down_grad, norm_grad)
    *grads, norm_total, total = reduced
    index = lax.axis_index("batch") * seqs + lax.axis_index("seq")
    owned = [sds(w.shape, F32) for w in state[:5]]
    grad_norm, *fresh, shift_clipped = pl.pallas_call(
        update_kernel,
        in_specs=[SCALARS] + [pl.BlockSpec(memory_space=pltpu.VMEM)] * 20,
        out_shape=[sds((1, 1), F32), *owned, *owned, *owned, sds((1, state[4].shape[1]), F32)],
        compiler_params=PARAMS,
        name="update",
    )(index.astype(jnp.int32)[None], total, *grads, norm_total, *state)
    return (outputs[None], input_grad[None], grad_norm[0, 0], *fresh, shift_clipped[0])


def solution(mesh):
    tokens = P("batch", "seq", None)
    owned = P(("batch", "seq"), None)
    columns = P(None, ("batch", "seq"))
    state = (owned, owned, owned, owned, columns)
    return jax.shard_map(
        functools.partial(body, mesh.shape["batch"], mesh.shape["seq"]),
        mesh=mesh,
        in_specs=(tokens, tokens, P("batch")) + state * 3,
        out_specs=(tokens, tokens, P()) + state * 3 + (P(("batch", "seq")),),
        check_vma=False,
    )
```

```python
import functools
import jax
import jax.numpy as jnp
from jax import lax
from jax.experimental import pallas as pl
from jax.experimental.pallas import tpu as pltpu
from jax.sharding import PartitionSpec as P

HEADS = 8
HD = 64
SPAN = 128
STEP = 10
LN_EPS = 1e-05
NEG_FILL = -1e30
CLIP = 1.0
BETA = 0.5
ADAM_EPS = 1e-08
DECAY = 0.1
RATES = (0.02, 0.3, 0.02, 0.02, 0.5)
BF = jnp.bfloat16
F32 = jnp.float32
LANES = 128
VMEM_LIMIT = 56 * 1024 * 1024


def dot(a, b, dims=((1,), (0,))):
    return lax.dot_general(a, b, (dims, ((), ())), preferred_element_type=F32)


def dot_nt(a, b):
    return dot(a, b, ((1,), (1,)))


def normalize(x):
    inv = 1.0 / x.shape[-1]
    centred = x - jnp.sum(x, axis=-1, keepdims=True) * inv
    spread = jnp.sum(centred * centred, axis=-1, keepdims=True) * inv
    rstd = lax.rsqrt(spread + LN_EPS)
    return centred * rstd, rstd


def norm_back(grad, gain, xhat, rstd):
    inv = 1.0 / grad.shape[-1]
    e = grad * gain
    mean_e = jnp.sum(e, axis=-1, keepdims=True) * inv
    mean_ex = jnp.sum(e * xhat, axis=-1, keepdims=True) * inv
    return rstd * (e - mean_e - xhat * mean_ex)


def qkv_tile(x, norms_ref, weight_ref):
    xhat, _ = normalize(x.astype(F32))
    normed = (xhat * norms_ref[0:1, :] + norms_ref[1:2, :]).astype(BF)
    return dot(normed, weight_ref[...]).astype(BF)


def span_scale(length, begin, shape):
    count = jnp.clip(length - begin, 1, SPAN)
    return lax.rsqrt(jnp.full(shape, count, jnp.int32).astype(F32))


def span_sum(kv, length, begin):
    row = lax.broadcasted_iota(jnp.int32, kv.shape, 0)
    kept = jnp.where(row < length - begin, kv.astype(F32), 0.0)
    total = jnp.sum(kept, axis=0, keepdims=True)
    return total * span_scale(length, begin, total.shape)


def stack_heads(pair):
    lane = lax.broadcasted_iota(jnp.int32, pair.shape, 1)
    zero = jnp.zeros_like(pair)
    return jnp.concatenate(
        [jnp.where(lane < HD, pair, zero), jnp.where(lane >= HD, pair, zero)], axis=0
    )


def fold_heads(both):
    picked = jnp.concatenate([both[:HD, :SPAN], both[HD:, SPAN:]], axis=0)
    return picked.T


def masked_scores(keys, query2, near_cap, far_cap):
    raw = dot_nt(keys, query2)
    far = raw.shape[0] - SPAN
    key_pos = lax.broadcasted_iota(jnp.int32, (SPAN, 2 * SPAN), 0)
    near = jnp.where(key_pos <= near_cap, raw[:SPAN], NEG_FILL)
    summ_pos = lax.broadcasted_iota(jnp.int32, (far, 2 * SPAN), 0)
    far = jnp.where(summ_pos < far_cap, raw[SPAN:], NEG_FILL)
    return jnp.concatenate([near, far], axis=0)


def span_caps(length, span):
    query_pos = lax.broadcasted_iota(jnp.int32, (1, 2 * SPAN), 1) & (SPAN - 1)
    near_cap = jnp.minimum(query_pos, length - span * SPAN - 1)
    far_cap = jnp.minimum(span, (length + SPAN - 1) // SPAN)
    return near_cap, far_cap


def attend_span(mixed_ref, row, width, summ_ref, summ_vt_ref, caps, out_ref, out_row, lse_store):
    near_cap, far_cap = caps
    rows = pl.ds(row, SPAN)
    for pair in range(width // LANES):
        at = pair * LANES
        query2 = stack_heads(mixed_ref[rows, at : at + LANES] * BF(0.125))
        keys = jnp.concatenate(
            [mixed_ref[rows, width + at : width + at + LANES], summ_ref[:, at : at + LANES]], axis=0
        )
        values_t = jnp.concatenate(
            [
                mixed_ref[rows, 2 * width + at : 2 * width + at + LANES].T,
                summ_vt_ref[at : at + LANES, :],
            ],
            axis=1,
        )
        scores = masked_scores(keys, query2, near_cap, far_cap)
        peak = jnp.max(scores, axis=0, keepdims=True)
        expo = jnp.exp(scores - peak)
        total = jnp.sum(expo, axis=0, keepdims=True)
        out_t = dot(values_t, expo.astype(BF)) * (1.0 / total)
        out_ref[pl.ds(out_row, SPAN), at : at + LANES] = fold_heads(out_t).astype(BF)
        lse_store(pair, peak + jnp.log(total))


def attend_back_span(
    mixed_ref, grad_ref, row, width, summ_ref, summ_kt_ref, caps, lse_load, dq_ref, dkv_ref, out_row, dsumm_ref
):
    near_cap, far_cap = caps
    rows = pl.ds(row, SPAN)
    for pair in range(width // LANES):
        at = pair * LANES
        query2 = stack_heads(mixed_ref[rows, at : at + LANES] * BF(0.125))
        grad2 = stack_heads(grad_ref[rows, at : at + LANES])
        near_k = mixed_ref[rows, width + at : width + at + LANES]
        keys = jnp.concatenate([near_k, summ_ref[:, at : at + LANES]], axis=0)
        keys_t = jnp.concatenate([near_k.T, summ_kt_ref[at : at + LANES, :]], axis=1)
        values = jnp.concatenate(
            [
                mixed_ref[rows, 2 * width + at : 2 * width + at + LANES],
                summ_ref[:, width + at : width + at + LANES],
            ],
            axis=0,
        )
        scores = masked_scores(keys, query2, near_cap, far_cap)
        probs = jnp.exp(scores - lse_load(pair))
        dprob = dot_nt(values, grad2)
        delta = jnp.sum(probs * dprob, axis=0, keepdims=True)
        dscore = (probs * (dprob - delta)).astype(BF)
        dq = fold_heads(dot(keys_t, dscore)) * 0.125
        dk = dot(dscore, query2)
        dv = dot(probs.astype(BF), grad2)
        out = pl.ds(out_row, SPAN)
        dq_ref[out, at : at + LANES] = dq.astype(dq_ref.dtype)
        dkv_ref[out, at : at + LANES] = dk[:SPAN]
        dkv_ref[out, width + at : width + at + LANES] = dv[:SPAN]
        dsumm_ref[:, at : at + LANES] += dk[SPAN:]
        dsumm_ref[:, width + at : width + at + LANES] += dv[SPAN:]


GELU_A = 0.7978845608
GELU_B = 0.044715


def gelu_parts(t):
    sq = t * t
    th = jnp.tanh(t * (GELU_A + (GELU_A * GELU_B) * sq))
    half = 0.5 * th + 0.5
    slope = half + (2.0 * t) * (half * (1.0 - half)) * (GELU_A + (3.0 * GELU_A * GELU_B) * sq)
    return t * half, slope


MESH = pl.DeviceIdType.MESH


class Place:
    def __init__(self, groups, seqs):
        self.groups, self.chips = groups, seqs // 2
        self.b = lax.axis_index("batch")
        seq = lax.axis_index("seq")
        self.z, self.c = seq // 2, seq % 2
        self.other = 1 - self.c
        self.b1 = self.b + 1 - 2 * (self.b % 2)
        self.b2 = (self.b + 2) % 4
        self.b3 = self.b1 + 2 - 4 * (self.b1 // 2)

    def at(self, b, z, c):
        return (b, 2 * z + c)

    def sibling(self):
        return self.at(self.b, self.z, self.other)

    def along(self, step):
        return (self.z + step) % self.chips


def meet(place):
    barrier = pltpu.get_barrier_semaphore()
    partners = [place.sibling(), place.at(place.b1, place.z, place.c), place.at(place.b2, place.z, place.c)]
    partners += [place.at(place.b, place.along(k), place.c) for k in range(1, place.chips)]
    for partner in partners:
        pl.semaphore_signal(barrier, inc=1, device_id=partner, device_id_type=MESH)
    pl.semaphore_wait(barrier, len(partners))


class Copies:
    def __init__(self, send_sems, recv_sems):
        self.send, self.recv, self.made = send_sems, recv_sems, []

    def start(self, src, dst, device):
        at = len(self.made)
        assert at < self.send.shape[0]
        copy = pltpu.make_async_remote_copy(
            src_ref=src, dst_ref=dst, send_sem=self.send.at[at], recv_sem=self.recv.at[at],
            device_id=device, device_id_type=MESH,
        )
        copy.start()
        self.made.append(copy)
        return copy

    def finish(self):
        for copy in self.made:
            copy.wait_send()


def gather_steps(place, copies, full):
    p, half = place, place.chips // 2
    low, high = pl.ds(0, half), pl.ds(half, place.chips - half)
    own = full.at[p.b, p.z, p.c]
    along = [copies.start(own, own, p.at(p.b, p.along(k), p.c)) for k in range(1, p.chips)]
    yield
    for copy in along:
        copy.wait_recv()
    column = full.at[p.b, :, p.c]
    to_x = copies.start(column, column, p.at(p.b1, p.z, p.c))
    to_y = copies.start(column, column, p.at(p.b2, p.z, p.c))
    sib = [copies.start(column, column, p.sibling())]
    yield
    to_x.wait_recv()
    block = full.at[p.b1, low, p.c]
    on_y = copies.start(block, block, p.at(p.b2, p.z, p.c))
    to_y.wait_recv()
    block = full.at[p.b2, high, p.c]
    on_x = copies.start(block, block, p.at(p.b1, p.z, p.c))
    for b in (p.b1, p.b2):
        column = full.at[b, :, p.c]
        sib.append(copies.start(column, column, p.sibling()))
    yield
    for copy, part in ((on_y, low), (on_x, high)):
        copy.wait_recv()
        block = full.at[p.b3, part, p.c]
        sib.append(copies.start(block, block, p.sibling()))
    yield
    for copy in sib:
        copy.wait_recv()


GATHER_COPIES = 12


def add_into(acc, index, other, part=None):
    acc[index] = (acc[index].astype(F32) + other.astype(F32)).astype(acc.dtype)


def scatter_steps(place, copies, grad, acc, got, near, far, last, result):
    p, half = place, place.chips // 2
    low, high = pl.ds(0, half), pl.ds(half, place.chips - half)
    groups, chips = p.groups, p.chips
    swap = copies.start(grad.at[:, :, p.other], got, p.sibling())
    yield
    swap.wait_recv()

    def add_one(i, carry):
        b, z = i // chips, i % chips
        acc[b, z] = (grad[b, z, p.c].astype(F32) + got[b, z].astype(F32)).astype(BF)
        return carry

    lax.fori_loop(0, groups * chips, add_one, 0)
    on_y = copies.start(acc.at[p.b3, low], far.at[0], p.at(p.b2, p.z, p.c))
    on_x = copies.start(acc.at[p.b3, high], far.at[1], p.at(p.b1, p.z, p.c))
    early_x = copies.start(acc.at[p.b1, high], near.at[0, high], p.at(p.b1, p.z, p.c))
    early_y = copies.start(acc.at[p.b2, low], near.at[1, low], p.at(p.b2, p.z, p.c))
    yield
    on_y.wait_recv()
    for z in range(half):
        acc[p.b1, z] = (acc[p.b1, z].astype(F32) + far[0, z].astype(F32)).astype(BF)
    late_x = copies.start(acc.at[p.b1, low], near.at[0, low], p.at(p.b1, p.z, p.c))
    on_x.wait_recv()
    for z in range(half, chips):
        acc[p.b2, z] = (acc[p.b2, z].astype(F32) + far[1, z - half].astype(F32)).astype(BF)
    late_y = copies.start(acc.at[p.b2, high], near.at[1, high], p.at(p.b2, p.z, p.c))
    yield
    for copy in (early_x, early_y, late_x, late_y):
        copy.wait_recv()
    for z in range(chips):
        acc[p.b, z] = (acc[p.b, z].astype(F32) + near[0, z].astype(F32) + near[1, z].astype(F32)).astype(BF)
    along = []
    for k in range(1, chips):
        to = p.along(k)
        along.append(copies.start(acc.at[p.b, to], last.at[k - 1], p.at(p.b, to, p.c)))
    yield
    total = acc[p.b, p.z].astype(F32)
    for k, copy in enumerate(along):
        copy.wait_recv()
        total = total + last[k].astype(F32)
    result[...] = total


SCATTER_COPIES = 10


def scatter_scratch(groups, chips, rows, cols):
    half = chips // 2
    return [
        pltpu.VMEM((groups, chips, rows, cols), BF),
        pltpu.VMEM((groups, chips, rows, cols), BF),
        pltpu.VMEM((2, chips, rows, cols), BF),
        pltpu.VMEM((2, half, rows, cols), BF),
        pltpu.VMEM((chips - 1, rows, cols), BF),
    ]


def share_sum_steps(place, copies, mine, slots, column, result):
    p = place
    stage = mine[...]
    partners = (p.sibling(), p.at(p.b1, p.z, p.c), p.at(p.b2, p.z, p.c))
    for at, device in enumerate(partners):
        slots[3 + at] = stage
        copy = copies.start(slots.at[3 + at], slots.at[at], device)
        yield
        copy.wait_recv()
        stage = stage + slots[at]
    column[p.z] = stage
    own = column.at[p.z]
    along = [copies.start(own, own, p.at(p.b, p.along(k), p.c)) for k in range(1, p.chips)]
    yield
    for copy in along:
        copy.wait_recv()
    total = column[0]
    for z in range(1, p.chips):
        total = total + column[z]
    result[...] = total


SHARE_COPIES = 6


def run_all(*steps):
    live = list(steps)
    while live:
        for step in list(live):
            try:
                next(step)
            except StopIteration:
                live.remove(step)


def adam(grad, master, first, second, rate, moment_out, square_out, fresh_out):
    fix = 1.0 - BETA**STEP
    moment = BETA * first + (1.0 - BETA) * grad
    square = BETA * second + (1.0 - BETA) * grad * grad
    update = moment / fix / (jnp.sqrt(square / fix) + ADAM_EPS)
    moment_out[...] = moment
    square_out[...] = square
    fresh_out[...] = master - rate * (update + DECAY * master)


def update_kernel(index_ref, total_ref, qkv_grad, pu_grad, down_grad, norm_grad, *refs):
    state, outs = refs[:15], refs[15:]
    norm_out, moments, squares, fresh = outs[0], outs[1:6], outs[6:11], outs[11:16]
    grad_norm = jnp.sqrt(total_ref[0:1, 0:1])
    norm_out[...] = grad_norm
    factor = jnp.minimum(1.0, CLIP / (grad_norm + 1e-06))
    width = state[1].shape[1]
    piece = state[4].shape[1]
    per = LANES // piece
    index = index_ref[0]
    block = norm_grad[:, pl.ds(pl.multiple_of(index // per * LANES, LANES), LANES)]
    own = pltpu.roll(block, (LANES - index % per * piece) % LANES, 1)[:, :piece]
    grads = (qkv_grad[...], pu_grad[:, :width], pu_grad[:, width:], down_grad[...], own)
    for at, (grad, rate) in enumerate(zip(grads, RATES)):
        adam(
            grad * factor, state[at][...], state[5 + at][...], state[10 + at][...], rate,
            moments[at], squares[at], fresh[at],
        )
    outs[16][...] = own[3:4] * factor


def tick(*steps):
    for step in steps:
        next(step, None)


def cast_shards(p, seqs, qkv_ref, proj_ref, up_ref, down_ref, norm_ref, qkv_full, pu_full, down_full, norm_full):
    width = proj_ref.shape[1]
    b, z, c = p.b, p.z, p.c
    index = b * seqs + 2 * z + c
    qkv_full[b, z, c] = qkv_ref[...].astype(BF)
    pu_full[b, z, c, :, :width] = proj_ref[...].astype(BF)
    pu_full[b, z, c, :, width:] = up_ref[...].astype(BF)
    down_full[b, z, c] = down_ref[...].astype(BF)
    piece = norm_ref.shape[1]
    per = LANES // piece
    tiled = jnp.concatenate([norm_ref[...].astype(BF).astype(F32)] * per, axis=1)
    lane = lax.broadcasted_iota(jnp.int32, tiled.shape, 1)
    norm_full[b, z, c] = jnp.where(lane // piece == index % per, tiled, 0.0)


def join_norms(norm_full, seqs, per, norms_out):
    for block in range(norms_out.shape[1] // LANES):
        total = None
        for device in range(block * per, (block + 1) * per):
            one = norm_full[device // seqs, device % seqs // 2, device % 2]
            total = one if total is None else total + one
        norms_out[:, block * LANES : (block + 1) * LANES] = total


def tiles(first, last, size, one):
    def step(index, carry):
        one(pl.multiple_of(index * size, size), index)
        return carry

    lax.fori_loop(first, last, step, 0)


def front_kernel(
    groups, seqs, info_ref, x_ref, qkv_ref, proj_ref, up_ref, down_ref, norm_ref,
    qkv_full, pu_full, down_full, norms_out, mixed_ref, summ_ref, attn_ref, lse_ref,
    norm_full, xhat_scr, sum_scr, vt_scr, send_sems, recv_sems,
):
    p = Place(groups, seqs)
    rows, width = x_ref.shape
    local = rows // SPAN
    length, first_span = info_ref[0], info_ref[1]
    cast_shards(
        p, seqs, qkv_ref, proj_ref, up_ref, down_ref, norm_ref, qkv_full, pu_full, down_full, norm_full
    )
    meet(p)
    copies = Copies(send_sems, recv_sems)
    in_norm, in_qkv, in_pu, in_down = (
        gather_steps(p, copies, full) for full in (norm_full, qkv_full, pu_full, down_full)
    )
    tile = 256
    count = rows // tile

    def center(at, index):
        xhat_scr[pl.ds(at, tile), :] = normalize(x_ref[pl.ds(at, tile), :].astype(F32))[0]

    tick(in_norm, in_qkv)
    tiles(0, count // 4, tile, center)
    tick(in_norm, in_qkv, in_pu)
    tiles(count // 4, count // 2, tile, center)
    tick(in_norm, in_qkv)
    tiles(count // 2, count, tile, center)
    tick(in_norm, in_qkv)
    tick(in_norm, in_qkv)
    join_norms(norm_full, seqs, LANES // norm_ref.shape[1], norms_out)
    gain, shift = norms_out[0:1, :], norms_out[1:2, :]

    def weight(begin, size):
        return qkv_full[:, :, :, :, begin : begin + size].reshape(width, size)

    def normed_of(at):
        return (xhat_scr[pl.ds(at, tile), :] * gain + shift).astype(BF)

    def keys_values(at, index):
        mixed = dot(normed_of(at), weight(width, 2 * width)).astype(BF)
        mixed_ref[pl.ds(at, tile), width:] = mixed
        for part in range(tile // SPAN):
            span = index * (tile // SPAN) + part
            sum_scr[pl.ds(span, 1), :] = span_sum(
                mixed[part * SPAN : (part + 1) * SPAN], length, (first_span + span) * SPAN
            )

    def queries(at, index):
        mixed_ref[pl.ds(at, tile), :width] = dot(normed_of(at), weight(0, width)).astype(BF)

    tiles(0, count // 2, tile, keys_values)
    tick(in_pu, in_down)
    tiles(count // 2, count, tile, keys_values)
    summ_ref[p.z, p.c] = sum_scr[...].astype(BF)
    own = summ_ref.at[p.z, p.c]
    along = [copies.start(own, own, p.at(p.b, p.along(k), p.c)) for k in range(1, p.chips)]
    sib = [copies.start(own, own, p.sibling())]
    tiles(0, count, tile, queries)
    for k, copy in enumerate(along):
        copy.wait_recv()
        block = summ_ref.at[(p.z + p.chips - 1 - k) % p.chips, p.c]
        sib.append(copies.start(block, block, p.sibling()))
    tick(in_pu)
    for copy in sib:
        copy.wait_recv()
    summ = summ_ref[...].reshape(local * seqs, 2 * width)
    vt_scr[...] = summ[:, width:].T
    summ_rows = SummaryView(summ_ref, local * seqs)

    def attend(at, index):
        caps = span_caps(length, first_span + index)

        def keep(pair, value):
            lse_ref[index, pair : pair + 1, :] = value

        attend_span(mixed_ref, at, width, summ_rows, vt_scr, caps, attn_ref, at, keep)

    for part in range(4):
        tiles(part * local // 4, (part + 1) * local // 4, SPAN, attend)
        tick(in_down, in_pu)
    tick(in_down, in_pu)
    copies.finish()


class SummaryView:
    def __init__(self, ref, rows):
        self.ref, self.rows = ref, rows

    def __getitem__(self, key):
        cols = key[1]
        return self.ref[:, :, :, cols].reshape(self.rows, cols.stop - cols.start)


def back_kernel(
    groups, seqs, info_ref, x_ref, mixed_ref, grad_ref, lse_ref, summ_ref, resid_grad_ref, pu_ref, down_ref,
    norms_ref, weight_ref, norm_two_ref,
    input_grad_ref, qkv_out, pu_out, down_out, norm_out, total_out,
    mg_scr, dkv_scr, n1t_scr, kt_scr, dsumm_scr, dsumm_got, dsumm_low, dsumm_last, extra_scr, q_grad, kv_grad,
    *scratch,
):
    *buffers, kv_own, norm_mine, slots, column, sq_mine, sq_slots, sq_column, send_sems, recv_sems = scratch
    p = Place(groups, seqs)
    rows, width = x_ref.shape
    local = rows // SPAN
    spans = local * seqs
    length, first_span = info_ref[0], info_ref[1]
    meet(p)
    copies = Copies(send_sems, recv_sems)

    def scatter(grad, at, out):
        return scatter_steps(p, copies, grad, *buffers[5 * at : 5 * at + 5], out)

    out_down, out_pu = scatter(down_ref, 0, down_out), scatter(pu_ref, 1, pu_out)
    tick(out_down, out_pu)
    kt_scr[...] = summ_ref[:, :width].T
    dsumm_scr[...] = jnp.zeros_like(dsumm_scr)

    def attend_back(at, index):
        caps = span_caps(length, first_span + index)
        attend_back_span(
            mixed_ref, grad_ref, at, width, summ_ref, kt_scr, caps,
            lambda pair: lse_ref[index, pair : pair + 1, :], mg_scr, dkv_scr, at, dsumm_scr,
        )

    for part in range(4):
        tiles(part * local // 4, (part + 1) * local // 4, SPAN, attend_back)
        tick(out_down if part % 2 == 0 else out_pu)
    swap = []
    for z in range(p.chips):
        block = dsumm_scr.at[pl.ds(pl.multiple_of((2 * z + p.other) * local, local), local)]
        swap.append(copies.start(block, dsumm_got.at[z], p.sibling()))
    tile = 256
    count = rows // tile
    gain, shift = norms_ref[0:1, :], norms_ref[1:2, :]

    def recompute(at, index):
        xhat, _ = normalize(x_ref[pl.ds(at, tile), :].astype(F32))
        n1t_scr[:, pl.ds(at, tile)] = (xhat * gain + shift).astype(BF).T

    tiles(0, count, tile, recompute)
    for copy in swap:
        copy.wait_recv()

    def half_sum(z):
        mine = dsumm_scr[pl.ds(pl.multiple_of((2 * z + p.c) * local, local), local), :]
        return mine + dsumm_got[z]

    along = []
    for k in range(1, p.chips):
        to = p.along(k)
        dsumm_low[k - 1] = half_sum(to).astype(BF)
        along.append(copies.start(dsumm_low.at[k - 1], dsumm_last.at[k - 1], p.at(p.b, to, p.c)))
    per_block = n1t_scr.shape[0] // (groups * seqs)

    def weight_grad(into, begin, size):
        block = dot(n1t_scr[...], mg_scr[:, begin : begin + size]).astype(BF)
        return block.reshape(groups, p.chips, 2, per_block, size)

    cols = 256
    for at in range(0, width, cols):
        q_grad[:, :, :, :, at : at + cols] = weight_grad(q_grad, at, cols)
    out_q = scatter(q_grad, 2, qkv_out.at[:, :width])
    tick(out_q, out_down, out_pu)

    def back_q(at, index):
        input_grad_ref[pl.ds(at, tile), :] = dot_nt(mg_scr[pl.ds(at, tile), :width], weight_ref[:, :width])

    tiles(0, count, tile, back_q)
    total = half_sum(p.z)
    for k, copy in enumerate(along):
        copy.wait_recv()
        total = total + dsumm_last[k].astype(F32)
    extra_scr[...] = total
    tick(out_down)

    def add_extra(at, index):
        begin = (first_span + index) * SPAN
        extra = extra_scr[pl.ds(index, 1), :]
        extra = extra * span_scale(length, begin, extra.shape)
        here = dkv_scr[pl.ds(at, SPAN), :]
        pos = lax.broadcasted_iota(jnp.int32, here.shape, 0)
        mg_scr[pl.ds(at, SPAN), width:] = (here + jnp.where(pos < length - begin, extra, 0.0)).astype(BF)

    tiles(0, local, SPAN, add_extra)
    for at in range(0, 2 * width, cols):
        kv_grad[:, :, :, :, at : at + cols] = weight_grad(kv_grad, width + at, cols)
    out_kv = scatter(kv_grad, 3, kv_own)
    tick(out_kv, out_q, out_pu, out_down)
    norm_mine[0:2, :] = jnp.zeros_like(norm_mine[0:2, :])
    norm_mine[2:4, :] = norm_two_ref[...]

    def finish(at, index):
        here = pl.ds(at, tile)
        xhat, rstd = normalize(x_ref[here, :].astype(F32))
        back = input_grad_ref[here, :] + dot_nt(mg_scr[here, width:], weight_ref[:, width:])
        input_grad_ref[here, :] = resid_grad_ref[here, :] + norm_back(back, gain, xhat, rstd)
        norm_mine[0:1, :] += jnp.sum(back * xhat, axis=0, keepdims=True)
        norm_mine[1:2, :] += jnp.sum(back, axis=0, keepdims=True)

    for part in range(4):
        tiles(part * count // 4, (part + 1) * count // 4, tile, finish)
        tick(out_kv, out_q, out_pu, out_down)
    norm_sum = share_sum_steps(p, copies, norm_mine, slots, column, norm_out)
    run_all(norm_sum, out_kv, out_q, out_pu, out_down)
    qkv_out[:, width:] = kv_own[...]
    local_sum = sum(jnp.sum(jnp.square(out[...]), keepdims=True) for out in (qkv_out, pu_out, down_out))
    sq_mine[...] = jnp.broadcast_to(local_sum, sq_mine.shape)
    run_all(share_sum_steps(p, copies, sq_mine, sq_slots, sq_column, total_out))
    total_out[...] = total_out[...] + jnp.sum(jnp.square(norm_out[...]), keepdims=True)
    copies.finish()


FRONT_COPIES = 4 * GATHER_COPIES + 8
BACK_COPIES = 4 * SCATTER_COPIES + 2 * SHARE_COPIES + 8


def qkv_kernel(info_ref, x_ref, norms_ref, weight_ref, mixed_ref, summ_ref, sum_scr):
    step = pl.program_id(0)
    tile, width = x_ref.shape
    length, first_span = info_ref[0], info_ref[1]
    mixed = qkv_tile(x_ref[...], norms_ref, weight_ref)
    mixed_ref[...] = mixed
    per = tile // SPAN
    for part in range(per):
        span = step * per + part
        sum_scr[pl.ds(span, 1), :] = span_sum(
            mixed[part * SPAN : (part + 1) * SPAN, width:], length, (first_span + span) * SPAN
        )

    @pl.when(step == pl.num_programs(0) - 1)
    def _():
        summ_ref[...] = sum_scr[...].astype(BF)


def attend_kernel(info_ref, mixed_ref, summ_ref, out_ref, lse_ref, vt_scr):
    step = pl.program_id(0)
    width = out_ref.shape[1]

    @pl.when(step == 0)
    def _():
        vt_scr[...] = summ_ref[:, width:].T

    caps = span_caps(info_ref[0], info_ref[1] + step)

    def keep(pair, value):
        lse_ref[0, pair : pair + 1, :] = value

    attend_span(mixed_ref, 0, width, summ_ref, vt_scr, caps, out_ref, 0, keep)


def attend_back_kernel(info_ref, mixed_ref, grad_ref, lse_ref, summ_ref, dq_ref, dkv_ref, dsumm_ref, kt_scr):
    step = pl.program_id(0)
    width = dq_ref.shape[1]

    @pl.when(step == 0)
    def _():
        kt_scr[...] = summ_ref[:, :width].T
        dsumm_ref[...] = jnp.zeros_like(dsumm_ref)

    caps = span_caps(info_ref[0], info_ref[1] + step)
    attend_back_span(
        mixed_ref, grad_ref, 0, width, summ_ref, kt_scr, caps,
        lambda pair: lse_ref[0, pair : pair + 1, :], dq_ref, dkv_ref, 0, dsumm_ref,
    )


def mlp_kernel(
    x_ref, attn_ref, og_ref, norms_ref, pu_ref, down_ref,
    out_ref, resid_grad_ref, attn_grad_ref, pu_grad_ref, down_grad_ref, norm_grad_ref,
    activ_scr, pre_grad_scr, n2t_scr, attnt_scr, ogt_scr, pig_scr, norm_scr,
):
    step = pl.program_id(0)
    tile, width = x_ref.shape
    hidden = down_ref.shape[0]
    rows = pl.ds(pl.multiple_of(step * tile, tile), tile)
    chunk = 512
    attn = attn_ref[...]
    grad = og_ref[...]
    resid = x_ref[...].astype(F32) + dot(attn, pu_ref[:, :width])
    xhat, rstd = normalize(resid)
    gain = norms_ref[2:3, :]
    normed = (xhat * gain + norms_ref[3:4, :]).astype(BF)
    attnt_scr[:, rows] = attn.T
    n2t_scr[:, rows] = normed.T
    ogt_scr[:, rows] = grad.T
    acc = resid
    back = jnp.zeros_like(resid)
    for at in range(0, hidden, chunk):
        pre = dot(normed, pu_ref[:, width + at : width + at + chunk])
        act_grad = dot_nt(grad, down_ref[at : at + chunk, :])
        value, slope = gelu_parts(pre)
        activ = value.astype(BF)
        pre_grad = (act_grad * slope).astype(BF)
        activ_scr[rows, at : at + chunk] = activ
        pre_grad_scr[rows, at : at + chunk] = pre_grad
        acc = acc + dot(activ, down_ref[at : at + chunk, :])
        back = back + dot_nt(pre_grad, pu_ref[:, width + at : width + at + chunk])
    out_ref[...] = acc.astype(BF)
    resid_grad = grad.astype(F32) + norm_back(back, gain, xhat, rstd)
    resid_grad_ref[...] = resid_grad
    pig = resid_grad.astype(BF)
    pig_scr[rows, :] = pig
    attn_grad_ref[...] = dot_nt(pig, pu_ref[:, :width]).astype(BF)
    gain_part = jnp.sum(back * xhat, axis=0, keepdims=True)
    shift_part = jnp.sum(back, axis=0, keepdims=True)
    part = jnp.concatenate([gain_part, shift_part], axis=0)

    @pl.when(step == 0)
    def _():
        norm_scr[...] = part

    @pl.when(step > 0)
    def _():
        norm_scr[...] += part

    @pl.when(step == pl.num_programs(0) - 1)
    def _():
        norm_grad_ref[...] = norm_scr[...]
        pu_grad_ref[:, :width] = dot(attnt_scr[...], pig_scr[...]).astype(BF)
        cols = 256

        def one(index, carry):
            c = pl.ds(pl.multiple_of(index * cols, cols), cols)
            out = pl.ds(pl.multiple_of(width + index * cols, cols), cols)
            pu_grad_ref[:, out] = dot(n2t_scr[...], pre_grad_scr[:, c]).astype(BF)
            down_grad_ref[c, :] = dot(ogt_scr[...], activ_scr[:, c]).T.astype(BF)
            return carry

        lax.fori_loop(0, hidden // cols, one, 0)


def final_kernel(
    info_ref, x_ref, dq_ref, dkv_ref, extra_ref, resid_grad_ref, norms_ref, weight_ref,
    input_grad_ref, qkv_grad_ref, norm_grad_ref, mg_scr, n1t_scr, norm_scr,
):
    step = pl.program_id(0)
    tile, width = x_ref.shape
    rows = pl.ds(pl.multiple_of(step * tile, tile), tile)
    length, first_span = info_ref[0], info_ref[1]
    xhat, rstd = normalize(x_ref[...].astype(F32))
    gain = norms_ref[0:1, :]
    normed = (xhat * gain + norms_ref[1:2, :]).astype(BF)
    n1t_scr[:, rows] = normed.T
    per = tile // SPAN
    parts = []
    for part in range(per):
        span = step * per + part
        begin = (first_span + span) * SPAN
        extra = extra_ref[pl.ds(span, 1), :]
        extra = extra * span_scale(length, begin, extra.shape)
        local = dkv_ref[part * SPAN : (part + 1) * SPAN, :]
        pos = lax.broadcasted_iota(jnp.int32, local.shape, 0)
        parts.append(local + jnp.where(pos < length - begin, extra, 0.0))
    mg = jnp.concatenate([dq_ref[...], jnp.concatenate(parts, axis=0).astype(BF)], axis=1)
    mg_scr[rows, :] = mg
    back = dot_nt(mg, weight_ref[...])
    input_grad_ref[...] = resid_grad_ref[...] + norm_back(back, gain, xhat, rstd)
    gain_part = jnp.sum(back * xhat, axis=0, keepdims=True)
    shift_part = jnp.sum(back, axis=0, keepdims=True)
    part = jnp.concatenate([gain_part, shift_part], axis=0)

    @pl.when(step == 0)
    def _():
        norm_scr[...] = part

    @pl.when(step > 0)
    def _():
        norm_scr[...] += part

    @pl.when(step == pl.num_programs(0) - 1)
    def _():
        norm_grad_ref[...] = norm_scr[...]
        cols = 256

        def one(index, carry):
            c = pl.ds(pl.multiple_of(index * cols, cols), cols)
            qkv_grad_ref[:, c] = dot(n1t_scr[...], mg_scr[:, c]).astype(BF)
            return carry

        lax.fori_loop(0, qkv_grad_ref.shape[1] // cols, one, 0)


def whole(shape):
    return pl.BlockSpec(shape, lambda i: (0,) * len(shape))


def by_rows(tile, width):
    return pl.BlockSpec((tile, width), lambda i: (i, 0))


SCALARS = pl.BlockSpec(memory_space=pltpu.SMEM)
PARAMS = pltpu.CompilerParams(vmem_limit_bytes=VMEM_LIMIT)


def remote_call(kernel, groups, seqs, name, collective_id, out_shape, scratch, copies, in_specs):
    return pl.pallas_call(
        functools.partial(kernel, groups, seqs),
        in_specs=in_specs,
        out_shape=out_shape,
        scratch_shapes=list(scratch)
        + [pltpu.SemaphoreType.DMA((copies,)), pltpu.SemaphoreType.DMA((copies,))],
        compiler_params=pltpu.CompilerParams(
            vmem_limit_bytes=VMEM_LIMIT, collective_id=collective_id, has_side_effects=True
        ),
        name=name,
    )


def regroup(grad, dim, outer, inner):
    shape = grad.shape
    piece = shape[dim] // (outer * inner)
    split = grad.reshape(shape[:dim] + (outer, inner, piece) + shape[dim + 1 :])
    return jnp.swapaxes(split, dim, dim + 1).reshape(shape)


def gather_plain(state):
    both = ("batch", "seq")
    qkv, proj, up, down = (lax.all_gather(w.astype(BF), both, axis=0, tiled=True) for w in state[:4])
    norms = lax.all_gather(state[4].astype(BF), both, axis=1, tiled=True).astype(F32)
    return qkv, jnp.concatenate([proj, up], axis=1), down, norms


def reduce_plain(qkv_grad, pu_grad, down_grad, norm_grad):
    groups, seqs = lax.axis_size("batch"), lax.axis_size("seq")
    reduced = []
    for grad, dim in ((qkv_grad, 0), (pu_grad, 0), (down_grad, 0)):
        part = lax.psum_scatter(
            regroup(grad.astype(F32), dim, groups, seqs), "seq", scatter_dimension=dim, tiled=True
        )
        reduced.append(lax.psum_scatter(part, "batch", scatter_dimension=dim, tiled=True))
    norm_total = lax.psum(norm_grad, ("batch", "seq"))
    squares = lax.psum(sum(jnp.sum(grad * grad) for grad in reduced), ("batch", "seq"))
    squares = squares + jnp.sum(norm_total * norm_total)
    return (*reduced, norm_total, jnp.broadcast_to(squares, (8, LANES)))


def mlp_call(x, attn_out, grad_rows, norms, pu_full, down_full):
    sds = jax.ShapeDtypeStruct
    rows, width = x.shape
    hidden = down_full.shape[0]
    tile = 256
    steps = rows // tile
    return pl.pallas_call(
        mlp_kernel,
        grid=(steps,),
        in_specs=[by_rows(tile, width)] * 3
        + [whole(norms.shape), whole(pu_full.shape), whole(down_full.shape)],
        out_specs=[by_rows(tile, width)] * 3
        + [whole(pu_full.shape), whole(down_full.shape), whole((2, width))],
        out_shape=[
            sds((rows, width), BF), sds((rows, width), F32), sds((rows, width), BF),
            sds(pu_full.shape, BF), sds(down_full.shape, BF), sds((2, width), F32),
        ],
        scratch_shapes=[
            pltpu.VMEM((rows, hidden), BF), pltpu.VMEM((rows, hidden), BF),
            pltpu.VMEM((width, rows), BF), pltpu.VMEM((width, rows), BF), pltpu.VMEM((width, rows), BF),
            pltpu.VMEM((rows, width), BF), pltpu.VMEM((2, width), F32),
        ],
        compiler_params=PARAMS,
        name="mlp",
    )(x, attn_out, grad_rows, norms, pu_full, down_full)


def direct_body(groups, seqs, inputs, out_grad, lengths, *state):
    sds = jax.ShapeDtypeStruct
    rows, width = inputs.shape[1], inputs.shape[2]
    own_rows, down_rows = state[0].shape[0], state[3].shape[0]
    hidden = state[2].shape[1]
    chips = seqs // 2
    grid3 = (groups, chips, 2)
    local = rows // SPAN
    spans = local * seqs
    pairs = width // LANES
    info = jnp.stack([lengths[0], (lax.axis_index("seq") * local).astype(jnp.int32)])
    x, grad_rows = inputs[0], out_grad[0]
    scalars_first = lambda n: [SCALARS] + [pl.BlockSpec(memory_space=pltpu.VMEM)] * n
    qkv_full, pu_full, down_full, norms, mixed, summ, attn_out, lse = remote_call(
        front_kernel, groups, seqs, "front", 0,
        [
            sds((*grid3, own_rows, 3 * width), BF), sds((*grid3, own_rows, width + hidden), BF),
            sds((*grid3, down_rows, width), BF), sds((4, width), F32), sds((rows, 3 * width), BF),
            sds((chips, 2, local, 2 * width), BF), sds((rows, width), BF),
            sds((local, pairs, 2 * SPAN), F32),
        ],
        [
            pltpu.VMEM((*grid3, 4, LANES), F32), pltpu.VMEM((rows, width), F32),
            pltpu.VMEM((local, 2 * width), F32), pltpu.VMEM((width, spans), BF),
        ],
        FRONT_COPIES, scalars_first(6),
    )(info, x, *state[:5])
    qkv_full = qkv_full.reshape(width, 3 * width)
    outputs, resid_grad, attn_grad, pu_grad, down_grad, norm_two = mlp_call(
        x, attn_out, grad_rows, norms, pu_full.reshape(width, width + hidden), down_full.reshape(hidden, width)
    )
    shapes = ((down_rows, width), (own_rows, width + hidden), (own_rows, width), (own_rows, 2 * width))
    scratch = [
        pltpu.VMEM((rows, 3 * width), BF), pltpu.VMEM((rows, 2 * width), F32), pltpu.VMEM((width, rows), BF),
        pltpu.VMEM((width, spans), BF), pltpu.VMEM((spans, 2 * width), F32),
        pltpu.VMEM((chips, local, 2 * width), F32), pltpu.VMEM((chips - 1, local, 2 * width), BF),
        pltpu.VMEM((chips - 1, local, 2 * width), BF), pltpu.VMEM((local, 2 * width), F32),
        pltpu.VMEM((*grid3, own_rows, width), BF), pltpu.VMEM((*grid3, own_rows, 2 * width), BF),
    ]
    scratch += [buffer for shape in shapes for buffer in scatter_scratch(groups, chips, *shape)]
    scratch += [
        pltpu.VMEM((own_rows, 2 * width), F32),
        pltpu.VMEM((4, width), F32), pltpu.VMEM((6, 4, width), F32), pltpu.VMEM((chips, 4, width), F32),
        pltpu.VMEM((8, LANES), F32), pltpu.VMEM((6, 8, LANES), F32), pltpu.VMEM((chips, 8, LANES), F32),
    ]
    input_grad, *grads, norm_total, total = remote_call(
        back_kernel, groups, seqs, "back", 1,
        [
            sds((rows, width), F32), sds((own_rows, 3 * width), F32), sds((own_rows, width + hidden), F32),
            sds((down_rows, width), F32), sds((4, width), F32), sds((8, LANES), F32),
        ],
        scratch, BACK_COPIES, scalars_first(11),
    )(
        info, x, mixed, attn_grad, lse, summ.reshape(spans, 2 * width), resid_grad,
        pu_grad.reshape(*grid3, own_rows, width + hidden), down_grad.reshape(*grid3, down_rows, width),
        norms, qkv_full, norm_two,
    )
    return outputs, input_grad, grads, norm_total, total


def plain_body(groups, seqs, inputs, out_grad, lengths, *state):
    sds = jax.ShapeDtypeStruct
    rows, width = inputs.shape[1], inputs.shape[2]
    qkv_full, pu_full, down_full, norms = gather_plain(state[:5])
    local = rows // SPAN
    spans = local * seqs
    info = jnp.stack([lengths[0], (lax.axis_index("seq") * local).astype(jnp.int32)])
    x, grad_rows = inputs[0], out_grad[0]
    tile = 256
    steps = rows // tile
    mixed, own_summ = pl.pallas_call(
        qkv_kernel,
        grid=(steps,),
        in_specs=[SCALARS, by_rows(tile, width), whole(norms.shape), whole(qkv_full.shape)],
        out_specs=[by_rows(tile, 3 * width), whole((local, 2 * width))],
        out_shape=[sds((rows, 3 * width), BF), sds((local, 2 * width), BF)],
        scratch_shapes=[pltpu.VMEM((local, 2 * width), F32)],
        compiler_params=PARAMS,
        name="qkv",
    )(info, x, norms, qkv_full)
    summ = lax.all_gather(own_summ, "seq", axis=0, tiled=True)
    pairs = width // LANES
    lse_spec = pl.BlockSpec((1, pairs, 2 * SPAN), lambda i: (i, 0, 0))
    attn_out, lse = pl.pallas_call(
        attend_kernel,
        grid=(local,),
        in_specs=[SCALARS, by_rows(SPAN, 3 * width), whole(summ.shape)],
        out_specs=[by_rows(SPAN, width), lse_spec],
        out_shape=[sds((rows, width), BF), sds((local, pairs, 2 * SPAN), F32)],
        scratch_shapes=[pltpu.VMEM((width, spans), BF)],
        compiler_params=PARAMS,
        name="attend",
    )(info, mixed, summ)
    outputs, resid_grad, attn_grad, pu_grad, down_grad, norm_two = mlp_call(
        x, attn_out, grad_rows, norms, pu_full, down_full
    )
    dq, dkv, dsumm = pl.pallas_call(
        attend_back_kernel,
        grid=(local,),
        in_specs=[SCALARS, by_rows(SPAN, 3 * width), by_rows(SPAN, width), lse_spec, whole(summ.shape)],
        out_specs=[by_rows(SPAN, width), by_rows(SPAN, 2 * width), whole((spans, 2 * width))],
        out_shape=[sds((rows, width), BF), sds((rows, 2 * width), F32), sds((spans, 2 * width), F32)],
        scratch_shapes=[pltpu.VMEM((width, spans), BF)],
        compiler_params=PARAMS,
        name="attend_back",
    )(info, mixed, attn_grad, lse, summ)
    extra = lax.psum_scatter(dsumm, "seq", scatter_dimension=0, tiled=True)
    input_grad, qkv_grad, norm_one = pl.pallas_call(
        final_kernel,
        grid=(steps,),
        in_specs=[
            SCALARS, by_rows(tile, width), by_rows(tile, width), by_rows(tile, 2 * width),
            whole(extra.shape), by_rows(tile, width), whole(norms.shape), whole(qkv_full.shape),
        ],
        out_specs=[by_rows(tile, width), whole(qkv_full.shape), whole((2, width))],
        out_shape=[sds((rows, width), F32), sds(qkv_full.shape, BF), sds((2, width), F32)],
        scratch_shapes=[
            pltpu.VMEM((rows, 3 * width), BF), pltpu.VMEM((width, rows), BF), pltpu.VMEM((2, width), F32),
        ],
        compiler_params=PARAMS,
        name="final",
    )(info, x, dq, dkv, extra, resid_grad, norms, qkv_full)
    norm_grad = jnp.concatenate([norm_one, norm_two], axis=0)
    *grads, norm_total, total = reduce_plain(qkv_grad, pu_grad, down_grad, norm_grad)
    return outputs, input_grad, grads, norm_total, total


def body(groups, seqs, *args):
    state = args[3:]
    direct = groups == 4 and seqs % 4 == 0 and state[0].shape[0] % 16 == 0
    run = direct_body if direct else plain_body
    outputs, input_grad, grads, norm_total, total = run(groups, seqs, *args)
    sds = jax.ShapeDtypeStruct
    index = lax.axis_index("batch") * seqs + lax.axis_index("seq")
    owned = [sds(w.shape, F32) for w in state[:5]]
    grad_norm, *fresh, shift_clipped = pl.pallas_call(
        update_kernel,
        in_specs=[SCALARS] + [pl.BlockSpec(memory_space=pltpu.VMEM)] * 20,
        out_shape=[sds((1, 1), F32), *owned, *owned, *owned, sds((1, state[4].shape[1]), F32)],
        compiler_params=PARAMS,
        name="update",
    )(index.astype(jnp.int32)[None], total, *grads, norm_total, *state)
    return (outputs[None], input_grad[None], grad_norm[0, 0], *fresh, shift_clipped[0])


def solution(mesh):
    tokens = P("batch", "seq", None)
    owned = P(("batch", "seq"), None)
    columns = P(None, ("batch", "seq"))
    state = (owned, owned, owned, owned, columns)
    return jax.shard_map(
        functools.partial(body, mesh.shape["batch"], mesh.shape["seq"]),
        mesh=mesh,
        in_specs=(tokens, tokens, P("batch")) + state * 3,
        out_specs=(tokens, tokens, P()) + state * 3 + (P(("batch", "seq")),),
        check_vma=False,
    )
```

```python
import functools
import jax
import jax.numpy as jnp
from jax import lax
from jax.experimental import pallas as pl
from jax.experimental.pallas import tpu as pltpu
from jax.sharding import PartitionSpec as P

HEADS = 8
HD = 64
SPAN = 128
STEP = 10
LN_EPS = 1e-05
NEG_FILL = -1e30
CLIP = 1.0
BETA = 0.5
ADAM_EPS = 1e-08
DECAY = 0.1
RATES = (0.02, 0.3, 0.02, 0.02, 0.5)
BF = jnp.bfloat16
F32 = jnp.float32
LANES = 128
VMEM_LIMIT = 56 * 1024 * 1024


def dot(a, b, dims=((1,), (0,))):
    return lax.dot_general(a, b, (dims, ((), ())), preferred_element_type=F32)


def dot_nt(a, b):
    return dot(a, b, ((1,), (1,)))


def normalize(x):
    inv = 1.0 / x.shape[-1]
    centred = x - jnp.sum(x, axis=-1, keepdims=True) * inv
    spread = jnp.sum(centred * centred, axis=-1, keepdims=True) * inv
    rstd = lax.rsqrt(spread + LN_EPS)
    return centred * rstd, rstd


def norm_back(grad, gain, xhat, rstd):
    inv = 1.0 / grad.shape[-1]
    e = grad * gain
    mean_e = jnp.sum(e, axis=-1, keepdims=True) * inv
    mean_ex = jnp.sum(e * xhat, axis=-1, keepdims=True) * inv
    return rstd * (e - mean_e - xhat * mean_ex)


def qkv_tile(x, norms_ref, weight_ref):
    xhat, _ = normalize(x.astype(F32))
    normed = (xhat * norms_ref[0:1, :] + norms_ref[1:2, :]).astype(BF)
    return dot(normed, weight_ref[...]).astype(BF)


def span_scale(length, begin, shape):
    count = jnp.clip(length - begin, 1, SPAN)
    return lax.rsqrt(jnp.full(shape, count, jnp.int32).astype(F32))


def span_sum(kv, length, begin):
    row = lax.broadcasted_iota(jnp.int32, kv.shape, 0)
    kept = jnp.where(row < length - begin, kv.astype(F32), 0.0)
    total = jnp.sum(kept, axis=0, keepdims=True)
    return total * span_scale(length, begin, total.shape)


def stack_heads(pair):
    lane = lax.broadcasted_iota(jnp.int32, pair.shape, 1)
    zero = jnp.zeros_like(pair)
    return jnp.concatenate(
        [jnp.where(lane < HD, pair, zero), jnp.where(lane >= HD, pair, zero)], axis=0
    )


def fold_heads(both):
    picked = jnp.concatenate([both[:HD, :SPAN], both[HD:, SPAN:]], axis=0)
    return picked.T


def span_caps(length, span):
    query_pos = lax.broadcasted_iota(jnp.int32, (1, 2 * SPAN), 1) & (SPAN - 1)
    near_cap = jnp.minimum(query_pos, length - span * SPAN - 1)
    far_cap = jnp.minimum(span, (length + SPAN - 1) // SPAN)
    return near_cap, far_cap


def mask_scores(raw, caps):
    near_cap, far_cap = caps
    key_pos = lax.broadcasted_iota(jnp.int32, (SPAN, 2 * SPAN), 0)
    summ_pos = lax.broadcasted_iota(jnp.int32, (raw.shape[0] - SPAN, 2 * SPAN), 0)
    near = jnp.where(key_pos <= near_cap, raw[:SPAN], NEG_FILL)
    far = jnp.where(summ_pos < far_cap, raw[SPAN:], NEG_FILL)
    return jnp.concatenate([near, far], axis=0)


def attend_spans(spans, mixed_ref, width, summ_ref, summ_vt_ref, out_ref, lse_ref):
    units = [(pl.ds(row, SPAN), index, caps, pair) for row, index, caps in spans for pair in range(width // LANES)]
    queries, keys, values_t = [], [], []
    for rows, index, caps, pair in units:
        at = pair * LANES
        queries.append(stack_heads(mixed_ref[rows, at : at + LANES] * BF(0.125)))
        near_k = mixed_ref[rows, width + at : width + at + LANES]
        near_v = mixed_ref[rows, 2 * width + at : 2 * width + at + LANES]
        keys.append(jnp.concatenate([near_k, summ_ref[:, at : at + LANES]], axis=0))
        values_t.append(jnp.concatenate([near_v.T, summ_vt_ref[at : at + LANES, :]], axis=1))
    scores = [dot_nt(k, q) for k, q in zip(keys, queries)]
    scores = [mask_scores(s, unit[2]) for s, unit in zip(scores, units)]
    peaks = [jnp.max(s, axis=0, keepdims=True) for s in scores]
    expos = [jnp.exp(s - p) for s, p in zip(scores, peaks)]
    totals = [jnp.sum(e, axis=0, keepdims=True) for e in expos]
    expos = [e.astype(BF) for e in expos]
    outs = [dot(v, e) for v, e in zip(values_t, expos)]
    outs = [o * (1.0 / t) for o, t in zip(outs, totals)]
    for (rows, index, caps, pair), out, peak, total in zip(units, outs, peaks, totals):
        at = pair * LANES
        out_ref[rows, at : at + LANES] = fold_heads(out).astype(BF)
        lse_ref[index, pair : pair + 1, :] = peak + jnp.log(total)


def attend_back_spans(
    spans, mixed_ref, grad_ref, width, summ_ref, summ_kt_ref, lse_ref, dq_ref, dkv_ref, dsumm_ref
):
    pairs = width // LANES
    units = [(pl.ds(row, SPAN), index, caps, pair) for row, index, caps in spans for pair in range(pairs)]
    queries, grads, keys, keys_t, values = [], [], [], [], []
    for rows, index, caps, pair in units:
        at = pair * LANES
        queries.append(stack_heads(mixed_ref[rows, at : at + LANES] * BF(0.125)))
        grads.append(stack_heads(grad_ref[rows, at : at + LANES]))
        near_k = mixed_ref[rows, width + at : width + at + LANES]
        near_v = mixed_ref[rows, 2 * width + at : 2 * width + at + LANES]
        keys.append(jnp.concatenate([near_k, summ_ref[:, at : at + LANES]], axis=0))
        keys_t.append(jnp.concatenate([near_k.T, summ_kt_ref[at : at + LANES, :]], axis=1))
        values.append(jnp.concatenate([near_v, summ_ref[:, width + at : width + at + LANES]], axis=0))
    scores = [dot_nt(k, q) for k, q in zip(keys, queries)]
    dprobs = [dot_nt(v, g) for v, g in zip(values, grads)]
    scores = [mask_scores(s, unit[2]) for s, unit in zip(scores, units)]
    probs = [jnp.exp(s - lse_ref[index, pair : pair + 1, :]) for s, (_, index, _, pair) in zip(scores, units)]
    deltas = [jnp.sum(p * d, axis=0, keepdims=True) for p, d in zip(probs, dprobs)]
    dscores = [(p * (d - delta)).astype(BF) for p, d, delta in zip(probs, dprobs, deltas)]
    probs = [p.astype(BF) for p in probs]
    dqs = [dot(k, ds) for k, ds in zip(keys_t, dscores)]
    dks = [dot(ds, q) for ds, q in zip(dscores, queries)]
    dvs = [dot(p, g) for p, g in zip(probs, grads)]
    for (rows, index, caps, pair), dq, dk, dv in zip(units, dqs, dks, dvs):
        at = pair * LANES
        dq_ref[rows, at : at + LANES] = (fold_heads(dq) * 0.125).astype(dq_ref.dtype)
        dkv_ref[rows, at : at + LANES] = dk[:SPAN]
        dkv_ref[rows, width + at : width + at + LANES] = dv[:SPAN]
    for pair in range(pairs):
        at = pair * LANES
        dsumm_ref[:, at : at + LANES] += sum(dk[SPAN:] for dk in dks[pair::pairs])
        dsumm_ref[:, width + at : width + at + LANES] += sum(dv[SPAN:] for dv in dvs[pair::pairs])


GELU_A = 0.7978845608
GELU_B = 0.044715


def gelu_parts(t):
    sq = t * t
    th = jnp.tanh(t * (GELU_A + (GELU_A * GELU_B) * sq))
    half = 0.5 * th + 0.5
    slope = half + (2.0 * t) * (half * (1.0 - half)) * (GELU_A + (3.0 * GELU_A * GELU_B) * sq)
    return t * half, slope


MESH = pl.DeviceIdType.MESH


class Place:
    def __init__(self, groups, seqs):
        self.groups, self.chips = groups, seqs // 2
        self.b = lax.axis_index("batch")
        self.seq = lax.axis_index("seq")
        self.z, self.c = self.seq // 2, self.seq % 2
        self.other = 1 - self.c
        self.b1 = self.b + 1 - 2 * (self.b % 2)
        self.b2 = (self.b + 2) % 4
        self.b3 = self.b1 + 2 - 4 * (self.b1 // 2)

    def at(self, b, z, c):
        return (b, 2 * z + c)

    def sibling(self):
        return self.at(self.b, self.z, self.other)

    def along(self, step):
        return (self.z + step) % self.chips


def meet(place, seqs):
    barrier = pltpu.get_barrier_semaphore()
    partners = [place.at(b, place.z, place.c) for b in (place.b1, place.b2, place.b3)]
    partners += [(place.b, (place.seq + k) % seqs) for k in range(1, seqs)]
    for partner in partners:
        pl.semaphore_signal(barrier, inc=1, device_id=partner, device_id_type=MESH)
    pl.semaphore_wait(barrier, len(partners))


class Copies:
    def __init__(self, send_sems, recv_sems):
        self.send, self.recv, self.made = send_sems, recv_sems, []

    def start(self, src, dst, device):
        at = len(self.made)
        assert at < self.send.shape[0]
        copy = pltpu.make_async_remote_copy(
            src_ref=src, dst_ref=dst, send_sem=self.send.at[at], recv_sem=self.recv.at[at],
            device_id=device, device_id_type=MESH,
        )
        copy.start()
        self.made.append(copy)
        return copy

    def finish(self):
        for copy in self.made:
            copy.wait_send()


class Loads:
    def __init__(self, sems):
        self.sems, self.made = sems, 0

    def start(self, src, dst):
        assert self.made < self.sems.shape[0]
        copy = pltpu.make_async_copy(src, dst, self.sems.at[self.made])
        self.made += 1
        copy.start()
        return copy


def gather_steps(place, copies, full):
    p, half = place, place.chips // 2
    low, high = pl.ds(0, half), pl.ds(half, place.chips - half)
    own = full.at[p.b, p.z, p.c]
    along = [copies.start(own, own, p.at(p.b, p.along(k), p.c)) for k in range(1, p.chips)]
    yield
    for copy in along:
        copy.wait_recv()
    column = full.at[p.b, :, p.c]
    to_x = copies.start(column, column, p.at(p.b1, p.z, p.c))
    to_y = copies.start(column, column, p.at(p.b2, p.z, p.c))
    sib = [copies.start(column, column, p.sibling())]
    yield
    to_x.wait_recv()
    block = full.at[p.b1, low, p.c]
    on_y = copies.start(block, block, p.at(p.b2, p.z, p.c))
    to_y.wait_recv()
    block = full.at[p.b2, high, p.c]
    on_x = copies.start(block, block, p.at(p.b1, p.z, p.c))
    for b in (p.b1, p.b2):
        column = full.at[b, :, p.c]
        sib.append(copies.start(column, column, p.sibling()))
    yield
    for copy, part in ((on_y, low), (on_x, high)):
        copy.wait_recv()
        block = full.at[p.b3, part, p.c]
        sib.append(copies.start(block, block, p.sibling()))
    yield
    for copy in sib:
        copy.wait_recv()


GATHER_COPIES = 12


def fast_gather_steps(place, copies, full):
    p = place
    order = range(p.chips)
    early, late = order[: p.chips // 2], order[p.chips // 2 :]
    x, y, sibling = p.at(p.b1, p.z, p.c), p.at(p.b2, p.z, p.c), p.sibling()

    def block(b, k):
        return full.at[b, (p.z + p.chips - k) % p.chips, p.c]

    def push(b, k, device):
        return copies.start(block(b, k), block(b, k), device)

    along = [copies.start(block(p.b, 0), block(p.b, 0), p.at(p.b, p.along(k), p.c)) for k in order[1:]]
    to_x, to_y, sib = [push(p.b, 0, x)], [push(p.b, 0, y)], [push(p.b, 0, sibling)]
    yield
    for k, copy in enumerate(along, 1):
        copy.wait_recv()
        to_x.append(push(p.b, k, x))
        to_y.append(push(p.b, k, y))
        sib.append(push(p.b, k, sibling))
    yield
    on = []
    for k in early:
        to_x[k].wait_recv()
        on.append(push(p.b1, k, y))
        sib.append(push(p.b1, k, sibling))
    for k in late:
        to_y[k].wait_recv()
        on.append(push(p.b2, k, x))
        sib.append(push(p.b2, k, sibling))
    yield
    for k in late:
        to_x[k].wait_recv()
        sib.append(push(p.b1, k, sibling))
    for k in early:
        to_y[k].wait_recv()
        sib.append(push(p.b2, k, sibling))
    yield
    for k, copy in enumerate(on):
        copy.wait_recv()
        sib.append(push(p.b3, k, sibling))
    yield
    for copy in sib:
        copy.wait_recv()


def fast_gather_copies(chips):
    return chips - 1 + 3 * chips + 4 * chips


def scatter_steps(place, copies, loads, grad, acc, got, near, far, last, result):
    p, half = place, place.chips // 2
    low, high = pl.ds(0, half), pl.ds(half, place.chips - half)
    groups, chips = p.groups, p.chips
    swap = copies.start(grad.at[:, :, p.other], got, p.sibling())
    keep = loads.start(grad.at[:, :, p.c], acc)
    yield
    keep.wait()
    swap.wait_recv()

    def add_one(i, carry):
        b, z = i // chips, i % chips
        acc[b, z] = (acc[b, z].astype(F32) + got[b, z].astype(F32)).astype(BF)
        return carry

    lax.fori_loop(0, groups * chips, add_one, 0)
    on_y = copies.start(acc.at[p.b3, low], far.at[0], p.at(p.b2, p.z, p.c))
    on_x = copies.start(acc.at[p.b3, high], far.at[1], p.at(p.b1, p.z, p.c))
    early_x = copies.start(acc.at[p.b1, high], near.at[0, high], p.at(p.b1, p.z, p.c))
    early_y = copies.start(acc.at[p.b2, low], near.at[1, low], p.at(p.b2, p.z, p.c))
    yield
    on_y.wait_recv()
    for z in range(half):
        acc[p.b1, z] = (acc[p.b1, z].astype(F32) + far[0, z].astype(F32)).astype(BF)
    late_x = copies.start(acc.at[p.b1, low], near.at[0, low], p.at(p.b1, p.z, p.c))
    on_x.wait_recv()
    for z in range(half, chips):
        acc[p.b2, z] = (acc[p.b2, z].astype(F32) + far[1, z - half].astype(F32)).astype(BF)
    late_y = copies.start(acc.at[p.b2, high], near.at[1, high], p.at(p.b2, p.z, p.c))
    yield
    for copy in (early_x, early_y, late_x, late_y):
        copy.wait_recv()
    for z in range(chips):
        acc[p.b, z] = (acc[p.b, z].astype(F32) + near[0, z].astype(F32) + near[1, z].astype(F32)).astype(BF)
    along = []
    for k in range(1, chips):
        to = p.along(k)
        along.append(copies.start(acc.at[p.b, to], last.at[k - 1], p.at(p.b, to, p.c)))
    yield
    total = acc[p.b, p.z].astype(F32)
    for k, copy in enumerate(along):
        copy.wait_recv()
        total = total + last[k].astype(F32)
    result[...] = total


SCATTER_COPIES = 10


def scatter_scratch(groups, chips, rows, cols):
    half = chips // 2
    return [
        pltpu.VMEM((groups, chips, rows, cols), BF),
        pltpu.VMEM((groups, chips, rows, cols), BF),
        pltpu.VMEM((2, chips, rows, cols), BF),
        pltpu.VMEM((2, half, rows, cols), BF),
        pltpu.VMEM((chips - 1, rows, cols), BF),
    ]


def share_sum_steps(place, copies, mine, along, across, result):
    p, seqs = place, along.shape[0]
    along[p.seq] = mine[...]
    own = along.at[p.seq]
    sent = [copies.start(own, own, (p.b, (p.seq + k) % seqs)) for k in range(1, seqs)]
    yield
    for copy in sent:
        copy.wait_recv()
    across[p.b] = sum(along[s] for s in range(seqs))
    own = across.at[p.b]
    sent = [copies.start(own, own, p.at(b, p.z, p.c)) for b in (p.b1, p.b2, p.b3)]
    yield
    for copy in sent:
        copy.wait_recv()
    result[...] = sum(across[b] for b in range(p.groups))


def share_copies(groups, seqs):
    return groups + seqs - 2


def run_all(*steps):
    live = list(steps)
    while live:
        for step in list(live):
            try:
                next(step)
            except StopIteration:
                live.remove(step)


def adam(grad, master, first, second, rate, moment_out, square_out, fresh_out):
    fix = 1.0 - BETA**STEP
    moment = BETA * first + (1.0 - BETA) * grad
    square = BETA * second + (1.0 - BETA) * grad * grad
    update = moment / fix / (jnp.sqrt(square / fix) + ADAM_EPS)
    moment_out[...] = moment
    square_out[...] = square
    fresh_out[...] = master - rate * (update + DECAY * master)


def update_kernel(total_ref, part_ref, resid_grad_ref, qkv_grad, pu_grad, down_grad, norm_grad, *refs):
    state, outs = refs[:15], refs[15:]
    input_out, norm_out, moments, squares, fresh = outs[0], outs[1], outs[2:7], outs[7:12], outs[12:17]
    input_out[...] = part_ref[...] + resid_grad_ref[...]

    @pl.when(pl.program_id(0) == 0)
    def _():
        grad_norm = jnp.sqrt(total_ref[0:1, 0:1])
        norm_out[...] = grad_norm
        factor = jnp.minimum(1.0, CLIP / (grad_norm + 1e-06))
        width = state[1].shape[1]
        piece = state[4].shape[1]
        per = LANES // piece
        index = lax.axis_index("batch") * lax.axis_size("seq") + lax.axis_index("seq")
        block = norm_grad[:, pl.ds(pl.multiple_of(index // per * LANES, LANES), LANES)]
        own = pltpu.roll(block, (LANES - index % per * piece) % LANES, 1)[:, :piece]
        grads = (qkv_grad[...], pu_grad[:, :width], pu_grad[:, width:], down_grad[...], own)
        for at, (grad, rate) in enumerate(zip(grads, RATES)):
            adam(
                grad * factor, state[at][...], state[5 + at][...], state[10 + at][...], rate,
                moments[at], squares[at], fresh[at],
            )
        outs[17][...] = own[3:4] * factor


def tick(*steps):
    for step in steps:
        next(step, None)


def cast_shards(p, seqs, qkv_ref, proj_ref, up_ref, down_ref, norm_ref, qkv_full, pu_full, down_full, norm_full):
    width = proj_ref.shape[1]
    b, z, c = p.b, p.z, p.c
    index = b * seqs + 2 * z + c
    qkv_full[b, z, c] = qkv_ref[...].astype(BF)
    pu_full[b, z, c, :, :width] = proj_ref[...].astype(BF)
    pu_full[b, z, c, :, width:] = up_ref[...].astype(BF)
    down_full[b, z, c] = down_ref[...].astype(BF)
    piece = norm_ref.shape[1]
    per = LANES // piece
    tiled = jnp.concatenate([norm_ref[...].astype(BF).astype(F32)] * per, axis=1)
    lane = lax.broadcasted_iota(jnp.int32, tiled.shape, 1)
    norm_full[b, z, c] = jnp.where(lane // piece == index % per, tiled, 0.0)


def join_norms(norm_full, seqs, per, norms_out):
    for block in range(norms_out.shape[1] // LANES):
        total = None
        for device in range(block * per, (block + 1) * per):
            one = norm_full[device // seqs, device % seqs // 2, device % 2]
            total = one if total is None else total + one
        norms_out[:, block * LANES : (block + 1) * LANES] = total


def tiles(first, last, size, one):
    def step(index, carry):
        one(pl.multiple_of(index * size, size), index)
        return carry

    lax.fori_loop(first, last, step, 0)


def front_kernel(
    groups, seqs, length_ref, x_hbm, qkv_ref, proj_ref, up_ref, down_ref, norm_ref,
    qkv_hbm, pu_hbm, down_hbm, norms_out, mixed_hbm, summ_ref, attn_hbm, lse_ref,
    x_ref, qkv_full, pu_full, down_full, mixed_ref, attn_ref,
    norm_full, xhat_scr, sum_scr, vt_scr, load_sems, send_sems, recv_sems,
):
    p = Place(groups, seqs)
    rows, width = x_ref.shape
    local = rows // SPAN
    length, first_span = length_ref[0], p.seq * local
    loads = Loads(load_sems)
    x_load = loads.start(x_hbm, x_ref)
    cast_shards(
        p, seqs, qkv_ref, proj_ref, up_ref, down_ref, norm_ref, qkv_full, pu_full, down_full, norm_full
    )
    meet(p, seqs)
    copies = Copies(send_sems, recv_sems)
    in_qkv = fast_gather_steps(p, copies, qkv_full)
    in_norm, in_pu, in_down = (gather_steps(p, copies, full) for full in (norm_full, pu_full, down_full))
    tile = 256
    count = rows // tile

    def center(at, index):
        xhat_scr[pl.ds(at, tile), :] = normalize(x_ref[pl.ds(at, tile), :].astype(F32))[0]

    tick(in_norm, in_qkv)
    x_load.wait()
    tiles(0, count // 2, tile, center)
    tick(in_norm, in_qkv, in_pu)
    tiles(count // 2, 3 * count // 4, tile, center)
    tick(in_norm, in_qkv)
    tiles(3 * count // 4, count, tile, center)
    tick(in_norm, in_qkv)
    tick(in_norm, in_qkv)
    join_norms(norm_full, seqs, LANES // norm_ref.shape[1], norms_out)
    tick(in_qkv)
    stores = [loads.start(qkv_full, qkv_hbm)]
    gain, shift = norms_out[0:1, :], norms_out[1:2, :]
    tile = min(512, rows)
    count = rows // tile

    def weight(begin, size):
        return qkv_full[:, :, :, :, begin : begin + size].reshape(width, size)

    def normed_of(at):
        return (xhat_scr[pl.ds(at, tile), :] * gain + shift).astype(BF)

    def keys_values(at, index):
        mixed = dot(normed_of(at), weight(width, 2 * width)).astype(BF)
        mixed_ref[pl.ds(at, tile), width:] = mixed
        for part in range(tile // SPAN):
            span = index * (tile // SPAN) + part
            sum_scr[pl.ds(span, 1), :] = span_sum(
                mixed[part * SPAN : (part + 1) * SPAN], length, (first_span + span) * SPAN
            )

    def queries(at, index):
        mixed_ref[pl.ds(at, tile), :width] = dot(normed_of(at), weight(0, width)).astype(BF)

    tiles(0, count // 2, tile, keys_values)
    tick(in_pu, in_down)
    tiles(count // 2, count, tile, keys_values)
    summ_ref[p.z, p.c] = sum_scr[...].astype(BF)
    own = summ_ref.at[p.z, p.c]
    along = [copies.start(own, own, p.at(p.b, p.along(k), p.c)) for k in range(1, p.chips)]
    sib = [copies.start(own, own, p.sibling())]
    tiles(0, count, tile, queries)
    stores.append(loads.start(mixed_ref, mixed_hbm))
    for k, copy in enumerate(along):
        copy.wait_recv()
        block = summ_ref.at[(p.z + p.chips - 1 - k) % p.chips, p.c]
        sib.append(copies.start(block, block, p.sibling()))
    tick(in_pu)
    for copy in sib:
        copy.wait_recv()
    vt_scr[...] = summ_ref[:, :, :, width:].reshape(local * seqs, width).T
    summ_rows = SummaryView(summ_ref, local * seqs)
    group = min(4, local)

    def attend(at, index):
        spans = []
        for k in range(group):
            span = index * group + k
            spans.append((pl.multiple_of(at + k * SPAN, SPAN), span, span_caps(length, first_span + span)))
        attend_spans(spans, mixed_ref, width, summ_rows, vt_scr, attn_ref, lse_ref)

    for part in range(local // group):
        tiles(part, part + 1, group * SPAN, attend)
        done = pl.ds(part * group * SPAN, group * SPAN)
        stores.append(loads.start(attn_ref.at[done], attn_hbm.at[done]))
        tick(in_down, in_pu)
    stores.append(loads.start(pu_full, pu_hbm))
    run_all(in_down, in_pu)
    stores.append(loads.start(down_full, down_hbm))
    for store in stores:
        store.wait()
    copies.finish()


class SummaryView:
    def __init__(self, ref, rows):
        self.ref, self.rows = ref, rows

    def __getitem__(self, key):
        cols = key[1]
        return self.ref[:, :, :, cols].reshape(self.rows, cols.stop - cols.start)


def back_kernel(
    groups, seqs, length_ref, x_hbm, mixed_hbm, grad_hbm, lse_ref, summ_ref, pu_hbm, down_hbm,
    norms_ref, weight_hbm, norm_two_ref,
    part_hbm, qkv_out, pu_out, down_out, norm_out, total_out,
    x_ref, mixed_ref, grad_ref, weight_ref, part_ref,
    mg_scr, dkv_scr, n1t_scr, kt_scr, dsumm_scr, dsumm_got, dsumm_low, dsumm_last, extra_scr, q_grad, kv_grad,
    *scratch,
):
    *buffers, kv_own, norm_mine, along_norm, across_norm, sq_mine, along_sq, across_sq = scratch[:-3]
    load_sems, send_sems, recv_sems = scratch[-3:]
    p = Place(groups, seqs)
    rows, width = x_ref.shape
    local = rows // SPAN
    spans = local * seqs
    length, first_span = length_ref[0], p.seq * local
    loads = Loads(load_sems)
    group = min(4, local)
    parts = local // group
    reads = []
    for part in range(parts):
        here = pl.ds(part * group * SPAN, group * SPAN)
        reads.append(
            [loads.start(mixed_hbm.at[here], mixed_ref.at[here]), loads.start(grad_hbm.at[here], grad_ref.at[here])]
        )
    late = [loads.start(x_hbm, x_ref), loads.start(weight_hbm, weight_ref)]
    meet(p, seqs)
    copies = Copies(send_sems, recv_sems)

    def scatter(grad, at, out):
        return scatter_steps(p, copies, loads, grad, *buffers[5 * at : 5 * at + 5], out)

    out_down, out_pu = scatter(down_hbm, 0, down_out), scatter(pu_hbm, 1, pu_out)
    tick(out_down, out_pu)
    kt_scr[...] = summ_ref[:, :width].T
    dsumm_scr[...] = jnp.zeros_like(dsumm_scr)

    def attend_back(at, index):
        each = []
        for k in range(group):
            span = index * group + k
            each.append((pl.multiple_of(at + k * SPAN, SPAN), span, span_caps(length, first_span + span)))
        attend_back_spans(
            each, mixed_ref, grad_ref, width, summ_ref, kt_scr, lse_ref, mg_scr, dkv_scr, dsumm_scr
        )

    for part in range(parts):
        for read in reads[part]:
            read.wait()
        tiles(part, part + 1, group * SPAN, attend_back)
        tick(out_down if part % 2 == 0 else out_pu)
    swap = []
    for z in range(p.chips):
        block = dsumm_scr.at[pl.ds(pl.multiple_of((2 * z + p.other) * local, local), local)]
        swap.append(copies.start(block, dsumm_got.at[z], p.sibling()))
    tile = min(512, rows)
    count = rows // tile
    gain, shift = norms_ref[0:1, :], norms_ref[1:2, :]
    for read in late:
        read.wait()

    def recompute(at, index):
        xhat, _ = normalize(x_ref[pl.ds(at, tile), :].astype(F32))
        n1t_scr[:, pl.ds(at, tile)] = (xhat * gain + shift).astype(BF).T

    tiles(0, count // 2, tile, recompute)
    for copy in swap:
        copy.wait_recv()

    def half_sum(z):
        mine = dsumm_scr[pl.ds(pl.multiple_of((2 * z + p.c) * local, local), local), :]
        return mine + dsumm_got[z]

    along = []
    for k in range(1, p.chips):
        to = p.along(k)
        dsumm_low[k - 1] = half_sum(to).astype(BF)
        along.append(copies.start(dsumm_low.at[k - 1], dsumm_last.at[k - 1], p.at(p.b, to, p.c)))
    tiles(count // 2, count, tile, recompute)
    tick(out_pu, out_down)
    per_block = width // (groups * seqs)

    def weight_grad(begin, size):
        block = dot(n1t_scr[...], mg_scr[:, begin : begin + size]).astype(BF)
        return block.reshape(groups, p.chips, 2, per_block, size)

    cols = 512
    for at in range(0, width, cols):
        q_grad[:, :, :, :, at : at + cols] = weight_grad(at, cols)
    out_q = scatter(q_grad, 2, qkv_out.at[:, :width])
    tick(out_q)

    def back_q(at, index):
        part_ref[pl.ds(at, tile), :] = dot_nt(mg_scr[pl.ds(at, tile), :width], weight_ref[:, :width])

    tiles(0, count, tile, back_q)
    tick(out_q, out_down)
    total = half_sum(p.z)
    for k, copy in enumerate(along):
        copy.wait_recv()
        total = total + dsumm_last[k].astype(F32)
    extra_scr[...] = total

    def add_extra(at, index):
        begin = (first_span + index) * SPAN
        extra = extra_scr[pl.ds(index, 1), :]
        extra = extra * span_scale(length, begin, extra.shape)
        here = dkv_scr[pl.ds(at, SPAN), :]
        pos = lax.broadcasted_iota(jnp.int32, here.shape, 0)
        mg_scr[pl.ds(at, SPAN), width:] = (here + jnp.where(pos < length - begin, extra, 0.0)).astype(BF)

    tiles(0, local, SPAN, add_extra)
    for at in range(0, 2 * width, cols):
        kv_grad[:, :, :, :, at : at + cols] = weight_grad(width + at, cols)
    out_kv = scatter(kv_grad, 3, kv_own)
    tick(out_kv, out_q)
    norm_mine[0:2, :] = jnp.zeros_like(norm_mine[0:2, :])
    norm_mine[2:4, :] = norm_two_ref[...]

    def finish(at, index):
        here = pl.ds(at, tile)
        xhat, rstd = normalize(x_ref[here, :].astype(F32))
        back = part_ref[here, :] + dot_nt(mg_scr[here, width:], weight_ref[:, width:])
        part_ref[here, :] = norm_back(back, gain, xhat, rstd)
        norm_mine[0:1, :] += jnp.sum(back * xhat, axis=0, keepdims=True)
        norm_mine[1:2, :] += jnp.sum(back, axis=0, keepdims=True)

    stores = []
    for part in range(count):
        tiles(part, part + 1, tile, finish)
        here = pl.ds(part * tile, tile)
        stores.append(loads.start(part_ref.at[here], part_hbm.at[here]))
        tick(out_kv, out_q, out_pu, out_down)
    norm_sum = share_sum_steps(p, copies, norm_mine, along_norm, across_norm, norm_out)
    run_all(norm_sum, out_kv, out_q, out_pu, out_down)
    qkv_out[:, width:] = kv_own[...]
    local_sum = sum(jnp.sum(jnp.square(out[...]), keepdims=True) for out in (qkv_out, pu_out, down_out))
    sq_mine[...] = jnp.broadcast_to(local_sum, sq_mine.shape)
    run_all(share_sum_steps(p, copies, sq_mine, along_sq, across_sq, total_out))
    total_out[...] = total_out[...] + jnp.sum(jnp.square(norm_out[...]), keepdims=True)
    for store in stores:
        store.wait()
    copies.finish()


def qkv_kernel(info_ref, x_ref, norms_ref, weight_ref, mixed_ref, summ_ref, sum_scr):
    step = pl.program_id(0)
    tile, width = x_ref.shape
    length, first_span = info_ref[0], info_ref[1]
    mixed = qkv_tile(x_ref[...], norms_ref, weight_ref)
    mixed_ref[...] = mixed
    per = tile // SPAN
    for part in range(per):
        span = step * per + part
        sum_scr[pl.ds(span, 1), :] = span_sum(
            mixed[part * SPAN : (part + 1) * SPAN, width:], length, (first_span + span) * SPAN
        )

    @pl.when(step == pl.num_programs(0) - 1)
    def _():
        summ_ref[...] = sum_scr[...].astype(BF)


def attend_kernel(info_ref, mixed_ref, summ_ref, out_ref, lse_ref, vt_scr):
    step = pl.program_id(0)
    width = out_ref.shape[1]

    @pl.when(step == 0)
    def _():
        vt_scr[...] = summ_ref[:, width:].T

    caps = span_caps(info_ref[0], info_ref[1] + step)
    attend_spans([(0, 0, caps)], mixed_ref, width, summ_ref, vt_scr, out_ref, lse_ref)


def attend_back_kernel(info_ref, mixed_ref, grad_ref, lse_ref, summ_ref, dq_ref, dkv_ref, dsumm_ref, kt_scr):
    step = pl.program_id(0)
    width = dq_ref.shape[1]

    @pl.when(step == 0)
    def _():
        kt_scr[...] = summ_ref[:, :width].T
        dsumm_ref[...] = jnp.zeros_like(dsumm_ref)

    caps = span_caps(info_ref[0], info_ref[1] + step)
    attend_back_spans(
        [(0, 0, caps)], mixed_ref, grad_ref, width, summ_ref, kt_scr, lse_ref, dq_ref, dkv_ref, dsumm_ref
    )


def mlp_kernel(
    x_ref, attn_ref, og_ref, norms_ref, pu_ref, down_ref,
    out_ref, resid_grad_ref, attn_grad_ref, pu_grad_ref, down_grad_ref, norm_grad_ref,
    activ_scr, pre_grad_scr, n2t_scr, attnt_scr, ogt_scr, pig_scr, norm_scr,
):
    step = pl.program_id(0)
    tile, width = x_ref.shape
    hidden = down_ref.shape[0]
    rows = pl.ds(pl.multiple_of(step * tile, tile), tile)
    chunk = 256
    attn = attn_ref[...]
    grad = og_ref[...]
    resid = x_ref[...].astype(F32) + dot(attn, pu_ref[:, :width])
    xhat, rstd = normalize(resid)
    gain = norms_ref[2:3, :]
    normed = (xhat * gain + norms_ref[3:4, :]).astype(BF)
    attnt_scr[:, rows] = attn.T
    n2t_scr[:, rows] = normed.T
    ogt_scr[:, rows] = grad.T
    for at in range(0, hidden, chunk):
        pre = dot(normed, pu_ref[:, width + at : width + at + chunk])
        act_grad = dot_nt(grad, down_ref[at : at + chunk, :])
        value, slope = gelu_parts(pre)
        activ = value.astype(BF)
        pre_grad = (act_grad * slope).astype(BF)
        activ_scr[rows, at : at + chunk] = activ
        pre_grad_scr[rows, at : at + chunk] = pre_grad
    out_ref[...] = (resid + dot(activ_scr[rows, :], down_ref[...])).astype(BF)
    back = dot_nt(pre_grad_scr[rows, :], pu_ref[:, width:])
    resid_grad = grad.astype(F32) + norm_back(back, gain, xhat, rstd)
    resid_grad_ref[...] = resid_grad
    pig = resid_grad.astype(BF)
    pig_scr[rows, :] = pig
    attn_grad_ref[...] = dot_nt(pig, pu_ref[:, :width]).astype(BF)
    gain_part = jnp.sum(back * xhat, axis=0, keepdims=True)
    shift_part = jnp.sum(back, axis=0, keepdims=True)
    part = jnp.concatenate([gain_part, shift_part], axis=0)

    @pl.when(step == 0)
    def _():
        norm_scr[...] = part

    @pl.when(step > 0)
    def _():
        norm_scr[...] += part

    @pl.when(step == pl.num_programs(0) - 1)
    def _():
        norm_grad_ref[...] = norm_scr[...]
        pu_grad_ref[:, :width] = dot(attnt_scr[...], pig_scr[...]).astype(BF)
        cols = 512

        def one(index, carry):
            c = pl.ds(pl.multiple_of(index * cols, cols), cols)
            out = pl.ds(pl.multiple_of(width + index * cols, cols), cols)
            pu_grad_ref[:, out] = dot(n2t_scr[...], pre_grad_scr[:, c]).astype(BF)
            down_grad_ref[c, :] = dot(ogt_scr[...], activ_scr[:, c]).T.astype(BF)
            return carry

        lax.fori_loop(0, hidden // cols, one, 0)


def final_kernel(
    info_ref, x_ref, dq_ref, dkv_ref, extra_ref, norms_ref, weight_ref,
    part_ref, qkv_grad_ref, norm_grad_ref, mg_scr, n1t_scr, norm_scr,
):
    step = pl.program_id(0)
    tile, width = x_ref.shape
    rows = pl.ds(pl.multiple_of(step * tile, tile), tile)
    length, first_span = info_ref[0], info_ref[1]
    xhat, rstd = normalize(x_ref[...].astype(F32))
    gain = norms_ref[0:1, :]
    normed = (xhat * gain + norms_ref[1:2, :]).astype(BF)
    n1t_scr[:, rows] = normed.T
    per = tile // SPAN
    parts = []
    for part in range(per):
        span = step * per + part
        begin = (first_span + span) * SPAN
        extra = extra_ref[pl.ds(span, 1), :]
        extra = extra * span_scale(length, begin, extra.shape)
        local = dkv_ref[part * SPAN : (part + 1) * SPAN, :]
        pos = lax.broadcasted_iota(jnp.int32, local.shape, 0)
        parts.append(local + jnp.where(pos < length - begin, extra, 0.0))
    mg = jnp.concatenate([dq_ref[...], jnp.concatenate(parts, axis=0).astype(BF)], axis=1)
    mg_scr[rows, :] = mg
    back = dot_nt(mg, weight_ref[...])
    part_ref[...] = norm_back(back, gain, xhat, rstd)
    gain_part = jnp.sum(back * xhat, axis=0, keepdims=True)
    shift_part = jnp.sum(back, axis=0, keepdims=True)
    part = jnp.concatenate([gain_part, shift_part], axis=0)

    @pl.when(step == 0)
    def _():
        norm_scr[...] = part

    @pl.when(step > 0)
    def _():
        norm_scr[...] += part

    @pl.when(step == pl.num_programs(0) - 1)
    def _():
        norm_grad_ref[...] = norm_scr[...]
        cols = 256

        def one(index, carry):
            c = pl.ds(pl.multiple_of(index * cols, cols), cols)
            qkv_grad_ref[:, c] = dot(n1t_scr[...], mg_scr[:, c]).astype(BF)
            return carry

        lax.fori_loop(0, qkv_grad_ref.shape[1] // cols, one, 0)


def whole(shape):
    return pl.BlockSpec(shape, lambda i: (0,) * len(shape))


def by_rows(tile, width):
    return pl.BlockSpec((tile, width), lambda i: (i, 0))


SCALARS = pl.BlockSpec(memory_space=pltpu.SMEM)
PARAMS = pltpu.CompilerParams(vmem_limit_bytes=VMEM_LIMIT)


def remote_call(kernel, groups, seqs, name, collective_id, outs, ins, scratch, loads, copies):
    return pl.pallas_call(
        functools.partial(kernel, groups, seqs),
        in_specs=[pl.BlockSpec(memory_space=space) for space in ins],
        out_specs=[pl.BlockSpec(memory_space=space) for space, _, _ in outs],
        out_shape=[jax.ShapeDtypeStruct(shape, kind) for _, shape, kind in outs],
        scratch_shapes=list(scratch) + [pltpu.SemaphoreType.DMA((n,)) for n in (loads, copies, copies)],
        compiler_params=pltpu.CompilerParams(
            vmem_limit_bytes=VMEM_LIMIT, collective_id=collective_id, has_side_effects=True
        ),
        name=name,
    )


def regroup(grad, dim, outer, inner):
    shape = grad.shape
    piece = shape[dim] // (outer * inner)
    split = grad.reshape(shape[:dim] + (outer, inner, piece) + shape[dim + 1 :])
    return jnp.swapaxes(split, dim, dim + 1).reshape(shape)


def gather_plain(state):
    both = ("batch", "seq")
    qkv, proj, up, down = (lax.all_gather(w.astype(BF), both, axis=0, tiled=True) for w in state[:4])
    norms = lax.all_gather(state[4].astype(BF), both, axis=1, tiled=True).astype(F32)
    return qkv, jnp.concatenate([proj, up], axis=1), down, norms


def reduce_plain(qkv_grad, pu_grad, down_grad, norm_grad):
    groups, seqs = lax.axis_size("batch"), lax.axis_size("seq")
    reduced = []
    for grad, dim in ((qkv_grad, 0), (pu_grad, 0), (down_grad, 0)):
        part = lax.psum_scatter(
            regroup(grad.astype(F32), dim, groups, seqs), "seq", scatter_dimension=dim, tiled=True
        )
        reduced.append(lax.psum_scatter(part, "batch", scatter_dimension=dim, tiled=True))
    norm_total = lax.psum(norm_grad, ("batch", "seq"))
    squares = lax.psum(sum(jnp.sum(grad * grad) for grad in reduced), ("batch", "seq"))
    squares = squares + jnp.sum(norm_total * norm_total)
    return (*reduced, norm_total, jnp.broadcast_to(squares, (8, LANES)))


def mlp_call(x, attn_out, grad_rows, norms, pu_full, down_full):
    sds = jax.ShapeDtypeStruct
    rows, width = x.shape
    hidden = down_full.shape[0]
    tile = min(512, rows)
    steps = rows // tile
    return pl.pallas_call(
        mlp_kernel,
        grid=(steps,),
        in_specs=[by_rows(tile, width)] * 3
        + [whole(norms.shape), whole(pu_full.shape), whole(down_full.shape)],
        out_specs=[by_rows(tile, width)] * 3
        + [whole(pu_full.shape), whole(down_full.shape), whole((2, width))],
        out_shape=[
            sds((rows, width), BF), sds((rows, width), F32), sds((rows, width), BF),
            sds(pu_full.shape, BF), sds(down_full.shape, BF), sds((2, width), F32),
        ],
        scratch_shapes=[
            pltpu.VMEM((rows, hidden), BF), pltpu.VMEM((rows, hidden), BF),
            pltpu.VMEM((width, rows), BF), pltpu.VMEM((width, rows), BF), pltpu.VMEM((width, rows), BF),
            pltpu.VMEM((rows, width), BF), pltpu.VMEM((2, width), F32),
        ],
        compiler_params=PARAMS,
        name="mlp",
    )(x, attn_out, grad_rows, norms, pu_full, down_full)


def direct_body(groups, seqs, inputs, out_grad, lengths, *state):
    rows, width = inputs.shape[1], inputs.shape[2]
    own_rows, down_rows = state[0].shape[0], state[3].shape[0]
    hidden = state[2].shape[1]
    chips = seqs // 2
    grid3 = (groups, chips, 2)
    local = rows // SPAN
    spans = local * seqs
    pairs = width // LANES
    x, grad_rows = inputs[0], out_grad[0]
    vmem, hbm, smem = pltpu.VMEM, pl.ANY, pltpu.SMEM
    shapes = (
        (*grid3, own_rows, 3 * width), (*grid3, own_rows, width + hidden), (*grid3, down_rows, width),
    )
    qkv_full, pu_full, down_full, norms, mixed, summ, attn_out, lse = remote_call(
        front_kernel, groups, seqs, "front", 0,
        [
            *((hbm, shape, BF) for shape in shapes), (vmem, (4, width), F32), (hbm, (rows, 3 * width), BF),
            (vmem, (chips, 2, local, 2 * width), BF), (hbm, (rows, width), BF),
            (vmem, (local, pairs, 2 * SPAN), F32),
        ],
        [smem, hbm] + [vmem] * 5,
        [
            vmem((rows, width), BF), *(vmem(shape, BF) for shape in shapes), vmem((rows, 3 * width), BF),
            vmem((rows, width), BF),
            vmem((*grid3, 4, LANES), F32), vmem((rows, width), F32), vmem((local, 2 * width), F32),
            vmem((width, spans), BF),
        ],
        5 + local, 3 * GATHER_COPIES + fast_gather_copies(chips) + 2 * chips,
    )(lengths, x, *state[:5])
    qkv_full = qkv_full.reshape(width, 3 * width)
    outputs, resid_grad, attn_grad, pu_grad, down_grad, norm_two = mlp_call(
        x, attn_out, grad_rows, norms, pu_full.reshape(width, width + hidden), down_full.reshape(hidden, width)
    )
    blocks = ((down_rows, width), (own_rows, width + hidden), (own_rows, width), (own_rows, 2 * width))
    summ_block = (local, 2 * width)
    scratch = [
        vmem((rows, width), BF), vmem((rows, 3 * width), BF), vmem((rows, width), BF),
        vmem((width, 3 * width), BF), vmem((rows, width), F32),
        vmem((rows, 3 * width), BF), vmem((rows, 2 * width), F32), vmem((width, rows), BF),
        vmem((width, spans), BF), vmem((spans, 2 * width), F32),
        vmem((chips, *summ_block), F32), vmem((chips - 1, *summ_block), BF),
        vmem((chips - 1, *summ_block), BF), vmem(summ_block, F32),
        vmem((*grid3, own_rows, width), BF), vmem((*grid3, own_rows, 2 * width), BF),
    ]
    scratch += [buffer for block in blocks for buffer in scatter_scratch(groups, chips, *block)]
    scratch += [
        vmem((own_rows, 2 * width), F32),
        vmem((4, width), F32), vmem((seqs, 4, width), F32), vmem((groups, 4, width), F32),
        vmem((8, LANES), F32), vmem((seqs, 8, LANES), F32), vmem((groups, 8, LANES), F32),
    ]
    part, *grads, norm_total, total = remote_call(
        back_kernel, groups, seqs, "back", 1,
        [
            (hbm, (rows, width), F32), (vmem, (own_rows, 3 * width), F32),
            (vmem, (own_rows, width + hidden), F32), (vmem, (down_rows, width), F32),
            (vmem, (4, width), F32), (vmem, (8, LANES), F32),
        ],
        [smem, hbm, hbm, hbm, vmem, vmem, hbm, hbm, vmem, hbm, vmem],
        scratch, 2 * local + 2 + 4 + rows // 256,
        4 * SCATTER_COPIES + 2 * share_copies(groups, seqs) + 2 * chips,
    )(
        lengths, x, mixed, attn_grad, lse, summ.reshape(spans, 2 * width),
        pu_grad.reshape(shapes[1]), down_grad.reshape(shapes[2]), norms, qkv_full, norm_two,
    )
    return outputs, part, resid_grad, grads, norm_total, total


def plain_body(groups, seqs, inputs, out_grad, lengths, *state):
    sds = jax.ShapeDtypeStruct
    rows, width = inputs.shape[1], inputs.shape[2]
    qkv_full, pu_full, down_full, norms = gather_plain(state[:5])
    local = rows // SPAN
    spans = local * seqs
    info = jnp.stack([lengths[0], (lax.axis_index("seq") * local).astype(jnp.int32)])
    x, grad_rows = inputs[0], out_grad[0]
    tile = 256
    steps = rows // tile
    mixed, own_summ = pl.pallas_call(
        qkv_kernel,
        grid=(steps,),
        in_specs=[SCALARS, by_rows(tile, width), whole(norms.shape), whole(qkv_full.shape)],
        out_specs=[by_rows(tile, 3 * width), whole((local, 2 * width))],
        out_shape=[sds((rows, 3 * width), BF), sds((local, 2 * width), BF)],
        scratch_shapes=[pltpu.VMEM((local, 2 * width), F32)],
        compiler_params=PARAMS,
        name="qkv",
    )(info, x, norms, qkv_full)
    summ = lax.all_gather(own_summ, "seq", axis=0, tiled=True)
    pairs = width // LANES
    lse_spec = pl.BlockSpec((1, pairs, 2 * SPAN), lambda i: (i, 0, 0))
    attn_out, lse = pl.pallas_call(
        attend_kernel,
        grid=(local,),
        in_specs=[SCALARS, by_rows(SPAN, 3 * width), whole(summ.shape)],
        out_specs=[by_rows(SPAN, width), lse_spec],
        out_shape=[sds((rows, width), BF), sds((local, pairs, 2 * SPAN), F32)],
        scratch_shapes=[pltpu.VMEM((width, spans), BF)],
        compiler_params=PARAMS,
        name="attend",
    )(info, mixed, summ)
    outputs, resid_grad, attn_grad, pu_grad, down_grad, norm_two = mlp_call(
        x, attn_out, grad_rows, norms, pu_full, down_full
    )
    dq, dkv, dsumm = pl.pallas_call(
        attend_back_kernel,
        grid=(local,),
        in_specs=[SCALARS, by_rows(SPAN, 3 * width), by_rows(SPAN, width), lse_spec, whole(summ.shape)],
        out_specs=[by_rows(SPAN, width), by_rows(SPAN, 2 * width), whole((spans, 2 * width))],
        out_shape=[sds((rows, width), BF), sds((rows, 2 * width), F32), sds((spans, 2 * width), F32)],
        scratch_shapes=[pltpu.VMEM((width, spans), BF)],
        compiler_params=PARAMS,
        name="attend_back",
    )(info, mixed, attn_grad, lse, summ)
    extra = lax.psum_scatter(dsumm, "seq", scatter_dimension=0, tiled=True)
    part, qkv_grad, norm_one = pl.pallas_call(
        final_kernel,
        grid=(steps,),
        in_specs=[
            SCALARS, by_rows(tile, width), by_rows(tile, width), by_rows(tile, 2 * width),
            whole(extra.shape), whole(norms.shape), whole(qkv_full.shape),
        ],
        out_specs=[by_rows(tile, width), whole(qkv_full.shape), whole((2, width))],
        out_shape=[sds((rows, width), F32), sds(qkv_full.shape, BF), sds((2, width), F32)],
        scratch_shapes=[
            pltpu.VMEM((rows, 3 * width), BF), pltpu.VMEM((width, rows), BF), pltpu.VMEM((2, width), F32),
        ],
        compiler_params=PARAMS,
        name="final",
    )(info, x, dq, dkv, extra, norms, qkv_full)
    norm_grad = jnp.concatenate([norm_one, norm_two], axis=0)
    *grads, norm_total, total = reduce_plain(qkv_grad, pu_grad, down_grad, norm_grad)
    return outputs, part, resid_grad, grads, norm_total, total


def body(groups, seqs, *args):
    state = args[3:]
    direct = groups == 4 and seqs % 4 == 0 and state[0].shape[0] % 16 == 0
    run = direct_body if direct else plain_body
    outputs, part, resid_grad, grads, norm_total, total = run(groups, seqs, *args)
    sds = jax.ShapeDtypeStruct
    rows, width = part.shape
    tile = 256
    held = [whole(w.shape) for w in state[:5]]
    last = (1, state[4].shape[1])
    input_grad, grad_norm, *fresh, shift_clipped = pl.pallas_call(
        update_kernel,
        grid=(rows // tile,),
        in_specs=[whole(total.shape), by_rows(tile, width), by_rows(tile, width)]
        + [whole(g.shape) for g in (*grads, norm_total)] + held * 3,
        out_specs=[by_rows(tile, width), whole((1, 1)), *held * 3, whole(last)],
        out_shape=[sds((rows, width), F32), sds((1, 1), F32)]
        + [sds(w.shape, F32) for w in state[:5]] * 3 + [sds(last, F32)],
        compiler_params=PARAMS,
        name="update",
    )(total, part, resid_grad, *grads, norm_total, *state)
    return (outputs[None], input_grad[None], grad_norm[0, 0], *fresh, shift_clipped[0])


def solution(mesh):
    tokens = P("batch", "seq", None)
    owned = P(("batch", "seq"), None)
    columns = P(None, ("batch", "seq"))
    state = (owned, owned, owned, owned, columns)
    return jax.shard_map(
        functools.partial(body, mesh.shape["batch"], mesh.shape["seq"]),
        mesh=mesh,
        in_specs=(tokens, tokens, P("batch")) + state * 3,
        out_specs=(tokens, tokens, P()) + state * 3 + (P(("batch", "seq")),),
        check_vma=False,
    )
```

```python
import functools
import jax
import jax.numpy as jnp
from jax import lax
from jax.experimental import pallas as pl
from jax.experimental.pallas import tpu as pltpu
from jax.sharding import PartitionSpec as P

HEADS = 8
HD = 64
SPAN = 128
STEP = 10
LN_EPS = 1e-05
NEG_FILL = -1e30
CLIP = 1.0
BETA = 0.5
ADAM_EPS = 1e-08
DECAY = 0.1
RATES = (0.02, 0.3, 0.02, 0.02, 0.5)
BF = jnp.bfloat16
F32 = jnp.float32
LANES = 128
VMEM_LIMIT = 56 * 1024 * 1024


def dot(a, b, dims=((1,), (0,))):
    return lax.dot_general(a, b, (dims, ((), ())), preferred_element_type=F32)


def dot_tn(a, b):
    return dot(a, b, ((0,), (0,)))


def dot_nt(a, b):
    return dot(a, b, ((1,), (1,)))


def normalize(x):
    inv = 1.0 / x.shape[-1]
    centred = x - jnp.sum(x, axis=-1, keepdims=True) * inv
    spread = jnp.sum(centred * centred, axis=-1, keepdims=True) * inv
    rstd = lax.rsqrt(spread + LN_EPS)
    return centred * rstd, rstd


def norm_back(grad, gain, xhat, rstd):
    inv = 1.0 / grad.shape[-1]
    e = grad * gain
    mean_e = jnp.sum(e, axis=-1, keepdims=True) * inv
    mean_ex = jnp.sum(e * xhat, axis=-1, keepdims=True) * inv
    return rstd * (e - mean_e - xhat * mean_ex)


def qkv_tile(x, norms_ref, weight_ref):
    xhat, _ = normalize(x.astype(F32))
    normed = (xhat * norms_ref[0:1, :] + norms_ref[1:2, :]).astype(BF)
    return dot(normed, weight_ref[...]).astype(BF)


def span_scale(length, begin, shape):
    count = jnp.clip(length - begin, 1, SPAN)
    return lax.rsqrt(jnp.full(shape, count, jnp.int32).astype(F32))


def span_sum(kv, length, begin):
    row = lax.broadcasted_iota(jnp.int32, kv.shape, 0)
    kept = jnp.where(row < length - begin, kv.astype(F32), 0.0)
    total = jnp.sum(kept, axis=0, keepdims=True)
    return total * span_scale(length, begin, total.shape)


def stack_heads(pair):
    lane = lax.broadcasted_iota(jnp.int32, pair.shape, 1)
    zero = jnp.zeros_like(pair)
    return jnp.concatenate(
        [jnp.where(lane < HD, pair, zero), jnp.where(lane >= HD, pair, zero)], axis=0
    )


def fold_heads(both):
    picked = jnp.concatenate([both[:HD, :SPAN], both[HD:, SPAN:]], axis=0)
    return picked.T


def span_caps(length, span):
    query_pos = lax.broadcasted_iota(jnp.int32, (1, 2 * SPAN), 1) & (SPAN - 1)
    near_cap = jnp.minimum(query_pos, length - span * SPAN - 1)
    far_cap = jnp.minimum(span, (length + SPAN - 1) // SPAN)
    return near_cap, far_cap


def mask_scores(raw, caps):
    near_cap, far_cap = caps
    key_pos = lax.broadcasted_iota(jnp.int32, (SPAN, 2 * SPAN), 0)
    summ_pos = lax.broadcasted_iota(jnp.int32, (raw.shape[0] - SPAN, 2 * SPAN), 0)
    near = jnp.where(key_pos <= near_cap, raw[:SPAN], NEG_FILL)
    far = jnp.where(summ_pos < far_cap, raw[SPAN:], NEG_FILL)
    return jnp.concatenate([near, far], axis=0)


def attend_spans(spans, mixed_ref, width, summ_ref, summ_vt_ref, out_ref, lse_ref):
    units = [(pl.ds(row, SPAN), index, caps, pair) for row, index, caps in spans for pair in range(width // LANES)]
    queries, keys, values_t = [], [], []
    for rows, index, caps, pair in units:
        at = pair * LANES
        queries.append(stack_heads(mixed_ref[rows, at : at + LANES] * BF(0.125)))
        near_k = mixed_ref[rows, width + at : width + at + LANES]
        near_v = mixed_ref[rows, 2 * width + at : 2 * width + at + LANES]
        keys.append(jnp.concatenate([near_k, summ_ref[:, at : at + LANES]], axis=0))
        values_t.append(jnp.concatenate([near_v.T, summ_vt_ref[at : at + LANES, :]], axis=1))
    scores = [dot_nt(k, q) for k, q in zip(keys, queries)]
    scores = [mask_scores(s, unit[2]) for s, unit in zip(scores, units)]
    peaks = [jnp.max(s, axis=0, keepdims=True) for s in scores]
    expos = [jnp.exp(s - p) for s, p in zip(scores, peaks)]
    totals = [jnp.sum(e, axis=0, keepdims=True) for e in expos]
    expos = [e.astype(BF) for e in expos]
    outs = [dot(v, e) for v, e in zip(values_t, expos)]
    outs = [o * (1.0 / t) for o, t in zip(outs, totals)]
    for (rows, index, caps, pair), out, peak, total in zip(units, outs, peaks, totals):
        at = pair * LANES
        out_ref[rows, at : at + LANES] = fold_heads(out).astype(BF)
        lse_ref[index, pair : pair + 1, :] = peak + jnp.log(total)


def attend_back_spans(
    spans, mixed_ref, grad_ref, width, summ_ref, summ_kt_ref, lse_ref, back_ref, dsumm_ref
):
    pairs = width // LANES
    units = [(pl.ds(row, SPAN), index, caps, pair) for row, index, caps in spans for pair in range(pairs)]
    queries, grads, keys, keys_t, values = [], [], [], [], []
    for rows, index, caps, pair in units:
        at = pair * LANES
        queries.append(stack_heads(mixed_ref[rows, at : at + LANES] * BF(0.125)))
        grads.append(stack_heads(grad_ref[rows, at : at + LANES]))
        near_k = mixed_ref[rows, width + at : width + at + LANES]
        near_v = mixed_ref[rows, 2 * width + at : 2 * width + at + LANES]
        keys.append(jnp.concatenate([near_k, summ_ref[:, at : at + LANES]], axis=0))
        keys_t.append(jnp.concatenate([near_k.T, summ_kt_ref[at : at + LANES, :]], axis=1))
        values.append(jnp.concatenate([near_v, summ_ref[:, width + at : width + at + LANES]], axis=0))
    scores = [dot_nt(k, q) for k, q in zip(keys, queries)]
    dprobs = [dot_nt(v, g) for v, g in zip(values, grads)]
    scores = [mask_scores(s, unit[2]) for s, unit in zip(scores, units)]
    probs = [jnp.exp(s - lse_ref[index, pair : pair + 1, :]) for s, (_, index, _, pair) in zip(scores, units)]
    deltas = [jnp.sum(p * d, axis=0, keepdims=True) for p, d in zip(probs, dprobs)]
    dscores = [(p * (d - delta)).astype(BF) for p, d, delta in zip(probs, dprobs, deltas)]
    probs = [p.astype(BF) for p in probs]
    dqs = [dot(k, ds) for k, ds in zip(keys_t, dscores)]
    dks = [dot(ds, q) for ds, q in zip(dscores, queries)]
    dvs = [dot(p, g) for p, g in zip(probs, grads)]
    for (rows, index, caps, pair), dq, dk, dv in zip(units, dqs, dks, dvs):
        at = pair * LANES
        back_ref[rows, at : at + LANES] = (fold_heads(dq) * 0.125).astype(BF)
        back_ref[rows, width + at : width + at + LANES] = dk[:SPAN].astype(BF)
        back_ref[rows, 2 * width + at : 2 * width + at + LANES] = dv[:SPAN].astype(BF)
    for pair in range(pairs):
        at = pair * LANES
        dsumm_ref[:, at : at + LANES] += sum(dk[SPAN:] for dk in dks[pair::pairs])
        dsumm_ref[:, width + at : width + at + LANES] += sum(dv[SPAN:] for dv in dvs[pair::pairs])


def with_extra(back, extra, length, begin):
    extra = extra * span_scale(length, begin, extra.shape)
    pos = lax.broadcasted_iota(jnp.int32, back.shape, 0)
    return (back.astype(F32) + jnp.where(pos < length - begin, extra, 0.0)).astype(BF)


GELU_A = 0.7978845608
GELU_B = 0.044715


def gelu_parts(t):
    slow = GELU_A + (GELU_A * GELU_B) * (t * t)
    half = 0.5 * jnp.tanh(t * slow) + 0.5
    value = t * half
    return value, half + (value - value * half) * (6.0 * slow - 4.0 * GELU_A)


MESH = pl.DeviceIdType.MESH


class Place:
    def __init__(self, groups, seqs):
        self.groups, self.seqs, self.chips = groups, seqs, seqs // 2
        self.b = lax.axis_index("batch")
        self.seq = lax.axis_index("seq")
        self.z, self.c = self.seq // 2, self.seq % 2
        self.other = 1 - self.c
        self.b1 = self.b + 1 - 2 * (self.b % 2)
        self.b2 = (self.b + 2) % 4
        self.b3 = self.b1 + 2 - 4 * (self.b1 // 2)
        self.after = [(self.z + k) % self.chips for k in range(self.chips)]
        self.before = [(self.z + self.chips - k) % self.chips for k in range(self.chips)]
        self.sibling = (self.b, 2 * self.z + self.other)
        self.x, self.y, self.diagonal = (self.b1, self.seq), (self.b2, self.seq), (self.b3, self.seq)
        self.along = [(self.b, 2 * z + self.c) for z in self.after]
        self.ring = [(self.b, (self.seq + k) % seqs) for k in range(seqs)]


def meet(place):
    barrier = pltpu.get_barrier_semaphore()
    partners = [place.x, place.y, place.diagonal, *place.ring[1:]]
    for partner in partners:
        pl.semaphore_signal(barrier, inc=1, device_id=partner, device_id_type=MESH)
    pl.semaphore_wait(barrier, len(partners))


def part_of(ref, index):
    return ref if index is None else ref.at[index]


class Copy:
    def __init__(self, make):
        self.make = make
        make().start()

    def wait(self):
        self.make().wait()

    def wait_recv(self):
        self.make().wait_recv()

    def wait_send(self):
        self.make().wait_send()


class Copies:
    def __init__(self, send_sems, recv_sems):
        self.send, self.recv, self.made = send_sems, recv_sems, []

    def start(self, src, src_index, dst, dst_index, device):
        at = len(self.made)
        assert at < self.send.shape[0]
        copy = Copy(
            lambda: pltpu.make_async_remote_copy(
                src_ref=part_of(src, src_index), dst_ref=part_of(dst, dst_index),
                send_sem=self.send.at[at], recv_sem=self.recv.at[at],
                device_id=device, device_id_type=MESH,
            )
        )
        self.made.append(copy)
        return copy

    def push(self, ref, index, device):
        return self.start(ref, index, ref, index, device)

    def finish(self):
        for copy in self.made:
            copy.wait_send()


class Loads:
    def __init__(self, sems):
        self.sems, self.made = sems, 0

    def start(self, src, dst, src_index=None, dst_index=None):
        at = self.made
        assert at < self.sems.shape[0]
        self.made += 1
        return Copy(
            lambda: pltpu.make_async_copy(part_of(src, src_index), part_of(dst, dst_index), self.sems.at[at])
        )


def gather_steps(place, copies, full, rows=slice(None), cols=slice(None)):
    p, half = place, place.chips // 2
    low, high = slice(0, half), slice(half, place.chips)

    def push(b, z, device):
        return copies.push(full, (b, z, p.c, rows, cols), device)

    along = [push(p.b, p.z, device) for device in p.along[1:]]
    yield
    for copy in along:
        copy.wait_recv()
    every = slice(None)
    to_x, to_y, sib = push(p.b, every, p.x), push(p.b, every, p.y), [push(p.b, every, p.sibling)]
    yield
    to_x.wait_recv()
    on_y = push(p.b1, low, p.y)
    to_y.wait_recv()
    on_x = push(p.b2, high, p.x)
    sib += [push(p.b1, every, p.sibling), push(p.b2, every, p.sibling)]
    yield
    on_y.wait_recv()
    sib.append(push(p.b3, low, p.sibling))
    on_x.wait_recv()
    sib.append(push(p.b3, high, p.sibling))
    yield
    for copy in sib:
        copy.wait_recv()


GATHER_COPIES = 12


def fast_gather_steps(place, copies, full, rows=slice(None), cols=slice(None)):
    p = place
    order = range(p.chips)
    early, late = order[: p.chips // 2], order[p.chips // 2 :]

    def push(b, k, device):
        return copies.push(full, (b, p.before[k], p.c, rows, cols), device)

    along = [push(p.b, 0, device) for device in p.along[1:]]
    to_x, to_y, sib = [push(p.b, 0, p.x)], [push(p.b, 0, p.y)], [push(p.b, 0, p.sibling)]
    yield
    for k, copy in enumerate(along, 1):
        copy.wait_recv()
        to_x.append(push(p.b, k, p.x))
        to_y.append(push(p.b, k, p.y))
        sib.append(push(p.b, k, p.sibling))
    yield
    on = []
    for k in early:
        to_x[k].wait_recv()
        on.append(push(p.b1, k, p.y))
        sib.append(push(p.b1, k, p.sibling))
    for k in late:
        to_y[k].wait_recv()
        on.append(push(p.b2, k, p.x))
        sib.append(push(p.b2, k, p.sibling))
    yield
    for k in late:
        to_x[k].wait_recv()
        sib.append(push(p.b1, k, p.sibling))
    for k in early:
        to_y[k].wait_recv()
        sib.append(push(p.b2, k, p.sibling))
    for k, copy in enumerate(on):
        copy.wait_recv()
        sib.append(push(p.b3, k, p.sibling))
    yield
    for copy in sib:
        copy.wait_recv()


def fast_gather_copies(chips):
    return chips - 1 + 3 * chips + 4 * chips


def scatter_steps(place, copies, loads, grad, acc, got, near, far, last, result):
    p, half = place, place.chips // 2
    low, high = slice(0, half), slice(half, place.chips)
    chips = p.chips

    def add(into, *others):
        total = acc[into].astype(F32)
        for other in others:
            total = total + other.astype(F32)
        acc[into] = total.astype(BF)

    every = slice(None)
    swap = copies.start(grad, (every, every, p.other), got, None, p.sibling)
    keep = loads.start(grad, acc, (every, every, p.c))
    yield
    keep.wait()
    swap.wait_recv()
    for b in (p.b3, p.b1, p.b2):
        for z in range(chips):
            add((b, z), got[b, z])
    on_y = copies.start(acc, (p.b3, low), far, 0, p.y)
    on_x = copies.start(acc, (p.b3, high), far, 1, p.x)
    early_x = copies.start(acc, (p.b1, high), near, (0, high), p.x)
    early_y = copies.start(acc, (p.b2, low), near, (1, low), p.y)
    for z in range(chips):
        add((p.b, z), got[p.b, z])
    yield
    on_y.wait_recv()
    for z in range(half):
        add((p.b1, z), far[0, z])
    late_x = copies.start(acc, (p.b1, low), near, (0, low), p.x)
    on_x.wait_recv()
    for z in range(half, chips):
        add((p.b2, z), far[1, z - half])
    late_y = copies.start(acc, (p.b2, high), near, (1, high), p.y)
    yield
    for copy in (early_x, early_y, late_x, late_y):
        copy.wait_recv()
    for z in range(chips):
        add((p.b, z), near[0, z], near[1, z])
    along = []
    for k in range(1, chips):
        along.append(copies.start(acc, (p.b, p.after[k]), last, k - 1, p.along[k]))
    yield
    total = acc[p.b, p.z].astype(F32)
    for k, copy in enumerate(along):
        copy.wait_recv()
        total = total + last[k].astype(F32)
    result[...] = total


SCATTER_COPIES = 10


def scatter_scratch(groups, chips, rows, cols):
    half = chips // 2
    return [
        pltpu.VMEM((groups, chips, rows, cols), BF),
        pltpu.VMEM((groups, chips, rows, cols), BF),
        pltpu.VMEM((2, chips, rows, cols), BF),
        pltpu.VMEM((2, half, rows, cols), BF),
        pltpu.VMEM((chips - 1, rows, cols), BF),
    ]


def share_sum_steps(place, copies, mine, along, across, result):
    p, seqs = place, along.shape[0]
    along[p.seq] = mine[...]
    sent = [copies.push(along, p.seq, device) for device in p.ring[1:]]
    yield
    for copy in sent:
        copy.wait_recv()
    across[p.b] = sum(along[s] for s in range(seqs))
    sent = [copies.push(across, p.b, device) for device in (p.x, p.y, p.diagonal)]
    yield
    for copy in sent:
        copy.wait_recv()
    result[...] = sum(across[b] for b in range(p.groups))


def share_copies(groups, seqs):
    return groups + seqs - 2


class Ticker:
    def __init__(self, *starts):
        self.waiting, self.time = list(starts), 0

    def __call__(self):
        for start, steps in reversed(self.waiting):
            if self.time >= start:
                next(steps, None)
        self.time += 1

    def finish(self):
        run_all(*(steps for _, steps in self.waiting))


def tick(*steps):
    for step in steps:
        next(step, None)


def run_all(*steps):
    live = list(steps)
    while live:
        for step in list(live):
            try:
                next(step)
            except StopIteration:
                live.remove(step)


def loop(count, body, ticks=None):
    def step(index, carry):
        body(index)
        for k in sorted(ticks or {}):
            pl.when(index == k)(lambda run=ticks[k]: run())
        return carry

    lax.fori_loop(0, count, step, 0)


def adam(grad, master, first, second, rate, moment_out, square_out, fresh_out):
    fix = 1.0 - BETA**STEP
    moment = BETA * first + (1.0 - BETA) * grad
    square = BETA * second + (1.0 - BETA) * grad * grad
    update = moment / fix / (jnp.sqrt(square / fix) + ADAM_EPS)
    moment_out[...] = moment
    square_out[...] = square
    fresh_out[...] = master - rate * (update + DECAY * master)


def update_kernel(
    parts, total_ref, qkv_grad, pu_grad, down_grad, norm_grad, outputs_hbm, input_grad_hbm, *refs
):
    state, outs, (outputs_ref, input_ref, sems) = refs[:15], refs[15:-3], refs[-3:]
    outputs_out, input_out, norm_out, moments, squares, fresh = outs[0], outs[1], outs[2], outs[3:8], outs[8:13], outs[13:18]
    loads = Loads(sems)
    ways = ((input_grad_hbm, input_ref, input_out), (outputs_hbm, outputs_ref, outputs_out))
    reads = [Sliced(loads, src, via, parts).start_all() for src, via, _ in ways]
    stores = [Sliced(loads, via, dst, parts) for _, via, dst in ways]
    grad_norm = jnp.sqrt(total_ref[0:1, 0:1])
    norm_out[...] = grad_norm
    factor = jnp.minimum(1.0, CLIP / (grad_norm + 1e-06))
    width = state[1].shape[1]
    piece = state[4].shape[1]
    per = LANES // piece
    index = lax.axis_index("batch") * lax.axis_size("seq") + lax.axis_index("seq")
    block = norm_grad[:, pl.ds(pl.multiple_of(index // per * LANES, LANES), LANES)]
    own = pltpu.roll(block, (LANES - index % per * piece) % LANES, 1)[:, :piece]
    grads = (qkv_grad[...], pu_grad[:, :width], pu_grad[:, width:], down_grad[...], own)
    for at, (grad, rate) in enumerate(zip(grads, RATES)):
        adam(
            grad * factor, state[at][...], state[5 + at][...], state[10 + at][...], rate,
            moments[at], squares[at], fresh[at],
        )
    outs[18][...] = own[3:4] * factor
    for read, store in zip(reads, stores):
        for part in range(parts):
            read.wait(part)
            store.start(part)
    for store in stores:
        store.wait_all()


def cast_shards(p, seqs, qkv_ref, proj_ref, up_ref, down_ref, norm_ref, qkv_full, pu_full, down_full, norm_full):
    width = proj_ref.shape[1]
    b, z, c = p.b, p.z, p.c
    index = b * seqs + 2 * z + c
    qkv_full[b, z, c] = qkv_ref[...].astype(BF)
    pu_full[b, z, c, :, :width] = proj_ref[...].astype(BF)
    pu_full[b, z, c, :, width:] = up_ref[...].astype(BF)
    down_full[b, z, c] = down_ref[...].astype(BF)
    piece = norm_ref.shape[1]
    per = LANES // piece
    tiled = jnp.concatenate([norm_ref[...].astype(BF).astype(F32)] * per, axis=1)
    lane = lax.broadcasted_iota(jnp.int32, tiled.shape, 1)
    norm_full[b, z, c] = jnp.where(lane // piece == index % per, tiled, 0.0)


def join_norms(norm_full, seqs, per, norms_out):
    for block in range(norms_out.shape[1] // LANES):
        total = None
        for device in range(block * per, (block + 1) * per):
            one = norm_full[device // seqs, device % seqs // 2, device % 2]
            total = one if total is None else total + one
        norms_out[:, block * LANES : (block + 1) * LANES] = total


class Sliced:
    def __init__(self, loads, src, dst, count):
        self.src, self.dst, self.count, self.size = src, dst, count, src.shape[0] // count
        self.sems, self.first = loads.sems, loads.made
        loads.made += count
        assert loads.made <= loads.sems.shape[0]

    def copy(self, index):
        begin = index * self.size
        here = pl.ds(begin if isinstance(index, int) else pl.multiple_of(begin, self.size), self.size)
        return pltpu.make_async_copy(self.src.at[here], self.dst.at[here], self.sems.at[self.first + index])

    def start(self, index):
        self.copy(index).start()

    def wait(self, index):
        self.copy(index).wait()

    def start_next(self, index):
        pl.when(index < self.count)(lambda: self.start(index))

    def start_all(self):
        for index in range(self.count):
            self.start(index)
        return self

    def wait_all(self):
        for index in range(self.count):
            self.wait(index)


class SummaryView:
    def __init__(self, ref, rows):
        self.ref, self.rows = ref, rows

    def __getitem__(self, key):
        cols = key[1]
        return self.ref[:, :, :, cols].reshape(self.rows, cols.stop - cols.start)


def row_block(index, size):
    return pl.ds(pl.multiple_of(index * size, size), size)


TILE = 512


def front_kernel(
    groups, seqs, length_ref, x_hbm, og_hbm, qkv_ref, proj_ref, up_ref, down_ref, norm_ref,
    qkv_hbm, pu_hbm, down_hbm, norms_out, mixed_hbm, summ_ref, attn_hbm, lse_ref,
    outputs_hbm, resid_hbm, slope_hbm, down_grad_hbm,
    x_ref, og_ref, qkv_full, pu_full, down_full, mixed_ref, attn_ref, outputs_ref, resid_ref, activ_ref, slope_ref,
    down_grad_ref, norm_full, sum_scr, vt_scr, load_sems, send_sems, recv_sems,
):
    p = Place(groups, seqs)
    rows, width = x_ref.shape
    hidden = activ_ref.shape[1]
    local = rows // SPAN
    length, first_span = length_ref[0], p.seq * local
    count, per = rows // TILE, TILE // SPAN
    loads = Loads(load_sems)
    x_load = Sliced(loads, x_hbm, x_ref, count).start_all()
    cast_shards(
        p, seqs, qkv_ref, proj_ref, up_ref, down_ref, norm_ref, qkv_full, pu_full, down_full, norm_full
    )
    meet(p)
    og_load = loads.start(og_hbm, og_ref)
    copies = Copies(send_sems, recv_sems)
    half_down, half_pu = down_full.shape[3] // 2, pu_full.shape[4] // 2
    in_kv = fast_gather_steps(p, copies, qkv_full, cols=slice(width, 3 * width))
    in_norm = gather_steps(p, copies, norm_full)
    ticker = Ticker(
        (0, gather_steps(p, copies, qkv_full, cols=slice(0, width))),
        (1, gather_steps(p, copies, pu_full, cols=slice(0, half_pu))),
        (2, gather_steps(p, copies, pu_full, cols=slice(half_pu, 2 * half_pu))),
        (3, gather_steps(p, copies, down_full, rows=slice(0, half_down))),
        (4, gather_steps(p, copies, down_full, rows=slice(half_down, 2 * half_down))),
    )
    xhat_ref = resid_ref

    def center(index):
        here = row_block(index, TILE)
        x_load.wait(index)
        xhat_ref[here, :] = normalize(x_ref[here, :].astype(F32))[0]

    tick(in_norm, in_kv)

    def first():
        tick(in_norm, in_kv)
        ticker()

    def second():
        tick(in_norm, in_kv)

    def third():
        tick(in_norm, in_kv)
        ticker()

    loop(count, center, {0: first, count // 2: second, count - 1: third})
    tick(in_norm, in_kv)
    join_norms(norm_full, seqs, LANES // norm_ref.shape[1], norms_out)
    gain, shift = norms_out[0:1, :], norms_out[1:2, :]

    def columns(full, begin, size):
        return full[:, :, :, :, begin : begin + size].reshape(width, size)

    def normed_of(here):
        return (xhat_ref[here, :] * gain + shift).astype(BF)

    def keys_values(index):
        here = row_block(index, TILE)
        mixed = dot(normed_of(here), columns(qkv_full, width, 2 * width)).astype(BF)
        mixed_ref[here, width:] = mixed
        for part in range(per):
            span = index * per + part
            sum_scr[pl.ds(span, 1), :] = span_sum(
                mixed[part * SPAN : (part + 1) * SPAN], length, (first_span + span) * SPAN
            )

    loop(count, keys_values, {0: ticker, count // 2: ticker})
    summ_ref[p.z, p.c] = sum_scr[...].astype(BF)
    along = [copies.push(summ_ref, (p.z, p.c), device) for device in p.along[1:]]
    sib = [copies.push(summ_ref, (p.z, p.c), p.sibling)]
    ticker()
    stores = [loads.start(qkv_full, qkv_hbm)]
    mixed_store = Sliced(loads, mixed_ref, mixed_hbm, count)

    def queries(index):
        here = row_block(index, TILE)
        mixed_ref[here, :width] = dot(normed_of(here), columns(qkv_full, 0, width)).astype(BF)
        mixed_store.start(index)

    loop(count, queries)
    for k, copy in enumerate(along, 1):
        copy.wait_recv()
        sib.append(copies.push(summ_ref, (p.before[k], p.c), p.sibling))
    for copy in sib:
        copy.wait_recv()
    vt_scr[...] = summ_ref[:, :, :, width:].reshape(local * seqs, width).T
    summ_rows = SummaryView(summ_ref, local * seqs)
    attn_store = Sliced(loads, attn_ref, attn_hbm, count)

    def attend(index):
        spans = []
        for k in range(per):
            span = index * per + k
            spans.append((pl.multiple_of(span * SPAN, SPAN), span, span_caps(length, first_span + span)))
        attend_spans(spans, mixed_ref, width, summ_rows, vt_scr, attn_ref, lse_ref)
        attn_store.start(index)

    loop(count, attend, {k: ticker for k in range(1, count, 2)})
    gain_two, shift_two = norms_out[2:3, :], norms_out[3:4, :]
    resid_store, slope_store = (
        Sliced(loads, src, dst, count) for src, dst in ((resid_ref, resid_hbm), (slope_ref, slope_hbm))
    )
    chunk = 256

    def expand(index):
        here = row_block(index, TILE)
        resid = x_ref[here, :].astype(F32) + dot(attn_ref[here, :], columns(pu_full, 0, width))
        resid_ref[here, :] = resid
        resid_store.start(index)
        normed = (normalize(resid)[0] * gain_two + shift_two).astype(BF)
        for at in range(0, hidden, chunk):
            value, slope = gelu_parts(dot(normed, columns(pu_full, width + at, chunk)))
            activ_ref[here, at : at + chunk] = value.astype(BF)
            slope_ref[here, at : at + chunk] = slope.astype(BF)
        slope_store.start(index)

    loop(count, expand, {k: ticker for k in range(1, count, 2)})
    stores.append(loads.start(pu_full, pu_hbm))
    og_load.wait()
    parts = hidden // TILE
    grad_store = Sliced(loads, down_grad_ref, down_grad_hbm, parts)

    def down_grad(index):
        here = row_block(index, TILE)
        down_grad_ref[here, :] = dot_tn(activ_ref[:, here], og_ref[...]).astype(BF)
        grad_store.start(index)

    loop(parts, down_grad)
    ticker.finish()
    stores.append(loads.start(down_full, down_hbm))
    outputs_store = Sliced(loads, outputs_ref, outputs_hbm, count)

    def contract(index):
        here = row_block(index, TILE)
        out = resid_ref[here, :] + dot(activ_ref[here, :], down_full[...].reshape(hidden, width))
        outputs_ref[here, :] = out.astype(BF)
        outputs_store.start(index)

    loop(count, contract)
    for store in (mixed_store, attn_store, resid_store, slope_store, grad_store, outputs_store):
        store.wait_all()
    for store in stores:
        store.wait()
    copies.finish()


def middle_kernel(
    groups, seqs, og_hbm, resid_hbm, slope_hbm, attn_hbm, pu_hbm, down_hbm, norms_ref, down_grad_hbm,
    resid_grad_hbm, attn_grad_hbm, pu_grad_hbm, down_out, norm_grad_ref,
    og_ref, resid_ref, slope_ref, attn_ref, pu_ref, down_ref, resid_grad_ref, attn_grad_ref, pu_grad_ref,
    pre_grad_ref, normed_ref, pig_ref, *scratch,
):
    *buffers, load_sems, send_sems, recv_sems = scratch
    p = Place(groups, seqs)
    rows, width = og_ref.shape
    hidden = slope_ref.shape[1]
    count = rows // TILE
    loads = Loads(load_sems)
    early = [loads.start(down_hbm, down_ref)]
    tiled = [
        Sliced(loads, src, dst, count)
        for src, dst in ((og_hbm, og_ref), (slope_hbm, slope_ref), (resid_hbm, resid_ref))
    ]
    for load in tiled:
        load.start(0)
    early.append(loads.start(pu_hbm, pu_ref))
    for load in tiled:
        load.start(1)
    meet(p)
    copies = Copies(send_sems, recv_sems)
    half = down_out.shape[0] // 2
    ticker = Ticker(
        *(
            (
                at,
                scatter_steps(
                    p, copies, loads, down_grad_hbm.at[:, :, :, half * at : half * (at + 1)], *buffers[5 * at : 5 * at + 5],
                    down_out.at[half * at : half * (at + 1)],
                ),
            )
            for at in range(2)
        )
    )
    ticker()
    attn_load = loads.start(attn_hbm, attn_ref)
    norm_grad_ref[...] = jnp.zeros_like(norm_grad_ref)
    resid_grad_store, attn_grad_store = (
        Sliced(loads, src, dst, count)
        for src, dst in ((resid_grad_ref, resid_grad_hbm), (attn_grad_ref, attn_grad_hbm))
    )
    gain, shift = norms_ref[2:3, :], norms_ref[3:4, :]
    chunk = 256
    early[0].wait()

    def tile(index):
        here = row_block(index, TILE)
        for load in tiled:
            load.start_next(index + 2)
            load.wait(index)
        grad = og_ref[here, :]
        for at in range(0, hidden, chunk):
            act_grad = dot_nt(grad, down_ref[at : at + chunk, :])
            slope = slope_ref[here, at : at + chunk].astype(F32)
            pre_grad_ref[here, at : at + chunk] = (act_grad * slope).astype(BF)

        @pl.when(index == 0)
        def _():
            early[1].wait()

        back = dot_nt(pre_grad_ref[here, :], pu_ref[:, width:])
        xhat, rstd = normalize(resid_ref[here, :])
        normed_ref[here, :] = (xhat * gain + shift).astype(BF)
        resid_grad = grad.astype(F32) + norm_back(back, gain, xhat, rstd)
        resid_grad_ref[here, :] = resid_grad
        resid_grad_store.start(index)
        pig = resid_grad.astype(BF)
        pig_ref[here, :] = pig
        attn_grad_ref[here, :] = dot_nt(pig, pu_ref[:, :width]).astype(BF)
        attn_grad_store.start(index)
        norm_grad_ref[0:1, :] += jnp.sum(back * xhat, axis=0, keepdims=True)
        norm_grad_ref[1:2, :] += jnp.sum(back, axis=0, keepdims=True)

    loop(count, tile, {k: ticker for k in range(count)})
    attn_load.wait()
    pu_grad_ref[:, :width] = dot_tn(attn_ref[...], pig_ref[...]).astype(BF)

    def up_grad(index):
        at = pl.multiple_of(width + index * TILE, TILE)
        pu_grad_ref[:, pl.ds(at, TILE)] = dot_tn(normed_ref[...], pre_grad_ref[:, row_block(index, TILE)]).astype(BF)

    loop(hidden // TILE, up_grad, {1: ticker})
    pu_store = loads.start(pu_grad_ref, pu_grad_hbm)
    resid_grad_store.wait_all()
    attn_grad_store.wait_all()
    ticker.finish()
    pu_store.wait()
    copies.finish()


def back_kernel(
    groups, seqs, length_ref, x_hbm, mixed_hbm, grad_hbm, lse_ref, summ_ref, pu_hbm, resid_grad_hbm, down_ref,
    norms_ref, weight_hbm, norm_two_ref,
    input_grad_hbm, qkv_out, pu_out, norm_out, total_out,
    x_ref, mixed_ref, grad_ref, resid_grad_ref, weight_ref, input_grad_ref,
    mg_scr, xhat_ref, kt_scr, dsumm_scr, dsumm_got, dsumm_low, dsumm_last, extra_scr, q_grad, k_grad, v_grad,
    gain_cols, shift_cols,
    *scratch,
):
    *buffers, norm_mine, along_norm, across_norm, sq_mine, along_sq, across_sq = scratch[:-3]
    load_sems, send_sems, recv_sems = scratch[-3:]
    p = Place(groups, seqs)
    rows, width = x_ref.shape
    local = rows // SPAN
    length, first_span = length_ref[0], p.seq * local
    loads = Loads(load_sems)
    group = 2
    count, steps = rows // TILE, local // group
    reads = [
        Sliced(loads, src, dst, steps) for src, dst in ((mixed_hbm, mixed_ref), (grad_hbm, grad_ref))
    ]
    for index in range(2):
        for read in reads:
            read.start(index)
    meet(p)
    copies = Copies(send_sems, recv_sems)

    def scatter(grad, at, out):
        return scatter_steps(p, copies, loads, grad, *buffers[5 * at : 5 * at + 5], out)

    half = pu_hbm.shape[4] // 2
    ticker = Ticker(
        *((at, scatter(pu_hbm.at[:, :, :, :, half * at : half * (at + 1)], at, pu_out.at[:, half * at : half * (at + 1)]))
          for at in range(2))
    )
    ticker()
    late = [loads.start(src, dst) for src, dst in ((x_hbm, x_ref), (weight_hbm, weight_ref))]
    resid_grad_load = loads.start(resid_grad_hbm, resid_grad_ref)
    kt_scr[...] = summ_ref[:, :width].T
    dsumm_scr[...] = jnp.zeros_like(dsumm_scr)

    def attend_back(index):
        for read in reads:
            read.start_next(index + 2)
            read.wait(index)
        each = []
        for k in range(group):
            span = index * group + k
            each.append((pl.multiple_of(span * SPAN, SPAN), span, span_caps(length, first_span + span)))
        attend_back_spans(each, mixed_ref, grad_ref, width, summ_ref, kt_scr, lse_ref, mg_scr, dsumm_scr)

    loop(steps, attend_back, {at: ticker for at in range(0, steps, 2)})
    swap = []
    for z in range(p.chips):
        block = pl.ds(pl.multiple_of((2 * z + p.other) * local, local), local)
        swap.append(copies.start(dsumm_scr, block, dsumm_got, z, p.sibling))
    gain, shift = norms_ref[0:1, :], norms_ref[1:2, :]
    for read in late:
        read.wait()

    def recompute(index):
        here = row_block(index, TILE)
        xhat_ref[here, :] = normalize(x_ref[here, :].astype(F32))[0].astype(BF)

    loop(count // 2, recompute)
    for copy in swap:
        copy.wait_recv()

    def half_sum(z):
        mine = dsumm_scr[pl.ds(pl.multiple_of((2 * z + p.c) * local, local), local), :]
        return mine + dsumm_got[z]

    along = []
    for k in range(1, p.chips):
        dsumm_low[k - 1] = half_sum(p.after[k]).astype(BF)
        along.append(copies.start(dsumm_low, k - 1, dsumm_last, k - 1, p.along[k]))
    loop(count // 2, lambda index: recompute(index + count // 2))
    per_block = width // (groups * seqs)
    gain_cols[...] = jnp.broadcast_to(gain, (LANES, width)).T
    shift_cols[...] = jnp.broadcast_to(shift, (LANES, width)).T

    def weight_grad(into, at):
        begin = at * width
        back = mg_scr[:, begin : begin + width]
        moved = dot_tn(xhat_ref[...], back)
        total = jnp.sum(back.astype(F32), axis=0, keepdims=True)
        blocks, gains, shifts = [], 0.0, 0.0
        for k in range(0, width, LANES):
            part, sums = moved[:, k : k + LANES], total[:, k : k + LANES]
            blocks.append(gain_cols[...] * part + shift_cols[...] * sums)
            weight = weight_ref[:, begin + k : begin + k + LANES].astype(F32)
            gains += weight * part
            shifts += weight * sums
        into[...] = jnp.concatenate(blocks, axis=1).astype(BF).reshape(groups, p.chips, 2, per_block, width)
        gain_sums = jnp.sum(gains.T, axis=0, keepdims=True)
        shift_sums = jnp.sum(shifts.T, axis=0, keepdims=True)
        norm_mine[0:1, :] = gain_sums + (norm_mine[0:1, :] if at else 0.0)
        norm_mine[1:2, :] = shift_sums + (norm_mine[1:2, :] if at else 0.0)

    norm_mine[2:4, :] = norm_two_ref[...]
    outs = [qkv_out.at[:, width * at : width * (at + 1)] for at in range(3)]
    weight_grad(q_grad, 0)
    out_q = scatter(q_grad, 2, outs[0])
    tick(out_q)
    ticker()

    def back_q(index):
        here = row_block(index, TILE)
        input_grad_ref[here, :] = dot_nt(mg_scr[here, :width], weight_ref[:, :width])

    loop(count, back_q)
    tick(out_q)
    ticker()
    total = half_sum(p.z)
    for k, copy in enumerate(along):
        copy.wait_recv()
        total = total + dsumm_last[k].astype(F32)
    extra_scr[...] = total

    def add_extra(index):
        for k in range(2):
            span = index * 2 + k
            here = row_block(span, SPAN)
            mg_scr[here, width:] = with_extra(
                mg_scr[here, width:], extra_scr[pl.ds(span, 1), :], length, (first_span + span) * SPAN
            )

    loop(local // 2, add_extra)
    weight_grad(k_grad, 1)
    out_k = scatter(k_grad, 3, outs[1])
    tick(out_k, out_q)
    weight_grad(v_grad, 2)
    out_v = scatter(v_grad, 4, outs[2])
    norm_sum = share_sum_steps(p, copies, norm_mine, along_norm, across_norm, norm_out)
    tick(out_v, norm_sum, out_k, out_q)
    ticker()
    resid_grad_load.wait()
    store = Sliced(loads, input_grad_ref, input_grad_hbm, count)

    def finish(index):
        here = row_block(index, TILE)
        xhat, rstd = normalize(x_ref[here, :].astype(F32))
        back = input_grad_ref[here, :] + dot_nt(mg_scr[here, width:], weight_ref[:, width:])
        input_grad_ref[here, :] = resid_grad_ref[here, :] + norm_back(back, gain, xhat, rstd)
        store.start(index)

    def advance():
        tick(out_v, norm_sum, out_k, out_q)
        ticker()

    loop(count, finish, {k: advance for k in range(0, count, 2)})
    run_all(out_v, norm_sum, out_k, out_q)
    ticker.finish()
    local_sum = sum(jnp.sum(jnp.square(out[...]), keepdims=True) for out in (qkv_out, pu_out, down_ref))
    sq_mine[...] = jnp.broadcast_to(local_sum, sq_mine.shape)
    run_all(share_sum_steps(p, copies, sq_mine, along_sq, across_sq, total_out))
    total_out[...] = total_out[...] + jnp.sum(jnp.square(norm_out[...]), keepdims=True)
    store.wait_all()
    copies.finish()


def qkv_kernel(info_ref, x_ref, norms_ref, weight_ref, mixed_ref, summ_ref, sum_scr):
    step = pl.program_id(0)
    tile, width = x_ref.shape
    length, first_span = info_ref[0], info_ref[1]
    mixed = qkv_tile(x_ref[...], norms_ref, weight_ref)
    mixed_ref[...] = mixed
    per = tile // SPAN
    for part in range(per):
        span = step * per + part
        sum_scr[pl.ds(span, 1), :] = span_sum(
            mixed[part * SPAN : (part + 1) * SPAN, width:], length, (first_span + span) * SPAN
        )

    @pl.when(step == pl.num_programs(0) - 1)
    def _():
        summ_ref[...] = sum_scr[...].astype(BF)


def attend_kernel(info_ref, mixed_ref, summ_ref, out_ref, lse_ref, vt_scr):
    step = pl.program_id(0)
    width = out_ref.shape[1]

    @pl.when(step == 0)
    def _():
        vt_scr[...] = summ_ref[:, width:].T

    caps = span_caps(info_ref[0], info_ref[1] + step)
    attend_spans([(0, 0, caps)], mixed_ref, width, summ_ref, vt_scr, out_ref, lse_ref)


def attend_back_kernel(info_ref, mixed_ref, grad_ref, lse_ref, summ_ref, back_ref, dsumm_ref, kt_scr):
    step = pl.program_id(0)
    width = grad_ref.shape[1]

    @pl.when(step == 0)
    def _():
        kt_scr[...] = summ_ref[:, :width].T
        dsumm_ref[...] = jnp.zeros_like(dsumm_ref)

    caps = span_caps(info_ref[0], info_ref[1] + step)
    attend_back_spans(
        [(0, 0, caps)], mixed_ref, grad_ref, width, summ_ref, kt_scr, lse_ref, back_ref, dsumm_ref
    )


def mlp_kernel(
    x_ref, attn_ref, og_ref, norms_ref, pu_ref, down_ref,
    out_ref, resid_grad_ref, attn_grad_ref, pu_grad_ref, down_grad_ref, norm_grad_ref,
    activ_scr, pre_grad_scr, n2t_scr, attnt_scr, ogt_scr, pig_scr, norm_scr,
):
    step = pl.program_id(0)
    tile, width = x_ref.shape
    hidden = down_ref.shape[0]
    rows = pl.ds(pl.multiple_of(step * tile, tile), tile)
    chunk = 256
    attn = attn_ref[...]
    grad = og_ref[...]
    resid = x_ref[...].astype(F32) + dot(attn, pu_ref[:, :width])
    xhat, rstd = normalize(resid)
    gain = norms_ref[2:3, :]
    normed = (xhat * gain + norms_ref[3:4, :]).astype(BF)
    attnt_scr[:, rows] = attn.T
    n2t_scr[:, rows] = normed.T
    ogt_scr[:, rows] = grad.T
    for at in range(0, hidden, chunk):
        pre = dot(normed, pu_ref[:, width + at : width + at + chunk])
        act_grad = dot_nt(grad, down_ref[at : at + chunk, :])
        value, slope = gelu_parts(pre)
        activ = value.astype(BF)
        pre_grad = (act_grad * slope).astype(BF)
        activ_scr[rows, at : at + chunk] = activ
        pre_grad_scr[rows, at : at + chunk] = pre_grad
    out_ref[...] = (resid + dot(activ_scr[rows, :], down_ref[...])).astype(BF)
    back = dot_nt(pre_grad_scr[rows, :], pu_ref[:, width:])
    resid_grad = grad.astype(F32) + norm_back(back, gain, xhat, rstd)
    resid_grad_ref[...] = resid_grad
    pig = resid_grad.astype(BF)
    pig_scr[rows, :] = pig
    attn_grad_ref[...] = dot_nt(pig, pu_ref[:, :width]).astype(BF)
    gain_part = jnp.sum(back * xhat, axis=0, keepdims=True)
    shift_part = jnp.sum(back, axis=0, keepdims=True)
    part = jnp.concatenate([gain_part, shift_part], axis=0)

    @pl.when(step == 0)
    def _():
        norm_scr[...] = part

    @pl.when(step > 0)
    def _():
        norm_scr[...] += part

    @pl.when(step == pl.num_programs(0) - 1)
    def _():
        norm_grad_ref[...] = norm_scr[...]
        pu_grad_ref[:, :width] = dot(attnt_scr[...], pig_scr[...]).astype(BF)
        cols = 512

        def one(index, carry):
            c = pl.ds(pl.multiple_of(index * cols, cols), cols)
            out = pl.ds(pl.multiple_of(width + index * cols, cols), cols)
            pu_grad_ref[:, out] = dot(n2t_scr[...], pre_grad_scr[:, c]).astype(BF)
            down_grad_ref[c, :] = dot(ogt_scr[...], activ_scr[:, c]).T.astype(BF)
            return carry

        lax.fori_loop(0, hidden // cols, one, 0)


def final_kernel(
    info_ref, x_ref, back_ref, extra_ref, resid_grad_ref, norms_ref, weight_ref,
    input_grad_ref, qkv_grad_ref, norm_grad_ref, mg_scr, normed_scr,
):
    step = pl.program_id(0)
    tile, width = x_ref.shape
    rows = pl.ds(pl.multiple_of(step * tile, tile), tile)
    length, first_span = info_ref[0], info_ref[1]
    xhat, rstd = normalize(x_ref[...].astype(F32))
    gain = norms_ref[0:1, :]
    normed_scr[rows, :] = (xhat * gain + norms_ref[1:2, :]).astype(BF)
    per = tile // SPAN
    parts = []
    for part in range(per):
        span = step * per + part
        here = back_ref[part * SPAN : (part + 1) * SPAN, width:]
        parts.append(with_extra(here, extra_ref[pl.ds(span, 1), :], length, (first_span + span) * SPAN))
    mg = jnp.concatenate([back_ref[:, :width], jnp.concatenate(parts, axis=0)], axis=1)
    mg_scr[rows, :] = mg
    back = dot_nt(mg, weight_ref[...])
    input_grad_ref[...] = resid_grad_ref[...] + norm_back(back, gain, xhat, rstd)

    @pl.when(step == 0)
    def _():
        norm_grad_ref[...] = jnp.zeros_like(norm_grad_ref)

    norm_grad_ref[0:1, :] += jnp.sum(back * xhat, axis=0, keepdims=True)
    norm_grad_ref[1:2, :] += jnp.sum(back, axis=0, keepdims=True)

    @pl.when(step == pl.num_programs(0) - 1)
    def _():
        cols = 256

        def one(index, carry):
            c = pl.ds(pl.multiple_of(index * cols, cols), cols)
            qkv_grad_ref[:, c] = dot_tn(normed_scr[...], mg_scr[:, c]).astype(BF)
            return carry

        lax.fori_loop(0, qkv_grad_ref.shape[1] // cols, one, 0)


def whole(shape):
    return pl.BlockSpec(shape, lambda i: (0,) * len(shape))


def by_rows(tile, width):
    return pl.BlockSpec((tile, width), lambda i: (i, 0))


SCALARS = pl.BlockSpec(memory_space=pltpu.SMEM)
PARAMS = pltpu.CompilerParams(vmem_limit_bytes=VMEM_LIMIT)


def remote_call(kernel, groups, seqs, name, collective_id, outs, ins, scratch, loads, copies):
    return pl.pallas_call(
        functools.partial(kernel, groups, seqs),
        in_specs=[pl.BlockSpec(memory_space=space) for space in ins],
        out_specs=[pl.BlockSpec(memory_space=space) for space, _, _ in outs],
        out_shape=[jax.ShapeDtypeStruct(shape, kind) for _, shape, kind in outs],
        scratch_shapes=list(scratch) + [pltpu.SemaphoreType.DMA((n,)) for n in (loads, copies, copies)],
        compiler_params=pltpu.CompilerParams(
            vmem_limit_bytes=VMEM_LIMIT, collective_id=collective_id, has_side_effects=True
        ),
        name=name,
    )


def regroup(grad, dim, outer, inner):
    shape = grad.shape
    piece = shape[dim] // (outer * inner)
    split = grad.reshape(shape[:dim] + (outer, inner, piece) + shape[dim + 1 :])
    return jnp.swapaxes(split, dim, dim + 1).reshape(shape)


def gather_plain(state):
    both = ("batch", "seq")
    qkv, proj, up, down = (lax.all_gather(w.astype(BF), both, axis=0, tiled=True) for w in state[:4])
    norms = lax.all_gather(state[4].astype(BF), both, axis=1, tiled=True).astype(F32)
    return qkv, jnp.concatenate([proj, up], axis=1), down, norms


def reduce_plain(qkv_grad, pu_grad, down_grad, norm_grad):
    groups, seqs = lax.axis_size("batch"), lax.axis_size("seq")
    reduced = []
    for grad, dim in ((qkv_grad, 0), (pu_grad, 0), (down_grad, 0)):
        part = lax.psum_scatter(
            regroup(grad.astype(F32), dim, groups, seqs), "seq", scatter_dimension=dim, tiled=True
        )
        reduced.append(lax.psum_scatter(part, "batch", scatter_dimension=dim, tiled=True))
    norm_total = lax.psum(norm_grad, ("batch", "seq"))
    squares = lax.psum(sum(jnp.sum(grad * grad) for grad in reduced), ("batch", "seq"))
    squares = squares + jnp.sum(norm_total * norm_total)
    return (*reduced, norm_total, jnp.broadcast_to(squares, (8, LANES)))


def mlp_call(x, attn_out, grad_rows, norms, pu_full, down_full):
    sds = jax.ShapeDtypeStruct
    rows, width = x.shape
    hidden = down_full.shape[0]
    tile = min(512, rows)
    steps = rows // tile
    return pl.pallas_call(
        mlp_kernel,
        grid=(steps,),
        in_specs=[by_rows(tile, width)] * 3
        + [whole(norms.shape), whole(pu_full.shape), whole(down_full.shape)],
        out_specs=[by_rows(tile, width)] * 3
        + [whole(pu_full.shape), whole(down_full.shape), whole((2, width))],
        out_shape=[
            sds((rows, width), BF), sds((rows, width), F32), sds((rows, width), BF),
            sds(pu_full.shape, BF), sds(down_full.shape, BF), sds((2, width), F32),
        ],
        scratch_shapes=[
            pltpu.VMEM((rows, hidden), BF), pltpu.VMEM((rows, hidden), BF),
            pltpu.VMEM((width, rows), BF), pltpu.VMEM((width, rows), BF), pltpu.VMEM((width, rows), BF),
            pltpu.VMEM((rows, width), BF), pltpu.VMEM((2, width), F32),
        ],
        compiler_params=PARAMS,
        name="mlp",
    )(x, attn_out, grad_rows, norms, pu_full, down_full)


def direct_body(groups, seqs, inputs, out_grad, lengths, *state):
    rows, width = inputs.shape[1], inputs.shape[2]
    own_rows, down_rows = state[0].shape[0], state[3].shape[0]
    hidden = state[2].shape[1]
    chips = seqs // 2
    grid3 = (groups, chips, 2)
    local = rows // SPAN
    spans = local * seqs
    pairs = width // LANES
    count = rows // TILE
    x, grad_rows = inputs[0], out_grad[0]
    vmem, hbm, smem = pltpu.VMEM, pl.ANY, pltpu.SMEM
    shapes = (
        (*grid3, own_rows, 3 * width), (*grid3, own_rows, width + hidden), (*grid3, down_rows, width),
    )
    tokens = (rows, width)
    (
        qkv_full, pu_full, down_full, norms, mixed, summ, attn_out, lse, outputs, resid, slope, down_grad,
    ) = remote_call(
        front_kernel, groups, seqs, "front", 0,
        [
            *((hbm, shape, BF) for shape in shapes), (vmem, (4, width), F32), (hbm, (rows, 3 * width), BF),
            (vmem, (chips, 2, local, 2 * width), BF), (hbm, tokens, BF), (vmem, (local, pairs, 2 * SPAN), F32),
            (hbm, tokens, BF), (hbm, tokens, F32), (hbm, (rows, hidden), BF), (hbm, (hidden, width), BF),
        ],
        [smem, hbm, hbm] + [vmem] * 5,
        [
            vmem(tokens, BF), vmem(tokens, BF), *(vmem(shape, BF) for shape in shapes),
            vmem((rows, 3 * width), BF), vmem(tokens, BF), vmem(tokens, BF), vmem(tokens, F32),
            vmem((rows, hidden), BF), vmem((rows, hidden), BF), vmem((hidden, width), BF),
            vmem((*grid3, 4, LANES), F32), vmem((local, 2 * width), F32), vmem((width, spans), BF),
        ],
        4 + 6 * count + hidden // TILE, 6 * GATHER_COPIES + fast_gather_copies(chips) + 2 * chips,
    )(lengths, x, grad_rows, *state[:5])
    pu_flat, down_flat = pu_full.reshape(width, width + hidden), down_full.reshape(hidden, width)
    resid_grad, attn_grad, pu_grad, down_own, norm_two = remote_call(
        middle_kernel, groups, seqs, "middle", 1,
        [
            (hbm, tokens, F32), (hbm, tokens, BF), (hbm, pu_flat.shape, BF),
            (vmem, (down_rows, width), F32), (vmem, (2, width), F32),
        ],
        [hbm] * 6 + [vmem, hbm],
        [
            vmem(tokens, BF), vmem(tokens, F32), vmem((rows, hidden), BF), vmem(tokens, BF),
            vmem(pu_flat.shape, BF), vmem(down_flat.shape, BF), vmem(tokens, F32), vmem(tokens, BF),
            vmem(pu_flat.shape, BF), vmem((rows, hidden), BF), vmem(tokens, BF), vmem(tokens, BF),
            *scatter_scratch(groups, chips, down_rows // 2, width) * 2,
        ],
        6 + 5 * count, 2 * SCATTER_COPIES,
    )(grad_rows, resid, slope, attn_out, pu_flat, down_flat, norms, down_grad.reshape(shapes[2]))
    half = (width + hidden) // 2
    blocks = ((own_rows, half),) * 2 + ((own_rows, width),) * 3
    summ_block = (local, 2 * width)
    scratch = [
        vmem(tokens, BF), vmem((rows, 3 * width), BF), vmem(tokens, BF), vmem(tokens, F32),
        vmem((width, 3 * width), BF), vmem(tokens, F32),
        vmem((rows, 3 * width), BF), vmem(tokens, BF), vmem((width, spans), BF), vmem((spans, 2 * width), F32),
        vmem((chips, *summ_block), F32), vmem((chips - 1, *summ_block), BF),
        vmem((chips - 1, *summ_block), BF), vmem(summ_block, F32),
        *[vmem((*grid3, own_rows, width), BF)] * 3, *[vmem((width, LANES), F32)] * 2,
    ]
    scratch += [buffer for block in blocks for buffer in scatter_scratch(groups, chips, *block)]
    scratch += [
        vmem((4, width), F32), vmem((seqs, 4, width), F32), vmem((groups, 4, width), F32),
        vmem((8, LANES), F32), vmem((seqs, 8, LANES), F32), vmem((groups, 8, LANES), F32),
    ]
    input_grad, qkv_own, pu_own, norm_total, total = remote_call(
        back_kernel, groups, seqs, "back", 2,
        [
            (hbm, tokens, F32), (vmem, (own_rows, 3 * width), F32), (vmem, (own_rows, width + hidden), F32),
            (vmem, (4, width), F32), (vmem, (8, LANES), F32),
        ],
        [smem, hbm, hbm, hbm, vmem, vmem, hbm, hbm, vmem, vmem, hbm, vmem],
        scratch, local + 3 + 5 + count,
        5 * SCATTER_COPIES + 2 * share_copies(groups, seqs) + 2 * chips,
    )(
        lengths, x, mixed, attn_grad, lse, summ.reshape(spans, 2 * width), pu_grad.reshape(shapes[1]),
        resid_grad, down_own, norms, qkv_full.reshape(width, 3 * width), norm_two,
    )
    return outputs, input_grad, (qkv_own, pu_own, down_own), norm_total, total


def plain_body(groups, seqs, inputs, out_grad, lengths, *state):
    sds = jax.ShapeDtypeStruct
    rows, width = inputs.shape[1], inputs.shape[2]
    qkv_full, pu_full, down_full, norms = gather_plain(state[:5])
    local = rows // SPAN
    spans = local * seqs
    info = jnp.stack([lengths[0], (lax.axis_index("seq") * local).astype(jnp.int32)])
    x, grad_rows = inputs[0], out_grad[0]
    tile = 256
    steps = rows // tile
    mixed, own_summ = pl.pallas_call(
        qkv_kernel,
        grid=(steps,),
        in_specs=[SCALARS, by_rows(tile, width), whole(norms.shape), whole(qkv_full.shape)],
        out_specs=[by_rows(tile, 3 * width), whole((local, 2 * width))],
        out_shape=[sds((rows, 3 * width), BF), sds((local, 2 * width), BF)],
        scratch_shapes=[pltpu.VMEM((local, 2 * width), F32)],
        compiler_params=PARAMS,
        name="qkv",
    )(info, x, norms, qkv_full)
    summ = lax.all_gather(own_summ, "seq", axis=0, tiled=True)
    pairs = width // LANES
    lse_spec = pl.BlockSpec((1, pairs, 2 * SPAN), lambda i: (i, 0, 0))
    attn_out, lse = pl.pallas_call(
        attend_kernel,
        grid=(local,),
        in_specs=[SCALARS, by_rows(SPAN, 3 * width), whole(summ.shape)],
        out_specs=[by_rows(SPAN, width), lse_spec],
        out_shape=[sds((rows, width), BF), sds((local, pairs, 2 * SPAN), F32)],
        scratch_shapes=[pltpu.VMEM((width, spans), BF)],
        compiler_params=PARAMS,
        name="attend",
    )(info, mixed, summ)
    outputs, resid_grad, attn_grad, pu_grad, down_grad, norm_two = mlp_call(
        x, attn_out, grad_rows, norms, pu_full, down_full
    )
    back, dsumm = pl.pallas_call(
        attend_back_kernel,
        grid=(local,),
        in_specs=[SCALARS, by_rows(SPAN, 3 * width), by_rows(SPAN, width), lse_spec, whole(summ.shape)],
        out_specs=[by_rows(SPAN, 3 * width), whole((spans, 2 * width))],
        out_shape=[sds((rows, 3 * width), BF), sds((spans, 2 * width), F32)],
        scratch_shapes=[pltpu.VMEM((width, spans), BF)],
        compiler_params=PARAMS,
        name="attend_back",
    )(info, mixed, attn_grad, lse, summ)
    extra = lax.psum_scatter(dsumm, "seq", scatter_dimension=0, tiled=True)
    input_grad, qkv_grad, norm_one = pl.pallas_call(
        final_kernel,
        grid=(steps,),
        in_specs=[
            SCALARS, by_rows(tile, width), by_rows(tile, 3 * width), whole(extra.shape), by_rows(tile, width),
            whole(norms.shape), whole(qkv_full.shape),
        ],
        out_specs=[by_rows(tile, width), whole(qkv_full.shape), whole((2, width))],
        out_shape=[sds((rows, width), F32), sds(qkv_full.shape, BF), sds((2, width), F32)],
        scratch_shapes=[pltpu.VMEM((rows, 3 * width), BF), pltpu.VMEM((rows, width), BF)],
        compiler_params=PARAMS,
        name="final",
    )(info, x, back, extra, resid_grad, norms, qkv_full)
    norm_grad = jnp.concatenate([norm_one, norm_two], axis=0)
    *grads, norm_total, total = reduce_plain(qkv_grad, pu_grad, down_grad, norm_grad)
    return outputs, input_grad, grads, norm_total, total


def body(groups, seqs, *args):
    state = args[3:]
    direct = groups == 4 and seqs % 4 == 0 and state[0].shape[0] % 16 == 0 and args[0].shape[1] % TILE == 0
    run = direct_body if direct else plain_body
    outputs, input_grad, grads, norm_total, total = run(groups, seqs, *args)
    sds = jax.ShapeDtypeStruct
    vmem, hbm = pltpu.VMEM, pl.ANY
    spec = lambda space: pl.BlockSpec(memory_space=space)
    held = [sds(w.shape, F32) for w in state[:5]]
    parts = 8
    outputs, input_grad, grad_norm, *fresh, shift_clipped = pl.pallas_call(
        functools.partial(update_kernel, parts),
        in_specs=[spec(vmem)] * 5 + [spec(hbm)] * 2 + [spec(vmem)] * 15,
        out_specs=[spec(hbm)] * 2 + [spec(vmem)] * 17,
        out_shape=[
            sds(outputs.shape, BF), sds(input_grad.shape, F32), sds((1, 1), F32), *held * 3,
            sds((1, state[4].shape[1]), F32),
        ],
        scratch_shapes=[
            vmem(outputs.shape, BF), vmem(input_grad.shape, F32), pltpu.SemaphoreType.DMA((4 * parts,)),
        ],
        compiler_params=PARAMS,
        name="update",
    )(total, *grads, norm_total, outputs, input_grad, *state)
    return (outputs[None], input_grad[None], grad_norm[0, 0], *fresh, shift_clipped[0])


def solution(mesh):
    tokens = P("batch", "seq", None)
    owned = P(("batch", "seq"), None)
    columns = P(None, ("batch", "seq"))
    state = (owned, owned, owned, owned, columns)
    return jax.shard_map(
        functools.partial(body, mesh.shape["batch"], mesh.shape["seq"]),
        mesh=mesh,
        in_specs=(tokens, tokens, P("batch")) + state * 3,
        out_specs=(tokens, tokens, P()) + state * 3 + (P(("batch", "seq")),),
        check_vma=False,
    )
```

```python
import functools
import jax
import jax.numpy as jnp
from jax import lax
from jax.experimental import pallas as pl
from jax.experimental.pallas import tpu as pltpu
from jax.sharding import PartitionSpec as P

HEADS = 8
HD = 64
SPAN = 128
STEP = 10
LN_EPS = 1e-05
NEG_FILL = -1e30
CLIP = 1.0
BETA = 0.5
ADAM_EPS = 1e-08
DECAY = 0.1
RATES = (0.02, 0.3, 0.02, 0.02, 0.5)
BF = jnp.bfloat16
F32 = jnp.float32
LANES = 128
VMEM_LIMIT = 56 * 1024 * 1024


def dot(a, b, dims=((1,), (0,))):
    return lax.dot_general(a, b, (dims, ((), ())), preferred_element_type=F32)


def dot_tn(a, b):
    return dot(a, b, ((0,), (0,)))


def dot_nt(a, b):
    return dot(a, b, ((1,), (1,)))


def normalize(x):
    inv = 1.0 / x.shape[-1]
    centred = x - jnp.sum(x, axis=-1, keepdims=True) * inv
    spread = jnp.sum(centred * centred, axis=-1, keepdims=True) * inv
    rstd = lax.rsqrt(spread + LN_EPS)
    return centred * rstd, rstd


def norm_back(grad, gain, xhat, rstd):
    inv = 1.0 / grad.shape[-1]
    e = grad * gain
    mean_e = jnp.sum(e, axis=-1, keepdims=True) * inv
    mean_ex = jnp.sum(e * xhat, axis=-1, keepdims=True) * inv
    return rstd * (e - mean_e - xhat * mean_ex)


def qkv_tile(x, norms_ref, weight_ref):
    xhat, _ = normalize(x.astype(F32))
    normed = (xhat * norms_ref[0:1, :] + norms_ref[1:2, :]).astype(BF)
    return dot(normed, weight_ref[...]).astype(BF)


def span_scale(length, begin, shape):
    count = jnp.clip(length - begin, 1, SPAN)
    return lax.rsqrt(jnp.full(shape, count, jnp.int32).astype(F32))


def span_sum(kv, length, begin):
    row = lax.broadcasted_iota(jnp.int32, kv.shape, 0)
    kept = jnp.where(row < length - begin, kv.astype(F32), 0.0)
    total = jnp.sum(kept, axis=0, keepdims=True)
    return total * span_scale(length, begin, total.shape)


def stack_heads(pair):
    lane = lax.broadcasted_iota(jnp.int32, pair.shape, 1)
    zero = jnp.zeros_like(pair)
    return jnp.concatenate(
        [jnp.where(lane < HD, pair, zero), jnp.where(lane >= HD, pair, zero)], axis=0
    )


def fold_heads(both):
    picked = jnp.concatenate([both[:HD, :SPAN], both[HD:, SPAN:]], axis=0)
    return picked.T


def span_caps(length, span):
    query_pos = lax.broadcasted_iota(jnp.int32, (1, 2 * SPAN), 1) & (SPAN - 1)
    near_cap = jnp.minimum(query_pos, length - span * SPAN - 1)
    far_cap = jnp.minimum(span, (length + SPAN - 1) // SPAN)
    return near_cap, far_cap


def mask_scores(raw, caps):
    near_cap, far_cap = caps
    key_pos = lax.broadcasted_iota(jnp.int32, (SPAN, 2 * SPAN), 0)
    summ_pos = lax.broadcasted_iota(jnp.int32, (raw.shape[0] - SPAN, 2 * SPAN), 0)
    near = jnp.where(key_pos <= near_cap, raw[:SPAN], NEG_FILL)
    far = jnp.where(summ_pos < far_cap, raw[SPAN:], NEG_FILL)
    return jnp.concatenate([near, far], axis=0)


def attend_spans(spans, mixed_ref, width, summ_ref, summ_vt_ref, out_ref, lse_ref=None, probs_ref=None):
    units = [(pl.ds(row, SPAN), index, caps, pair) for row, index, caps in spans for pair in range(width // LANES)]
    queries, keys, values_t = [], [], []
    for rows, index, caps, pair in units:
        at = pair * LANES
        queries.append(stack_heads(mixed_ref[rows, at : at + LANES] * BF(0.125)))
        near_k = mixed_ref[rows, width + at : width + at + LANES]
        near_v = mixed_ref[rows, 2 * width + at : 2 * width + at + LANES]
        keys.append(jnp.concatenate([near_k, summ_ref[:, at : at + LANES]], axis=0))
        values_t.append(jnp.concatenate([near_v.T, summ_vt_ref[at : at + LANES, :]], axis=1))
    scores = [dot_nt(k, q) for k, q in zip(keys, queries)]
    scores = [mask_scores(s, unit[2]) for s, unit in zip(scores, units)]
    peaks = [jnp.max(s, axis=0, keepdims=True) for s in scores]
    expos = [jnp.exp(s - p) for s, p in zip(scores, peaks)]
    totals = [jnp.sum(e, axis=0, keepdims=True) for e in expos]
    probs = [(e * (1.0 / t)).astype(BF) for e, t in zip(expos, totals)]
    outs = [dot(v, p) for v, p in zip(values_t, probs)]
    for (rows, index, caps, pair), out, prob, peak, total in zip(units, outs, probs, peaks, totals):
        at = pair * LANES
        out_ref[rows, at : at + LANES] = fold_heads(out).astype(BF)
        if lse_ref is not None:
            lse_ref[index, pair : pair + 1, :] = peak + jnp.log(total)
        if probs_ref is not None:
            at = pair * 4 * SPAN
            probs_ref[rows, at : at + 2 * SPAN] = prob[:SPAN]
            probs_ref[rows, at + 2 * SPAN : at + 4 * SPAN] = prob[SPAN:]


def attend_back_spans(
    spans, mixed_ref, grad_ref, width, summ_ref, summ_kt_ref, lse_ref, back_ref, dsumm_ref, probs_ref=None
):
    pairs = width // LANES
    units = [(pl.ds(row, SPAN), index, caps, pair) for row, index, caps in spans for pair in range(pairs)]
    queries, grads, keys, keys_t, values = [], [], [], [], []
    for rows, index, caps, pair in units:
        at = pair * LANES
        queries.append(stack_heads(mixed_ref[rows, at : at + LANES] * BF(0.125)))
        grads.append(stack_heads(grad_ref[rows, at : at + LANES]))
        near_k = mixed_ref[rows, width + at : width + at + LANES]
        near_v = mixed_ref[rows, 2 * width + at : 2 * width + at + LANES]
        keys.append(jnp.concatenate([near_k, summ_ref[:, at : at + LANES]], axis=0))
        keys_t.append(jnp.concatenate([near_k.T, summ_kt_ref[at : at + LANES, :]], axis=1))
        values.append(jnp.concatenate([near_v, summ_ref[:, width + at : width + at + LANES]], axis=0))
    if probs_ref is None:
        scores = [dot_nt(k, q) for k, q in zip(keys, queries)]
        dprobs = [dot_nt(v, g) for v, g in zip(values, grads)]
        scores = [mask_scores(s, unit[2]) for s, unit in zip(scores, units)]
        probs = [jnp.exp(s - lse_ref[index, pair : pair + 1, :]) for s, (_, index, _, pair) in zip(scores, units)]
    else:
        dprobs = [dot_nt(v, g) for v, g in zip(values, grads)]
        probs = []
        for rows, _, _, pair in units:
            at = pair * 4 * SPAN
            near, far = probs_ref[rows, at : at + 2 * SPAN], probs_ref[rows, at + 2 * SPAN : at + 4 * SPAN]
            probs.append(jnp.concatenate([near, far], axis=0).astype(F32))
    deltas = [jnp.sum(p * d, axis=0, keepdims=True) for p, d in zip(probs, dprobs)]
    dscores = [(p * (d - delta)).astype(BF) for p, d, delta in zip(probs, dprobs, deltas)]
    probs = [p.astype(BF) for p in probs]
    dqs = [dot(k, ds) for k, ds in zip(keys_t, dscores)]
    dks = [dot(ds, q) for ds, q in zip(dscores, queries)]
    dvs = [dot(p, g) for p, g in zip(probs, grads)]
    for (rows, index, caps, pair), dq, dk, dv in zip(units, dqs, dks, dvs):
        at = pair * LANES
        back_ref[rows, at : at + LANES] = (fold_heads(dq) * 0.125).astype(BF)
        back_ref[rows, width + at : width + at + LANES] = dk[:SPAN].astype(BF)
        back_ref[rows, 2 * width + at : 2 * width + at + LANES] = dv[:SPAN].astype(BF)
    for pair in range(pairs):
        at = pair * LANES
        dsumm_ref[:, at : at + LANES] += sum(dk[SPAN:] for dk in dks[pair::pairs])
        dsumm_ref[:, width + at : width + at + LANES] += sum(dv[SPAN:] for dv in dvs[pair::pairs])


def with_extra(back, extra, length, begin):
    extra = extra * span_scale(length, begin, extra.shape)
    pos = lax.broadcasted_iota(jnp.int32, back.shape, 0)
    return (back.astype(F32) + jnp.where(pos < length - begin, extra, 0.0)).astype(BF)


GELU_A = 0.7978845608
GELU_B = 0.044715


def gelu_parts(t):
    slow = GELU_A + (GELU_A * GELU_B) * (t * t)
    half = 0.5 * jnp.tanh(t * slow) + 0.5
    value = t * half
    return value, half + (value - value * half) * (6.0 * slow - 4.0 * GELU_A)


MESH = pl.DeviceIdType.MESH


class Place:
    def __init__(self, groups, seqs):
        self.groups, self.seqs, self.chips = groups, seqs, seqs // 2
        self.b = lax.axis_index("batch")
        self.seq = lax.axis_index("seq")
        self.z, self.c = self.seq // 2, self.seq % 2
        self.other = 1 - self.c
        self.b1 = self.b + 1 - 2 * (self.b % 2)
        self.b2 = (self.b + 2) % 4
        self.b3 = self.b1 + 2 - 4 * (self.b1 // 2)
        self.after = [(self.z + k) % self.chips for k in range(self.chips)]
        self.before = [(self.z + self.chips - k) % self.chips for k in range(self.chips)]
        self.sibling = (self.b, 2 * self.z + self.other)
        self.x, self.y, self.diagonal = (self.b1, self.seq), (self.b2, self.seq), (self.b3, self.seq)
        self.along = [(self.b, 2 * z + self.c) for z in self.after]
        self.ring = [(self.b, (self.seq + k) % seqs) for k in range(seqs)]


def meet(place):
    barrier = pltpu.get_barrier_semaphore()
    partners = [place.x, place.y, place.diagonal, *place.ring[1:]]
    for partner in partners:
        pl.semaphore_signal(barrier, inc=1, device_id=partner, device_id_type=MESH)
    pl.semaphore_wait(barrier, len(partners))


def part_of(ref, index):
    return ref if index is None else ref.at[index]


class Copy:
    def __init__(self, make):
        self.make = make
        make().start()

    def wait(self):
        self.make().wait()

    def wait_recv(self):
        self.make().wait_recv()

    def wait_send(self):
        self.make().wait_send()


class Copies:
    def __init__(self, send_sems, recv_sems):
        self.send, self.recv, self.made, self.left = send_sems, recv_sems, [], 0

    def start(self, src, src_index, dst, dst_index, device):
        at = len(self.made)
        assert at < self.send.shape[0]
        copy = Copy(
            lambda: pltpu.make_async_remote_copy(
                src_ref=part_of(src, src_index), dst_ref=part_of(dst, dst_index),
                send_sem=self.send.at[at], recv_sem=self.recv.at[at],
                device_id=device, device_id_type=MESH,
            )
        )
        self.made.append(copy)
        return copy

    def push(self, ref, index, device):
        return self.start(ref, index, ref, index, device)

    def finish(self):
        for copy in self.made[self.left :]:
            copy.wait_send()
        self.left = len(self.made)


class Loads:
    def __init__(self, sems):
        self.sems, self.made = sems, 0

    def start(self, src, dst, src_index=None, dst_index=None):
        at = self.made
        assert at < self.sems.shape[0]
        self.made += 1
        return Copy(
            lambda: pltpu.make_async_copy(part_of(src, src_index), part_of(dst, dst_index), self.sems.at[at])
        )


def gather_steps(place, copies, full, rows=slice(None), cols=slice(None)):
    p, half = place, place.chips // 2
    low, high = slice(0, half), slice(half, place.chips)

    def push(b, z, device):
        return copies.push(full, (b, z, p.c, rows, cols), device)

    along = [push(p.b, p.z, device) for device in p.along[1:]]
    yield
    for copy in along:
        copy.wait_recv()
    every = slice(None)
    to_x, to_y, sib = push(p.b, every, p.x), push(p.b, every, p.y), [push(p.b, every, p.sibling)]
    yield
    to_x.wait_recv()
    on_y = push(p.b1, low, p.y)
    to_y.wait_recv()
    on_x = push(p.b2, high, p.x)
    sib += [push(p.b1, every, p.sibling), push(p.b2, every, p.sibling)]
    yield
    on_y.wait_recv()
    sib.append(push(p.b3, low, p.sibling))
    on_x.wait_recv()
    sib.append(push(p.b3, high, p.sibling))
    yield
    for copy in sib:
        copy.wait_recv()


GATHER_COPIES = 12


def fast_gather_steps(place, copies, full, rows=slice(None), cols=slice(None)):
    p = place
    order = range(p.chips)
    early, late = order[: p.chips // 2], order[p.chips // 2 :]

    def push(b, k, device):
        return copies.push(full, (b, p.before[k], p.c, rows, cols), device)

    along = [push(p.b, 0, device) for device in p.along[1:]]
    to_x, to_y, sib = [push(p.b, 0, p.x)], [push(p.b, 0, p.y)], [push(p.b, 0, p.sibling)]
    yield
    for k, copy in enumerate(along, 1):
        copy.wait_recv()
        to_x.append(push(p.b, k, p.x))
        to_y.append(push(p.b, k, p.y))
        sib.append(push(p.b, k, p.sibling))
    yield
    on = []
    for k in early:
        to_x[k].wait_recv()
        on.append(push(p.b1, k, p.y))
        sib.append(push(p.b1, k, p.sibling))
    for k in late:
        to_y[k].wait_recv()
        on.append(push(p.b2, k, p.x))
        sib.append(push(p.b2, k, p.sibling))
    yield
    for k in late:
        to_x[k].wait_recv()
        sib.append(push(p.b1, k, p.sibling))
    for k in early:
        to_y[k].wait_recv()
        sib.append(push(p.b2, k, p.sibling))
    for k, copy in enumerate(on):
        copy.wait_recv()
        sib.append(push(p.b3, k, p.sibling))
    yield
    for copy in sib:
        copy.wait_recv()


def fast_gather_copies(chips):
    return chips - 1 + 3 * chips + 4 * chips


def scatter_steps(place, copies, loads, grad, acc, got, near, far, last, result):
    p, half = place, place.chips // 2
    low, high = slice(0, half), slice(half, place.chips)
    chips = p.chips

    def add(into, *others):
        total = acc[into].astype(F32)
        for other in others:
            total = total + other.astype(F32)
        acc[into] = total.astype(BF)

    every = slice(None)
    swap = copies.start(grad, (every, every, p.other), got, None, p.sibling)
    keep = loads.start(grad, acc, (every, every, p.c))
    yield
    keep.wait()
    swap.wait_recv()
    for b in (p.b3, p.b1, p.b2):
        for z in range(chips):
            add((b, z), got[b, z])
    on_y = copies.start(acc, (p.b3, low), far, 0, p.y)
    on_x = copies.start(acc, (p.b3, high), far, 1, p.x)
    early_x = copies.start(acc, (p.b1, high), near, (0, high), p.x)
    early_y = copies.start(acc, (p.b2, low), near, (1, low), p.y)
    for z in range(chips):
        add((p.b, z), got[p.b, z])
    yield
    on_y.wait_recv()
    for z in range(half):
        add((p.b1, z), far[0, z])
    late_x = copies.start(acc, (p.b1, low), near, (0, low), p.x)
    on_x.wait_recv()
    for z in range(half, chips):
        add((p.b2, z), far[1, z - half])
    late_y = copies.start(acc, (p.b2, high), near, (1, high), p.y)
    yield
    for copy in (early_x, early_y, late_x, late_y):
        copy.wait_recv()
    for z in range(chips):
        add((p.b, z), near[0, z], near[1, z])
    along = []
    for k in range(1, chips):
        along.append(copies.start(acc, (p.b, p.after[k]), last, k - 1, p.along[k]))
    yield
    total = acc[p.b, p.z].astype(F32)
    for k, copy in enumerate(along):
        copy.wait_recv()
        total = total + last[k].astype(F32)
    result[...] = total


SCATTER_COPIES = 10


def scatter_scratch(groups, chips, rows, cols):
    half = chips // 2
    return [
        pltpu.VMEM((groups, chips, rows, cols), BF),
        pltpu.VMEM((groups, chips, rows, cols), BF),
        pltpu.VMEM((2, chips, rows, cols), BF),
        pltpu.VMEM((2, half, rows, cols), BF),
        pltpu.VMEM((chips - 1, rows, cols), BF),
    ]


def share_sum_steps(place, copies, mine, along, across, result):
    p, seqs = place, along.shape[0]
    along[p.seq] = mine[...]
    sent = [copies.push(along, p.seq, device) for device in p.ring[1:]]
    yield
    for copy in sent:
        copy.wait_recv()
    across[p.b] = sum(along[s] for s in range(seqs))
    sent = [copies.push(across, p.b, device) for device in (p.x, p.y, p.diagonal)]
    yield
    for copy in sent:
        copy.wait_recv()
    result[...] = sum(across[b] for b in range(p.groups))


def share_copies(groups, seqs):
    return groups + seqs - 2


def square_sums(value):
    total = 0.0
    for at in range(0, value.shape[1], LANES):
        block = jnp.square(value[:, at : at + LANES])
        if block.shape[0] < 8:
            total = total + jnp.concatenate([block, jnp.zeros((8 - block.shape[0], LANES), F32)], axis=0)
        for row in range(0, block.shape[0] // 8 * 8, 8):
            total = total + block[row : row + 8]
    return total


class Schedule:
    def __init__(self, **steps):
        self.steps = steps

    def __call__(self, *names):
        for name in names:
            next(self.steps[name], None)

    def plan(self, *calls):
        return {at: functools.partial(self, *names.split()) for at, names in enumerate(calls) if names}

    def finish(self, *names):
        run_all(*(self.steps[name] for name in names or self.steps))


def run_all(*steps):
    live = list(steps)
    while live:
        for step in list(live):
            try:
                next(step)
            except StopIteration:
                live.remove(step)


def loop(count, body, ticks=None):
    def step(index, carry):
        body(index)
        for k in sorted(ticks or {}):
            pl.when(index == k)(lambda run=ticks[k]: run())
        return carry

    lax.fori_loop(0, count, step, 0)


def adam(grad, master, first, second, rate, moment_out, square_out, fresh_out):
    fix = 1.0 - BETA**STEP
    moment = BETA * first + (1.0 - BETA) * grad
    square = BETA * second + (1.0 - BETA) * grad * grad
    update = moment / fix / (jnp.sqrt(square / fix) + ADAM_EPS)
    moment_out[...] = moment
    square_out[...] = square
    fresh_out[...] = master - rate * (update + DECAY * master)


def update_kernel(parts, total_ref, norm_grad, *refs):
    sources, results, held, sems = refs[:20], refs[20:39], refs[39:-1], refs[-1]
    outputs_ref, input_ref, grad_refs, state, made, wide_ref = held[0], held[1], held[2:5], held[5:20], held[20:35], held[35]
    outputs_hbm, input_hbm, grads_hbm, state_hbm = sources[0], sources[1], sources[2:5], sources[5:]
    loads = Loads(sems)
    ways = ((input_hbm, input_ref, wide_ref, results[1]), (outputs_hbm, outputs_ref, outputs_ref, results[0]))
    small = [loads.start(src, via) for src, via in zip((*grads_hbm, *state_hbm), (*grad_refs, *state))]
    reads = [Sliced(loads, src, via, parts).start_all() for src, via, _, _ in ways]
    stores = [Sliced(loads, via, dst, parts) for _, _, via, dst in ways]
    for load in small:
        load.wait()
    grad_norm = jnp.sqrt(jnp.sum(total_ref[...], keepdims=True))
    results[2][...] = grad_norm
    factor = jnp.minimum(1.0, CLIP / (grad_norm + 1e-06))
    width = state[1].shape[1]
    piece = state[4].shape[1]
    per = LANES // piece
    index = lax.axis_index("batch") * lax.axis_size("seq") + lax.axis_index("seq")
    block = norm_grad[:, pl.ds(pl.multiple_of(index // per * LANES, LANES), LANES)]
    own = pltpu.roll(block, (LANES - index % per * piece) % LANES, 1)[:, :piece]
    qkv_grad, pu_grad, down_grad = grad_refs
    grads = (qkv_grad[...], pu_grad[:, :width], pu_grad[:, width:], down_grad[...], own)
    results[18][...] = own[3:4] * factor
    last = []
    for at, (grad, rate) in enumerate(zip(grads, RATES)):
        adam(
            grad * factor, state[at][...], state[5 + at][...], state[10 + at][...], rate,
            made[at], made[5 + at], made[10 + at],
        )
        last += [loads.start(made[k], results[3 + k]) for k in (at, 5 + at, 10 + at)]
    for read, store in zip(reads, stores):
        for part in range(parts):
            read.wait(part)
            if read.dst is input_ref:
                here = pl.ds(part * read.size, read.size)
                wide_ref[here, :] = input_ref[here, :].astype(F32)
            store.start(part)
    for store in stores:
        store.wait_all()
    for store in last:
        store.wait()


def cast_shards(p, seqs, qkv_ref, proj_ref, up_ref, down_ref, norm_ref, qkv_full, pu_full, down_full, norm_full):
    width = proj_ref.shape[1]
    b, z, c = p.b, p.z, p.c
    index = b * seqs + 2 * z + c
    qkv_full[b, z, c] = qkv_ref[...].astype(BF)
    pu_full[b, z, c, :, :width] = proj_ref[...].astype(BF)
    pu_full[b, z, c, :, width:] = up_ref[...].astype(BF)
    down_full[b, z, c] = down_ref[...].astype(BF)
    piece = norm_ref.shape[1]
    per = LANES // piece
    tiled = jnp.concatenate([norm_ref[...].astype(BF).astype(F32)] * per, axis=1)
    lane = lax.broadcasted_iota(jnp.int32, tiled.shape, 1)
    norm_full[b, z, c] = jnp.where(lane // piece == index % per, tiled, 0.0)


def join_norms(norm_full, seqs, per, norms_out):
    for block in range(norms_out.shape[1] // LANES):
        total = None
        for device in range(block * per, (block + 1) * per):
            one = norm_full[device // seqs, device % seqs // 2, device % 2]
            total = one if total is None else total + one
        norms_out[:, block * LANES : (block + 1) * LANES] = total


class Sliced:
    def __init__(self, loads, src, dst, count):
        self.src, self.dst, self.count, self.size = src, dst, count, src.shape[0] // count
        self.sems, self.first = loads.sems, loads.made
        loads.made += count
        assert loads.made <= loads.sems.shape[0]

    def copy(self, index):
        begin = index * self.size
        here = pl.ds(begin if isinstance(index, int) else pl.multiple_of(begin, self.size), self.size)
        return pltpu.make_async_copy(self.src.at[here], self.dst.at[here], self.sems.at[self.first + index])

    def start(self, index):
        self.copy(index).start()

    def wait(self, index):
        self.copy(index).wait()

    def start_next(self, index):
        pl.when(index < self.count)(lambda: self.start(index))

    def start_all(self):
        for index in range(self.count):
            self.start(index)
        return self

    def wait_all(self):
        for index in range(self.count):
            self.wait(index)


class SummaryView:
    def __init__(self, ref, rows):
        self.ref, self.rows = ref, rows

    def __getitem__(self, key):
        cols = key[1]
        return self.ref[:, :, :, cols].reshape(self.rows, cols.stop - cols.start)


def row_block(index, size):
    return pl.ds(pl.multiple_of(index * size, size), size)


TILE = 512


def front_kernel(
    groups, seqs, length_ref, x_hbm, og_hbm, qkv_ref, proj_ref, up_ref, down_ref, norm_ref,
    qkv_hbm, pu_hbm, down_hbm, norms_out, mixed_hbm, summ_ref, attn_hbm, probs_hbm,
    outputs_hbm, resid_hbm, slope_hbm, down_grad_hbm,
    x_ref, og_ref, qkv_full, pu_full, down_full, mixed_ref, attn_ref, outputs_ref, resid_ref, activ_ref, slope_ref,
    down_grad_ref, norm_full, sum_scr, vt_scr, load_sems, send_sems, recv_sems,
):
    p = Place(groups, seqs)
    rows, width = x_ref.shape
    hidden = activ_ref.shape[1]
    local = rows // SPAN
    length, first_span = length_ref[0], p.seq * local
    count, per = rows // TILE, TILE // SPAN
    loads = Loads(load_sems)
    x_load = Sliced(loads, x_hbm, x_ref, count).start_all()
    cast_shards(
        p, seqs, qkv_ref, proj_ref, up_ref, down_ref, norm_ref, qkv_full, pu_full, down_full, norm_full
    )
    meet(p)
    og_load = loads.start(og_hbm, og_ref)
    copies = Copies(send_sems, recv_sems)
    half_down, half_pu = down_full.shape[3] // 2, pu_full.shape[4] // 2
    move = Schedule(
        kv=fast_gather_steps(p, copies, qkv_full, cols=slice(width, 3 * width)),
        norm=gather_steps(p, copies, norm_full),
        q=gather_steps(p, copies, qkv_full, cols=slice(0, width)),
        pu0=gather_steps(p, copies, pu_full, cols=slice(0, half_pu)),
        pu1=gather_steps(p, copies, pu_full, cols=slice(half_pu, 2 * half_pu)),
        down0=gather_steps(p, copies, down_full, rows=slice(0, half_down)),
        down1=gather_steps(p, copies, down_full, rows=slice(half_down, 2 * half_down)),
    )
    xhat_ref = resid_ref

    def center(index):
        here = row_block(index, TILE)
        x_load.wait(index)
        xhat_ref[here, :] = normalize(x_ref[here, :].astype(F32))[0]

    move("norm", "kv")
    loop(count, center, move.plan("norm kv q pu0", "", "norm kv", "norm kv q pu1"))
    move("norm", "kv")
    move("pu0")
    join_norms(norm_full, seqs, LANES // norm_ref.shape[1], norms_out)
    gain, shift = norms_out[0:1, :], norms_out[1:2, :]

    def columns(full, begin, size):
        return full[:, :, :, :, begin : begin + size].reshape(width, size)

    def normed_of(here):
        return (xhat_ref[here, :] * gain + shift).astype(BF)

    def keys_values(index):
        here = row_block(index, TILE)
        mixed = dot(normed_of(here), columns(qkv_full, width, 2 * width)).astype(BF)
        mixed_ref[here, width:] = mixed
        for part in range(per):
            span = index * per + part
            sum_scr[pl.ds(span, 1), :] = span_sum(
                mixed[part * SPAN : (part + 1) * SPAN], length, (first_span + span) * SPAN
            )

    loop(count, keys_values, move.plan("q", "pu1", "q"))
    summ_ref[p.z, p.c] = sum_scr[...].astype(BF)
    along = [copies.push(summ_ref, (p.z, p.c), device) for device in p.along[1:]]
    sib = [copies.push(summ_ref, (p.z, p.c), p.sibling)]
    move("q")
    stores = [loads.start(qkv_full, qkv_hbm)]
    mixed_store = Sliced(loads, mixed_ref, mixed_hbm, count)

    def queries(index):
        here = row_block(index, TILE)
        mixed_ref[here, :width] = dot(normed_of(here), columns(qkv_full, 0, width)).astype(BF)
        mixed_store.start(index)

    loop(count, queries)
    move("pu0")
    for k, copy in enumerate(along, 1):
        copy.wait_recv()
        sib.append(copies.push(summ_ref, (p.before[k], p.c), p.sibling))
    for copy in sib:
        copy.wait_recv()
    move("pu1", "down0")
    vt_scr[...] = summ_ref[:, :, :, width:].reshape(local * seqs, width).T
    summ_rows = SummaryView(summ_ref, local * seqs)
    attn_store = Sliced(loads, attn_ref, attn_hbm, count)
    probs_ref = activ_ref
    probs_store = Sliced(loads, probs_ref, probs_hbm, count)

    def attend(index):
        spans = []
        for k in range(per):
            span = index * per + k
            spans.append((pl.multiple_of(span * SPAN, SPAN), span, span_caps(length, first_span + span)))
        attend_spans(spans, mixed_ref, width, summ_rows, vt_scr, attn_ref, probs_ref=probs_ref)
        attn_store.start(index)
        probs_store.start(index)

    loop(count, attend, move.plan("pu0 down0 down1", "pu1", "pu0 down1", "pu1 down0"))
    gain_two, shift_two = norms_out[2:3, :], norms_out[3:4, :]
    resid_store, slope_store = (
        Sliced(loads, src, dst, count) for src, dst in ((resid_ref, resid_hbm), (slope_ref, slope_hbm))
    )
    chunk = 256

    def expand(index):
        here = row_block(index, TILE)
        resid = x_ref[here, :].astype(F32) + dot(attn_ref[here, :], columns(pu_full, 0, width))
        resid_ref[here, :] = resid
        resid_store.start(index)
        normed = (normalize(resid)[0] * gain_two + shift_two).astype(BF)
        probs_store.wait(index)
        for at in range(0, hidden, chunk):
            value, slope = gelu_parts(dot(normed, columns(pu_full, width + at, chunk)))
            activ_ref[here, at : at + chunk] = value.astype(BF)
            slope_ref[here, at : at + chunk] = slope.astype(BF)
        slope_store.start(index)

    loop(count, expand, move.plan("down1", "down0", "down1"))
    stores.append(loads.start(pu_full, pu_hbm))
    og_load.wait()
    parts = hidden // TILE
    grad_store = Sliced(loads, down_grad_ref, down_grad_hbm, parts)

    def down_grad(index):
        here = row_block(index, TILE)
        down_grad_ref[here, :] = dot_tn(activ_ref[:, here], og_ref[...]).astype(BF)
        grad_store.start(index)

    loop(parts, down_grad)
    move.finish()
    stores.append(loads.start(down_full, down_hbm))
    outputs_store = Sliced(loads, outputs_ref, outputs_hbm, count)

    def contract(index):
        here = row_block(index, TILE)
        out = resid_ref[here, :] + dot(activ_ref[here, :], down_full[...].reshape(hidden, width))
        outputs_ref[here, :] = out.astype(BF)
        outputs_store.start(index)

    loop(count, contract)
    for store in (mixed_store, attn_store, resid_store, slope_store, grad_store, outputs_store):
        store.wait_all()
    for store in stores:
        store.wait()
    copies.finish()


def middle_kernel(
    groups, seqs, og_hbm, resid_hbm, slope_hbm, attn_hbm, pu_hbm, down_hbm, norms_ref, down_grad_hbm,
    resid_grad_hbm, attn_grad_hbm, pu_grad_hbm, down_out, norm_grad_ref,
    og_ref, resid_ref, slope_ref, attn_ref, pu_ref, down_ref, resid_grad_ref, attn_grad_ref, pu_grad_ref,
    pre_grad_ref, normed_ref, pig_ref, *scratch,
):
    *buffers, load_sems, send_sems, recv_sems = scratch
    p = Place(groups, seqs)
    rows, width = og_ref.shape
    hidden = slope_ref.shape[1]
    count = rows // TILE
    loads = Loads(load_sems)
    early = [loads.start(down_hbm, down_ref)]
    tiled = [
        Sliced(loads, src, dst, count)
        for src, dst in ((og_hbm, og_ref), (slope_hbm, slope_ref), (resid_hbm, resid_ref))
    ]
    for load in tiled:
        load.start(0)
    early.append(loads.start(pu_hbm, pu_ref))
    for load in tiled:
        load.start(1)
    meet(p)
    copies = Copies(send_sems, recv_sems)
    half = down_out.shape[0] // 2
    move = Schedule(
        **{
            f"down{at}": scatter_steps(
                p, copies, loads, down_grad_hbm.at[:, :, :, half * at : half * (at + 1)], *buffers[5 * at : 5 * at + 5],
                down_out.at[half * at : half * (at + 1)],
            )
            for at in range(2)
        }
    )
    move("down0", "down1")
    attn_load = loads.start(attn_hbm, attn_ref)
    norm_grad_ref[...] = jnp.zeros_like(norm_grad_ref)
    resid_grad_store, attn_grad_store = (
        Sliced(loads, src, dst, count)
        for src, dst in ((resid_grad_ref, resid_grad_hbm), (attn_grad_ref, attn_grad_hbm))
    )
    gain, shift = norms_ref[2:3, :], norms_ref[3:4, :]
    chunk = 256
    early[0].wait()

    def tile(index):
        here = row_block(index, TILE)
        for load in tiled:
            load.start_next(index + 2)
            load.wait(index)
        grad = og_ref[here, :]
        for at in range(0, hidden, chunk):
            act_grad = dot_nt(grad, down_ref[at : at + chunk, :])
            slope = slope_ref[here, at : at + chunk].astype(F32)
            pre_grad_ref[here, at : at + chunk] = (act_grad * slope).astype(BF)

        @pl.when(index == 0)
        def _():
            early[1].wait()

        back = dot_nt(pre_grad_ref[here, :], pu_ref[:, width:])
        xhat, rstd = normalize(resid_ref[here, :])
        normed_ref[here, :] = (xhat * gain + shift).astype(BF)
        resid_grad = grad.astype(F32) + norm_back(back, gain, xhat, rstd)
        resid_grad_ref[here, :] = resid_grad
        resid_grad_store.start(index)
        pig = resid_grad.astype(BF)
        pig_ref[here, :] = pig
        attn_grad_ref[here, :] = dot_nt(pig, pu_ref[:, :width]).astype(BF)
        attn_grad_store.start(index)
        norm_grad_ref[0:1, :] += jnp.sum(back * xhat, axis=0, keepdims=True)
        norm_grad_ref[1:2, :] += jnp.sum(back, axis=0, keepdims=True)

    loop(count, tile, move.plan("down0", "down1", "down0", "down1 down0"))
    attn_load.wait()
    pu_grad_ref[:, :width] = dot_tn(attn_ref[...], pig_ref[...]).astype(BF)

    def up_grad(index):
        at = pl.multiple_of(width + index * TILE, TILE)
        pu_grad_ref[:, pl.ds(at, TILE)] = dot_tn(normed_ref[...], pre_grad_ref[:, row_block(index, TILE)]).astype(BF)

    loop(hidden // TILE, up_grad, move.plan("down1", "", "down0"))
    pu_store = loads.start(pu_grad_ref, pu_grad_hbm)
    resid_grad_store.wait_all()
    attn_grad_store.wait_all()
    move.finish()
    pu_store.wait()
    copies.finish()


def back_kernel(
    groups, seqs, length_ref, x_hbm, mixed_hbm, grad_hbm, probs_hbm, summ_ref, pu_hbm, resid_grad_hbm, down_ref,
    norms_ref, weight_hbm, norm_two_ref,
    input_grad_hbm, qkv_out, pu_out, norm_out, total_out,
    x_ref, mixed_ref, grad_ref, probs_ref, resid_grad_ref, weight_ref, input_low_ref,
    mg_scr, xhat_ref, kt_scr, dsumm_scr, dsumm_got, dsumm_low, dsumm_last, extra_scr, q_grad, k_grad, v_grad,
    gain_cols, shift_cols,
    *scratch,
):
    *buffers, norm_mine, along_norm, across_norm, sq_mine, along_sq, across_sq = scratch[:-3]
    load_sems, send_sems, recv_sems = scratch[-3:]
    p = Place(groups, seqs)
    rows, width = x_ref.shape
    local = rows // SPAN
    length, first_span = length_ref[0], p.seq * local
    loads = Loads(load_sems)
    group = 2
    count, steps = rows // TILE, local // group
    reads = [
        Sliced(loads, src, dst, steps)
        for src, dst in ((mixed_hbm, mixed_ref), (grad_hbm, grad_ref), (probs_hbm, probs_ref))
    ]
    for index in range(2):
        for read in reads:
            read.start(index)
    meet(p)
    copies = Copies(send_sems, recv_sems)

    def scatter(grad, at, out):
        return scatter_steps(p, copies, loads, grad, *buffers[5 * at : 5 * at + 5], out)

    half = pu_hbm.shape[4] // 2
    outs = [qkv_out.at[:, width * at : width * (at + 1)] for at in range(3)]
    move = Schedule(
        pu0=scatter(pu_hbm.at[:, :, :, :, :half], 0, pu_out.at[:, :half]),
        pu1=scatter(pu_hbm.at[:, :, :, :, half:], 1, pu_out.at[:, half:]),
        q=scatter(q_grad, 2, outs[0]), k=scatter(k_grad, 3, outs[1]), v=scatter(v_grad, 4, outs[2]),
        norm=share_sum_steps(p, copies, norm_mine, along_norm, across_norm, norm_out),
    )
    move("pu0", "pu1")
    late = [loads.start(src, dst) for src, dst in ((x_hbm, x_ref), (weight_hbm, weight_ref))]
    resid_grad_load = loads.start(resid_grad_hbm, resid_grad_ref)
    kt_scr[...] = summ_ref[:, :width].T
    dsumm_scr[...] = jnp.zeros_like(dsumm_scr)

    def attend_back(index):
        for read in reads:
            read.start_next(index + 2)
            read.wait(index)
        each = []
        for k in range(group):
            span = index * group + k
            each.append((pl.multiple_of(span * SPAN, SPAN), span, None))
        attend_back_spans(each, mixed_ref, grad_ref, width, summ_ref, kt_scr, None, mg_scr, dsumm_scr, probs_ref)

    loop(steps, attend_back, move.plan("pu0", "", "pu1", "pu0", "", "pu1 pu0", "", "pu1"))
    swap = []
    for z in range(p.chips):
        block = pl.ds(pl.multiple_of((2 * z + p.other) * local, local), local)
        swap.append(copies.start(dsumm_scr, block, dsumm_got, z, p.sibling))
    gain, shift = norms_ref[0:1, :], norms_ref[1:2, :]
    for read in late:
        read.wait()

    def recompute(index):
        here = row_block(index, TILE)
        xhat_ref[here, :] = normalize(x_ref[here, :].astype(F32))[0].astype(BF)

    loop(count // 2, recompute)
    for copy in swap:
        copy.wait_recv()

    def half_sum(z):
        mine = dsumm_scr[pl.ds(pl.multiple_of((2 * z + p.c) * local, local), local), :]
        return mine + dsumm_got[z]

    along = []
    for k in range(1, p.chips):
        dsumm_low[k - 1] = half_sum(p.after[k]).astype(BF)
        along.append(copies.start(dsumm_low, k - 1, dsumm_last, k - 1, p.along[k]))
    loop(count // 2, lambda index: recompute(index + count // 2))
    per_block = width // (groups * seqs)
    gain_cols[...] = jnp.broadcast_to(gain, (LANES, width)).T
    shift_cols[...] = jnp.broadcast_to(shift, (LANES, width)).T

    def weight_grad(into, at):
        begin = at * width
        back = mg_scr[:, begin : begin + width]
        moved = dot_tn(xhat_ref[...], back)
        total = jnp.sum(back.astype(F32), axis=0, keepdims=True)
        blocks, gains, shifts = [], 0.0, 0.0
        for k in range(0, width, LANES):
            part, sums = moved[:, k : k + LANES], total[:, k : k + LANES]
            blocks.append(gain_cols[...] * part + shift_cols[...] * sums)
            weight = weight_ref[:, begin + k : begin + k + LANES].astype(F32)
            gains += weight * part
            shifts += weight * sums
        into[...] = jnp.concatenate(blocks, axis=1).astype(BF).reshape(groups, p.chips, 2, per_block, width)
        gain_sums = jnp.sum(gains.T, axis=0, keepdims=True)
        shift_sums = jnp.sum(shifts.T, axis=0, keepdims=True)
        norm_mine[0:1, :] = gain_sums + (norm_mine[0:1, :] if at else 0.0)
        norm_mine[1:2, :] = shift_sums + (norm_mine[1:2, :] if at else 0.0)

    norm_mine[2:4, :] = norm_two_ref[...]
    weight_grad(q_grad, 0)
    move("q", "pu0")

    move("pu1")
    total = half_sum(p.z)
    for k, copy in enumerate(along):
        copy.wait_recv()
        total = total + dsumm_last[k].astype(F32)
    extra_scr[...] = total

    def add_extra(index):
        for k in range(2):
            span = index * 2 + k
            here = row_block(span, SPAN)
            mg_scr[here, width:] = with_extra(
                mg_scr[here, width:], extra_scr[pl.ds(span, 1), :], length, (first_span + span) * SPAN
            )

    loop(local // 2, add_extra)
    weight_grad(k_grad, 1)
    move("k", "q")
    weight_grad(v_grad, 2)
    move("v", "norm", "k", "q")
    resid_grad_load.wait()
    store = Sliced(loads, input_low_ref, input_grad_hbm, count)

    def finish(index):
        here = row_block(index, TILE)
        xhat, rstd = normalize(x_ref[here, :].astype(F32))
        back = dot_nt(mg_scr[here, :], weight_ref[...])
        input_low_ref[here, :] = (resid_grad_ref[here, :] + norm_back(back, gain, xhat, rstd)).astype(BF)
        store.start(index)

    loop(count, finish, move.plan("v k", "v norm q", "k", "v"))
    sq_mine[...] = square_sums(pu_out[...]) + square_sums(down_ref[...])
    move("k", "q", "norm")
    copies.finish()
    move.finish()
    sq_mine[...] += square_sums(qkv_out[...])
    run_all(share_sum_steps(p, copies, sq_mine, along_sq, across_sq, total_out))
    total_out[...] += square_sums(norm_out[...])
    store.wait_all()
    copies.finish()


def qkv_kernel(info_ref, x_ref, norms_ref, weight_ref, mixed_ref, summ_ref, sum_scr):
    step = pl.program_id(0)
    tile, width = x_ref.shape
    length, first_span = info_ref[0], info_ref[1]
    mixed = qkv_tile(x_ref[...], norms_ref, weight_ref)
    mixed_ref[...] = mixed
    per = tile // SPAN
    for part in range(per):
        span = step * per + part
        sum_scr[pl.ds(span, 1), :] = span_sum(
            mixed[part * SPAN : (part + 1) * SPAN, width:], length, (first_span + span) * SPAN
        )

    @pl.when(step == pl.num_programs(0) - 1)
    def _():
        summ_ref[...] = sum_scr[...].astype(BF)


def attend_kernel(info_ref, mixed_ref, summ_ref, out_ref, lse_ref, vt_scr):
    step = pl.program_id(0)
    width = out_ref.shape[1]

    @pl.when(step == 0)
    def _():
        vt_scr[...] = summ_ref[:, width:].T

    caps = span_caps(info_ref[0], info_ref[1] + step)
    attend_spans([(0, 0, caps)], mixed_ref, width, summ_ref, vt_scr, out_ref, lse_ref)


def attend_back_kernel(info_ref, mixed_ref, grad_ref, lse_ref, summ_ref, back_ref, dsumm_ref, kt_scr):
    step = pl.program_id(0)
    width = grad_ref.shape[1]

    @pl.when(step == 0)
    def _():
        kt_scr[...] = summ_ref[:, :width].T
        dsumm_ref[...] = jnp.zeros_like(dsumm_ref)

    caps = span_caps(info_ref[0], info_ref[1] + step)
    attend_back_spans(
        [(0, 0, caps)], mixed_ref, grad_ref, width, summ_ref, kt_scr, lse_ref, back_ref, dsumm_ref
    )


def mlp_kernel(
    x_ref, attn_ref, og_ref, norms_ref, pu_ref, down_ref,
    out_ref, resid_grad_ref, attn_grad_ref, pu_grad_ref, down_grad_ref, norm_grad_ref,
    activ_scr, pre_grad_scr, n2t_scr, attnt_scr, ogt_scr, pig_scr, norm_scr,
):
    step = pl.program_id(0)
    tile, width = x_ref.shape
    hidden = down_ref.shape[0]
    rows = pl.ds(pl.multiple_of(step * tile, tile), tile)
    chunk = 256
    attn = attn_ref[...]
    grad = og_ref[...]
    resid = x_ref[...].astype(F32) + dot(attn, pu_ref[:, :width])
    xhat, rstd = normalize(resid)
    gain = norms_ref[2:3, :]
    normed = (xhat * gain + norms_ref[3:4, :]).astype(BF)
    attnt_scr[:, rows] = attn.T
    n2t_scr[:, rows] = normed.T
    ogt_scr[:, rows] = grad.T
    for at in range(0, hidden, chunk):
        pre = dot(normed, pu_ref[:, width + at : width + at + chunk])
        act_grad = dot_nt(grad, down_ref[at : at + chunk, :])
        value, slope = gelu_parts(pre)
        activ = value.astype(BF)
        pre_grad = (act_grad * slope).astype(BF)
        activ_scr[rows, at : at + chunk] = activ
        pre_grad_scr[rows, at : at + chunk] = pre_grad
    out_ref[...] = (resid + dot(activ_scr[rows, :], down_ref[...])).astype(BF)
    back = dot_nt(pre_grad_scr[rows, :], pu_ref[:, width:])
    resid_grad = grad.astype(F32) + norm_back(back, gain, xhat, rstd)
    resid_grad_ref[...] = resid_grad
    pig = resid_grad.astype(BF)
    pig_scr[rows, :] = pig
    attn_grad_ref[...] = dot_nt(pig, pu_ref[:, :width]).astype(BF)
    gain_part = jnp.sum(back * xhat, axis=0, keepdims=True)
    shift_part = jnp.sum(back, axis=0, keepdims=True)
    part = jnp.concatenate([gain_part, shift_part], axis=0)

    @pl.when(step == 0)
    def _():
        norm_scr[...] = part

    @pl.when(step > 0)
    def _():
        norm_scr[...] += part

    @pl.when(step == pl.num_programs(0) - 1)
    def _():
        norm_grad_ref[...] = norm_scr[...]
        pu_grad_ref[:, :width] = dot(attnt_scr[...], pig_scr[...]).astype(BF)
        cols = 512

        def one(index, carry):
            c = pl.ds(pl.multiple_of(index * cols, cols), cols)
            out = pl.ds(pl.multiple_of(width + index * cols, cols), cols)
            pu_grad_ref[:, out] = dot(n2t_scr[...], pre_grad_scr[:, c]).astype(BF)
            down_grad_ref[c, :] = dot(ogt_scr[...], activ_scr[:, c]).T.astype(BF)
            return carry

        lax.fori_loop(0, hidden // cols, one, 0)


def final_kernel(
    info_ref, x_ref, back_ref, extra_ref, resid_grad_ref, norms_ref, weight_ref,
    input_grad_ref, qkv_grad_ref, norm_grad_ref, mg_scr, normed_scr,
):
    step = pl.program_id(0)
    tile, width = x_ref.shape
    rows = pl.ds(pl.multiple_of(step * tile, tile), tile)
    length, first_span = info_ref[0], info_ref[1]
    xhat, rstd = normalize(x_ref[...].astype(F32))
    gain = norms_ref[0:1, :]
    normed_scr[rows, :] = (xhat * gain + norms_ref[1:2, :]).astype(BF)
    per = tile // SPAN
    parts = []
    for part in range(per):
        span = step * per + part
        here = back_ref[part * SPAN : (part + 1) * SPAN, width:]
        parts.append(with_extra(here, extra_ref[pl.ds(span, 1), :], length, (first_span + span) * SPAN))
    mg = jnp.concatenate([back_ref[:, :width], jnp.concatenate(parts, axis=0)], axis=1)
    mg_scr[rows, :] = mg
    back = dot_nt(mg, weight_ref[...])
    input_grad_ref[...] = resid_grad_ref[...] + norm_back(back, gain, xhat, rstd)

    @pl.when(step == 0)
    def _():
        norm_grad_ref[...] = jnp.zeros_like(norm_grad_ref)

    norm_grad_ref[0:1, :] += jnp.sum(back * xhat, axis=0, keepdims=True)
    norm_grad_ref[1:2, :] += jnp.sum(back, axis=0, keepdims=True)

    @pl.when(step == pl.num_programs(0) - 1)
    def _():
        cols = 256

        def one(index, carry):
            c = pl.ds(pl.multiple_of(index * cols, cols), cols)
            qkv_grad_ref[:, c] = dot_tn(normed_scr[...], mg_scr[:, c]).astype(BF)
            return carry

        lax.fori_loop(0, qkv_grad_ref.shape[1] // cols, one, 0)


def whole(shape):
    return pl.BlockSpec(shape, lambda i: (0,) * len(shape))


def by_rows(tile, width):
    return pl.BlockSpec((tile, width), lambda i: (i, 0))


SCALARS = pl.BlockSpec(memory_space=pltpu.SMEM)
PARAMS = pltpu.CompilerParams(vmem_limit_bytes=VMEM_LIMIT)


def remote_call(kernel, groups, seqs, name, collective_id, outs, ins, scratch, loads, copies):
    return pl.pallas_call(
        functools.partial(kernel, groups, seqs),
        in_specs=[pl.BlockSpec(memory_space=space) for space in ins],
        out_specs=[pl.BlockSpec(memory_space=space) for space, _, _ in outs],
        out_shape=[jax.ShapeDtypeStruct(shape, kind) for _, shape, kind in outs],
        scratch_shapes=list(scratch) + [pltpu.SemaphoreType.DMA((n,)) for n in (loads, copies, copies)],
        compiler_params=pltpu.CompilerParams(
            vmem_limit_bytes=VMEM_LIMIT, collective_id=collective_id, has_side_effects=True
        ),
        name=name,
    )


def regroup(grad, dim, outer, inner):
    shape = grad.shape
    piece = shape[dim] // (outer * inner)
    split = grad.reshape(shape[:dim] + (outer, inner, piece) + shape[dim + 1 :])
    return jnp.swapaxes(split, dim, dim + 1).reshape(shape)


def gather_plain(state):
    both = ("batch", "seq")
    qkv, proj, up, down = (lax.all_gather(w.astype(BF), both, axis=0, tiled=True) for w in state[:4])
    norms = lax.all_gather(state[4].astype(BF), both, axis=1, tiled=True).astype(F32)
    return qkv, jnp.concatenate([proj, up], axis=1), down, norms


def reduce_plain(qkv_grad, pu_grad, down_grad, norm_grad):
    groups, seqs = lax.axis_size("batch"), lax.axis_size("seq")
    reduced = []
    for grad, dim in ((qkv_grad, 0), (pu_grad, 0), (down_grad, 0)):
        part = lax.psum_scatter(
            regroup(grad.astype(F32), dim, groups, seqs), "seq", scatter_dimension=dim, tiled=True
        )
        reduced.append(lax.psum_scatter(part, "batch", scatter_dimension=dim, tiled=True))
    norm_total = lax.psum(norm_grad, ("batch", "seq"))
    squares = lax.psum(sum(jnp.sum(grad * grad) for grad in reduced), ("batch", "seq"))
    squares = squares + jnp.sum(norm_total * norm_total)
    return (*reduced, norm_total, jnp.zeros((8, LANES), F32).at[0, 0].set(squares))


def mlp_call(x, attn_out, grad_rows, norms, pu_full, down_full):
    sds = jax.ShapeDtypeStruct
    rows, width = x.shape
    hidden = down_full.shape[0]
    tile = min(512, rows)
    steps = rows // tile
    return pl.pallas_call(
        mlp_kernel,
        grid=(steps,),
        in_specs=[by_rows(tile, width)] * 3
        + [whole(norms.shape), whole(pu_full.shape), whole(down_full.shape)],
        out_specs=[by_rows(tile, width)] * 3
        + [whole(pu_full.shape), whole(down_full.shape), whole((2, width))],
        out_shape=[
            sds((rows, width), BF), sds((rows, width), F32), sds((rows, width), BF),
            sds(pu_full.shape, BF), sds(down_full.shape, BF), sds((2, width), F32),
        ],
        scratch_shapes=[
            pltpu.VMEM((rows, hidden), BF), pltpu.VMEM((rows, hidden), BF),
            pltpu.VMEM((width, rows), BF), pltpu.VMEM((width, rows), BF), pltpu.VMEM((width, rows), BF),
            pltpu.VMEM((rows, width), BF), pltpu.VMEM((2, width), F32),
        ],
        compiler_params=PARAMS,
        name="mlp",
    )(x, attn_out, grad_rows, norms, pu_full, down_full)


def direct_body(groups, seqs, inputs, out_grad, lengths, *state):
    rows, width = inputs.shape[1], inputs.shape[2]
    own_rows, down_rows = state[0].shape[0], state[3].shape[0]
    hidden = state[2].shape[1]
    chips = seqs // 2
    grid3 = (groups, chips, 2)
    local = rows // SPAN
    spans = local * seqs
    pairs = width // LANES
    count = rows // TILE
    x, grad_rows = inputs[0], out_grad[0]
    vmem, hbm, smem = pltpu.VMEM, pl.ANY, pltpu.SMEM
    shapes = (
        (*grid3, own_rows, 3 * width), (*grid3, own_rows, width + hidden), (*grid3, down_rows, width),
    )
    tokens = (rows, width)
    (
        qkv_full, pu_full, down_full, norms, mixed, summ, attn_out, probs, outputs, resid, slope, down_grad,
    ) = remote_call(
        front_kernel, groups, seqs, "front", 0,
        [
            *((hbm, shape, BF) for shape in shapes), (vmem, (4, width), F32), (hbm, (rows, 3 * width), BF),
            (vmem, (chips, 2, local, 2 * width), BF), (hbm, tokens, BF), (hbm, (rows, 4 * SPAN * pairs), BF),
            (hbm, tokens, BF), (hbm, tokens, F32), (hbm, (rows, hidden), BF), (hbm, (hidden, width), BF),
        ],
        [smem, hbm, hbm] + [vmem] * 5,
        [
            vmem(tokens, BF), vmem(tokens, BF), *(vmem(shape, BF) for shape in shapes),
            vmem((rows, 3 * width), BF), vmem(tokens, BF), vmem(tokens, BF), vmem(tokens, F32),
            vmem((rows, hidden), BF), vmem((rows, hidden), BF), vmem((hidden, width), BF),
            vmem((*grid3, 4, LANES), F32), vmem((local, 2 * width), F32), vmem((width, spans), BF),
        ],
        4 + 7 * count + hidden // TILE, 6 * GATHER_COPIES + fast_gather_copies(chips) + 2 * chips,
    )(lengths, x, grad_rows, *state[:5])
    pu_flat, down_flat = pu_full.reshape(width, width + hidden), down_full.reshape(hidden, width)
    resid_grad, attn_grad, pu_grad, down_own, norm_two = remote_call(
        middle_kernel, groups, seqs, "middle", 1,
        [
            (hbm, tokens, F32), (hbm, tokens, BF), (hbm, pu_flat.shape, BF),
            (vmem, (down_rows, width), F32), (vmem, (2, width), F32),
        ],
        [hbm] * 6 + [vmem, hbm],
        [
            vmem(tokens, BF), vmem(tokens, F32), vmem((rows, hidden), BF), vmem(tokens, BF),
            vmem(pu_flat.shape, BF), vmem(down_flat.shape, BF), vmem(tokens, F32), vmem(tokens, BF),
            vmem(pu_flat.shape, BF), vmem((rows, hidden), BF), vmem(tokens, BF), vmem(tokens, BF),
            *scatter_scratch(groups, chips, down_rows // 2, width) * 2,
        ],
        6 + 5 * count, 2 * SCATTER_COPIES,
    )(grad_rows, resid, slope, attn_out, pu_flat, down_flat, norms, down_grad.reshape(shapes[2]))
    half = (width + hidden) // 2
    blocks = ((own_rows, half),) * 2 + ((own_rows, width),) * 3
    summ_block = (local, 2 * width)
    scratch = [
        vmem(tokens, BF), vmem((rows, 3 * width), BF), vmem(tokens, BF), vmem(probs.shape, BF), vmem(tokens, F32),
        vmem((width, 3 * width), BF), vmem(tokens, BF),
        vmem((rows, 3 * width), BF), vmem(tokens, BF), vmem((width, spans), BF), vmem((spans, 2 * width), F32),
        vmem((chips, *summ_block), F32), vmem((chips - 1, *summ_block), BF),
        vmem((chips - 1, *summ_block), BF), vmem(summ_block, F32),
        *[vmem((*grid3, own_rows, width), BF)] * 3, *[vmem((width, LANES), F32)] * 2,
    ]
    scratch += [buffer for block in blocks for buffer in scatter_scratch(groups, chips, *block)]
    scratch += [
        vmem((4, width), F32), vmem((seqs, 4, width), F32), vmem((groups, 4, width), F32),
        vmem((8, LANES), F32), vmem((seqs, 8, LANES), F32), vmem((groups, 8, LANES), F32),
    ]
    input_grad, qkv_own, pu_own, norm_total, total = remote_call(
        back_kernel, groups, seqs, "back", 2,
        [
            (hbm, tokens, BF), (vmem, (own_rows, 3 * width), F32), (vmem, (own_rows, width + hidden), F32),
            (vmem, (4, width), F32), (vmem, (8, LANES), F32),
        ],
        [smem, hbm, hbm, hbm, hbm, vmem, hbm, hbm, vmem, vmem, hbm, vmem],
        scratch, 3 * local // 2 + 3 + 5 + count,
        5 * SCATTER_COPIES + 2 * share_copies(groups, seqs) + 2 * chips,
    )(
        lengths, x, mixed, attn_grad, probs, summ.reshape(spans, 2 * width), pu_grad.reshape(shapes[1]),
        resid_grad, down_own, norms, qkv_full.reshape(width, 3 * width), norm_two,
    )
    return outputs, input_grad, (qkv_own, pu_own, down_own), norm_total, total


def plain_body(groups, seqs, inputs, out_grad, lengths, *state):
    sds = jax.ShapeDtypeStruct
    rows, width = inputs.shape[1], inputs.shape[2]
    qkv_full, pu_full, down_full, norms = gather_plain(state[:5])
    local = rows // SPAN
    spans = local * seqs
    info = jnp.stack([lengths[0], (lax.axis_index("seq") * local).astype(jnp.int32)])
    x, grad_rows = inputs[0], out_grad[0]
    tile = 256
    steps = rows // tile
    mixed, own_summ = pl.pallas_call(
        qkv_kernel,
        grid=(steps,),
        in_specs=[SCALARS, by_rows(tile, width), whole(norms.shape), whole(qkv_full.shape)],
        out_specs=[by_rows(tile, 3 * width), whole((local, 2 * width))],
        out_shape=[sds((rows, 3 * width), BF), sds((local, 2 * width), BF)],
        scratch_shapes=[pltpu.VMEM((local, 2 * width), F32)],
        compiler_params=PARAMS,
        name="qkv",
    )(info, x, norms, qkv_full)
    summ = lax.all_gather(own_summ, "seq", axis=0, tiled=True)
    pairs = width // LANES
    lse_spec = pl.BlockSpec((1, pairs, 2 * SPAN), lambda i: (i, 0, 0))
    attn_out, lse = pl.pallas_call(
        attend_kernel,
        grid=(local,),
        in_specs=[SCALARS, by_rows(SPAN, 3 * width), whole(summ.shape)],
        out_specs=[by_rows(SPAN, width), lse_spec],
        out_shape=[sds((rows, width), BF), sds((local, pairs, 2 * SPAN), F32)],
        scratch_shapes=[pltpu.VMEM((width, spans), BF)],
        compiler_params=PARAMS,
        name="attend",
    )(info, mixed, summ)
    outputs, resid_grad, attn_grad, pu_grad, down_grad, norm_two = mlp_call(
        x, attn_out, grad_rows, norms, pu_full, down_full
    )
    back, dsumm = pl.pallas_call(
        attend_back_kernel,
        grid=(local,),
        in_specs=[SCALARS, by_rows(SPAN, 3 * width), by_rows(SPAN, width), lse_spec, whole(summ.shape)],
        out_specs=[by_rows(SPAN, 3 * width), whole((spans, 2 * width))],
        out_shape=[sds((rows, 3 * width), BF), sds((spans, 2 * width), F32)],
        scratch_shapes=[pltpu.VMEM((width, spans), BF)],
        compiler_params=PARAMS,
        name="attend_back",
    )(info, mixed, attn_grad, lse, summ)
    extra = lax.psum_scatter(dsumm, "seq", scatter_dimension=0, tiled=True)
    input_grad, qkv_grad, norm_one = pl.pallas_call(
        final_kernel,
        grid=(steps,),
        in_specs=[
            SCALARS, by_rows(tile, width), by_rows(tile, 3 * width), whole(extra.shape), by_rows(tile, width),
            whole(norms.shape), whole(qkv_full.shape),
        ],
        out_specs=[by_rows(tile, width), whole(qkv_full.shape), whole((2, width))],
        out_shape=[sds((rows, width), F32), sds(qkv_full.shape, BF), sds((2, width), F32)],
        scratch_shapes=[pltpu.VMEM((rows, 3 * width), BF), pltpu.VMEM((rows, width), BF)],
        compiler_params=PARAMS,
        name="final",
    )(info, x, back, extra, resid_grad, norms, qkv_full)
    norm_grad = jnp.concatenate([norm_one, norm_two], axis=0)
    *grads, norm_total, total = reduce_plain(qkv_grad, pu_grad, down_grad, norm_grad)
    return outputs, input_grad, grads, norm_total, total


def body(groups, seqs, *args):
    state = args[3:]
    rows, width = args[0].shape[1:]
    direct = groups == 4 and seqs % 4 == 0 and state[0].shape[0] % 16 == 0 and rows % TILE == 0
    direct = direct and rows // SPAN * seqs == SPAN and state[2].shape[1] == 4 * SPAN * (width // LANES)
    run = direct_body if direct else plain_body
    outputs, input_grad, grads, norm_total, total = run(groups, seqs, *args)
    input_grad = input_grad.astype(BF)
    sds = jax.ShapeDtypeStruct
    vmem, hbm = pltpu.VMEM, pl.ANY
    spec = lambda space: pl.BlockSpec(memory_space=space)
    held = [sds(w.shape, F32) for w in state[:5]]
    parts = 8
    operands = (outputs, input_grad, *grads, *state)
    outputs, input_grad, grad_norm, *fresh, shift_clipped = pl.pallas_call(
        functools.partial(update_kernel, parts),
        in_specs=[spec(vmem)] * 2 + [spec(hbm)] * 20,
        out_specs=[spec(hbm)] * 2 + [spec(vmem)] + [spec(hbm)] * 15 + [spec(vmem)],
        out_shape=[
            sds(outputs.shape, BF), sds(outputs.shape, F32), sds((1, 1), F32), *held * 3,
            sds((1, state[4].shape[1]), F32),
        ],
        scratch_shapes=[vmem(a.shape, a.dtype) for a in operands]
        + [vmem(w.shape, F32) for w in held * 3] + [vmem(outputs.shape, F32), pltpu.SemaphoreType.DMA((4 * parts + 33,))],
        compiler_params=PARAMS,
        name="update",
    )(total, norm_total, *operands)
    return (outputs[None], input_grad[None], grad_norm[0, 0], *fresh, shift_clipped[0])


def solution(mesh):
    tokens = P("batch", "seq", None)
    owned = P(("batch", "seq"), None)
    columns = P(None, ("batch", "seq"))
    state = (owned, owned, owned, owned, columns)
    return jax.shard_map(
        functools.partial(body, mesh.shape["batch"], mesh.shape["seq"]),
        mesh=mesh,
        in_specs=(tokens, tokens, P("batch")) + state * 3,
        out_specs=(tokens, tokens, P()) + state * 3 + (P(("batch", "seq")),),
        check_vma=False,
    )
```

```python
import functools
import jax
import jax.numpy as jnp
from jax import lax
from jax.experimental import pallas as pl
from jax.experimental.pallas import tpu as pltpu
from jax.sharding import PartitionSpec as P

HEADS = 8
HD = 64
SPAN = 128
STEP = 10
LN_EPS = 1e-05
NEG_FILL = -1e30
CLIP = 1.0
BETA = 0.5
ADAM_EPS = 1e-08
DECAY = 0.1
RATES = (0.02, 0.3, 0.02, 0.02, 0.5)
BF = jnp.bfloat16
F32 = jnp.float32
LANES = 128
VMEM_LIMIT = 56 * 1024 * 1024


def dot(a, b, dims=((1,), (0,))):
    return lax.dot_general(a, b, (dims, ((), ())), preferred_element_type=F32)


def dot_tn(a, b):
    return dot(a, b, ((0,), (0,)))


def dot_nt(a, b):
    return dot(a, b, ((1,), (1,)))


def normalize(x):
    inv = 1.0 / x.shape[-1]
    centred = x - jnp.sum(x, axis=-1, keepdims=True) * inv
    spread = jnp.sum(centred * centred, axis=-1, keepdims=True) * inv
    rstd = lax.rsqrt(spread + LN_EPS)
    return centred * rstd, rstd


def norm_back(grad, gain, xhat, rstd):
    inv = 1.0 / grad.shape[-1]
    e = grad * gain
    mean_e = jnp.sum(e, axis=-1, keepdims=True) * inv
    mean_ex = jnp.sum(e * xhat, axis=-1, keepdims=True) * inv
    return rstd * (e - mean_e - xhat * mean_ex)


def qkv_tile(x, norms_ref, weight_ref):
    xhat, _ = normalize(x.astype(F32))
    normed = (xhat * norms_ref[0:1, :] + norms_ref[1:2, :]).astype(BF)
    return dot(normed, weight_ref[...]).astype(BF)


def span_scale(length, begin, shape):
    count = jnp.clip(length - begin, 1, SPAN)
    return lax.rsqrt(jnp.full(shape, count, jnp.int32).astype(F32))


def span_sum(kv, length, begin):
    row = lax.broadcasted_iota(jnp.int32, kv.shape, 0)
    kept = jnp.where(row < length - begin, kv.astype(F32), 0.0)
    total = jnp.sum(kept, axis=0, keepdims=True)
    return total * span_scale(length, begin, total.shape)


def stack_heads(pair):
    lane = lax.broadcasted_iota(jnp.int32, pair.shape, 1)
    zero = jnp.zeros_like(pair)
    return jnp.concatenate(
        [jnp.where(lane < HD, pair, zero), jnp.where(lane >= HD, pair, zero)], axis=0
    )


def fold_heads(both):
    picked = jnp.concatenate([both[:HD, :SPAN], both[HD:, SPAN:]], axis=0)
    return picked.T


def span_caps(length, span):
    query_pos = lax.broadcasted_iota(jnp.int32, (1, 2 * SPAN), 1) & (SPAN - 1)
    near_cap = jnp.minimum(query_pos, length - span * SPAN - 1)
    far_cap = jnp.minimum(span, (length + SPAN - 1) // SPAN)
    return near_cap, far_cap


def mask_scores(raw, caps):
    near_cap, far_cap = caps
    key_pos = lax.broadcasted_iota(jnp.int32, (SPAN, 2 * SPAN), 0)
    summ_pos = lax.broadcasted_iota(jnp.int32, (raw.shape[0] - SPAN, 2 * SPAN), 0)
    near = jnp.where(key_pos <= near_cap, raw[:SPAN], NEG_FILL)
    far = jnp.where(summ_pos < far_cap, raw[SPAN:], NEG_FILL)
    return jnp.concatenate([near, far], axis=0)


def attend_spans(spans, mixed_ref, width, summ_ref, summ_vt_ref, out_ref, lse_ref=None, probs_ref=None):
    units = [(pl.ds(row, SPAN), index, caps, pair) for row, index, caps in spans for pair in range(width // LANES)]
    queries, keys, values_t = [], [], []
    for rows, index, caps, pair in units:
        at = pair * LANES
        queries.append(stack_heads(mixed_ref[rows, at : at + LANES] * BF(0.125)))
        near_k = mixed_ref[rows, width + at : width + at + LANES]
        near_v = mixed_ref[rows, 2 * width + at : 2 * width + at + LANES]
        keys.append(jnp.concatenate([near_k, summ_ref[:, at : at + LANES]], axis=0))
        values_t.append(jnp.concatenate([near_v.T, summ_vt_ref[at : at + LANES, :]], axis=1))
    scores = [dot_nt(k, q) for k, q in zip(keys, queries)]
    scores = [mask_scores(s, unit[2]) for s, unit in zip(scores, units)]
    peaks = [jnp.max(s, axis=0, keepdims=True) for s in scores]
    expos = [jnp.exp(s - p) for s, p in zip(scores, peaks)]
    totals = [jnp.sum(e, axis=0, keepdims=True) for e in expos]
    probs = [(e * (1.0 / t)).astype(BF) for e, t in zip(expos, totals)]
    outs = [dot(v, p) for v, p in zip(values_t, probs)]
    for (rows, index, caps, pair), out, prob, peak, total in zip(units, outs, probs, peaks, totals):
        at = pair * LANES
        out_ref[rows, at : at + LANES] = fold_heads(out).astype(BF)
        if lse_ref is not None:
            lse_ref[index, pair : pair + 1, :] = peak + jnp.log(total)
        if probs_ref is not None:
            at = pair * 4 * SPAN
            probs_ref[rows, at : at + 2 * SPAN] = prob[:SPAN]
            probs_ref[rows, at + 2 * SPAN : at + 4 * SPAN] = prob[SPAN:]


def attend_back_spans(
    spans, mixed_ref, grad_ref, width, summ_ref, summ_kt_ref, lse_ref, back_ref, dsumm_ref, probs_ref=None
):
    pairs = width // LANES
    units = [(pl.ds(row, SPAN), index, caps, pair) for row, index, caps in spans for pair in range(pairs)]
    queries, grads, keys, keys_t, values = [], [], [], [], []
    for rows, index, caps, pair in units:
        at = pair * LANES
        queries.append(stack_heads(mixed_ref[rows, at : at + LANES] * BF(0.125)))
        grads.append(stack_heads(grad_ref[rows, at : at + LANES]))
        near_k = mixed_ref[rows, width + at : width + at + LANES]
        near_v = mixed_ref[rows, 2 * width + at : 2 * width + at + LANES]
        keys.append(jnp.concatenate([near_k, summ_ref[:, at : at + LANES]], axis=0))
        keys_t.append(jnp.concatenate([near_k.T, summ_kt_ref[at : at + LANES, :]], axis=1))
        values.append(jnp.concatenate([near_v, summ_ref[:, width + at : width + at + LANES]], axis=0))
    if probs_ref is None:
        scores = [dot_nt(k, q) for k, q in zip(keys, queries)]
        dprobs = [dot_nt(v, g) for v, g in zip(values, grads)]
        scores = [mask_scores(s, unit[2]) for s, unit in zip(scores, units)]
        probs = [jnp.exp(s - lse_ref[index, pair : pair + 1, :]) for s, (_, index, _, pair) in zip(scores, units)]
    else:
        dprobs = [dot_nt(v, g) for v, g in zip(values, grads)]
        probs = []
        for rows, _, _, pair in units:
            at = pair * 4 * SPAN
            near, far = probs_ref[rows, at : at + 2 * SPAN], probs_ref[rows, at + 2 * SPAN : at + 4 * SPAN]
            probs.append(jnp.concatenate([near, far], axis=0).astype(F32))
    deltas = [jnp.sum(p * d, axis=0, keepdims=True) for p, d in zip(probs, dprobs)]
    dscores = [(p * (d - delta)).astype(BF) for p, d, delta in zip(probs, dprobs, deltas)]
    probs = [p.astype(BF) for p in probs]
    dqs = [dot(k, ds) for k, ds in zip(keys_t, dscores)]
    dks = [dot(ds, q) for ds, q in zip(dscores, queries)]
    dvs = [dot(p, g) for p, g in zip(probs, grads)]
    for (rows, index, caps, pair), dq, dk, dv in zip(units, dqs, dks, dvs):
        at = pair * LANES
        back_ref[rows, at : at + LANES] = (fold_heads(dq) * 0.125).astype(BF)
        back_ref[rows, width + at : width + at + LANES] = dk[:SPAN].astype(BF)
        back_ref[rows, 2 * width + at : 2 * width + at + LANES] = dv[:SPAN].astype(BF)
    for pair in range(pairs):
        at = pair * LANES
        dsumm_ref[:, at : at + LANES] += sum(dk[SPAN:] for dk in dks[pair::pairs])
        dsumm_ref[:, width + at : width + at + LANES] += sum(dv[SPAN:] for dv in dvs[pair::pairs])


def with_extra(back, extra, length, begin):
    extra = extra * span_scale(length, begin, extra.shape)
    pos = lax.broadcasted_iota(jnp.int32, back.shape, 0)
    return (back.astype(F32) + jnp.where(pos < length - begin, extra, 0.0)).astype(BF)


GELU_A = 0.7978845608
GELU_B = 0.044715


def gelu_parts(t):
    slow = GELU_A + (GELU_A * GELU_B) * (t * t)
    half = 0.5 * jnp.tanh(t * slow) + 0.5
    value = t * half
    return value, half + (value - value * half) * (6.0 * slow - 4.0 * GELU_A)


MESH = pl.DeviceIdType.MESH


class Place:
    def __init__(self, groups, seqs):
        self.groups, self.seqs, self.chips = groups, seqs, seqs // 2
        self.b = lax.axis_index("batch")
        self.seq = lax.axis_index("seq")
        self.z, self.c = self.seq // 2, self.seq % 2
        self.other = 1 - self.c
        self.b1 = self.b + 1 - 2 * (self.b % 2)
        self.b2 = (self.b + 2) % 4
        self.b3 = self.b1 + 2 - 4 * (self.b1 // 2)
        self.after = [(self.z + k) % self.chips for k in range(self.chips)]
        self.before = [(self.z + self.chips - k) % self.chips for k in range(self.chips)]
        self.sibling = (self.b, 2 * self.z + self.other)
        self.x, self.y, self.diagonal = (self.b1, self.seq), (self.b2, self.seq), (self.b3, self.seq)
        self.along = [(self.b, 2 * z + self.c) for z in self.after]
        self.ring = [(self.b, (self.seq + k) % seqs) for k in range(seqs)]


def meet(place):
    barrier = pltpu.get_barrier_semaphore()
    partners = [place.x, place.y, place.diagonal, *place.ring[1:]]
    for partner in partners:
        pl.semaphore_signal(barrier, inc=1, device_id=partner, device_id_type=MESH)
    pl.semaphore_wait(barrier, len(partners))


def part_of(ref, index):
    return ref if index is None else ref.at[index]


class Copy:
    def __init__(self, make):
        self.make = make
        make().start()

    def wait(self):
        self.make().wait()

    def wait_recv(self):
        self.make().wait_recv()

    def wait_send(self):
        self.make().wait_send()


class Copies:
    def __init__(self, send_sems, recv_sems):
        self.send, self.recv, self.made, self.left = send_sems, recv_sems, [], 0

    def start(self, src, src_index, dst, dst_index, device):
        at = len(self.made)
        assert at < self.send.shape[0]
        copy = Copy(
            lambda: pltpu.make_async_remote_copy(
                src_ref=part_of(src, src_index), dst_ref=part_of(dst, dst_index),
                send_sem=self.send.at[at], recv_sem=self.recv.at[at],
                device_id=device, device_id_type=MESH,
            )
        )
        self.made.append(copy)
        return copy

    def push(self, ref, index, device):
        return self.start(ref, index, ref, index, device)

    def finish(self):
        for copy in self.made[self.left :]:
            copy.wait_send()
        self.left = len(self.made)


class Loads:
    def __init__(self, sems):
        self.sems, self.made = sems, 0

    def start(self, src, dst, src_index=None, dst_index=None):
        at = self.made
        assert at < self.sems.shape[0]
        self.made += 1
        return Copy(
            lambda: pltpu.make_async_copy(part_of(src, src_index), part_of(dst, dst_index), self.sems.at[at])
        )


def gather_steps(place, copies, full, rows=slice(None), cols=slice(None)):
    p, half = place, place.chips // 2
    low, high = slice(0, half), slice(half, place.chips)

    def push(b, z, device):
        return copies.push(full, (b, z, p.c, rows, cols), device)

    along = [push(p.b, p.z, device) for device in p.along[1:]]
    yield
    for copy in along:
        copy.wait_recv()
    every = slice(None)
    to_x, to_y, sib = push(p.b, every, p.x), push(p.b, every, p.y), [push(p.b, every, p.sibling)]
    yield
    to_x.wait_recv()
    on_y = push(p.b1, low, p.y)
    to_y.wait_recv()
    on_x = push(p.b2, high, p.x)
    sib += [push(p.b1, every, p.sibling), push(p.b2, every, p.sibling)]
    yield
    on_y.wait_recv()
    sib.append(push(p.b3, low, p.sibling))
    on_x.wait_recv()
    sib.append(push(p.b3, high, p.sibling))
    yield
    for copy in sib:
        copy.wait_recv()


GATHER_COPIES = 12


def fast_gather_steps(place, copies, full, rows=slice(None), cols=slice(None)):
    p = place
    order = range(p.chips)
    early, late = order[: p.chips // 2], order[p.chips // 2 :]

    def push(b, k, device):
        return copies.push(full, (b, p.before[k], p.c, rows, cols), device)

    along = [push(p.b, 0, device) for device in p.along[1:]]
    to_x, to_y, sib = [push(p.b, 0, p.x)], [push(p.b, 0, p.y)], [push(p.b, 0, p.sibling)]
    yield
    for k, copy in enumerate(along, 1):
        copy.wait_recv()
        to_x.append(push(p.b, k, p.x))
        to_y.append(push(p.b, k, p.y))
        sib.append(push(p.b, k, p.sibling))
    yield
    on = []
    for k in early:
        to_x[k].wait_recv()
        on.append(push(p.b1, k, p.y))
        sib.append(push(p.b1, k, p.sibling))
    for k in late:
        to_y[k].wait_recv()
        on.append(push(p.b2, k, p.x))
        sib.append(push(p.b2, k, p.sibling))
    yield
    for k in late:
        to_x[k].wait_recv()
        sib.append(push(p.b1, k, p.sibling))
    for k in early:
        to_y[k].wait_recv()
        sib.append(push(p.b2, k, p.sibling))
    for k, copy in enumerate(on):
        copy.wait_recv()
        sib.append(push(p.b3, k, p.sibling))
    yield
    for copy in sib:
        copy.wait_recv()


def fast_gather_copies(chips):
    return chips - 1 + 3 * chips + 4 * chips


def scatter_steps(place, copies, loads, grad, acc, got, near, far, last, result):
    p, half = place, place.chips // 2
    low, high = slice(0, half), slice(half, place.chips)
    chips = p.chips

    def add(into, *others):
        total = acc[into].astype(F32)
        for other in others:
            total = total + other.astype(F32)
        acc[into] = total.astype(BF)

    every = slice(None)
    swap = copies.start(grad, (every, every, p.other), got, None, p.sibling)
    keep = loads.start(grad, acc, (every, every, p.c))
    yield
    keep.wait()
    swap.wait_recv()
    for b in (p.b3, p.b1, p.b2):
        for z in range(chips):
            add((b, z), got[b, z])
    on_y = copies.start(acc, (p.b3, low), far, 0, p.y)
    on_x = copies.start(acc, (p.b3, high), far, 1, p.x)
    early_x = copies.start(acc, (p.b1, high), near, (0, high), p.x)
    early_y = copies.start(acc, (p.b2, low), near, (1, low), p.y)
    for z in range(chips):
        add((p.b, z), got[p.b, z])
    yield
    on_y.wait_recv()
    for z in range(half):
        add((p.b1, z), far[0, z])
    late_x = copies.start(acc, (p.b1, low), near, (0, low), p.x)
    on_x.wait_recv()
    for z in range(half, chips):
        add((p.b2, z), far[1, z - half])
    late_y = copies.start(acc, (p.b2, high), near, (1, high), p.y)
    yield
    for copy in (early_x, early_y, late_x, late_y):
        copy.wait_recv()
    for z in range(chips):
        add((p.b, z), near[0, z], near[1, z])
    along = []
    for k in range(1, chips):
        along.append(copies.start(acc, (p.b, p.after[k]), last, k - 1, p.along[k]))
    yield
    total = acc[p.b, p.z].astype(F32)
    for k, copy in enumerate(along):
        copy.wait_recv()
        total = total + last[k].astype(F32)
    result[...] = total


SCATTER_COPIES = 10


def scatter_scratch(groups, chips, rows, cols):
    half = chips // 2
    return [
        pltpu.VMEM((groups, chips, rows, cols), BF),
        pltpu.VMEM((groups, chips, rows, cols), BF),
        pltpu.VMEM((2, chips, rows, cols), BF),
        pltpu.VMEM((2, half, rows, cols), BF),
        pltpu.VMEM((chips - 1, rows, cols), BF),
    ]


def share_sum_steps(place, copies, mine, along, across, result):
    p, seqs = place, along.shape[0]
    along[p.seq] = mine[...]
    sent = [copies.push(along, p.seq, device) for device in p.ring[1:]]
    yield
    for copy in sent:
        copy.wait_recv()
    across[p.b] = sum(along[s] for s in range(seqs))
    sent = [copies.push(across, p.b, device) for device in (p.x, p.y, p.diagonal)]
    yield
    for copy in sent:
        copy.wait_recv()
    result[...] = sum(across[b] for b in range(p.groups))


def share_copies(groups, seqs):
    return groups + seqs - 2


def square_sums(value):
    total = 0.0
    for at in range(0, value.shape[1], LANES):
        block = jnp.square(value[:, at : at + LANES])
        if block.shape[0] < 8:
            total = total + jnp.concatenate([block, jnp.zeros((8 - block.shape[0], LANES), F32)], axis=0)
        for row in range(0, block.shape[0] // 8 * 8, 8):
            total = total + block[row : row + 8]
    return total


class Schedule:
    def __init__(self, **steps):
        self.steps = steps

    def __call__(self, *names):
        for name in names:
            next(self.steps[name], None)

    def plan(self, *calls):
        return {at: functools.partial(self, *names.split()) for at, names in enumerate(calls) if names}

    def finish(self, *names):
        run_all(*(self.steps[name] for name in names or self.steps))


def run_all(*steps):
    live = list(steps)
    while live:
        for step in list(live):
            try:
                next(step)
            except StopIteration:
                live.remove(step)


def loop(count, body, ticks=None):
    def step(index, carry):
        body(index)
        for k in sorted(ticks or {}):
            pl.when(index == k)(lambda run=ticks[k]: run())
        return carry

    lax.fori_loop(0, count, step, 0)


def adam(grad, master, first, second, rate, moment_out, square_out, fresh_out):
    fix = 1.0 - BETA**STEP
    moment = BETA * first + (1.0 - BETA) * grad
    square = BETA * second + (1.0 - BETA) * grad * grad
    update = moment / fix / (jnp.sqrt(square / fix) + ADAM_EPS)
    moment_out[...] = moment
    square_out[...] = square
    fresh_out[...] = master - rate * (update + DECAY * master)


def update_kernel(parts, total_ref, norm_grad, *refs):
    sources, results, held, sems = refs[:20], refs[20:39], refs[39:-1], refs[-1]
    outputs_ref, input_ref, grad_refs, state, made, wide_ref = held[0], held[1], held[2:5], held[5:20], held[20:35], held[35]
    outputs_hbm, input_hbm, grads_hbm, state_hbm = sources[0], sources[1], sources[2:5], sources[5:]
    loads = Loads(sems)
    ways = ((input_hbm, input_ref, wide_ref, results[1]), (outputs_hbm, outputs_ref, outputs_ref, results[0]))
    small = [loads.start(src, via) for src, via in zip((*grads_hbm, *state_hbm), (*grad_refs, *state))]
    reads = [Sliced(loads, src, via, parts).start_all() for src, via, _, _ in ways]
    stores = [Sliced(loads, via, dst, parts) for _, _, via, dst in ways]
    for load in small:
        load.wait()
    grad_norm = jnp.sqrt(jnp.sum(total_ref[...], keepdims=True))
    results[2][...] = grad_norm
    factor = jnp.minimum(1.0, CLIP / (grad_norm + 1e-06))
    width = state[1].shape[1]
    piece = state[4].shape[1]
    per = LANES // piece
    index = lax.axis_index("batch") * lax.axis_size("seq") + lax.axis_index("seq")
    block = norm_grad[:, pl.ds(pl.multiple_of(index // per * LANES, LANES), LANES)]
    own = pltpu.roll(block, (LANES - index % per * piece) % LANES, 1)[:, :piece]
    qkv_grad, pu_grad, down_grad = grad_refs
    grads = (qkv_grad[...], pu_grad[:, :width], pu_grad[:, width:], down_grad[...], own)
    results[18][...] = own[3:4] * factor
    last = []
    for at, (grad, rate) in enumerate(zip(grads, RATES)):
        adam(
            grad * factor, state[at][...], state[5 + at][...], state[10 + at][...], rate,
            made[at], made[5 + at], made[10 + at],
        )
        last += [loads.start(made[k], results[3 + k]) for k in (at, 5 + at, 10 + at)]
    for read, store in zip(reads, stores):
        for part in range(parts):
            read.wait(part)
            if read.dst is input_ref:
                here = pl.ds(part * read.size, read.size)
                wide_ref[here, :] = input_ref[here, :].astype(F32)
            store.start(part)
    for store in stores:
        store.wait_all()
    for store in last:
        store.wait()


def cast_shards(p, seqs, qkv_ref, proj_ref, up_ref, down_ref, norm_ref, qkv_full, pu_full, down_full, norm_full):
    width = proj_ref.shape[1]
    b, z, c = p.b, p.z, p.c
    index = b * seqs + 2 * z + c
    qkv_full[b, z, c] = qkv_ref[...].astype(BF)
    pu_full[b, z, c, :, :width] = proj_ref[...].astype(BF)
    pu_full[b, z, c, :, width:] = up_ref[...].astype(BF)
    down_full[b, z, c] = down_ref[...].astype(BF)
    piece = norm_ref.shape[1]
    per = LANES // piece
    tiled = jnp.concatenate([norm_ref[...].astype(BF).astype(F32)] * per, axis=1)
    lane = lax.broadcasted_iota(jnp.int32, tiled.shape, 1)
    norm_full[b, z, c] = jnp.where(lane // piece == index % per, tiled, 0.0)


def join_norms(norm_full, seqs, per, norms_out):
    for block in range(norms_out.shape[1] // LANES):
        total = None
        for device in range(block * per, (block + 1) * per):
            one = norm_full[device // seqs, device % seqs // 2, device % 2]
            total = one if total is None else total + one
        norms_out[:, block * LANES : (block + 1) * LANES] = total


class Sliced:
    def __init__(self, loads, src, dst, count):
        self.src, self.dst, self.count, self.size = src, dst, count, src.shape[0] // count
        self.sems, self.first = loads.sems, loads.made
        loads.made += count
        assert loads.made <= loads.sems.shape[0]

    def copy(self, index):
        begin = index * self.size
        here = pl.ds(begin if isinstance(index, int) else pl.multiple_of(begin, self.size), self.size)
        return pltpu.make_async_copy(self.src.at[here], self.dst.at[here], self.sems.at[self.first + index])

    def start(self, index):
        self.copy(index).start()

    def wait(self, index):
        self.copy(index).wait()

    def start_next(self, index):
        pl.when(index < self.count)(lambda: self.start(index))

    def start_all(self):
        for index in range(self.count):
            self.start(index)
        return self

    def wait_all(self):
        for index in range(self.count):
            self.wait(index)


class SummaryView:
    def __init__(self, ref, rows):
        self.ref, self.rows = ref, rows

    def __getitem__(self, key):
        cols = key[1]
        return self.ref[:, :, :, cols].reshape(self.rows, cols.stop - cols.start)


def row_block(index, size):
    return pl.ds(pl.multiple_of(index * size, size), size)


TILE = 512


def front_kernel(
    groups, seqs, length_ref, x_hbm, og_hbm, qkv_ref, proj_ref, up_ref, down_ref, norm_ref,
    qkv_hbm, pu_hbm, down_hbm, norms_out, mixed_hbm, summ_ref, attn_hbm, probs_hbm,
    activ_hbm, resid_hbm, slope_hbm, down_grad_hbm,
    x_ref, og_ref, qkv_full, pu_full, down_full, mixed_ref, attn_ref, resid_ref, activ_ref, slope_ref,
    down_grad_ref, norm_full, sum_scr, vt_scr, load_sems, send_sems, recv_sems,
):
    p = Place(groups, seqs)
    rows, width = x_ref.shape
    hidden = activ_ref.shape[1]
    local = rows // SPAN
    length, first_span = length_ref[0], p.seq * local
    count, per = rows // TILE, TILE // SPAN
    loads = Loads(load_sems)
    x_load = Sliced(loads, x_hbm, x_ref, count).start_all()
    cast_shards(
        p, seqs, qkv_ref, proj_ref, up_ref, down_ref, norm_ref, qkv_full, pu_full, down_full, norm_full
    )
    meet(p)
    og_load = loads.start(og_hbm, og_ref)
    copies = Copies(send_sems, recv_sems)
    half_down, half_pu = down_full.shape[3] // 2, pu_full.shape[4] // 2
    move = Schedule(
        kv=fast_gather_steps(p, copies, qkv_full, cols=slice(width, 3 * width)),
        norm=gather_steps(p, copies, norm_full),
        q=gather_steps(p, copies, qkv_full, cols=slice(0, width)),
        pu0=gather_steps(p, copies, pu_full, cols=slice(0, half_pu)),
        pu1=gather_steps(p, copies, pu_full, cols=slice(half_pu, 2 * half_pu)),
        down0=gather_steps(p, copies, down_full, rows=slice(0, half_down)),
        down1=gather_steps(p, copies, down_full, rows=slice(half_down, 2 * half_down)),
    )
    xhat_ref = resid_ref

    def center(index):
        here = row_block(index, TILE)
        x_load.wait(index)
        xhat_ref[here, :] = normalize(x_ref[here, :].astype(F32))[0]

    move("norm", "kv")
    loop(count, center, move.plan("norm kv q pu0", "", "norm kv", "norm kv q pu1"))
    move("norm", "kv")
    move("pu0")
    join_norms(norm_full, seqs, LANES // norm_ref.shape[1], norms_out)
    gain, shift = norms_out[0:1, :], norms_out[1:2, :]

    def columns(full, begin, size):
        return full[:, :, :, :, begin : begin + size].reshape(width, size)

    def normed_of(here):
        return (xhat_ref[here, :] * gain + shift).astype(BF)

    def keys_values(index):
        here = row_block(index, TILE)
        mixed = dot(normed_of(here), columns(qkv_full, width, 2 * width)).astype(BF)
        mixed_ref[here, width:] = mixed
        for part in range(per):
            span = index * per + part
            sum_scr[pl.ds(span, 1), :] = span_sum(
                mixed[part * SPAN : (part + 1) * SPAN], length, (first_span + span) * SPAN
            )

    loop(count, keys_values, move.plan("q", "pu1 down0", "q"))
    summ_ref[p.z, p.c] = sum_scr[...].astype(BF)
    along = [copies.push(summ_ref, (p.z, p.c), device) for device in p.along[1:]]
    sib = [copies.push(summ_ref, (p.z, p.c), p.sibling)]
    move("down1", "pu0")
    for k, copy in enumerate(along, 1):
        copy.wait_recv()
        sib.append(copies.push(summ_ref, (p.before[k], p.c), p.sibling))
    move("q")
    stores = [loads.start(qkv_full, qkv_hbm)]
    mixed_store = Sliced(loads, mixed_ref, mixed_hbm, count)

    def queries(index):
        here = row_block(index, TILE)
        mixed_ref[here, :width] = dot(normed_of(here), columns(qkv_full, 0, width)).astype(BF)
        mixed_store.start(index)

    loop(count, queries)
    move("pu1")
    for copy in sib:
        copy.wait_recv()
    vt_scr[...] = summ_ref[:, :, :, width:].reshape(local * seqs, width).T
    summ_rows = SummaryView(summ_ref, local * seqs)
    attn_store = Sliced(loads, attn_ref, attn_hbm, count)
    probs_ref = activ_ref
    probs_store = Sliced(loads, probs_ref, probs_hbm, count)

    def attend(index):
        spans = []
        for k in range(per):
            span = index * per + k
            spans.append((pl.multiple_of(span * SPAN, SPAN), span, span_caps(length, first_span + span)))
        attend_spans(spans, mixed_ref, width, summ_rows, vt_scr, attn_ref, probs_ref=probs_ref)
        attn_store.start(index)
        probs_store.start(index)

    loop(count, attend, move.plan("pu0 down0", "pu1 down1", "pu0", "pu1"))
    gain_two, shift_two = norms_out[2:3, :], norms_out[3:4, :]
    resid_store, slope_store, activ_store = (
        Sliced(loads, src, dst, count)
        for src, dst in ((resid_ref, resid_hbm), (slope_ref, slope_hbm), (activ_ref, activ_hbm))
    )
    chunk = 256

    def expand(index):
        here = row_block(index, TILE)
        resid = x_ref[here, :].astype(F32) + dot(attn_ref[here, :], columns(pu_full, 0, width))
        resid_ref[here, :] = resid
        resid_store.start(index)
        normed = (normalize(resid)[0] * gain_two + shift_two).astype(BF)
        probs_store.wait(index)
        for at in range(0, hidden, chunk):
            value, slope = gelu_parts(dot(normed, columns(pu_full, width + at, chunk)))
            activ_ref[here, at : at + chunk] = value.astype(BF)
            slope_ref[here, at : at + chunk] = slope.astype(BF)
        slope_store.start(index)
        activ_store.start(index)

    loop(count, expand, move.plan("down0", "down1", "down0", "down1"))
    stores.append(loads.start(pu_full, pu_hbm))
    og_load.wait()
    parts = hidden // TILE
    grad_store = Sliced(loads, down_grad_ref, down_grad_hbm, parts)

    def down_grad(index):
        here = row_block(index, TILE)
        down_grad_ref[here, :] = dot_tn(activ_ref[:, here], og_ref[...]).astype(BF)
        grad_store.start(index)

    loop(parts, down_grad)
    move.finish()
    stores.append(loads.start(down_full, down_hbm))
    for store in (mixed_store, attn_store, resid_store, slope_store, activ_store, grad_store):
        store.wait_all()
    for store in stores:
        store.wait()
    copies.finish()


def middle_kernel(
    groups, seqs, og_hbm, resid_hbm, slope_hbm, attn_hbm, pu_hbm, down_hbm, norms_ref, down_grad_hbm,
    resid_grad_hbm, attn_grad_hbm, pu_grad_hbm, down_out, norm_grad_ref,
    og_ref, resid_ref, slope_ref, attn_ref, pu_ref, down_ref, resid_grad_ref, attn_grad_ref, pu_grad_ref,
    pre_grad_ref, normed_ref, pig_ref, *scratch,
):
    *buffers, load_sems, send_sems, recv_sems = scratch
    p = Place(groups, seqs)
    rows, width = og_ref.shape
    hidden = slope_ref.shape[1]
    count = rows // TILE
    loads = Loads(load_sems)
    early = [loads.start(down_hbm, down_ref)]
    tiled = [
        Sliced(loads, src, dst, count)
        for src, dst in ((og_hbm, og_ref), (slope_hbm, slope_ref), (resid_hbm, resid_ref))
    ]
    for load in tiled:
        load.start(0)
    early.append(loads.start(pu_hbm, pu_ref))
    for load in tiled:
        load.start(1)
    meet(p)
    copies = Copies(send_sems, recv_sems)
    half = down_out.shape[0] // 2
    move = Schedule(
        **{
            f"down{at}": scatter_steps(
                p, copies, loads, down_grad_hbm.at[:, :, :, half * at : half * (at + 1)], *buffers[5 * at : 5 * at + 5],
                down_out.at[half * at : half * (at + 1)],
            )
            for at in range(2)
        }
    )
    move("down0", "down1")
    attn_load = loads.start(attn_hbm, attn_ref)
    norm_grad_ref[...] = jnp.zeros_like(norm_grad_ref)
    resid_grad_store, attn_grad_store = (
        Sliced(loads, src, dst, count)
        for src, dst in ((resid_grad_ref, resid_grad_hbm), (attn_grad_ref, attn_grad_hbm))
    )
    gain, shift = norms_ref[2:3, :], norms_ref[3:4, :]
    chunk = 256
    early[0].wait()

    def tile(index):
        here = row_block(index, TILE)
        for load in tiled:
            load.start_next(index + 2)
            load.wait(index)
        grad = og_ref[here, :]
        for at in range(0, hidden, chunk):
            act_grad = dot_nt(grad, down_ref[at : at + chunk, :])
            slope = slope_ref[here, at : at + chunk].astype(F32)
            pre_grad_ref[here, at : at + chunk] = (act_grad * slope).astype(BF)

        @pl.when(index == 0)
        def _():
            early[1].wait()

        back = dot_nt(pre_grad_ref[here, :], pu_ref[:, width:])
        xhat, rstd = normalize(resid_ref[here, :])
        normed_ref[here, :] = (xhat * gain + shift).astype(BF)
        resid_grad = grad.astype(F32) + norm_back(back, gain, xhat, rstd)
        resid_grad_ref[here, :] = resid_grad
        resid_grad_store.start(index)
        pig = resid_grad.astype(BF)
        pig_ref[here, :] = pig
        attn_grad_ref[here, :] = dot_nt(pig, pu_ref[:, :width]).astype(BF)
        attn_grad_store.start(index)
        norm_grad_ref[0:1, :] += jnp.sum(back * xhat, axis=0, keepdims=True)
        norm_grad_ref[1:2, :] += jnp.sum(back, axis=0, keepdims=True)

    loop(count, tile, move.plan("down0", "down1", "down0", "down1 down0"))
    attn_load.wait()
    pu_grad_ref[:, :width] = dot_tn(attn_ref[...], pig_ref[...]).astype(BF)

    def up_grad(index):
        at = pl.multiple_of(width + index * TILE, TILE)
        pu_grad_ref[:, pl.ds(at, TILE)] = dot_tn(normed_ref[...], pre_grad_ref[:, row_block(index, TILE)]).astype(BF)

    loop(hidden // TILE, up_grad, move.plan("down1", "", "down0"))
    pu_store = loads.start(pu_grad_ref, pu_grad_hbm)
    resid_grad_store.wait_all()
    attn_grad_store.wait_all()
    move.finish()
    pu_store.wait()
    copies.finish()


def back_kernel(
    groups, seqs, length_ref, x_hbm, mixed_hbm, grad_hbm, probs_hbm, summ_ref, pu_hbm, resid_grad_hbm, down_ref,
    norms_ref, weight_hbm, norm_two_ref, activ_hbm, resid_hbm, down_hbm,
    input_grad_hbm, outputs_hbm, qkv_out, pu_out, norm_out, total_out,
    x_ref, mixed_ref, grad_ref, probs_ref, resid_grad_ref, weight_ref, input_low_ref, resid_ref, down_full_ref, outputs_ref,
    mg_scr, xhat_ref, kt_scr, dsumm_scr, dsumm_got, dsumm_low, dsumm_last, extra_scr, q_grad, k_grad, v_grad,
    gain_cols, shift_cols,
    *scratch,
):
    *buffers, norm_mine, along_norm, across_norm, sq_mine, along_sq, across_sq = scratch[:-3]
    load_sems, send_sems, recv_sems = scratch[-3:]
    p = Place(groups, seqs)
    rows, width = x_ref.shape
    local = rows // SPAN
    length, first_span = length_ref[0], p.seq * local
    loads = Loads(load_sems)
    group = 2
    count, steps = rows // TILE, local // group
    reads = [
        Sliced(loads, src, dst, steps)
        for src, dst in ((mixed_hbm, mixed_ref), (grad_hbm, grad_ref), (probs_hbm, probs_ref))
    ]
    for index in range(2):
        for read in reads:
            read.start(index)
    meet(p)
    copies = Copies(send_sems, recv_sems)

    def scatter(grad, at, out):
        return scatter_steps(p, copies, loads, grad, *buffers[5 * at : 5 * at + 5], out)

    half = pu_hbm.shape[4] // 2
    outs = [qkv_out.at[:, width * at : width * (at + 1)] for at in range(3)]
    move = Schedule(
        pu0=scatter(pu_hbm.at[:, :, :, :, :half], 0, pu_out.at[:, :half]),
        pu1=scatter(pu_hbm.at[:, :, :, :, half:], 1, pu_out.at[:, half:]),
        q=scatter(q_grad, 2, outs[0]), k=scatter(k_grad, 3, outs[1]), v=scatter(v_grad, 4, outs[2]),
        norm=share_sum_steps(p, copies, norm_mine, along_norm, across_norm, norm_out),
        squares=share_sum_steps(p, copies, sq_mine, along_sq, across_sq, total_out),
    )
    move("pu0", "pu1")
    late = [loads.start(src, dst) for src, dst in ((x_hbm, x_ref), (weight_hbm, weight_ref))]
    resid_grad_load = loads.start(resid_grad_hbm, resid_grad_ref)
    kt_scr[...] = summ_ref[:, :width].T
    dsumm_scr[...] = jnp.zeros_like(dsumm_scr)

    def attend_back(index):
        for read in reads:
            read.start_next(index + 2)
            read.wait(index)
        each = []
        for k in range(group):
            span = index * group + k
            each.append((pl.multiple_of(span * SPAN, SPAN), span, None))
        attend_back_spans(each, mixed_ref, grad_ref, width, summ_ref, kt_scr, None, mg_scr, dsumm_scr, probs_ref)

    loop(steps, attend_back, move.plan("", "pu0", "", "pu1", "pu0", "", "pu1"))
    activ_ref = probs_ref
    late += [loads.start(*ends) for ends in ((activ_hbm, activ_ref), (resid_hbm, resid_ref), (down_hbm, down_full_ref))]
    swap = []
    for z in range(p.chips):
        block = pl.ds(pl.multiple_of((2 * z + p.other) * local, local), local)
        swap.append(copies.start(dsumm_scr, block, dsumm_got, z, p.sibling))
    gain, shift = norms_ref[0:1, :], norms_ref[1:2, :]
    for read in late[:2]:
        read.wait()

    def recompute(index):
        here = row_block(index, TILE)
        xhat_ref[here, :] = normalize(x_ref[here, :].astype(F32))[0].astype(BF)

    loop(count // 2, recompute)
    for copy in swap:
        copy.wait_recv()

    def half_sum(z):
        mine = dsumm_scr[pl.ds(pl.multiple_of((2 * z + p.c) * local, local), local), :]
        return mine + dsumm_got[z]

    along = []
    for k in range(1, p.chips):
        dsumm_low[k - 1] = half_sum(p.after[k]).astype(BF)
        along.append(copies.start(dsumm_low, k - 1, dsumm_last, k - 1, p.along[k]))
    loop(count // 2, lambda index: recompute(index + count // 2))
    per_block = width // (groups * seqs)
    gain_cols[...] = jnp.broadcast_to(gain, (LANES, width)).T
    shift_cols[...] = jnp.broadcast_to(shift, (LANES, width)).T

    def weight_grad(into, at):
        begin = at * width
        back = mg_scr[:, begin : begin + width]
        moved = dot_tn(xhat_ref[...], back)
        total = jnp.sum(back.astype(F32), axis=0, keepdims=True)
        blocks, gains, shifts = [], 0.0, 0.0
        for k in range(0, width, LANES):
            part, sums = moved[:, k : k + LANES], total[:, k : k + LANES]
            blocks.append(gain_cols[...] * part + shift_cols[...] * sums)
            weight = weight_ref[:, begin + k : begin + k + LANES].astype(F32)
            gains += weight * part
            shifts += weight * sums
        into[...] = jnp.concatenate(blocks, axis=1).astype(BF).reshape(groups, p.chips, 2, per_block, width)
        gain_sums = jnp.sum(gains.T, axis=0, keepdims=True)
        shift_sums = jnp.sum(shifts.T, axis=0, keepdims=True)
        norm_mine[0:1, :] = gain_sums + (norm_mine[0:1, :] if at else 0.0)
        norm_mine[1:2, :] = shift_sums + (norm_mine[1:2, :] if at else 0.0)

    norm_mine[2:4, :] = norm_two_ref[...]
    weight_grad(q_grad, 0)
    move("q", "pu0")

    move("pu1")
    total = half_sum(p.z)
    for k, copy in enumerate(along):
        copy.wait_recv()
        total = total + dsumm_last[k].astype(F32)
    extra_scr[...] = total

    def add_extra(index):
        for k in range(2):
            span = index * 2 + k
            here = row_block(span, SPAN)
            mg_scr[here, width:] = with_extra(
                mg_scr[here, width:], extra_scr[pl.ds(span, 1), :], length, (first_span + span) * SPAN
            )

    loop(local // 2, add_extra)
    weight_grad(k_grad, 1)
    move("k", "q")
    weight_grad(v_grad, 2)
    move("v", "norm", "k", "q")
    resid_grad_load.wait()
    store = Sliced(loads, input_low_ref, input_grad_hbm, count)

    def finish(index):
        here = row_block(index, TILE)
        xhat, rstd = normalize(x_ref[here, :].astype(F32))
        back = dot_nt(mg_scr[here, :], weight_ref[...])
        input_low_ref[here, :] = (resid_grad_ref[here, :] + norm_back(back, gain, xhat, rstd)).astype(BF)
        store.start(index)

    loop(count, finish, move.plan("v k", "norm q", "v k pu0", "v pu1"))
    for read in late[2:]:
        read.wait()
    outputs_store = Sliced(loads, outputs_ref, outputs_hbm, count)

    def contract(index):
        here = row_block(index, TILE)
        out = resid_ref[here, :] + dot(activ_ref[here, :], down_full_ref[...])
        outputs_ref[here, :] = out.astype(BF)
        outputs_store.start(index)

    loop(count // 2, contract, move.plan("k norm q"))
    sq_mine[...] = square_sums(pu_out[...]) + square_sums(down_ref[...])
    copies.finish()
    move.finish("pu0", "pu1", "q", "k", "v", "norm")
    sq_mine[...] += square_sums(qkv_out[...])
    move("squares")
    loop(count // 2, lambda index: contract(index + count // 2), move.plan("squares"))
    move.finish("squares")
    total_out[...] += square_sums(norm_out[...])
    store.wait_all()
    outputs_store.wait_all()
    copies.finish()


def qkv_kernel(info_ref, x_ref, norms_ref, weight_ref, mixed_ref, summ_ref, sum_scr):
    step = pl.program_id(0)
    tile, width = x_ref.shape
    length, first_span = info_ref[0], info_ref[1]
    mixed = qkv_tile(x_ref[...], norms_ref, weight_ref)
    mixed_ref[...] = mixed
    per = tile // SPAN
    for part in range(per):
        span = step * per + part
        sum_scr[pl.ds(span, 1), :] = span_sum(
            mixed[part * SPAN : (part + 1) * SPAN, width:], length, (first_span + span) * SPAN
        )

    @pl.when(step == pl.num_programs(0) - 1)
    def _():
        summ_ref[...] = sum_scr[...].astype(BF)


def attend_kernel(info_ref, mixed_ref, summ_ref, out_ref, lse_ref, vt_scr):
    step = pl.program_id(0)
    width = out_ref.shape[1]

    @pl.when(step == 0)
    def _():
        vt_scr[...] = summ_ref[:, width:].T

    caps = span_caps(info_ref[0], info_ref[1] + step)
    attend_spans([(0, 0, caps)], mixed_ref, width, summ_ref, vt_scr, out_ref, lse_ref)


def attend_back_kernel(info_ref, mixed_ref, grad_ref, lse_ref, summ_ref, back_ref, dsumm_ref, kt_scr):
    step = pl.program_id(0)
    width = grad_ref.shape[1]

    @pl.when(step == 0)
    def _():
        kt_scr[...] = summ_ref[:, :width].T
        dsumm_ref[...] = jnp.zeros_like(dsumm_ref)

    caps = span_caps(info_ref[0], info_ref[1] + step)
    attend_back_spans(
        [(0, 0, caps)], mixed_ref, grad_ref, width, summ_ref, kt_scr, lse_ref, back_ref, dsumm_ref
    )


def mlp_kernel(
    x_ref, attn_ref, og_ref, norms_ref, pu_ref, down_ref,
    out_ref, resid_grad_ref, attn_grad_ref, pu_grad_ref, down_grad_ref, norm_grad_ref,
    activ_scr, pre_grad_scr, n2t_scr, attnt_scr, ogt_scr, pig_scr, norm_scr,
):
    step = pl.program_id(0)
    tile, width = x_ref.shape
    hidden = down_ref.shape[0]
    rows = pl.ds(pl.multiple_of(step * tile, tile), tile)
    chunk = 256
    attn = attn_ref[...]
    grad = og_ref[...]
    resid = x_ref[...].astype(F32) + dot(attn, pu_ref[:, :width])
    xhat, rstd = normalize(resid)
    gain = norms_ref[2:3, :]
    normed = (xhat * gain + norms_ref[3:4, :]).astype(BF)
    attnt_scr[:, rows] = attn.T
    n2t_scr[:, rows] = normed.T
    ogt_scr[:, rows] = grad.T
    for at in range(0, hidden, chunk):
        pre = dot(normed, pu_ref[:, width + at : width + at + chunk])
        act_grad = dot_nt(grad, down_ref[at : at + chunk, :])
        value, slope = gelu_parts(pre)
        activ = value.astype(BF)
        pre_grad = (act_grad * slope).astype(BF)
        activ_scr[rows, at : at + chunk] = activ
        pre_grad_scr[rows, at : at + chunk] = pre_grad
    out_ref[...] = (resid + dot(activ_scr[rows, :], down_ref[...])).astype(BF)
    back = dot_nt(pre_grad_scr[rows, :], pu_ref[:, width:])
    resid_grad = grad.astype(F32) + norm_back(back, gain, xhat, rstd)
    resid_grad_ref[...] = resid_grad
    pig = resid_grad.astype(BF)
    pig_scr[rows, :] = pig
    attn_grad_ref[...] = dot_nt(pig, pu_ref[:, :width]).astype(BF)
    gain_part = jnp.sum(back * xhat, axis=0, keepdims=True)
    shift_part = jnp.sum(back, axis=0, keepdims=True)
    part = jnp.concatenate([gain_part, shift_part], axis=0)

    @pl.when(step == 0)
    def _():
        norm_scr[...] = part

    @pl.when(step > 0)
    def _():
        norm_scr[...] += part

    @pl.when(step == pl.num_programs(0) - 1)
    def _():
        norm_grad_ref[...] = norm_scr[...]
        pu_grad_ref[:, :width] = dot(attnt_scr[...], pig_scr[...]).astype(BF)
        cols = 512

        def one(index, carry):
            c = pl.ds(pl.multiple_of(index * cols, cols), cols)
            out = pl.ds(pl.multiple_of(width + index * cols, cols), cols)
            pu_grad_ref[:, out] = dot(n2t_scr[...], pre_grad_scr[:, c]).astype(BF)
            down_grad_ref[c, :] = dot(ogt_scr[...], activ_scr[:, c]).T.astype(BF)
            return carry

        lax.fori_loop(0, hidden // cols, one, 0)


def final_kernel(
    info_ref, x_ref, back_ref, extra_ref, resid_grad_ref, norms_ref, weight_ref,
    input_grad_ref, qkv_grad_ref, norm_grad_ref, mg_scr, normed_scr,
):
    step = pl.program_id(0)
    tile, width = x_ref.shape
    rows = pl.ds(pl.multiple_of(step * tile, tile), tile)
    length, first_span = info_ref[0], info_ref[1]
    xhat, rstd = normalize(x_ref[...].astype(F32))
    gain = norms_ref[0:1, :]
    normed_scr[rows, :] = (xhat * gain + norms_ref[1:2, :]).astype(BF)
    per = tile // SPAN
    parts = []
    for part in range(per):
        span = step * per + part
        here = back_ref[part * SPAN : (part + 1) * SPAN, width:]
        parts.append(with_extra(here, extra_ref[pl.ds(span, 1), :], length, (first_span + span) * SPAN))
    mg = jnp.concatenate([back_ref[:, :width], jnp.concatenate(parts, axis=0)], axis=1)
    mg_scr[rows, :] = mg
    back = dot_nt(mg, weight_ref[...])
    input_grad_ref[...] = resid_grad_ref[...] + norm_back(back, gain, xhat, rstd)

    @pl.when(step == 0)
    def _():
        norm_grad_ref[...] = jnp.zeros_like(norm_grad_ref)

    norm_grad_ref[0:1, :] += jnp.sum(back * xhat, axis=0, keepdims=True)
    norm_grad_ref[1:2, :] += jnp.sum(back, axis=0, keepdims=True)

    @pl.when(step == pl.num_programs(0) - 1)
    def _():
        cols = 256

        def one(index, carry):
            c = pl.ds(pl.multiple_of(index * cols, cols), cols)
            qkv_grad_ref[:, c] = dot_tn(normed_scr[...], mg_scr[:, c]).astype(BF)
            return carry

        lax.fori_loop(0, qkv_grad_ref.shape[1] // cols, one, 0)


def whole(shape):
    return pl.BlockSpec(shape, lambda i: (0,) * len(shape))


def by_rows(tile, width):
    return pl.BlockSpec((tile, width), lambda i: (i, 0))


SCALARS = pl.BlockSpec(memory_space=pltpu.SMEM)
PARAMS = pltpu.CompilerParams(vmem_limit_bytes=VMEM_LIMIT)


def remote_call(kernel, groups, seqs, name, collective_id, outs, ins, scratch, loads, copies):
    return pl.pallas_call(
        functools.partial(kernel, groups, seqs),
        in_specs=[pl.BlockSpec(memory_space=space) for space in ins],
        out_specs=[pl.BlockSpec(memory_space=space) for space, _, _ in outs],
        out_shape=[jax.ShapeDtypeStruct(shape, kind) for _, shape, kind in outs],
        scratch_shapes=list(scratch) + [pltpu.SemaphoreType.DMA((n,)) for n in (loads, copies, copies)],
        compiler_params=pltpu.CompilerParams(
            vmem_limit_bytes=VMEM_LIMIT, collective_id=collective_id, has_side_effects=True
        ),
        name=name,
    )


def regroup(grad, dim, outer, inner):
    shape = grad.shape
    piece = shape[dim] // (outer * inner)
    split = grad.reshape(shape[:dim] + (outer, inner, piece) + shape[dim + 1 :])
    return jnp.swapaxes(split, dim, dim + 1).reshape(shape)


def gather_plain(state):
    both = ("batch", "seq")
    qkv, proj, up, down = (lax.all_gather(w.astype(BF), both, axis=0, tiled=True) for w in state[:4])
    norms = lax.all_gather(state[4].astype(BF), both, axis=1, tiled=True).astype(F32)
    return qkv, jnp.concatenate([proj, up], axis=1), down, norms


def reduce_plain(qkv_grad, pu_grad, down_grad, norm_grad):
    groups, seqs = lax.axis_size("batch"), lax.axis_size("seq")
    reduced = []
    for grad, dim in ((qkv_grad, 0), (pu_grad, 0), (down_grad, 0)):
        part = lax.psum_scatter(
            regroup(grad.astype(F32), dim, groups, seqs), "seq", scatter_dimension=dim, tiled=True
        )
        reduced.append(lax.psum_scatter(part, "batch", scatter_dimension=dim, tiled=True))
    norm_total = lax.psum(norm_grad, ("batch", "seq"))
    squares = lax.psum(sum(jnp.sum(grad * grad) for grad in reduced), ("batch", "seq"))
    squares = squares + jnp.sum(norm_total * norm_total)
    return (*reduced, norm_total, jnp.zeros((8, LANES), F32).at[0, 0].set(squares))


def mlp_call(x, attn_out, grad_rows, norms, pu_full, down_full):
    sds = jax.ShapeDtypeStruct
    rows, width = x.shape
    hidden = down_full.shape[0]
    tile = min(512, rows)
    steps = rows // tile
    return pl.pallas_call(
        mlp_kernel,
        grid=(steps,),
        in_specs=[by_rows(tile, width)] * 3
        + [whole(norms.shape), whole(pu_full.shape), whole(down_full.shape)],
        out_specs=[by_rows(tile, width)] * 3
        + [whole(pu_full.shape), whole(down_full.shape), whole((2, width))],
        out_shape=[
            sds((rows, width), BF), sds((rows, width), F32), sds((rows, width), BF),
            sds(pu_full.shape, BF), sds(down_full.shape, BF), sds((2, width), F32),
        ],
        scratch_shapes=[
            pltpu.VMEM((rows, hidden), BF), pltpu.VMEM((rows, hidden), BF),
            pltpu.VMEM((width, rows), BF), pltpu.VMEM((width, rows), BF), pltpu.VMEM((width, rows), BF),
            pltpu.VMEM((rows, width), BF), pltpu.VMEM((2, width), F32),
        ],
        compiler_params=PARAMS,
        name="mlp",
    )(x, attn_out, grad_rows, norms, pu_full, down_full)


def direct_body(groups, seqs, inputs, out_grad, lengths, *state):
    rows, width = inputs.shape[1], inputs.shape[2]
    own_rows, down_rows = state[0].shape[0], state[3].shape[0]
    hidden = state[2].shape[1]
    chips = seqs // 2
    grid3 = (groups, chips, 2)
    local = rows // SPAN
    spans = local * seqs
    pairs = width // LANES
    count = rows // TILE
    x, grad_rows = inputs[0], out_grad[0]
    vmem, hbm, smem = pltpu.VMEM, pl.ANY, pltpu.SMEM
    shapes = (
        (*grid3, own_rows, 3 * width), (*grid3, own_rows, width + hidden), (*grid3, down_rows, width),
    )
    tokens = (rows, width)
    (
        qkv_full, pu_full, down_full, norms, mixed, summ, attn_out, probs, activ, resid, slope, down_grad,
    ) = remote_call(
        front_kernel, groups, seqs, "front", 0,
        [
            *((hbm, shape, BF) for shape in shapes), (vmem, (4, width), F32), (hbm, (rows, 3 * width), BF),
            (vmem, (chips, 2, local, 2 * width), BF), (hbm, tokens, BF), (hbm, (rows, 4 * SPAN * pairs), BF),
            (hbm, (rows, hidden), BF), (hbm, tokens, F32), (hbm, (rows, hidden), BF), (hbm, (hidden, width), BF),
        ],
        [smem, hbm, hbm] + [vmem] * 5,
        [
            vmem(tokens, BF), vmem(tokens, BF), *(vmem(shape, BF) for shape in shapes),
            vmem((rows, 3 * width), BF), vmem(tokens, BF), vmem(tokens, F32),
            vmem((rows, hidden), BF), vmem((rows, hidden), BF), vmem((hidden, width), BF),
            vmem((*grid3, 4, LANES), F32), vmem((local, 2 * width), F32), vmem((width, spans), BF),
        ],
        4 + 7 * count + hidden // TILE, 6 * GATHER_COPIES + fast_gather_copies(chips) + 2 * chips,
    )(lengths, x, grad_rows, *state[:5])
    pu_flat, down_flat = pu_full.reshape(width, width + hidden), down_full.reshape(hidden, width)
    resid_grad, attn_grad, pu_grad, down_own, norm_two = remote_call(
        middle_kernel, groups, seqs, "middle", 1,
        [
            (hbm, tokens, F32), (hbm, tokens, BF), (hbm, pu_flat.shape, BF),
            (vmem, (down_rows, width), F32), (vmem, (2, width), F32),
        ],
        [hbm] * 6 + [vmem, hbm],
        [
            vmem(tokens, BF), vmem(tokens, F32), vmem((rows, hidden), BF), vmem(tokens, BF),
            vmem(pu_flat.shape, BF), vmem(down_flat.shape, BF), vmem(tokens, F32), vmem(tokens, BF),
            vmem(pu_flat.shape, BF), vmem((rows, hidden), BF), vmem(tokens, BF), vmem(tokens, BF),
            *scatter_scratch(groups, chips, down_rows // 2, width) * 2,
        ],
        6 + 5 * count, 2 * SCATTER_COPIES,
    )(grad_rows, resid, slope, attn_out, pu_flat, down_flat, norms, down_grad.reshape(shapes[2]))
    half = (width + hidden) // 2
    blocks = ((own_rows, half),) * 2 + ((own_rows, width),) * 3
    summ_block = (local, 2 * width)
    scratch = [
        vmem(tokens, BF), vmem((rows, 3 * width), BF), vmem(tokens, BF), vmem(probs.shape, BF), vmem(tokens, F32),
        vmem((width, 3 * width), BF), vmem(tokens, BF), vmem(tokens, F32), vmem(down_flat.shape, BF), vmem(tokens, BF),
        vmem((rows, 3 * width), BF), vmem(tokens, BF), vmem((width, spans), BF), vmem((spans, 2 * width), F32),
        vmem((chips, *summ_block), F32), vmem((chips - 1, *summ_block), BF),
        vmem((chips - 1, *summ_block), BF), vmem(summ_block, F32),
        *[vmem((*grid3, own_rows, width), BF)] * 3, *[vmem((width, LANES), F32)] * 2,
    ]
    scratch += [buffer for block in blocks for buffer in scatter_scratch(groups, chips, *block)]
    scratch += [
        vmem((4, width), F32), vmem((seqs, 4, width), F32), vmem((groups, 4, width), F32),
        vmem((8, LANES), F32), vmem((seqs, 8, LANES), F32), vmem((groups, 8, LANES), F32),
    ]
    input_grad, outputs, qkv_own, pu_own, norm_total, total = remote_call(
        back_kernel, groups, seqs, "back", 2,
        [
            (hbm, tokens, BF), (hbm, tokens, BF), (vmem, (own_rows, 3 * width), F32),
            (vmem, (own_rows, width + hidden), F32), (vmem, (4, width), F32), (vmem, (8, LANES), F32),
        ],
        [smem, hbm, hbm, hbm, hbm, vmem, hbm, hbm, vmem, vmem, hbm, vmem, hbm, hbm, hbm],
        scratch, 3 * local // 2 + 6 + 5 + 2 * count,
        5 * SCATTER_COPIES + 2 * share_copies(groups, seqs) + 2 * chips,
    )(
        lengths, x, mixed, attn_grad, probs, summ.reshape(spans, 2 * width), pu_grad.reshape(shapes[1]),
        resid_grad, down_own, norms, qkv_full.reshape(width, 3 * width), norm_two, activ, resid, down_flat,
    )
    return outputs, input_grad, (qkv_own, pu_own, down_own), norm_total, total


def plain_body(groups, seqs, inputs, out_grad, lengths, *state):
    sds = jax.ShapeDtypeStruct
    rows, width = inputs.shape[1], inputs.shape[2]
    qkv_full, pu_full, down_full, norms = gather_plain(state[:5])
    local = rows // SPAN
    spans = local * seqs
    info = jnp.stack([lengths[0], (lax.axis_index("seq") * local).astype(jnp.int32)])
    x, grad_rows = inputs[0], out_grad[0]
    tile = 256
    steps = rows // tile
    mixed, own_summ = pl.pallas_call(
        qkv_kernel,
        grid=(steps,),
        in_specs=[SCALARS, by_rows(tile, width), whole(norms.shape), whole(qkv_full.shape)],
        out_specs=[by_rows(tile, 3 * width), whole((local, 2 * width))],
        out_shape=[sds((rows, 3 * width), BF), sds((local, 2 * width), BF)],
        scratch_shapes=[pltpu.VMEM((local, 2 * width), F32)],
        compiler_params=PARAMS,
        name="qkv",
    )(info, x, norms, qkv_full)
    summ = lax.all_gather(own_summ, "seq", axis=0, tiled=True)
    pairs = width // LANES
    lse_spec = pl.BlockSpec((1, pairs, 2 * SPAN), lambda i: (i, 0, 0))
    attn_out, lse = pl.pallas_call(
        attend_kernel,
        grid=(local,),
        in_specs=[SCALARS, by_rows(SPAN, 3 * width), whole(summ.shape)],
        out_specs=[by_rows(SPAN, width), lse_spec],
        out_shape=[sds((rows, width), BF), sds((local, pairs, 2 * SPAN), F32)],
        scratch_shapes=[pltpu.VMEM((width, spans), BF)],
        compiler_params=PARAMS,
        name="attend",
    )(info, mixed, summ)
    outputs, resid_grad, attn_grad, pu_grad, down_grad, norm_two = mlp_call(
        x, attn_out, grad_rows, norms, pu_full, down_full
    )
    back, dsumm = pl.pallas_call(
        attend_back_kernel,
        grid=(local,),
        in_specs=[SCALARS, by_rows(SPAN, 3 * width), by_rows(SPAN, width), lse_spec, whole(summ.shape)],
        out_specs=[by_rows(SPAN, 3 * width), whole((spans, 2 * width))],
        out_shape=[sds((rows, 3 * width), BF), sds((spans, 2 * width), F32)],
        scratch_shapes=[pltpu.VMEM((width, spans), BF)],
        compiler_params=PARAMS,
        name="attend_back",
    )(info, mixed, attn_grad, lse, summ)
    extra = lax.psum_scatter(dsumm, "seq", scatter_dimension=0, tiled=True)
    input_grad, qkv_grad, norm_one = pl.pallas_call(
        final_kernel,
        grid=(steps,),
        in_specs=[
            SCALARS, by_rows(tile, width), by_rows(tile, 3 * width), whole(extra.shape), by_rows(tile, width),
            whole(norms.shape), whole(qkv_full.shape),
        ],
        out_specs=[by_rows(tile, width), whole(qkv_full.shape), whole((2, width))],
        out_shape=[sds((rows, width), F32), sds(qkv_full.shape, BF), sds((2, width), F32)],
        scratch_shapes=[pltpu.VMEM((rows, 3 * width), BF), pltpu.VMEM((rows, width), BF)],
        compiler_params=PARAMS,
        name="final",
    )(info, x, back, extra, resid_grad, norms, qkv_full)
    norm_grad = jnp.concatenate([norm_one, norm_two], axis=0)
    *grads, norm_total, total = reduce_plain(qkv_grad, pu_grad, down_grad, norm_grad)
    return outputs, input_grad, grads, norm_total, total


def body(groups, seqs, *args):
    state = args[3:]
    rows, width = args[0].shape[1:]
    direct = groups == 4 and seqs % 4 == 0 and state[0].shape[0] % 16 == 0 and rows % TILE == 0
    direct = direct and rows // SPAN * seqs == SPAN and state[2].shape[1] == 4 * SPAN * (width // LANES)
    run = direct_body if direct else plain_body
    outputs, input_grad, grads, norm_total, total = run(groups, seqs, *args)
    input_grad = input_grad.astype(BF)
    sds = jax.ShapeDtypeStruct
    vmem, hbm = pltpu.VMEM, pl.ANY
    spec = lambda space: pl.BlockSpec(memory_space=space)
    held = [sds(w.shape, F32) for w in state[:5]]
    parts = 8
    operands = (outputs, input_grad, *grads, *state)
    outputs, input_grad, grad_norm, *fresh, shift_clipped = pl.pallas_call(
        functools.partial(update_kernel, parts),
        in_specs=[spec(vmem)] * 2 + [spec(hbm)] * 20,
        out_specs=[spec(hbm)] * 2 + [spec(vmem)] + [spec(hbm)] * 15 + [spec(vmem)],
        out_shape=[
            sds(outputs.shape, BF), sds(outputs.shape, F32), sds((1, 1), F32), *held * 3,
            sds((1, state[4].shape[1]), F32),
        ],
        scratch_shapes=[vmem(a.shape, a.dtype) for a in operands]
        + [vmem(w.shape, F32) for w in held * 3] + [vmem(outputs.shape, F32), pltpu.SemaphoreType.DMA((4 * parts + 33,))],
        compiler_params=PARAMS,
        name="update",
    )(total, norm_total, *operands)
    return (outputs[None], input_grad[None], grad_norm[0, 0], *fresh, shift_clipped[0])


def solution(mesh):
    tokens = P("batch", "seq", None)
    owned = P(("batch", "seq"), None)
    columns = P(None, ("batch", "seq"))
    state = (owned, owned, owned, owned, columns)
    return jax.shard_map(
        functools.partial(body, mesh.shape["batch"], mesh.shape["seq"]),
        mesh=mesh,
        in_specs=(tokens, tokens, P("batch")) + state * 3,
        out_specs=(tokens, tokens, P()) + state * 3 + (P(("batch", "seq")),),
        check_vma=False,
    )
```

```python
import functools
import jax
import jax.numpy as jnp
from jax import lax
from jax.experimental import pallas as pl
from jax.experimental.pallas import tpu as pltpu
from jax.sharding import PartitionSpec as P

HEADS = 8
HD = 64
SPAN = 128
STEP = 10
LN_EPS = 1e-05
NEG_FILL = -1e30
CLIP = 1.0
BETA = 0.5
ADAM_EPS = 1e-08
DECAY = 0.1
RATES = (0.02, 0.3, 0.02, 0.02, 0.5)
BF = jnp.bfloat16
F32 = jnp.float32
LANES = 128
VMEM_LIMIT = 56 * 1024 * 1024


def dot(a, b, dims=((1,), (0,))):
    return lax.dot_general(a, b, (dims, ((), ())), preferred_element_type=F32)


def dot_tn(a, b):
    return dot(a, b, ((0,), (0,)))


def dot_nt(a, b):
    return dot(a, b, ((1,), (1,)))


def normalize(x):
    inv = 1.0 / x.shape[-1]
    centred = x - jnp.sum(x, axis=-1, keepdims=True) * inv
    spread = jnp.sum(centred * centred, axis=-1, keepdims=True) * inv
    rstd = lax.rsqrt(spread + LN_EPS)
    return centred * rstd, rstd


def norm_back(grad, gain, xhat, rstd):
    inv = 1.0 / grad.shape[-1]
    e = grad * gain
    mean_e = jnp.sum(e, axis=-1, keepdims=True) * inv
    mean_ex = jnp.sum(e * xhat, axis=-1, keepdims=True) * inv
    return rstd * (e - mean_e - xhat * mean_ex)


def qkv_tile(x, norms_ref, weight_ref):
    xhat, _ = normalize(x.astype(F32))
    normed = (xhat * norms_ref[0:1, :] + norms_ref[1:2, :]).astype(BF)
    return dot(normed, weight_ref[...]).astype(BF)


def span_scale(length, begin, shape):
    count = jnp.clip(length - begin, 1, SPAN)
    return lax.rsqrt(jnp.full(shape, count, jnp.int32).astype(F32))


def span_sum(kv, length, begin):
    row = lax.broadcasted_iota(jnp.int32, kv.shape, 0)
    kept = jnp.where(row < length - begin, kv.astype(F32), 0.0)
    total = jnp.sum(kept, axis=0, keepdims=True)
    return total * span_scale(length, begin, total.shape)


def stack_heads(pair):
    lane = lax.broadcasted_iota(jnp.int32, pair.shape, 1)
    zero = jnp.zeros_like(pair)
    return jnp.concatenate(
        [jnp.where(lane < HD, pair, zero), jnp.where(lane >= HD, pair, zero)], axis=0
    )


def fold_heads(both):
    picked = jnp.concatenate([both[:HD, :SPAN], both[HD:, SPAN:]], axis=0)
    return picked.T


def span_caps(length, span):
    query_pos = lax.broadcasted_iota(jnp.int32, (1, 2 * SPAN), 1) & (SPAN - 1)
    near_cap = jnp.minimum(query_pos, length - span * SPAN - 1)
    far_cap = jnp.minimum(span, (length + SPAN - 1) // SPAN)
    return near_cap, far_cap


def mask_scores(raw, caps):
    near_cap, far_cap = caps
    key_pos = lax.broadcasted_iota(jnp.int32, (SPAN, 2 * SPAN), 0)
    summ_pos = lax.broadcasted_iota(jnp.int32, (raw.shape[0] - SPAN, 2 * SPAN), 0)
    near = jnp.where(key_pos <= near_cap, raw[:SPAN], NEG_FILL)
    far = jnp.where(summ_pos < far_cap, raw[SPAN:], NEG_FILL)
    return jnp.concatenate([near, far], axis=0)


def attend_spans(spans, mixed_ref, width, summ_ref, summ_vt_ref, out_ref, lse_ref=None, probs_ref=None):
    units = [(pl.ds(row, SPAN), index, caps, pair) for row, index, caps in spans for pair in range(width // LANES)]
    queries, keys, values_t = [], [], []
    for rows, index, caps, pair in units:
        at = pair * LANES
        queries.append(stack_heads(mixed_ref[rows, at : at + LANES] * BF(0.125)))
        near_k = mixed_ref[rows, width + at : width + at + LANES]
        near_v = mixed_ref[rows, 2 * width + at : 2 * width + at + LANES]
        keys.append(jnp.concatenate([near_k, summ_ref[:, at : at + LANES]], axis=0))
        values_t.append(jnp.concatenate([near_v.T, summ_vt_ref[at : at + LANES, :]], axis=1))
    scores = [dot_nt(k, q) for k, q in zip(keys, queries)]
    scores = [mask_scores(s, unit[2]) for s, unit in zip(scores, units)]
    peaks = [jnp.max(s, axis=0, keepdims=True) for s in scores]
    expos = [jnp.exp(s - p) for s, p in zip(scores, peaks)]
    totals = [jnp.sum(e, axis=0, keepdims=True) for e in expos]
    probs = [(e * (1.0 / t)).astype(BF) for e, t in zip(expos, totals)]
    outs = [dot(v, p) for v, p in zip(values_t, probs)]
    for (rows, index, caps, pair), out, prob, peak, total in zip(units, outs, probs, peaks, totals):
        at = pair * LANES
        out_ref[rows, at : at + LANES] = fold_heads(out).astype(BF)
        if lse_ref is not None:
            lse_ref[index, pair : pair + 1, :] = peak + jnp.log(total)
        if probs_ref is not None:
            at = pair * 4 * SPAN
            probs_ref[rows, at : at + 2 * SPAN] = prob[:SPAN]
            probs_ref[rows, at + 2 * SPAN : at + 4 * SPAN] = prob[SPAN:]


def attend_back_spans(
    spans, mixed_ref, grad_ref, width, summ_ref, summ_kt_ref, lse_ref, back_ref, dsumm_ref, probs_ref=None
):
    pairs = width // LANES
    units = [(pl.ds(row, SPAN), index, caps, pair) for row, index, caps in spans for pair in range(pairs)]
    queries, grads, keys, keys_t, values = [], [], [], [], []
    for rows, index, caps, pair in units:
        at = pair * LANES
        queries.append(stack_heads(mixed_ref[rows, at : at + LANES] * BF(0.125)))
        grads.append(stack_heads(grad_ref[rows, at : at + LANES]))
        near_k = mixed_ref[rows, width + at : width + at + LANES]
        near_v = mixed_ref[rows, 2 * width + at : 2 * width + at + LANES]
        keys.append(jnp.concatenate([near_k, summ_ref[:, at : at + LANES]], axis=0))
        keys_t.append(jnp.concatenate([near_k.T, summ_kt_ref[at : at + LANES, :]], axis=1))
        values.append(jnp.concatenate([near_v, summ_ref[:, width + at : width + at + LANES]], axis=0))
    if probs_ref is None:
        scores = [dot_nt(k, q) for k, q in zip(keys, queries)]
        dprobs = [dot_nt(v, g) for v, g in zip(values, grads)]
        scores = [mask_scores(s, unit[2]) for s, unit in zip(scores, units)]
        probs = [jnp.exp(s - lse_ref[index, pair : pair + 1, :]) for s, (_, index, _, pair) in zip(scores, units)]
    else:
        dprobs = [dot_nt(v, g) for v, g in zip(values, grads)]
        probs = []
        for rows, _, _, pair in units:
            at = pair * 4 * SPAN
            near, far = probs_ref[rows, at : at + 2 * SPAN], probs_ref[rows, at + 2 * SPAN : at + 4 * SPAN]
            probs.append(jnp.concatenate([near, far], axis=0).astype(F32))
    deltas = [jnp.sum(p * d, axis=0, keepdims=True) for p, d in zip(probs, dprobs)]
    dscores = [(p * (d - delta)).astype(BF) for p, d, delta in zip(probs, dprobs, deltas)]
    probs = [p.astype(BF) for p in probs]
    dqs = [dot(k, ds) for k, ds in zip(keys_t, dscores)]
    dks = [dot(ds, q) for ds, q in zip(dscores, queries)]
    dvs = [dot(p, g) for p, g in zip(probs, grads)]
    for (rows, index, caps, pair), dq, dk, dv in zip(units, dqs, dks, dvs):
        at = pair * LANES
        back_ref[rows, at : at + LANES] = (fold_heads(dq) * 0.125).astype(BF)
        back_ref[rows, width + at : width + at + LANES] = dk[:SPAN].astype(BF)
        back_ref[rows, 2 * width + at : 2 * width + at + LANES] = dv[:SPAN].astype(BF)
    for pair in range(pairs):
        at = pair * LANES
        dsumm_ref[:, at : at + LANES] += sum(dk[SPAN:] for dk in dks[pair::pairs])
        dsumm_ref[:, width + at : width + at + LANES] += sum(dv[SPAN:] for dv in dvs[pair::pairs])


def with_extra(back, extra, length, begin):
    extra = extra * span_scale(length, begin, extra.shape)
    pos = lax.broadcasted_iota(jnp.int32, back.shape, 0)
    return (back.astype(F32) + jnp.where(pos < length - begin, extra, 0.0)).astype(BF)


GELU_A = 0.7978845608
GELU_B = 0.044715


def gelu_parts(t):
    slow = GELU_A + (GELU_A * GELU_B) * (t * t)
    half = 0.5 * jnp.tanh(t * slow) + 0.5
    value = t * half
    return value, half + (value - value * half) * (6.0 * slow - 4.0 * GELU_A)


MESH = pl.DeviceIdType.MESH


class Place:
    def __init__(self, groups, seqs):
        self.groups, self.seqs, self.chips = groups, seqs, seqs // 2
        self.b = lax.axis_index("batch")
        self.seq = lax.axis_index("seq")
        self.z, self.c = self.seq // 2, self.seq % 2
        self.other = 1 - self.c
        self.b1 = self.b + 1 - 2 * (self.b % 2)
        self.b2 = (self.b + 2) % 4
        self.b3 = self.b1 + 2 - 4 * (self.b1 // 2)
        self.after = [(self.z + k) % self.chips for k in range(self.chips)]
        self.before = [(self.z + self.chips - k) % self.chips for k in range(self.chips)]
        self.sibling = (self.b, 2 * self.z + self.other)
        self.x, self.y, self.diagonal = (self.b1, self.seq), (self.b2, self.seq), (self.b3, self.seq)
        self.along = [(self.b, 2 * z + self.c) for z in self.after]
        self.ring = [(self.b, (self.seq + k) % seqs) for k in range(seqs)]


def meet(place):
    barrier = pltpu.get_barrier_semaphore()
    partners = [place.x, place.y, place.diagonal, *place.ring[1:]]
    for partner in partners:
        pl.semaphore_signal(barrier, inc=1, device_id=partner, device_id_type=MESH)
    pl.semaphore_wait(barrier, len(partners))


def part_of(ref, index):
    return ref if index is None else ref.at[index]


class Copy:
    def __init__(self, make):
        self.make = make
        make().start()

    def wait(self):
        self.make().wait()

    def wait_recv(self):
        self.make().wait_recv()

    def wait_send(self):
        self.make().wait_send()


class Copies:
    def __init__(self, send_sems, recv_sems):
        self.send, self.recv, self.made, self.left = send_sems, recv_sems, [], 0

    def start(self, src, src_index, dst, dst_index, device):
        at = len(self.made)
        assert at < self.send.shape[0]
        copy = Copy(
            lambda: pltpu.make_async_remote_copy(
                src_ref=part_of(src, src_index), dst_ref=part_of(dst, dst_index),
                send_sem=self.send.at[at], recv_sem=self.recv.at[at],
                device_id=device, device_id_type=MESH,
            )
        )
        self.made.append(copy)
        return copy

    def push(self, ref, index, device):
        return self.start(ref, index, ref, index, device)

    def finish(self):
        for copy in self.made[self.left :]:
            copy.wait_send()
        self.left = len(self.made)


class Loads:
    def __init__(self, sems):
        self.sems, self.made = sems, 0

    def start(self, src, dst, src_index=None, dst_index=None):
        at = self.made
        assert at < self.sems.shape[0]
        self.made += 1
        return Copy(
            lambda: pltpu.make_async_copy(part_of(src, src_index), part_of(dst, dst_index), self.sems.at[at])
        )


def gather_steps(place, copies, full, rows=slice(None), cols=slice(None)):
    p, half = place, place.chips // 2
    low, high = slice(0, half), slice(half, place.chips)

    def push(b, z, device):
        return copies.push(full, (b, z, p.c, rows, cols), device)

    along = [push(p.b, p.z, device) for device in p.along[1:]]
    yield
    for copy in along:
        copy.wait_recv()
    every = slice(None)
    to_x, to_y, sib = push(p.b, every, p.x), push(p.b, every, p.y), [push(p.b, every, p.sibling)]
    yield
    to_x.wait_recv()
    on_y = push(p.b1, low, p.y)
    to_y.wait_recv()
    on_x = push(p.b2, high, p.x)
    sib += [push(p.b1, every, p.sibling), push(p.b2, every, p.sibling)]
    yield
    on_y.wait_recv()
    sib.append(push(p.b3, low, p.sibling))
    on_x.wait_recv()
    sib.append(push(p.b3, high, p.sibling))
    yield
    for copy in sib:
        copy.wait_recv()


GATHER_COPIES = 12


def fast_gather_steps(place, copies, full, rows=slice(None), cols=slice(None)):
    p = place
    order = range(p.chips)
    early, late = order[: p.chips // 2], order[p.chips // 2 :]

    def push(b, k, device):
        return copies.push(full, (b, p.before[k], p.c, rows, cols), device)

    def pass_over(b):
        sib.append(copies.push(full, (b, slice(None), p.c, rows, cols), p.sibling))

    along = [push(p.b, 0, device) for device in p.along[1:]]
    to_x, to_y, sib = [push(p.b, 0, p.x)], [push(p.b, 0, p.y)], []
    yield
    for k, copy in enumerate(along, 1):
        copy.wait_recv()
        to_x.append(push(p.b, k, p.x))
        to_y.append(push(p.b, k, p.y))
    pass_over(p.b)
    yield
    on = []
    for k in early:
        to_x[k].wait_recv()
        on.append(push(p.b1, k, p.y))
    for k in late:
        to_y[k].wait_recv()
        on.append(push(p.b2, k, p.x))
    yield
    for k in late:
        to_x[k].wait_recv()
    pass_over(p.b1)
    for k in early:
        to_y[k].wait_recv()
    pass_over(p.b2)
    for copy in on:
        copy.wait_recv()
    pass_over(p.b3)
    yield
    for copy in sib:
        copy.wait_recv()


def fast_gather_copies(chips):
    return chips - 1 + 3 * chips + 4


def scatter_steps(place, copies, loads, grad, acc, got, near, far, last, result):
    p, half = place, place.chips // 2
    low, high = slice(0, half), slice(half, place.chips)
    chips = p.chips

    def add(into, *others):
        total = acc[into].astype(F32)
        for other in others:
            total = total + other.astype(F32)
        acc[into] = total.astype(BF)

    every = slice(None)
    swap = copies.start(grad, (every, every, p.other), got, None, p.sibling)
    keep = loads.start(grad, acc, (every, every, p.c))
    yield
    keep.wait()
    swap.wait_recv()
    for b in (p.b3, p.b1, p.b2):
        for z in range(chips):
            add((b, z), got[b, z])
    on_y = copies.start(acc, (p.b3, low), far, 0, p.y)
    on_x = copies.start(acc, (p.b3, high), far, 1, p.x)
    early_x = copies.start(acc, (p.b1, high), near, (0, high), p.x)
    early_y = copies.start(acc, (p.b2, low), near, (1, low), p.y)
    for z in range(chips):
        add((p.b, z), got[p.b, z])
    yield
    on_y.wait_recv()
    for z in range(half):
        add((p.b1, z), far[0, z])
    late_x = copies.start(acc, (p.b1, low), near, (0, low), p.x)
    on_x.wait_recv()
    for z in range(half, chips):
        add((p.b2, z), far[1, z - half])
    late_y = copies.start(acc, (p.b2, high), near, (1, high), p.y)
    yield
    for copy in (early_x, early_y, late_x, late_y):
        copy.wait_recv()
    for z in range(chips):
        add((p.b, z), near[0, z], near[1, z])
    along = []
    for k in range(1, chips):
        along.append(copies.start(acc, (p.b, p.after[k]), last, k - 1, p.along[k]))
    yield
    total = acc[p.b, p.z].astype(F32)
    for k, copy in enumerate(along):
        copy.wait_recv()
        total = total + last[k].astype(F32)
    result[...] = total


SCATTER_COPIES = 10


def scatter_scratch(groups, chips, rows, cols):
    half = chips // 2
    return [
        pltpu.VMEM((groups, chips, rows, cols), BF),
        pltpu.VMEM((groups, chips, rows, cols), BF),
        pltpu.VMEM((2, chips, rows, cols), BF),
        pltpu.VMEM((2, half, rows, cols), BF),
        pltpu.VMEM((chips - 1, rows, cols), BF),
    ]


def share_sum_steps(place, copies, mine, along, across, result):
    p, seqs = place, along.shape[0]
    along[p.seq] = mine[...]
    sent = [copies.push(along, p.seq, device) for device in p.ring[1:]]
    yield
    for copy in sent:
        copy.wait_recv()
    across[p.b] = sum(along[s] for s in range(seqs))
    sent = [copies.push(across, p.b, device) for device in (p.x, p.y, p.diagonal)]
    yield
    for copy in sent:
        copy.wait_recv()
    result[...] = sum(across[b] for b in range(p.groups))


def share_copies(groups, seqs):
    return groups + seqs - 2


def square_sums(value):
    total = 0.0
    for at in range(0, value.shape[1], LANES):
        block = jnp.square(value[:, at : at + LANES])
        if block.shape[0] < 8:
            total = total + jnp.concatenate([block, jnp.zeros((8 - block.shape[0], LANES), F32)], axis=0)
        for row in range(0, block.shape[0] // 8 * 8, 8):
            total = total + block[row : row + 8]
    return total


class Schedule:
    def __init__(self, **steps):
        self.steps = steps

    def __call__(self, *names):
        for name in names:
            next(self.steps[name], None)

    def plan(self, *calls):
        return {at: functools.partial(self, *names.split()) for at, names in enumerate(calls) if names}

    def finish(self, *names):
        run_all(*(self.steps[name] for name in names or self.steps))


def run_all(*steps):
    live = list(steps)
    while live:
        for step in list(live):
            try:
                next(step)
            except StopIteration:
                live.remove(step)


def loop(count, body, ticks=None):
    def step(index, carry):
        body(index)
        for k in sorted(ticks or {}):
            pl.when(index == k)(lambda run=ticks[k]: run())
        return carry

    lax.fori_loop(0, count, step, 0)


def adam(grad, master, first, second, rate, moment_out, square_out, fresh_out):
    fix = 1.0 - BETA**STEP
    moment = BETA * first + (1.0 - BETA) * grad
    square = BETA * second + (1.0 - BETA) * grad * grad
    update = moment / fix / (jnp.sqrt(square / fix) + ADAM_EPS)
    moment_out[...] = moment
    square_out[...] = square
    fresh_out[...] = master - rate * (update + DECAY * master)


def update_kernel(parts, total_ref, norm_grad, *refs):
    sources, results, held, sems = refs[:20], refs[20:39], refs[39:-1], refs[-1]
    outputs_ref, input_ref, grad_refs, state, made, wide_ref = held[0], held[1], held[2:5], held[5:20], held[20:35], held[35]
    outputs_hbm, input_hbm, grads_hbm, state_hbm = sources[0], sources[1], sources[2:5], sources[5:]
    loads = Loads(sems)
    ways = ((input_hbm, input_ref, wide_ref, results[1]), (outputs_hbm, outputs_ref, outputs_ref, results[0]))
    small = [loads.start(src, via) for src, via in zip((*grads_hbm, *state_hbm), (*grad_refs, *state))]
    reads = [Sliced(loads, src, via, parts).start_all() for src, via, _, _ in ways]
    stores = [Sliced(loads, via, dst, parts) for _, _, via, dst in ways]
    for load in small:
        load.wait()
    grad_norm = jnp.sqrt(jnp.sum(total_ref[...], keepdims=True))
    results[2][...] = grad_norm
    factor = jnp.minimum(1.0, CLIP / (grad_norm + 1e-06))
    width = state[1].shape[1]
    piece = state[4].shape[1]
    per = LANES // piece
    index = lax.axis_index("batch") * lax.axis_size("seq") + lax.axis_index("seq")
    block = norm_grad[:, pl.ds(pl.multiple_of(index // per * LANES, LANES), LANES)]
    own = pltpu.roll(block, (LANES - index % per * piece) % LANES, 1)[:, :piece]
    qkv_grad, pu_grad, down_grad = grad_refs
    grads = (qkv_grad[...], pu_grad[:, :width], pu_grad[:, width:], down_grad[...], own)
    results[18][...] = own[3:4] * factor
    last = []
    for at, (grad, rate) in enumerate(zip(grads, RATES)):
        adam(
            grad * factor, state[at][...], state[5 + at][...], state[10 + at][...], rate,
            made[at], made[5 + at], made[10 + at],
        )
        last += [loads.start(made[k], results[3 + k]) for k in (at, 5 + at, 10 + at)]
    for read, store in zip(reads, stores):
        for part in range(parts):
            read.wait(part)
            if read.dst is input_ref:
                here = pl.ds(part * read.size, read.size)
                wide_ref[here, :] = input_ref[here, :].astype(F32)
            store.start(part)
    for store in stores:
        store.wait_all()
    for store in last:
        store.wait()


def cast_shards(p, seqs, qkv_ref, proj_ref, up_ref, down_ref, norm_ref, qkv_full, pu_full, down_full, norm_full):
    width = proj_ref.shape[1]
    b, z, c = p.b, p.z, p.c
    index = b * seqs + 2 * z + c
    qkv_full[b, z, c] = qkv_ref[...].astype(BF)
    pu_full[b, z, c, :, :width] = proj_ref[...].astype(BF)
    pu_full[b, z, c, :, width:] = up_ref[...].astype(BF)
    down_full[b, z, c] = down_ref[...].astype(BF)
    piece = norm_ref.shape[1]
    per = LANES // piece
    tiled = jnp.concatenate([norm_ref[...].astype(BF).astype(F32)] * per, axis=1)
    lane = lax.broadcasted_iota(jnp.int32, tiled.shape, 1)
    norm_full[b, z, c] = jnp.where(lane // piece == index % per, tiled, 0.0)


def join_norms(norm_full, seqs, per, norms_out):
    for block in range(norms_out.shape[1] // LANES):
        total = None
        for device in range(block * per, (block + 1) * per):
            one = norm_full[device // seqs, device % seqs // 2, device % 2]
            total = one if total is None else total + one
        norms_out[:, block * LANES : (block + 1) * LANES] = total


class Sliced:
    def __init__(self, loads, src, dst, count):
        self.src, self.dst, self.count, self.size = src, dst, count, src.shape[0] // count
        self.sems, self.first = loads.sems, loads.made
        loads.made += count
        assert loads.made <= loads.sems.shape[0]

    def copy(self, index):
        begin = index * self.size
        here = pl.ds(begin if isinstance(index, int) else pl.multiple_of(begin, self.size), self.size)
        return pltpu.make_async_copy(self.src.at[here], self.dst.at[here], self.sems.at[self.first + index])

    def start(self, index):
        self.copy(index).start()

    def wait(self, index):
        self.copy(index).wait()

    def start_next(self, index):
        pl.when(index < self.count)(lambda: self.start(index))

    def start_all(self):
        for index in range(self.count):
            self.start(index)
        return self

    def wait_all(self):
        for index in range(self.count):
            self.wait(index)


class SummaryView:
    def __init__(self, ref, rows):
        self.ref, self.rows = ref, rows

    def __getitem__(self, key):
        cols = key[1]
        return self.ref[:, :, :, cols].reshape(self.rows, cols.stop - cols.start)


def row_block(index, size):
    return pl.ds(pl.multiple_of(index * size, size), size)


TILE = 512


def front_kernel(
    groups, seqs, length_ref, x_hbm, og_hbm, qkv_ref, proj_ref, up_ref, down_ref, norm_ref,
    qkv_hbm, pu_hbm, down_hbm, norms_out, mixed_hbm, summ_ref, attn_hbm, probs_hbm,
    activ_hbm, resid_hbm, slope_hbm, down_grad_hbm,
    x_ref, og_ref, qkv_full, pu_full, down_full, mixed_ref, attn_ref, resid_ref, activ_ref, slope_ref,
    down_grad_ref, norm_full, sum_scr, vt_scr, load_sems, send_sems, recv_sems,
):
    p = Place(groups, seqs)
    rows, width = x_ref.shape
    hidden = activ_ref.shape[1]
    local = rows // SPAN
    length, first_span = length_ref[0], p.seq * local
    count, per = rows // TILE, TILE // SPAN
    loads = Loads(load_sems)
    x_load = Sliced(loads, x_hbm, x_ref, count).start_all()
    cast_shards(
        p, seqs, qkv_ref, proj_ref, up_ref, down_ref, norm_ref, qkv_full, pu_full, down_full, norm_full
    )
    meet(p)
    og_load = loads.start(og_hbm, og_ref)
    copies = Copies(send_sems, recv_sems)
    move = Schedule(
        qkv=fast_gather_steps(p, copies, qkv_full),
        norm=gather_steps(p, copies, norm_full),
        pu=gather_steps(p, copies, pu_full),
        down=gather_steps(p, copies, down_full),
    )
    xhat_ref = resid_ref

    def center(index):
        here = row_block(index, TILE)
        x_load.wait(index)
        xhat_ref[here, :] = normalize(x_ref[here, :].astype(F32))[0]

    move("norm", "qkv")
    loop(count, center, move.plan("norm qkv pu", "", "norm qkv", "norm qkv"))
    move("norm", "qkv", "pu")
    join_norms(norm_full, seqs, LANES // norm_ref.shape[1], norms_out)
    gain, shift = norms_out[0:1, :], norms_out[1:2, :]

    def columns(full, begin, size):
        return full[:, :, :, :, begin : begin + size].reshape(width, size)

    def normed_of(here):
        return (xhat_ref[here, :] * gain + shift).astype(BF)

    def keys_values(index):
        here = row_block(index, TILE)
        mixed = dot(normed_of(here), columns(qkv_full, width, 2 * width)).astype(BF)
        mixed_ref[here, width:] = mixed
        for part in range(per):
            span = index * per + part
            sum_scr[pl.ds(span, 1), :] = span_sum(
                mixed[part * SPAN : (part + 1) * SPAN], length, (first_span + span) * SPAN
            )

    loop(count, keys_values)
    summ_ref[p.z, p.c] = sum_scr[...].astype(BF)
    along = [copies.push(summ_ref, (p.z, p.c), device) for device in p.along[1:]]
    sib = [copies.push(summ_ref, (p.z, p.c), p.sibling)]
    for k, copy in enumerate(along, 1):
        copy.wait_recv()
        sib.append(copies.push(summ_ref, (p.before[k], p.c), p.sibling))
    stores = [loads.start(qkv_full, qkv_hbm)]
    mixed_store = Sliced(loads, mixed_ref, mixed_hbm, count)

    def queries(index):
        here = row_block(index, TILE)
        mixed_ref[here, :width] = dot(normed_of(here), columns(qkv_full, 0, width)).astype(BF)
        mixed_store.start(index)

    loop(count, queries)
    for copy in sib:
        copy.wait_recv()
    move("pu")
    vt_scr[...] = summ_ref[:, :, :, width:].reshape(local * seqs, width).T
    summ_rows = SummaryView(summ_ref, local * seqs)
    attn_store = Sliced(loads, attn_ref, attn_hbm, count)
    probs_ref = activ_ref
    probs_store = Sliced(loads, probs_ref, probs_hbm, count)

    def attend(index):
        spans = []
        for k in range(per):
            span = index * per + k
            spans.append((pl.multiple_of(span * SPAN, SPAN), span, span_caps(length, first_span + span)))
        attend_spans(spans, mixed_ref, width, summ_rows, vt_scr, attn_ref, probs_ref=probs_ref)
        attn_store.start(index)
        probs_store.start(index)

    loop(count, attend, move.plan("down", "pu", "", "down pu"))
    gain_two, shift_two = norms_out[2:3, :], norms_out[3:4, :]
    resid_store, slope_store, activ_store = (
        Sliced(loads, src, dst, count)
        for src, dst in ((resid_ref, resid_hbm), (slope_ref, slope_hbm), (activ_ref, activ_hbm))
    )
    chunk = 256

    def expand(index):
        here = row_block(index, TILE)
        resid = x_ref[here, :].astype(F32) + dot(attn_ref[here, :], columns(pu_full, 0, width))
        resid_ref[here, :] = resid
        resid_store.start(index)
        normed = (normalize(resid)[0] * gain_two + shift_two).astype(BF)
        probs_store.wait(index)
        for at in range(0, hidden, chunk):
            value, slope = gelu_parts(dot(normed, columns(pu_full, width + at, chunk)))
            activ_ref[here, at : at + chunk] = value.astype(BF)
            slope_ref[here, at : at + chunk] = slope.astype(BF)
        slope_store.start(index)
        activ_store.start(index)

    loop(count, expand, move.plan("", "down", "", "down"))
    stores.append(loads.start(pu_full, pu_hbm))
    og_load.wait()
    parts = hidden // TILE
    grad_store = Sliced(loads, down_grad_ref, down_grad_hbm, parts)

    def down_grad(index):
        here = row_block(index, TILE)
        down_grad_ref[here, :] = dot_tn(activ_ref[:, here], og_ref[...]).astype(BF)
        grad_store.start(index)

    loop(parts, down_grad)
    move.finish()
    stores.append(loads.start(down_full, down_hbm))
    for store in (mixed_store, attn_store, resid_store, slope_store, activ_store, grad_store):
        store.wait_all()
    for store in stores:
        store.wait()
    copies.finish()


def middle_kernel(
    groups, seqs, og_hbm, resid_hbm, slope_hbm, attn_hbm, pu_hbm, down_hbm, norms_ref, down_grad_hbm,
    resid_grad_hbm, attn_grad_hbm, pu_grad_hbm, down_out, norm_grad_ref,
    og_ref, resid_ref, slope_ref, attn_ref, pu_ref, down_ref, resid_grad_ref, attn_grad_ref, pu_grad_ref,
    pre_grad_ref, normed_ref, pig_ref, *scratch,
):
    *buffers, load_sems, send_sems, recv_sems = scratch
    p = Place(groups, seqs)
    rows, width = og_ref.shape
    hidden = slope_ref.shape[1]
    count = rows // TILE
    loads = Loads(load_sems)
    early = [loads.start(down_hbm, down_ref)]
    tiled = [
        Sliced(loads, src, dst, count)
        for src, dst in ((og_hbm, og_ref), (slope_hbm, slope_ref), (resid_hbm, resid_ref))
    ]
    for load in tiled:
        load.start(0)
    early.append(loads.start(pu_hbm, pu_ref))
    for load in tiled:
        load.start(1)
    meet(p)
    copies = Copies(send_sems, recv_sems)
    half = down_out.shape[0] // 2
    move = Schedule(
        **{
            f"down{at}": scatter_steps(
                p, copies, loads, down_grad_hbm.at[:, :, :, half * at : half * (at + 1)], *buffers[5 * at : 5 * at + 5],
                down_out.at[half * at : half * (at + 1)],
            )
            for at in range(2)
        }
    )
    move("down0", "down1")
    attn_load = loads.start(attn_hbm, attn_ref)
    norm_grad_ref[...] = jnp.zeros_like(norm_grad_ref)
    resid_grad_store, attn_grad_store = (
        Sliced(loads, src, dst, count)
        for src, dst in ((resid_grad_ref, resid_grad_hbm), (attn_grad_ref, attn_grad_hbm))
    )
    gain, shift = norms_ref[2:3, :], norms_ref[3:4, :]
    chunk = 256
    early[0].wait()

    def tile(index):
        here = row_block(index, TILE)
        for load in tiled:
            load.start_next(index + 2)
            load.wait(index)
        grad = og_ref[here, :]
        for at in range(0, hidden, chunk):
            act_grad = dot_nt(grad, down_ref[at : at + chunk, :])
            slope = slope_ref[here, at : at + chunk].astype(F32)
            pre_grad_ref[here, at : at + chunk] = (act_grad * slope).astype(BF)

        @pl.when(index == 0)
        def _():
            early[1].wait()

        back = dot_nt(pre_grad_ref[here, :], pu_ref[:, width:])
        xhat, rstd = normalize(resid_ref[here, :])
        normed_ref[here, :] = (xhat * gain + shift).astype(BF)
        resid_grad = grad.astype(F32) + norm_back(back, gain, xhat, rstd)
        resid_grad_ref[here, :] = resid_grad
        resid_grad_store.start(index)
        pig = resid_grad.astype(BF)
        pig_ref[here, :] = pig
        attn_grad_ref[here, :] = dot_nt(pig, pu_ref[:, :width]).astype(BF)
        attn_grad_store.start(index)
        norm_grad_ref[0:1, :] += jnp.sum(back * xhat, axis=0, keepdims=True)
        norm_grad_ref[1:2, :] += jnp.sum(back, axis=0, keepdims=True)

    loop(count, tile, move.plan("down0", "down1", "down0", "down1 down0"))
    attn_load.wait()
    pu_grad_ref[:, :width] = dot_tn(attn_ref[...], pig_ref[...]).astype(BF)

    def up_grad(index):
        at = pl.multiple_of(width + index * TILE, TILE)
        pu_grad_ref[:, pl.ds(at, TILE)] = dot_tn(normed_ref[...], pre_grad_ref[:, row_block(index, TILE)]).astype(BF)

    loop(hidden // TILE, up_grad, move.plan("down1", "", "down0"))
    pu_store = loads.start(pu_grad_ref, pu_grad_hbm)
    resid_grad_store.wait_all()
    attn_grad_store.wait_all()
    move.finish()
    pu_store.wait()
    copies.finish()


def back_kernel(
    groups, seqs, length_ref, x_hbm, mixed_hbm, grad_hbm, probs_hbm, summ_ref, pu_hbm, resid_grad_hbm, down_ref,
    norms_ref, weight_hbm, norm_two_ref, activ_hbm, resid_hbm, down_hbm,
    input_grad_hbm, outputs_hbm, qkv_out, pu_out, norm_out, total_out,
    x_ref, mixed_ref, grad_ref, probs_ref, resid_grad_ref, weight_ref, input_low_ref, resid_ref, down_full_ref, outputs_ref,
    mg_scr, xhat_ref, kt_scr, dsumm_scr, dsumm_got, dsumm_low, dsumm_last, extra_scr, q_grad, k_grad, v_grad,
    gain_cols, shift_cols,
    *scratch,
):
    *buffers, norm_mine, along_norm, across_norm, sq_mine, along_sq, across_sq = scratch[:-3]
    load_sems, send_sems, recv_sems = scratch[-3:]
    p = Place(groups, seqs)
    rows, width = x_ref.shape
    local = rows // SPAN
    length, first_span = length_ref[0], p.seq * local
    loads = Loads(load_sems)
    group = 2
    count, steps = rows // TILE, local // group
    reads = [
        Sliced(loads, src, dst, steps)
        for src, dst in ((mixed_hbm, mixed_ref), (grad_hbm, grad_ref), (probs_hbm, probs_ref))
    ]
    for index in range(2):
        for read in reads:
            read.start(index)
    meet(p)
    copies = Copies(send_sems, recv_sems)

    def scatter(grad, at, out):
        return scatter_steps(p, copies, loads, grad, *buffers[5 * at : 5 * at + 5], out)

    half = pu_hbm.shape[4] // 2
    outs = [qkv_out.at[:, width * at : width * (at + 1)] for at in range(3)]
    move = Schedule(
        pu0=scatter(pu_hbm.at[:, :, :, :, :half], 0, pu_out.at[:, :half]),
        pu1=scatter(pu_hbm.at[:, :, :, :, half:], 1, pu_out.at[:, half:]),
        q=scatter(q_grad, 2, outs[0]), k=scatter(k_grad, 3, outs[1]), v=scatter(v_grad, 4, outs[2]),
        norm=share_sum_steps(p, copies, norm_mine, along_norm, across_norm, norm_out),
        squares=share_sum_steps(p, copies, sq_mine, along_sq, across_sq, total_out),
    )
    move("pu0", "pu1")
    late = [loads.start(src, dst) for src, dst in ((x_hbm, x_ref), (weight_hbm, weight_ref))]
    resid_grad_load = loads.start(resid_grad_hbm, resid_grad_ref)
    kt_scr[...] = summ_ref[:, :width].T
    dsumm_scr[...] = jnp.zeros_like(dsumm_scr)

    def attend_back(index):
        for read in reads:
            read.start_next(index + 2)
            read.wait(index)
        each = []
        for k in range(group):
            span = index * group + k
            each.append((pl.multiple_of(span * SPAN, SPAN), span, None))
        attend_back_spans(each, mixed_ref, grad_ref, width, summ_ref, kt_scr, None, mg_scr, dsumm_scr, probs_ref)

    loop(steps, attend_back, move.plan("", "pu0", "", "pu1", "pu0", "", "pu1"))
    activ_ref = probs_ref
    late += [loads.start(*ends) for ends in ((activ_hbm, activ_ref), (resid_hbm, resid_ref), (down_hbm, down_full_ref))]
    swap = []
    for z in range(p.chips):
        block = pl.ds(pl.multiple_of((2 * z + p.other) * local, local), local)
        swap.append(copies.start(dsumm_scr, block, dsumm_got, z, p.sibling))
    gain, shift = norms_ref[0:1, :], norms_ref[1:2, :]
    for read in late[:2]:
        read.wait()

    def recompute(index):
        here = row_block(index, TILE)
        xhat_ref[here, :] = normalize(x_ref[here, :].astype(F32))[0].astype(BF)

    loop(count // 2, recompute)
    for copy in swap:
        copy.wait_recv()

    def half_sum(z):
        mine = dsumm_scr[pl.ds(pl.multiple_of((2 * z + p.c) * local, local), local), :]
        return mine + dsumm_got[z]

    along = []
    for k in range(1, p.chips):
        dsumm_low[k - 1] = half_sum(p.after[k]).astype(BF)
        along.append(copies.start(dsumm_low, k - 1, dsumm_last, k - 1, p.along[k]))
    loop(count // 2, lambda index: recompute(index + count // 2))
    per_block = width // (groups * seqs)
    gain_cols[...] = jnp.broadcast_to(gain, (LANES, width)).T
    shift_cols[...] = jnp.broadcast_to(shift, (LANES, width)).T

    def weight_grad(into, at):
        begin = at * width
        back = mg_scr[:, begin : begin + width]
        moved = dot_tn(xhat_ref[...], back)
        total = jnp.sum(back.astype(F32), axis=0, keepdims=True)
        blocks, gains, shifts = [], 0.0, 0.0
        for k in range(0, width, LANES):
            part, sums = moved[:, k : k + LANES], total[:, k : k + LANES]
            blocks.append(gain_cols[...] * part + shift_cols[...] * sums)
            weight = weight_ref[:, begin + k : begin + k + LANES].astype(F32)
            gains += weight * part
            shifts += weight * sums
        into[...] = jnp.concatenate(blocks, axis=1).astype(BF).reshape(groups, p.chips, 2, per_block, width)
        gain_sums = jnp.sum(gains.T, axis=0, keepdims=True)
        shift_sums = jnp.sum(shifts.T, axis=0, keepdims=True)
        norm_mine[0:1, :] = gain_sums + (norm_mine[0:1, :] if at else 0.0)
        norm_mine[1:2, :] = shift_sums + (norm_mine[1:2, :] if at else 0.0)

    norm_mine[2:4, :] = norm_two_ref[...]
    weight_grad(q_grad, 0)
    move("q", "pu0")

    move("pu1")
    total = half_sum(p.z)
    for k, copy in enumerate(along):
        copy.wait_recv()
        total = total + dsumm_last[k].astype(F32)
    extra_scr[...] = total

    def add_extra(index):
        for k in range(2):
            span = index * 2 + k
            here = row_block(span, SPAN)
            mg_scr[here, width:] = with_extra(
                mg_scr[here, width:], extra_scr[pl.ds(span, 1), :], length, (first_span + span) * SPAN
            )

    loop(local // 2, add_extra)
    weight_grad(k_grad, 1)
    move("k", "q")
    weight_grad(v_grad, 2)
    move("v", "norm", "k", "q")
    resid_grad_load.wait()
    store = Sliced(loads, input_low_ref, input_grad_hbm, count)

    def finish(index):
        here = row_block(index, TILE)
        xhat, rstd = normalize(x_ref[here, :].astype(F32))
        back = dot_nt(mg_scr[here, :], weight_ref[...])
        input_low_ref[here, :] = (resid_grad_ref[here, :] + norm_back(back, gain, xhat, rstd)).astype(BF)
        store.start(index)

    loop(count, finish, move.plan("v k", "norm q", "v k pu0", "v pu1"))
    for read in late[2:]:
        read.wait()
    outputs_store = Sliced(loads, outputs_ref, outputs_hbm, count)

    def contract(index):
        here = row_block(index, TILE)
        out = resid_ref[here, :] + dot(activ_ref[here, :], down_full_ref[...])
        outputs_ref[here, :] = out.astype(BF)
        outputs_store.start(index)

    loop(count // 2, contract, move.plan("k norm q"))
    sq_mine[...] = square_sums(pu_out[...]) + square_sums(down_ref[...])
    copies.finish()
    move.finish("pu0", "pu1", "q", "k", "v", "norm")
    sq_mine[...] += square_sums(qkv_out[...])
    move("squares")
    loop(count // 2, lambda index: contract(index + count // 2), move.plan("squares"))
    move.finish("squares")
    total_out[...] += square_sums(norm_out[...])
    store.wait_all()
    outputs_store.wait_all()
    copies.finish()


def qkv_kernel(info_ref, x_ref, norms_ref, weight_ref, mixed_ref, summ_ref, sum_scr):
    step = pl.program_id(0)
    tile, width = x_ref.shape
    length, first_span = info_ref[0], info_ref[1]
    mixed = qkv_tile(x_ref[...], norms_ref, weight_ref)
    mixed_ref[...] = mixed
    per = tile // SPAN
    for part in range(per):
        span = step * per + part
        sum_scr[pl.ds(span, 1), :] = span_sum(
            mixed[part * SPAN : (part + 1) * SPAN, width:], length, (first_span + span) * SPAN
        )

    @pl.when(step == pl.num_programs(0) - 1)
    def _():
        summ_ref[...] = sum_scr[...].astype(BF)


def attend_kernel(info_ref, mixed_ref, summ_ref, out_ref, lse_ref, vt_scr):
    step = pl.program_id(0)
    width = out_ref.shape[1]

    @pl.when(step == 0)
    def _():
        vt_scr[...] = summ_ref[:, width:].T

    caps = span_caps(info_ref[0], info_ref[1] + step)
    attend_spans([(0, 0, caps)], mixed_ref, width, summ_ref, vt_scr, out_ref, lse_ref)


def attend_back_kernel(info_ref, mixed_ref, grad_ref, lse_ref, summ_ref, back_ref, dsumm_ref, kt_scr):
    step = pl.program_id(0)
    width = grad_ref.shape[1]

    @pl.when(step == 0)
    def _():
        kt_scr[...] = summ_ref[:, :width].T
        dsumm_ref[...] = jnp.zeros_like(dsumm_ref)

    caps = span_caps(info_ref[0], info_ref[1] + step)
    attend_back_spans(
        [(0, 0, caps)], mixed_ref, grad_ref, width, summ_ref, kt_scr, lse_ref, back_ref, dsumm_ref
    )


def mlp_kernel(
    x_ref, attn_ref, og_ref, norms_ref, pu_ref, down_ref,
    out_ref, resid_grad_ref, attn_grad_ref, pu_grad_ref, down_grad_ref, norm_grad_ref,
    activ_scr, pre_grad_scr, n2t_scr, attnt_scr, ogt_scr, pig_scr, norm_scr,
):
    step = pl.program_id(0)
    tile, width = x_ref.shape
    hidden = down_ref.shape[0]
    rows = pl.ds(pl.multiple_of(step * tile, tile), tile)
    chunk = 256
    attn = attn_ref[...]
    grad = og_ref[...]
    resid = x_ref[...].astype(F32) + dot(attn, pu_ref[:, :width])
    xhat, rstd = normalize(resid)
    gain = norms_ref[2:3, :]
    normed = (xhat * gain + norms_ref[3:4, :]).astype(BF)
    attnt_scr[:, rows] = attn.T
    n2t_scr[:, rows] = normed.T
    ogt_scr[:, rows] = grad.T
    for at in range(0, hidden, chunk):
        pre = dot(normed, pu_ref[:, width + at : width + at + chunk])
        act_grad = dot_nt(grad, down_ref[at : at + chunk, :])
        value, slope = gelu_parts(pre)
        activ = value.astype(BF)
        pre_grad = (act_grad * slope).astype(BF)
        activ_scr[rows, at : at + chunk] = activ
        pre_grad_scr[rows, at : at + chunk] = pre_grad
    out_ref[...] = (resid + dot(activ_scr[rows, :], down_ref[...])).astype(BF)
    back = dot_nt(pre_grad_scr[rows, :], pu_ref[:, width:])
    resid_grad = grad.astype(F32) + norm_back(back, gain, xhat, rstd)
    resid_grad_ref[...] = resid_grad
    pig = resid_grad.astype(BF)
    pig_scr[rows, :] = pig
    attn_grad_ref[...] = dot_nt(pig, pu_ref[:, :width]).astype(BF)
    gain_part = jnp.sum(back * xhat, axis=0, keepdims=True)
    shift_part = jnp.sum(back, axis=0, keepdims=True)
    part = jnp.concatenate([gain_part, shift_part], axis=0)

    @pl.when(step == 0)
    def _():
        norm_scr[...] = part

    @pl.when(step > 0)
    def _():
        norm_scr[...] += part

    @pl.when(step == pl.num_programs(0) - 1)
    def _():
        norm_grad_ref[...] = norm_scr[...]
        pu_grad_ref[:, :width] = dot(attnt_scr[...], pig_scr[...]).astype(BF)
        cols = 512

        def one(index, carry):
            c = pl.ds(pl.multiple_of(index * cols, cols), cols)
            out = pl.ds(pl.multiple_of(width + index * cols, cols), cols)
            pu_grad_ref[:, out] = dot(n2t_scr[...], pre_grad_scr[:, c]).astype(BF)
            down_grad_ref[c, :] = dot(ogt_scr[...], activ_scr[:, c]).T.astype(BF)
            return carry

        lax.fori_loop(0, hidden // cols, one, 0)


def final_kernel(
    info_ref, x_ref, back_ref, extra_ref, resid_grad_ref, norms_ref, weight_ref,
    input_grad_ref, qkv_grad_ref, norm_grad_ref, mg_scr, normed_scr,
):
    step = pl.program_id(0)
    tile, width = x_ref.shape
    rows = pl.ds(pl.multiple_of(step * tile, tile), tile)
    length, first_span = info_ref[0], info_ref[1]
    xhat, rstd = normalize(x_ref[...].astype(F32))
    gain = norms_ref[0:1, :]
    normed_scr[rows, :] = (xhat * gain + norms_ref[1:2, :]).astype(BF)
    per = tile // SPAN
    parts = []
    for part in range(per):
        span = step * per + part
        here = back_ref[part * SPAN : (part + 1) * SPAN, width:]
        parts.append(with_extra(here, extra_ref[pl.ds(span, 1), :], length, (first_span + span) * SPAN))
    mg = jnp.concatenate([back_ref[:, :width], jnp.concatenate(parts, axis=0)], axis=1)
    mg_scr[rows, :] = mg
    back = dot_nt(mg, weight_ref[...])
    input_grad_ref[...] = resid_grad_ref[...] + norm_back(back, gain, xhat, rstd)

    @pl.when(step == 0)
    def _():
        norm_grad_ref[...] = jnp.zeros_like(norm_grad_ref)

    norm_grad_ref[0:1, :] += jnp.sum(back * xhat, axis=0, keepdims=True)
    norm_grad_ref[1:2, :] += jnp.sum(back, axis=0, keepdims=True)

    @pl.when(step == pl.num_programs(0) - 1)
    def _():
        cols = 256

        def one(index, carry):
            c = pl.ds(pl.multiple_of(index * cols, cols), cols)
            qkv_grad_ref[:, c] = dot_tn(normed_scr[...], mg_scr[:, c]).astype(BF)
            return carry

        lax.fori_loop(0, qkv_grad_ref.shape[1] // cols, one, 0)


def whole(shape):
    return pl.BlockSpec(shape, lambda i: (0,) * len(shape))


def by_rows(tile, width):
    return pl.BlockSpec((tile, width), lambda i: (i, 0))


SCALARS = pl.BlockSpec(memory_space=pltpu.SMEM)
PARAMS = pltpu.CompilerParams(vmem_limit_bytes=VMEM_LIMIT)


def remote_call(kernel, groups, seqs, name, collective_id, outs, ins, scratch, loads, copies):
    return pl.pallas_call(
        functools.partial(kernel, groups, seqs),
        in_specs=[pl.BlockSpec(memory_space=space) for space in ins],
        out_specs=[pl.BlockSpec(memory_space=space) for space, _, _ in outs],
        out_shape=[jax.ShapeDtypeStruct(shape, kind) for _, shape, kind in outs],
        scratch_shapes=list(scratch) + [pltpu.SemaphoreType.DMA((n,)) for n in (loads, copies, copies)],
        compiler_params=pltpu.CompilerParams(
            vmem_limit_bytes=VMEM_LIMIT, collective_id=collective_id, has_side_effects=True
        ),
        name=name,
    )


def regroup(grad, dim, outer, inner):
    shape = grad.shape
    piece = shape[dim] // (outer * inner)
    split = grad.reshape(shape[:dim] + (outer, inner, piece) + shape[dim + 1 :])
    return jnp.swapaxes(split, dim, dim + 1).reshape(shape)


def gather_plain(state):
    both = ("batch", "seq")
    qkv, proj, up, down = (lax.all_gather(w.astype(BF), both, axis=0, tiled=True) for w in state[:4])
    norms = lax.all_gather(state[4].astype(BF), both, axis=1, tiled=True).astype(F32)
    return qkv, jnp.concatenate([proj, up], axis=1), down, norms


def reduce_plain(qkv_grad, pu_grad, down_grad, norm_grad):
    groups, seqs = lax.axis_size("batch"), lax.axis_size("seq")
    reduced = []
    for grad, dim in ((qkv_grad, 0), (pu_grad, 0), (down_grad, 0)):
        part = lax.psum_scatter(
            regroup(grad.astype(F32), dim, groups, seqs), "seq", scatter_dimension=dim, tiled=True
        )
        reduced.append(lax.psum_scatter(part, "batch", scatter_dimension=dim, tiled=True))
    norm_total = lax.psum(norm_grad, ("batch", "seq"))
    squares = lax.psum(sum(jnp.sum(grad * grad) for grad in reduced), ("batch", "seq"))
    squares = squares + jnp.sum(norm_total * norm_total)
    return (*reduced, norm_total, jnp.zeros((8, LANES), F32).at[0, 0].set(squares))


def mlp_call(x, attn_out, grad_rows, norms, pu_full, down_full):
    sds = jax.ShapeDtypeStruct
    rows, width = x.shape
    hidden = down_full.shape[0]
    tile = min(512, rows)
    steps = rows // tile
    return pl.pallas_call(
        mlp_kernel,
        grid=(steps,),
        in_specs=[by_rows(tile, width)] * 3
        + [whole(norms.shape), whole(pu_full.shape), whole(down_full.shape)],
        out_specs=[by_rows(tile, width)] * 3
        + [whole(pu_full.shape), whole(down_full.shape), whole((2, width))],
        out_shape=[
            sds((rows, width), BF), sds((rows, width), F32), sds((rows, width), BF),
            sds(pu_full.shape, BF), sds(down_full.shape, BF), sds((2, width), F32),
        ],
        scratch_shapes=[
            pltpu.VMEM((rows, hidden), BF), pltpu.VMEM((rows, hidden), BF),
            pltpu.VMEM((width, rows), BF), pltpu.VMEM((width, rows), BF), pltpu.VMEM((width, rows), BF),
            pltpu.VMEM((rows, width), BF), pltpu.VMEM((2, width), F32),
        ],
        compiler_params=PARAMS,
        name="mlp",
    )(x, attn_out, grad_rows, norms, pu_full, down_full)


def direct_body(groups, seqs, inputs, out_grad, lengths, *state):
    rows, width = inputs.shape[1], inputs.shape[2]
    own_rows, down_rows = state[0].shape[0], state[3].shape[0]
    hidden = state[2].shape[1]
    chips = seqs // 2
    grid3 = (groups, chips, 2)
    local = rows // SPAN
    spans = local * seqs
    pairs = width // LANES
    count = rows // TILE
    x, grad_rows = inputs[0], out_grad[0]
    vmem, hbm, smem = pltpu.VMEM, pl.ANY, pltpu.SMEM
    shapes = (
        (*grid3, own_rows, 3 * width), (*grid3, own_rows, width + hidden), (*grid3, down_rows, width),
    )
    tokens = (rows, width)
    (
        qkv_full, pu_full, down_full, norms, mixed, summ, attn_out, probs, activ, resid, slope, down_grad,
    ) = remote_call(
        front_kernel, groups, seqs, "front", 0,
        [
            *((hbm, shape, BF) for shape in shapes), (vmem, (4, width), F32), (hbm, (rows, 3 * width), BF),
            (vmem, (chips, 2, local, 2 * width), BF), (hbm, tokens, BF), (hbm, (rows, 4 * SPAN * pairs), BF),
            (hbm, (rows, hidden), BF), (hbm, tokens, F32), (hbm, (rows, hidden), BF), (hbm, (hidden, width), BF),
        ],
        [smem, hbm, hbm] + [vmem] * 5,
        [
            vmem(tokens, BF), vmem(tokens, BF), *(vmem(shape, BF) for shape in shapes),
            vmem((rows, 3 * width), BF), vmem(tokens, BF), vmem(tokens, F32),
            vmem((rows, hidden), BF), vmem((rows, hidden), BF), vmem((hidden, width), BF),
            vmem((*grid3, 4, LANES), F32), vmem((local, 2 * width), F32), vmem((width, spans), BF),
        ],
        4 + 7 * count + hidden // TILE, 3 * GATHER_COPIES + fast_gather_copies(chips) + 2 * chips,
    )(lengths, x, grad_rows, *state[:5])
    pu_flat, down_flat = pu_full.reshape(width, width + hidden), down_full.reshape(hidden, width)
    resid_grad, attn_grad, pu_grad, down_own, norm_two = remote_call(
        middle_kernel, groups, seqs, "middle", 1,
        [
            (hbm, tokens, F32), (hbm, tokens, BF), (hbm, pu_flat.shape, BF),
            (vmem, (down_rows, width), F32), (vmem, (2, width), F32),
        ],
        [hbm] * 6 + [vmem, hbm],
        [
            vmem(tokens, BF), vmem(tokens, F32), vmem((rows, hidden), BF), vmem(tokens, BF),
            vmem(pu_flat.shape, BF), vmem(down_flat.shape, BF), vmem(tokens, F32), vmem(tokens, BF),
            vmem(pu_flat.shape, BF), vmem((rows, hidden), BF), vmem(tokens, BF), vmem(tokens, BF),
            *scatter_scratch(groups, chips, down_rows // 2, width) * 2,
        ],
        6 + 5 * count, 2 * SCATTER_COPIES,
    )(grad_rows, resid, slope, attn_out, pu_flat, down_flat, norms, down_grad.reshape(shapes[2]))
    half = (width + hidden) // 2
    blocks = ((own_rows, half),) * 2 + ((own_rows, width),) * 3
    summ_block = (local, 2 * width)
    scratch = [
        vmem(tokens, BF), vmem((rows, 3 * width), BF), vmem(tokens, BF), vmem(probs.shape, BF), vmem(tokens, F32),
        vmem((width, 3 * width), BF), vmem(tokens, BF), vmem(tokens, F32), vmem(down_flat.shape, BF), vmem(tokens, BF),
        vmem((rows, 3 * width), BF), vmem(tokens, BF), vmem((width, spans), BF), vmem((spans, 2 * width), F32),
        vmem((chips, *summ_block), F32), vmem((chips - 1, *summ_block), BF),
        vmem((chips - 1, *summ_block), BF), vmem(summ_block, F32),
        *[vmem((*grid3, own_rows, width), BF)] * 3, *[vmem((width, LANES), F32)] * 2,
    ]
    scratch += [buffer for block in blocks for buffer in scatter_scratch(groups, chips, *block)]
    scratch += [
        vmem((4, width), F32), vmem((seqs, 4, width), F32), vmem((groups, 4, width), F32),
        vmem((8, LANES), F32), vmem((seqs, 8, LANES), F32), vmem((groups, 8, LANES), F32),
    ]
    input_grad, outputs, qkv_own, pu_own, norm_total, total = remote_call(
        back_kernel, groups, seqs, "back", 2,
        [
            (hbm, tokens, BF), (hbm, tokens, BF), (vmem, (own_rows, 3 * width), F32),
            (vmem, (own_rows, width + hidden), F32), (vmem, (4, width), F32), (vmem, (8, LANES), F32),
        ],
        [smem, hbm, hbm, hbm, hbm, vmem, hbm, hbm, vmem, vmem, hbm, vmem, hbm, hbm, hbm],
        scratch, 3 * local // 2 + 6 + 5 + 2 * count,
        5 * SCATTER_COPIES + 2 * share_copies(groups, seqs) + 2 * chips,
    )(
        lengths, x, mixed, attn_grad, probs, summ.reshape(spans, 2 * width), pu_grad.reshape(shapes[1]),
        resid_grad, down_own, norms, qkv_full.reshape(width, 3 * width), norm_two, activ, resid, down_flat,
    )
    return outputs, input_grad, (qkv_own, pu_own, down_own), norm_total, total


def plain_body(groups, seqs, inputs, out_grad, lengths, *state):
    sds = jax.ShapeDtypeStruct
    rows, width = inputs.shape[1], inputs.shape[2]
    qkv_full, pu_full, down_full, norms = gather_plain(state[:5])
    local = rows // SPAN
    spans = local * seqs
    info = jnp.stack([lengths[0], (lax.axis_index("seq") * local).astype(jnp.int32)])
    x, grad_rows = inputs[0], out_grad[0]
    tile = 256
    steps = rows // tile
    mixed, own_summ = pl.pallas_call(
        qkv_kernel,
        grid=(steps,),
        in_specs=[SCALARS, by_rows(tile, width), whole(norms.shape), whole(qkv_full.shape)],
        out_specs=[by_rows(tile, 3 * width), whole((local, 2 * width))],
        out_shape=[sds((rows, 3 * width), BF), sds((local, 2 * width), BF)],
        scratch_shapes=[pltpu.VMEM((local, 2 * width), F32)],
        compiler_params=PARAMS,
        name="qkv",
    )(info, x, norms, qkv_full)
    summ = lax.all_gather(own_summ, "seq", axis=0, tiled=True)
    pairs = width // LANES
    lse_spec = pl.BlockSpec((1, pairs, 2 * SPAN), lambda i: (i, 0, 0))
    attn_out, lse = pl.pallas_call(
        attend_kernel,
        grid=(local,),
        in_specs=[SCALARS, by_rows(SPAN, 3 * width), whole(summ.shape)],
        out_specs=[by_rows(SPAN, width), lse_spec],
        out_shape=[sds((rows, width), BF), sds((local, pairs, 2 * SPAN), F32)],
        scratch_shapes=[pltpu.VMEM((width, spans), BF)],
        compiler_params=PARAMS,
        name="attend",
    )(info, mixed, summ)
    outputs, resid_grad, attn_grad, pu_grad, down_grad, norm_two = mlp_call(
        x, attn_out, grad_rows, norms, pu_full, down_full
    )
    back, dsumm = pl.pallas_call(
        attend_back_kernel,
        grid=(local,),
        in_specs=[SCALARS, by_rows(SPAN, 3 * width), by_rows(SPAN, width), lse_spec, whole(summ.shape)],
        out_specs=[by_rows(SPAN, 3 * width), whole((spans, 2 * width))],
        out_shape=[sds((rows, 3 * width), BF), sds((spans, 2 * width), F32)],
        scratch_shapes=[pltpu.VMEM((width, spans), BF)],
        compiler_params=PARAMS,
        name="attend_back",
    )(info, mixed, attn_grad, lse, summ)
    extra = lax.psum_scatter(dsumm, "seq", scatter_dimension=0, tiled=True)
    input_grad, qkv_grad, norm_one = pl.pallas_call(
        final_kernel,
        grid=(steps,),
        in_specs=[
            SCALARS, by_rows(tile, width), by_rows(tile, 3 * width), whole(extra.shape), by_rows(tile, width),
            whole(norms.shape), whole(qkv_full.shape),
        ],
        out_specs=[by_rows(tile, width), whole(qkv_full.shape), whole((2, width))],
        out_shape=[sds((rows, width), F32), sds(qkv_full.shape, BF), sds((2, width), F32)],
        scratch_shapes=[pltpu.VMEM((rows, 3 * width), BF), pltpu.VMEM((rows, width), BF)],
        compiler_params=PARAMS,
        name="final",
    )(info, x, back, extra, resid_grad, norms, qkv_full)
    norm_grad = jnp.concatenate([norm_one, norm_two], axis=0)
    *grads, norm_total, total = reduce_plain(qkv_grad, pu_grad, down_grad, norm_grad)
    return outputs, input_grad, grads, norm_total, total


def body(groups, seqs, *args):
    state = args[3:]
    rows, width = args[0].shape[1:]
    direct = groups == 4 and seqs % 4 == 0 and state[0].shape[0] % 16 == 0 and rows % TILE == 0
    direct = direct and rows // SPAN * seqs == SPAN and state[2].shape[1] == 4 * SPAN * (width // LANES)
    run = direct_body if direct else plain_body
    outputs, input_grad, grads, norm_total, total = run(groups, seqs, *args)
    input_grad = input_grad.astype(BF)
    sds = jax.ShapeDtypeStruct
    vmem, hbm = pltpu.VMEM, pl.ANY
    spec = lambda space: pl.BlockSpec(memory_space=space)
    held = [sds(w.shape, F32) for w in state[:5]]
    parts = 8
    operands = (outputs, input_grad, *grads, *state)
    outputs, input_grad, grad_norm, *fresh, shift_clipped = pl.pallas_call(
        functools.partial(update_kernel, parts),
        in_specs=[spec(vmem)] * 2 + [spec(hbm)] * 20,
        out_specs=[spec(hbm)] * 2 + [spec(vmem)] + [spec(hbm)] * 15 + [spec(vmem)],
        out_shape=[
            sds(outputs.shape, BF), sds(outputs.shape, F32), sds((1, 1), F32), *held * 3,
            sds((1, state[4].shape[1]), F32),
        ],
        scratch_shapes=[vmem(a.shape, a.dtype) for a in operands]
        + [vmem(w.shape, F32) for w in held * 3] + [vmem(outputs.shape, F32), pltpu.SemaphoreType.DMA((4 * parts + 33,))],
        compiler_params=PARAMS,
        name="update",
    )(total, norm_total, *operands)
    return (outputs[None], input_grad[None], grad_norm[0, 0], *fresh, shift_clipped[0])


def solution(mesh):
    tokens = P("batch", "seq", None)
    owned = P(("batch", "seq"), None)
    columns = P(None, ("batch", "seq"))
    state = (owned, owned, owned, owned, columns)
    return jax.shard_map(
        functools.partial(body, mesh.shape["batch"], mesh.shape["seq"]),
        mesh=mesh,
        in_specs=(tokens, tokens, P("batch")) + state * 3,
        out_specs=(tokens, tokens, P()) + state * 3 + (P(("batch", "seq")),),
        check_vma=False,
    )
```

```python
import functools
import jax
import jax.numpy as jnp
from jax import lax
from jax.experimental import pallas as pl
from jax.experimental.pallas import tpu as pltpu
from jax.sharding import PartitionSpec as P

HEADS = 8
HD = 64
SPAN = 128
STEP = 10
LN_EPS = 1e-05
NEG_FILL = -1e30
CLIP = 1.0
BETA = 0.5
ADAM_EPS = 1e-08
DECAY = 0.1
RATES = (0.02, 0.3, 0.02, 0.02, 0.5)
BF = jnp.bfloat16
F32 = jnp.float32
LANES = 128
VMEM_LIMIT = 56 * 1024 * 1024


def dot(a, b, dims=((1,), (0,))):
    return lax.dot_general(a, b, (dims, ((), ())), preferred_element_type=F32)


def dot_tn(a, b):
    return dot(a, b, ((0,), (0,)))


def dot_nt(a, b):
    return dot(a, b, ((1,), (1,)))


def normalize(x):
    inv = 1.0 / x.shape[-1]
    centred = x - jnp.sum(x, axis=-1, keepdims=True) * inv
    spread = jnp.sum(centred * centred, axis=-1, keepdims=True) * inv
    rstd = lax.rsqrt(spread + LN_EPS)
    return centred * rstd, rstd


def norm_back(grad, gain, xhat, rstd):
    inv = 1.0 / grad.shape[-1]
    e = grad * gain
    mean_e = jnp.sum(e, axis=-1, keepdims=True) * inv
    mean_ex = jnp.sum(e * xhat, axis=-1, keepdims=True) * inv
    return rstd * (e - mean_e - xhat * mean_ex)


def qkv_tile(x, norms_ref, weight_ref):
    xhat, _ = normalize(x.astype(F32))
    normed = (xhat * norms_ref[0:1, :] + norms_ref[1:2, :]).astype(BF)
    return dot(normed, weight_ref[...]).astype(BF)


def span_scale(length, begin, shape):
    count = jnp.clip(length - begin, 1, SPAN)
    return lax.rsqrt(jnp.full(shape, count, jnp.int32).astype(F32))


def span_sum(kv, length, begin):
    row = lax.broadcasted_iota(jnp.int32, kv.shape, 0)
    kept = jnp.where(row < length - begin, kv.astype(F32), 0.0)
    total = jnp.sum(kept, axis=0, keepdims=True)
    return total * span_scale(length, begin, total.shape)


def stack_heads(pair):
    lane = lax.broadcasted_iota(jnp.int32, pair.shape, 1)
    zero = jnp.zeros_like(pair)
    return jnp.concatenate(
        [jnp.where(lane < HD, pair, zero), jnp.where(lane >= HD, pair, zero)], axis=0
    )


def fold_heads(both):
    picked = jnp.concatenate([both[:HD, :SPAN], both[HD:, SPAN:]], axis=0)
    return picked.T


def span_caps(length, span):
    query_pos = lax.broadcasted_iota(jnp.int32, (1, 2 * SPAN), 1) & (SPAN - 1)
    near_cap = jnp.minimum(query_pos, length - span * SPAN - 1)
    far_cap = jnp.minimum(span, (length + SPAN - 1) // SPAN)
    return near_cap, far_cap


def mask_scores(raw, caps):
    near_cap, far_cap = caps
    key_pos = lax.broadcasted_iota(jnp.int32, (SPAN, 2 * SPAN), 0)
    summ_pos = lax.broadcasted_iota(jnp.int32, (raw.shape[0] - SPAN, 2 * SPAN), 0)
    near = jnp.where(key_pos <= near_cap, raw[:SPAN], NEG_FILL)
    far = jnp.where(summ_pos < far_cap, raw[SPAN:], NEG_FILL)
    return jnp.concatenate([near, far], axis=0)


def attend_spans(spans, mixed_ref, width, summ_ref, summ_vt_ref, out_ref, lse_ref=None, probs_ref=None):
    units = [(pl.ds(row, SPAN), index, caps, pair) for row, index, caps in spans for pair in range(width // LANES)]
    queries, keys, values_t = [], [], []
    for rows, index, caps, pair in units:
        at = pair * LANES
        queries.append(stack_heads(mixed_ref[rows, at : at + LANES] * BF(0.125)))
        near_k = mixed_ref[rows, width + at : width + at + LANES]
        near_v = mixed_ref[rows, 2 * width + at : 2 * width + at + LANES]
        keys.append(jnp.concatenate([near_k, summ_ref[:, at : at + LANES]], axis=0))
        values_t.append(jnp.concatenate([near_v.T, summ_vt_ref[at : at + LANES, :]], axis=1))
    scores = [dot_nt(k, q) for k, q in zip(keys, queries)]
    scores = [mask_scores(s, unit[2]) for s, unit in zip(scores, units)]
    peaks = [jnp.max(s, axis=0, keepdims=True) for s in scores]
    expos = [jnp.exp(s - p) for s, p in zip(scores, peaks)]
    totals = [jnp.sum(e, axis=0, keepdims=True) for e in expos]
    probs = [(e * (1.0 / t)).astype(BF) for e, t in zip(expos, totals)]
    outs = [dot(v, p) for v, p in zip(values_t, probs)]
    for (rows, index, caps, pair), out, prob, peak, total in zip(units, outs, probs, peaks, totals):
        at = pair * LANES
        out_ref[rows, at : at + LANES] = fold_heads(out).astype(BF)
        if lse_ref is not None:
            lse_ref[index, pair : pair + 1, :] = peak + jnp.log(total)
        if probs_ref is not None:
            at = pair * 4 * SPAN
            probs_ref[rows, at : at + 2 * SPAN] = prob[:SPAN]
            probs_ref[rows, at + 2 * SPAN : at + 4 * SPAN] = prob[SPAN:]


def attend_back_spans(
    spans, mixed_ref, grad_ref, width, summ_ref, summ_kt_ref, lse_ref, back_ref, dsumm_ref, probs_ref=None
):
    pairs = width // LANES
    units = [(pl.ds(row, SPAN), index, caps, pair) for row, index, caps in spans for pair in range(pairs)]
    queries, grads, keys, keys_t, values = [], [], [], [], []
    for rows, index, caps, pair in units:
        at = pair * LANES
        queries.append(stack_heads(mixed_ref[rows, at : at + LANES] * BF(0.125)))
        grads.append(stack_heads(grad_ref[rows, at : at + LANES]))
        near_k = mixed_ref[rows, width + at : width + at + LANES]
        near_v = mixed_ref[rows, 2 * width + at : 2 * width + at + LANES]
        keys.append(jnp.concatenate([near_k, summ_ref[:, at : at + LANES]], axis=0))
        keys_t.append(jnp.concatenate([near_k.T, summ_kt_ref[at : at + LANES, :]], axis=1))
        values.append(jnp.concatenate([near_v, summ_ref[:, width + at : width + at + LANES]], axis=0))
    if probs_ref is None:
        scores = [dot_nt(k, q) for k, q in zip(keys, queries)]
        dprobs = [dot_nt(v, g) for v, g in zip(values, grads)]
        scores = [mask_scores(s, unit[2]) for s, unit in zip(scores, units)]
        probs = [jnp.exp(s - lse_ref[index, pair : pair + 1, :]) for s, (_, index, _, pair) in zip(scores, units)]
        lows = [p.astype(BF) for p in probs]
    else:
        dprobs = [dot_nt(v, g) for v, g in zip(values, grads)]
        lows = []
        for rows, _, _, pair in units:
            at = pair * 4 * SPAN
            near, far = probs_ref[rows, at : at + 2 * SPAN], probs_ref[rows, at + 2 * SPAN : at + 4 * SPAN]
            lows.append(jnp.concatenate([near, far], axis=0))
        probs = [low.astype(F32) for low in lows]
    dvs = [dot(low, g) for low, g in zip(lows, grads)]
    deltas = [jnp.sum(p * d, axis=0, keepdims=True) for p, d in zip(probs, dprobs)]
    dscores = [(p * (d - delta)).astype(BF) for p, d, delta in zip(probs, dprobs, deltas)]
    dqs = [dot(k, ds) for k, ds in zip(keys_t, dscores)]
    dks = [dot(ds, q) for ds, q in zip(dscores, queries)]
    for (rows, index, caps, pair), dq, dk, dv in zip(units, dqs, dks, dvs):
        at = pair * LANES
        back_ref[rows, at : at + LANES] = (fold_heads(dq) * 0.125).astype(BF)
        back_ref[rows, width + at : width + at + LANES] = dk[:SPAN].astype(BF)
        back_ref[rows, 2 * width + at : 2 * width + at + LANES] = dv[:SPAN].astype(BF)
    for pair in range(pairs):
        at = pair * LANES
        dsumm_ref[:, at : at + LANES] += sum(dk[SPAN:] for dk in dks[pair::pairs])
        dsumm_ref[:, width + at : width + at + LANES] += sum(dv[SPAN:] for dv in dvs[pair::pairs])


def with_extra(back, extra, length, begin):
    extra = extra * span_scale(length, begin, extra.shape)
    pos = lax.broadcasted_iota(jnp.int32, back.shape, 0)
    return (back.astype(F32) + jnp.where(pos < length - begin, extra, 0.0)).astype(BF)


GELU_A = 0.7978845608
GELU_B = 0.044715


def gelu_parts(t):
    slow = GELU_A + (GELU_A * GELU_B) * (t * t)
    half = 0.5 * jnp.tanh(t * slow) + 0.5
    value = t * half
    return value, half + (value - value * half) * (6.0 * slow - 4.0 * GELU_A)


MESH = pl.DeviceIdType.MESH


class Place:
    def __init__(self, groups, seqs):
        self.groups, self.seqs, self.chips = groups, seqs, seqs // 2
        self.b = lax.axis_index("batch")
        self.seq = lax.axis_index("seq")
        self.z, self.c = self.seq // 2, self.seq % 2
        self.other = 1 - self.c
        self.b1 = self.b + 1 - 2 * (self.b % 2)
        self.b2 = (self.b + 2) % 4
        self.b3 = self.b1 + 2 - 4 * (self.b1 // 2)
        self.after = [(self.z + k) % self.chips for k in range(self.chips)]
        self.before = [(self.z + self.chips - k) % self.chips for k in range(self.chips)]
        self.sibling = (self.b, 2 * self.z + self.other)
        self.x, self.y, self.diagonal = (self.b1, self.seq), (self.b2, self.seq), (self.b3, self.seq)
        self.along = [(self.b, 2 * z + self.c) for z in self.after]
        self.ring = [(self.b, (self.seq + k) % seqs) for k in range(seqs)]


def meet(place):
    barrier = pltpu.get_barrier_semaphore()
    partners = [place.x, place.y, place.diagonal, *place.ring[1:]]
    for partner in partners:
        pl.semaphore_signal(barrier, inc=1, device_id=partner, device_id_type=MESH)
    pl.semaphore_wait(barrier, len(partners))


def part_of(ref, index):
    return ref if index is None else ref.at[index]


class Copy:
    def __init__(self, make):
        self.make = make
        make().start()

    def wait(self):
        self.make().wait()

    def wait_recv(self):
        self.make().wait_recv()

    def wait_send(self):
        self.make().wait_send()


class Copies:
    def __init__(self, send_sems, recv_sems):
        self.send, self.recv, self.made, self.left = send_sems, recv_sems, [], 0

    def start(self, src, src_index, dst, dst_index, device):
        at = len(self.made)
        assert at < self.send.shape[0]
        copy = Copy(
            lambda: pltpu.make_async_remote_copy(
                src_ref=part_of(src, src_index), dst_ref=part_of(dst, dst_index),
                send_sem=self.send.at[at], recv_sem=self.recv.at[at],
                device_id=device, device_id_type=MESH,
            )
        )
        self.made.append(copy)
        return copy

    def push(self, ref, index, device):
        return self.start(ref, index, ref, index, device)

    def finish(self):
        for copy in self.made[self.left :]:
            copy.wait_send()
        self.left = len(self.made)


class Loads:
    def __init__(self, sems):
        self.sems, self.made = sems, 0

    def start(self, src, dst, src_index=None, dst_index=None):
        at = self.made
        assert at < self.sems.shape[0]
        self.made += 1
        return Copy(
            lambda: pltpu.make_async_copy(part_of(src, src_index), part_of(dst, dst_index), self.sems.at[at])
        )


def gather_steps(place, copies, full, rows=slice(None), cols=slice(None)):
    p, half = place, place.chips // 2
    low, high = slice(0, half), slice(half, place.chips)

    def push(b, z, device):
        return copies.push(full, (b, z, p.c, rows, cols), device)

    along = [push(p.b, p.z, device) for device in p.along[1:]]
    yield
    for copy in along:
        copy.wait_recv()
    every = slice(None)
    to_x, to_y, sib = push(p.b, every, p.x), push(p.b, every, p.y), [push(p.b, every, p.sibling)]
    yield
    to_x.wait_recv()
    on_y = push(p.b1, low, p.y)
    to_y.wait_recv()
    on_x = push(p.b2, high, p.x)
    sib += [push(p.b1, every, p.sibling), push(p.b2, every, p.sibling)]
    yield
    on_y.wait_recv()
    sib.append(push(p.b3, low, p.sibling))
    on_x.wait_recv()
    sib.append(push(p.b3, high, p.sibling))
    yield
    for copy in sib:
        copy.wait_recv()


GATHER_COPIES = 12


def fast_gather_steps(place, copies, full, rows=slice(None), cols=slice(None)):
    p = place
    order = range(p.chips)
    early, late = order[: p.chips // 2], order[p.chips // 2 :]

    def push(b, k, device):
        return copies.push(full, (b, p.before[k], p.c, rows, cols), device)

    def pass_over(b):
        sib.append(copies.push(full, (b, slice(None), p.c, rows, cols), p.sibling))

    along = [push(p.b, 0, device) for device in p.along[1:]]
    to_x, to_y, sib = [push(p.b, 0, p.x)], [push(p.b, 0, p.y)], []
    yield
    for k, copy in enumerate(along, 1):
        copy.wait_recv()
        to_x.append(push(p.b, k, p.x))
        to_y.append(push(p.b, k, p.y))
    pass_over(p.b)
    yield
    on = []
    for k in early:
        to_x[k].wait_recv()
        on.append(push(p.b1, k, p.y))
    for k in late:
        to_y[k].wait_recv()
        on.append(push(p.b2, k, p.x))
    yield
    for k in late:
        to_x[k].wait_recv()
    pass_over(p.b1)
    for k in early:
        to_y[k].wait_recv()
    pass_over(p.b2)
    for copy in on:
        copy.wait_recv()
    pass_over(p.b3)
    yield
    for copy in sib:
        copy.wait_recv()


def fast_gather_copies(chips):
    return chips - 1 + 3 * chips + 4


def scatter_steps(place, copies, loads, grad, acc, got, near, far, last, result):
    p, half = place, place.chips // 2
    low, high = slice(0, half), slice(half, place.chips)
    chips = p.chips

    def add(into, *others):
        total = acc[into].astype(F32)
        for other in others:
            total = total + other.astype(F32)
        acc[into] = total.astype(BF)

    every = slice(None)
    swap = copies.start(grad, (every, every, p.other), got, None, p.sibling)
    keep = loads.start(grad, acc, (every, every, p.c))
    yield
    keep.wait()
    swap.wait_recv()
    for b in (p.b3, p.b1, p.b2):
        for z in range(chips):
            add((b, z), got[b, z])
    on_y = copies.start(acc, (p.b3, low), far, 0, p.y)
    on_x = copies.start(acc, (p.b3, high), far, 1, p.x)
    early_x = copies.start(acc, (p.b1, high), near, (0, high), p.x)
    early_y = copies.start(acc, (p.b2, low), near, (1, low), p.y)
    for z in range(chips):
        add((p.b, z), got[p.b, z])
    yield
    on_y.wait_recv()
    for z in range(half):
        add((p.b1, z), far[0, z])
    late_x = copies.start(acc, (p.b1, low), near, (0, low), p.x)
    on_x.wait_recv()
    for z in range(half, chips):
        add((p.b2, z), far[1, z - half])
    late_y = copies.start(acc, (p.b2, high), near, (1, high), p.y)
    yield
    for copy in (early_x, early_y, late_x, late_y):
        copy.wait_recv()
    for z in range(chips):
        add((p.b, z), near[0, z], near[1, z])
    along = []
    for k in range(1, chips):
        along.append(copies.start(acc, (p.b, p.after[k]), last, k - 1, p.along[k]))
    yield
    total = acc[p.b, p.z].astype(F32)
    for k, copy in enumerate(along):
        copy.wait_recv()
        total = total + last[k].astype(F32)
    result[...] = total


SCATTER_COPIES = 10


def scatter_scratch(groups, chips, rows, cols):
    half = chips // 2
    return [
        pltpu.VMEM((groups, chips, rows, cols), BF),
        pltpu.VMEM((groups, chips, rows, cols), BF),
        pltpu.VMEM((2, chips, rows, cols), BF),
        pltpu.VMEM((2, half, rows, cols), BF),
        pltpu.VMEM((chips - 1, rows, cols), BF),
    ]


def share_sum_steps(place, copies, mine, along, across, result):
    p, seqs = place, along.shape[0]
    along[p.seq] = mine[...]
    sent = [copies.push(along, p.seq, device) for device in p.ring[1:]]
    yield
    for copy in sent:
        copy.wait_recv()
    across[p.b] = sum(along[s] for s in range(seqs))
    sent = [copies.push(across, p.b, device) for device in (p.x, p.y, p.diagonal)]
    yield
    for copy in sent:
        copy.wait_recv()
    result[...] = sum(across[b] for b in range(p.groups))


def share_copies(groups, seqs):
    return groups + seqs - 2


def square_sums(value):
    total = 0.0
    for at in range(0, value.shape[1], LANES):
        block = jnp.square(value[:, at : at + LANES])
        if block.shape[0] < 8:
            total = total + jnp.concatenate([block, jnp.zeros((8 - block.shape[0], LANES), F32)], axis=0)
        for row in range(0, block.shape[0] // 8 * 8, 8):
            total = total + block[row : row + 8]
    return total


class Schedule:
    def __init__(self, **steps):
        self.steps = steps

    def __call__(self, *names):
        for name in names:
            next(self.steps[name], None)

    def plan(self, *calls):
        return {at: functools.partial(self, *names.split()) for at, names in enumerate(calls) if names}

    def finish(self, *names):
        run_all(*(self.steps[name] for name in names or self.steps))


def run_all(*steps):
    live = list(steps)
    while live:
        for step in list(live):
            try:
                next(step)
            except StopIteration:
                live.remove(step)


def loop(count, body, ticks=None):
    def step(index, carry):
        body(index)
        for k in sorted(ticks or {}):
            pl.when(index == k)(lambda run=ticks[k]: run())
        return carry

    lax.fori_loop(0, count, step, 0)


def adam(grad, master, first, second, rate, moment_out, square_out, fresh_out):
    fix = 1.0 - BETA**STEP
    moment = BETA * first + (1.0 - BETA) * grad
    square = BETA * second + (1.0 - BETA) * grad * grad
    update = moment / fix / (jnp.sqrt(square / fix) + ADAM_EPS)
    moment_out[...] = moment
    square_out[...] = square
    fresh_out[...] = master - rate * (update + DECAY * master)


def update_kernel(parts, total_ref, norm_grad, *refs):
    sources, results, held, sems = refs[:20], refs[20:39], refs[39:-1], refs[-1]
    outputs_ref, input_ref, grad_refs, state, made, wide_ref = held[0], held[1], held[2:5], held[5:20], held[20:35], held[35]
    outputs_hbm, input_hbm, grads_hbm, state_hbm = sources[0], sources[1], sources[2:5], sources[5:]
    loads = Loads(sems)
    ways = ((input_hbm, input_ref, wide_ref, results[1]), (outputs_hbm, outputs_ref, outputs_ref, results[0]))
    small = [loads.start(src, via) for src, via in zip((*grads_hbm, *state_hbm), (*grad_refs, *state))]
    reads = [Sliced(loads, src, via, parts).start_all() for src, via, _, _ in ways]
    stores = [Sliced(loads, via, dst, parts) for _, _, via, dst in ways]
    for load in small:
        load.wait()
    grad_norm = jnp.sqrt(jnp.sum(total_ref[...], keepdims=True))
    results[2][...] = grad_norm
    factor = jnp.minimum(1.0, CLIP / (grad_norm + 1e-06))
    width = state[1].shape[1]
    piece = state[4].shape[1]
    per = LANES // piece
    index = lax.axis_index("batch") * lax.axis_size("seq") + lax.axis_index("seq")
    block = norm_grad[:, pl.ds(pl.multiple_of(index // per * LANES, LANES), LANES)]
    own = pltpu.roll(block, (LANES - index % per * piece) % LANES, 1)[:, :piece]
    qkv_grad, pu_grad, down_grad = grad_refs
    grads = (qkv_grad[...], pu_grad[:, :width], pu_grad[:, width:], down_grad[...], own)
    results[18][...] = own[3:4] * factor
    last = []
    for at, (grad, rate) in enumerate(zip(grads, RATES)):
        adam(
            grad * factor, state[at][...], state[5 + at][...], state[10 + at][...], rate,
            made[at], made[5 + at], made[10 + at],
        )
        last += [loads.start(made[k], results[3 + k]) for k in (at, 5 + at, 10 + at)]
    for read, store in zip(reads, stores):
        for part in range(parts):
            read.wait(part)
            if read.dst is input_ref:
                here = pl.ds(part * read.size, read.size)
                wide_ref[here, :] = input_ref[here, :].astype(F32)
            store.start(part)
    for store in stores:
        store.wait_all()
    for store in last:
        store.wait()


def cast_shards(p, seqs, qkv_ref, proj_ref, up_ref, down_ref, norm_ref, qkv_full, pu_full, down_full, norm_full):
    width = proj_ref.shape[1]
    b, z, c = p.b, p.z, p.c
    index = b * seqs + 2 * z + c
    qkv_full[b, z, c] = qkv_ref[...].astype(BF)
    pu_full[b, z, c, :, :width] = proj_ref[...].astype(BF)
    pu_full[b, z, c, :, width:] = up_ref[...].astype(BF)
    down_full[b, z, c] = down_ref[...].astype(BF)
    piece = norm_ref.shape[1]
    per = LANES // piece
    tiled = jnp.concatenate([norm_ref[...].astype(BF).astype(F32)] * per, axis=1)
    lane = lax.broadcasted_iota(jnp.int32, tiled.shape, 1)
    norm_full[b, z, c] = jnp.where(lane // piece == index % per, tiled, 0.0)


def join_norms(norm_full, seqs, per, norms_out):
    for block in range(norms_out.shape[1] // LANES):
        total = None
        for device in range(block * per, (block + 1) * per):
            one = norm_full[device // seqs, device % seqs // 2, device % 2]
            total = one if total is None else total + one
        norms_out[:, block * LANES : (block + 1) * LANES] = total


class Sliced:
    def __init__(self, loads, src, dst, count, dim=0):
        self.src, self.dst, self.count, self.size, self.dim = src, dst, count, src.shape[dim] // count, dim
        self.sems, self.first = loads.sems, loads.made
        loads.made += count
        assert loads.made <= loads.sems.shape[0]

    def copy(self, index):
        begin = index * self.size
        here = pl.ds(begin if isinstance(index, int) else pl.multiple_of(begin, self.size), self.size)
        where = (slice(None),) * self.dim + (here,)
        return pltpu.make_async_copy(self.src.at[where], self.dst.at[where], self.sems.at[self.first + index])

    def start(self, index):
        self.copy(index).start()

    def wait(self, index):
        self.copy(index).wait()

    def start_next(self, index):
        pl.when(index < self.count)(lambda: self.start(index))

    def start_all(self):
        for index in range(self.count):
            self.start(index)
        return self

    def wait_all(self):
        for index in range(self.count):
            self.wait(index)


class SummaryView:
    def __init__(self, ref, rows):
        self.ref, self.rows = ref, rows

    def __getitem__(self, key):
        cols = key[1]
        return self.ref[:, :, :, cols].reshape(self.rows, cols.stop - cols.start)


def row_block(index, size):
    return pl.ds(pl.multiple_of(index * size, size), size)


TILE = 512


def front_kernel(
    groups, seqs, length_ref, x_hbm, og_hbm, qkv_ref, proj_ref, up_ref, down_ref, norm_ref,
    qkv_hbm, pu_hbm, down_hbm, norms_out, mixed_hbm, summ_ref, attn_hbm, probs_hbm,
    activ_hbm, resid_hbm, slope_hbm, down_grad_hbm,
    x_ref, og_ref, qkv_full, pu_full, down_full, mixed_ref, attn_ref, resid_ref, activ_ref, slope_ref,
    down_grad_ref, norm_full, sum_scr, vt_scr, load_sems, send_sems, recv_sems,
):
    p = Place(groups, seqs)
    rows, width = x_ref.shape
    hidden = activ_ref.shape[1]
    local = rows // SPAN
    length, first_span = length_ref[0], p.seq * local
    count, per = rows // TILE, TILE // SPAN
    loads = Loads(load_sems)
    x_load = Sliced(loads, x_hbm, x_ref, count).start_all()
    cast_shards(
        p, seqs, qkv_ref, proj_ref, up_ref, down_ref, norm_ref, qkv_full, pu_full, down_full, norm_full
    )
    meet(p)
    og_load = loads.start(og_hbm, og_ref)
    copies = Copies(send_sems, recv_sems)
    move = Schedule(
        qkv=fast_gather_steps(p, copies, qkv_full),
        norm=gather_steps(p, copies, norm_full),
        pu=gather_steps(p, copies, pu_full),
        down=gather_steps(p, copies, down_full),
    )
    xhat_ref = resid_ref

    def center(index):
        here = row_block(index, TILE)
        x_load.wait(index)
        xhat_ref[here, :] = normalize(x_ref[here, :].astype(F32))[0]

    move("norm", "qkv")
    loop(count, center, move.plan("norm qkv pu", "", "norm qkv", "norm qkv"))
    move("norm", "qkv", "pu")
    join_norms(norm_full, seqs, LANES // norm_ref.shape[1], norms_out)
    gain, shift = norms_out[0:1, :], norms_out[1:2, :]

    def columns(full, begin, size):
        return full[:, :, :, :, begin : begin + size].reshape(width, size)

    def normed_of(here):
        return (xhat_ref[here, :] * gain + shift).astype(BF)

    def keys_values(index):
        here = row_block(index, TILE)
        mixed = dot(normed_of(here), columns(qkv_full, width, 2 * width)).astype(BF)
        mixed_ref[here, width:] = mixed
        for part in range(per):
            span = index * per + part
            sum_scr[pl.ds(span, 1), :] = span_sum(
                mixed[part * SPAN : (part + 1) * SPAN], length, (first_span + span) * SPAN
            )

    loop(count, keys_values)
    summ_ref[p.z, p.c] = sum_scr[...].astype(BF)
    along = [copies.push(summ_ref, (p.z, p.c), device) for device in p.along[1:]]
    sib = [copies.push(summ_ref, (p.z, p.c), p.sibling)]
    for k, copy in enumerate(along, 1):
        copy.wait_recv()
        sib.append(copies.push(summ_ref, (p.before[k], p.c), p.sibling))
    stores = [loads.start(qkv_full, qkv_hbm)]
    mixed_store = Sliced(loads, mixed_ref, mixed_hbm, count)

    def queries(index):
        here = row_block(index, TILE)
        mixed_ref[here, :width] = dot(normed_of(here), columns(qkv_full, 0, width)).astype(BF)
        mixed_store.start(index)

    loop(count, queries)
    for copy in sib:
        copy.wait_recv()
    move("pu")
    vt_scr[...] = summ_ref[:, :, :, width:].reshape(local * seqs, width).T
    summ_rows = SummaryView(summ_ref, local * seqs)
    attn_store = Sliced(loads, attn_ref, attn_hbm, count)
    probs_ref = activ_ref
    probs_store = Sliced(loads, probs_ref, probs_hbm, count)

    def attend(index):
        spans = []
        for k in range(per):
            span = index * per + k
            spans.append((pl.multiple_of(span * SPAN, SPAN), span, span_caps(length, first_span + span)))
        attend_spans(spans, mixed_ref, width, summ_rows, vt_scr, attn_ref, probs_ref=probs_ref)
        attn_store.start(index)
        probs_store.start(index)

    loop(count, attend, move.plan("down", "pu", "", "down pu"))
    gain_two, shift_two = norms_out[2:3, :], norms_out[3:4, :]
    resid_store, slope_store, activ_store = (
        Sliced(loads, src, dst, count)
        for src, dst in ((resid_ref, resid_hbm), (slope_ref, slope_hbm), (activ_ref, activ_hbm))
    )
    chunk = 256

    def expand(index):
        here = row_block(index, TILE)
        resid = x_ref[here, :].astype(F32) + dot(attn_ref[here, :], columns(pu_full, 0, width))
        resid_ref[here, :] = resid
        resid_store.start(index)
        normed = (normalize(resid)[0] * gain_two + shift_two).astype(BF)
        probs_store.wait(index)
        for at in range(0, hidden, chunk):
            value, slope = gelu_parts(dot(normed, columns(pu_full, width + at, chunk)))
            activ_ref[here, at : at + chunk] = value.astype(BF)
            slope_ref[here, at : at + chunk] = slope.astype(BF)
        slope_store.start(index)
        activ_store.start(index)

    loop(count, expand, move.plan("", "down", "", "down"))
    stores.append(loads.start(pu_full, pu_hbm))
    og_load.wait()
    parts = hidden // TILE
    grad_store = Sliced(loads, down_grad_ref, down_grad_hbm, parts)

    def down_grad(index):
        here = row_block(index, TILE)
        down_grad_ref[here, :] = dot_tn(activ_ref[:, here], og_ref[...]).astype(BF)
        grad_store.start(index)

    loop(parts, down_grad)
    move.finish()
    stores.append(loads.start(down_full, down_hbm))
    for store in (mixed_store, attn_store, resid_store, slope_store, activ_store, grad_store):
        store.wait_all()
    for store in stores:
        store.wait()
    copies.finish()


def middle_kernel(
    groups, seqs, og_hbm, resid_hbm, slope_hbm, attn_hbm, pu_hbm, down_hbm, norms_ref, down_grad_hbm,
    resid_grad_hbm, attn_grad_hbm, pu_grad_hbm, down_out, norm_grad_ref,
    og_ref, resid_ref, slope_ref, attn_ref, pu_ref, down_ref, resid_grad_ref, attn_grad_ref, pu_grad_ref,
    pre_grad_ref, normed_ref, pig_ref, *scratch,
):
    *buffers, load_sems, send_sems, recv_sems = scratch
    p = Place(groups, seqs)
    rows, width = og_ref.shape
    hidden = slope_ref.shape[1]
    count = rows // TILE
    loads = Loads(load_sems)
    early = [loads.start(down_hbm, down_ref)]
    tiled = [
        Sliced(loads, src, dst, count)
        for src, dst in ((og_hbm, og_ref), (slope_hbm, slope_ref), (resid_hbm, resid_ref))
    ]
    for load in tiled:
        load.start(0)
    early.append(loads.start(pu_hbm, pu_ref))
    for load in tiled:
        load.start(1)
    meet(p)
    copies = Copies(send_sems, recv_sems)
    half = down_out.shape[0] // 2
    move = Schedule(
        **{
            f"down{at}": scatter_steps(
                p, copies, loads, down_grad_hbm.at[:, :, :, half * at : half * (at + 1)], *buffers[5 * at : 5 * at + 5],
                down_out.at[half * at : half * (at + 1)],
            )
            for at in range(2)
        }
    )
    move("down0", "down1")
    attn_load = loads.start(attn_hbm, attn_ref)
    norm_grad_ref[...] = jnp.zeros_like(norm_grad_ref)
    resid_grad_store, attn_grad_store = (
        Sliced(loads, src, dst, count)
        for src, dst in ((resid_grad_ref, resid_grad_hbm), (attn_grad_ref, attn_grad_hbm))
    )
    gain, shift = norms_ref[2:3, :], norms_ref[3:4, :]
    chunk = 256
    early[0].wait()

    def tile(index):
        here = row_block(index, TILE)
        for load in tiled:
            load.start_next(index + 2)
            load.wait(index)
        grad = og_ref[here, :]
        for at in range(0, hidden, chunk):
            act_grad = dot_nt(grad, down_ref[at : at + chunk, :])
            slope = slope_ref[here, at : at + chunk].astype(F32)
            pre_grad_ref[here, at : at + chunk] = (act_grad * slope).astype(BF)

        @pl.when(index == 0)
        def _():
            early[1].wait()

        back = dot_nt(pre_grad_ref[here, :], pu_ref[:, width:])
        xhat, rstd = normalize(resid_ref[here, :])
        normed_ref[here, :] = (xhat * gain + shift).astype(BF)
        resid_grad = grad.astype(F32) + norm_back(back, gain, xhat, rstd)
        resid_grad_ref[here, :] = resid_grad
        resid_grad_store.start(index)
        pig = resid_grad.astype(BF)
        pig_ref[here, :] = pig
        attn_grad_ref[here, :] = dot_nt(pig, pu_ref[:, :width]).astype(BF)
        attn_grad_store.start(index)
        norm_grad_ref[0:1, :] += jnp.sum(back * xhat, axis=0, keepdims=True)
        norm_grad_ref[1:2, :] += jnp.sum(back, axis=0, keepdims=True)

    loop(count, tile, move.plan("down0", "down1", "down0", "down1 down0"))
    attn_load.wait()
    pu_store = Sliced(loads, pu_grad_ref, pu_grad_hbm, (width + hidden) // TILE, dim=1)
    proj = width // TILE
    pu_grad_ref[:, :width] = dot_tn(attn_ref[...], pig_ref[...]).astype(BF)
    for index in range(proj):
        pu_store.start(index)

    def up_grad(index):
        here = row_block(index + proj, TILE)
        pu_grad_ref[:, here] = dot_tn(normed_ref[...], pre_grad_ref[:, row_block(index, TILE)]).astype(BF)
        pu_store.start(index + proj)

    loop(hidden // TILE, up_grad, move.plan("down1", "", "down0"))
    resid_grad_store.wait_all()
    attn_grad_store.wait_all()
    move.finish()
    pu_store.wait_all()
    copies.finish()


def back_kernel(
    groups, seqs, length_ref, x_hbm, mixed_hbm, grad_hbm, probs_hbm, summ_ref, pu_hbm, resid_grad_hbm, down_ref,
    norms_ref, weight_hbm, norm_two_ref, activ_hbm, resid_hbm, down_hbm,
    input_grad_hbm, outputs_hbm, qkv_out, pu_out, norm_out, total_out,
    x_ref, mixed_ref, grad_ref, probs_ref, resid_grad_ref, weight_ref, input_low_ref, resid_ref, down_full_ref, outputs_ref,
    mg_scr, xhat_ref, kt_scr, dsumm_scr, dsumm_got, dsumm_low, dsumm_last, extra_scr, q_grad, k_grad, v_grad,
    gain_cols, shift_cols,
    *scratch,
):
    *buffers, norm_mine, along_norm, across_norm, sq_mine, along_sq, across_sq = scratch[:-3]
    load_sems, send_sems, recv_sems = scratch[-3:]
    p = Place(groups, seqs)
    rows, width = x_ref.shape
    local = rows // SPAN
    length, first_span = length_ref[0], p.seq * local
    loads = Loads(load_sems)
    group = 2
    count, steps = rows // TILE, local // group
    reads = [
        Sliced(loads, src, dst, steps)
        for src, dst in ((mixed_hbm, mixed_ref), (grad_hbm, grad_ref), (probs_hbm, probs_ref))
    ]
    for index in range(2):
        for read in reads:
            read.start(index)
    meet(p)
    copies = Copies(send_sems, recv_sems)

    def scatter(grad, at, out):
        return scatter_steps(p, copies, loads, grad, *buffers[5 * at : 5 * at + 5], out)

    half = pu_hbm.shape[4] // 2
    outs = [qkv_out.at[:, width * at : width * (at + 1)] for at in range(3)]
    move = Schedule(
        pu0=scatter(pu_hbm.at[:, :, :, :, :half], 0, pu_out.at[:, :half]),
        pu1=scatter(pu_hbm.at[:, :, :, :, half:], 1, pu_out.at[:, half:]),
        q=scatter(q_grad, 2, outs[0]), k=scatter(k_grad, 3, outs[1]), v=scatter(v_grad, 4, outs[2]),
        norm=share_sum_steps(p, copies, norm_mine, along_norm, across_norm, norm_out),
        squares=share_sum_steps(p, copies, sq_mine, along_sq, across_sq, total_out),
    )
    move("pu0", "pu1")
    late = [loads.start(src, dst) for src, dst in ((x_hbm, x_ref), (weight_hbm, weight_ref))]
    resid_grad_load = loads.start(resid_grad_hbm, resid_grad_ref)
    kt_scr[...] = summ_ref[:, :width].T
    dsumm_scr[...] = jnp.zeros_like(dsumm_scr)

    def attend_back(index):
        for read in reads:
            read.start_next(index + 2)
            read.wait(index)
        each = []
        for k in range(group):
            span = index * group + k
            each.append((pl.multiple_of(span * SPAN, SPAN), span, None))
        attend_back_spans(each, mixed_ref, grad_ref, width, summ_ref, kt_scr, None, mg_scr, dsumm_scr, probs_ref)

    loop(steps, attend_back, move.plan("", "pu0", "", "pu1", "pu0", "", "pu1"))
    activ_ref = probs_ref
    late += [loads.start(*ends) for ends in ((activ_hbm, activ_ref), (resid_hbm, resid_ref), (down_hbm, down_full_ref))]
    swap = []
    for z in range(p.chips):
        block = pl.ds(pl.multiple_of((2 * z + p.other) * local, local), local)
        swap.append(copies.start(dsumm_scr, block, dsumm_got, z, p.sibling))
    gain, shift = norms_ref[0:1, :], norms_ref[1:2, :]
    for read in late[:2]:
        read.wait()

    def recompute(index):
        here = row_block(index, TILE)
        xhat_ref[here, :] = normalize(x_ref[here, :].astype(F32))[0].astype(BF)

    loop(count // 2, recompute)
    for copy in swap:
        copy.wait_recv()

    def half_sum(z):
        mine = dsumm_scr[pl.ds(pl.multiple_of((2 * z + p.c) * local, local), local), :]
        return mine + dsumm_got[z]

    along = []
    for k in range(1, p.chips):
        dsumm_low[k - 1] = half_sum(p.after[k]).astype(BF)
        along.append(copies.start(dsumm_low, k - 1, dsumm_last, k - 1, p.along[k]))
    loop(count // 2, lambda index: recompute(index + count // 2))
    per_block = width // (groups * seqs)
    gain_cols[...] = jnp.broadcast_to(gain, (LANES, width)).T
    shift_cols[...] = jnp.broadcast_to(shift, (LANES, width)).T

    def weight_grad(into, at):
        begin = at * width
        back = mg_scr[:, begin : begin + width]
        moved = dot_tn(xhat_ref[...], back)
        total = jnp.sum(back.astype(F32), axis=0, keepdims=True)
        blocks, gains, shifts = [], 0.0, 0.0
        for k in range(0, width, LANES):
            part, sums = moved[:, k : k + LANES], total[:, k : k + LANES]
            blocks.append(gain_cols[...] * part + shift_cols[...] * sums)
            weight = weight_ref[:, begin + k : begin + k + LANES].astype(F32)
            gains += weight * part
            shifts += weight * sums
        into[...] = jnp.concatenate(blocks, axis=1).astype(BF).reshape(groups, p.chips, 2, per_block, width)
        gain_sums = jnp.sum(gains.T, axis=0, keepdims=True)
        shift_sums = jnp.sum(shifts.T, axis=0, keepdims=True)
        norm_mine[0:1, :] = gain_sums + (norm_mine[0:1, :] if at else 0.0)
        norm_mine[1:2, :] = shift_sums + (norm_mine[1:2, :] if at else 0.0)

    norm_mine[2:4, :] = norm_two_ref[...]
    weight_grad(q_grad, 0)
    move("q", "pu0")

    move("pu1")
    total = half_sum(p.z)
    for k, copy in enumerate(along):
        copy.wait_recv()
        total = total + dsumm_last[k].astype(F32)
    extra_scr[...] = total

    def add_extra(index):
        for k in range(2):
            span = index * 2 + k
            here = row_block(span, SPAN)
            mg_scr[here, width:] = with_extra(
                mg_scr[here, width:], extra_scr[pl.ds(span, 1), :], length, (first_span + span) * SPAN
            )

    loop(local // 2, add_extra)
    weight_grad(k_grad, 1)
    move("k", "q")
    weight_grad(v_grad, 2)
    move("v", "norm", "k", "q")
    resid_grad_load.wait()
    store = Sliced(loads, input_low_ref, input_grad_hbm, count)

    def finish(index):
        here = row_block(index, TILE)
        xhat, rstd = normalize(x_ref[here, :].astype(F32))
        back = dot_nt(mg_scr[here, :], weight_ref[...])
        input_low_ref[here, :] = (resid_grad_ref[here, :] + norm_back(back, gain, xhat, rstd)).astype(BF)
        store.start(index)

    loop(count, finish, move.plan("v k", "norm q", "v k pu0", "v pu1"))
    for read in late[2:]:
        read.wait()
    outputs_store = Sliced(loads, outputs_ref, outputs_hbm, count)

    def contract(index):
        here = row_block(index, TILE)
        out = resid_ref[here, :] + dot(activ_ref[here, :], down_full_ref[...])
        outputs_ref[here, :] = out.astype(BF)
        outputs_store.start(index)

    loop(count // 2, contract, move.plan("k norm q"))
    sq_mine[...] = square_sums(pu_out[...]) + square_sums(down_ref[...])
    copies.finish()
    move.finish("pu0", "pu1", "q", "k", "v", "norm")
    sq_mine[...] += square_sums(qkv_out[...])
    move("squares")
    loop(count // 2, lambda index: contract(index + count // 2), move.plan("squares"))
    move.finish("squares")
    total_out[...] += square_sums(norm_out[...])
    store.wait_all()
    outputs_store.wait_all()
    copies.finish()


def qkv_kernel(info_ref, x_ref, norms_ref, weight_ref, mixed_ref, summ_ref, sum_scr):
    step = pl.program_id(0)
    tile, width = x_ref.shape
    length, first_span = info_ref[0], info_ref[1]
    mixed = qkv_tile(x_ref[...], norms_ref, weight_ref)
    mixed_ref[...] = mixed
    per = tile // SPAN
    for part in range(per):
        span = step * per + part
        sum_scr[pl.ds(span, 1), :] = span_sum(
            mixed[part * SPAN : (part + 1) * SPAN, width:], length, (first_span + span) * SPAN
        )

    @pl.when(step == pl.num_programs(0) - 1)
    def _():
        summ_ref[...] = sum_scr[...].astype(BF)


def attend_kernel(info_ref, mixed_ref, summ_ref, out_ref, lse_ref, vt_scr):
    step = pl.program_id(0)
    width = out_ref.shape[1]

    @pl.when(step == 0)
    def _():
        vt_scr[...] = summ_ref[:, width:].T

    caps = span_caps(info_ref[0], info_ref[1] + step)
    attend_spans([(0, 0, caps)], mixed_ref, width, summ_ref, vt_scr, out_ref, lse_ref)


def attend_back_kernel(info_ref, mixed_ref, grad_ref, lse_ref, summ_ref, back_ref, dsumm_ref, kt_scr):
    step = pl.program_id(0)
    width = grad_ref.shape[1]

    @pl.when(step == 0)
    def _():
        kt_scr[...] = summ_ref[:, :width].T
        dsumm_ref[...] = jnp.zeros_like(dsumm_ref)

    caps = span_caps(info_ref[0], info_ref[1] + step)
    attend_back_spans(
        [(0, 0, caps)], mixed_ref, grad_ref, width, summ_ref, kt_scr, lse_ref, back_ref, dsumm_ref
    )


def mlp_kernel(
    x_ref, attn_ref, og_ref, norms_ref, pu_ref, down_ref,
    out_ref, resid_grad_ref, attn_grad_ref, pu_grad_ref, down_grad_ref, norm_grad_ref,
    activ_scr, pre_grad_scr, n2t_scr, attnt_scr, ogt_scr, pig_scr, norm_scr,
):
    step = pl.program_id(0)
    tile, width = x_ref.shape
    hidden = down_ref.shape[0]
    rows = pl.ds(pl.multiple_of(step * tile, tile), tile)
    chunk = 256
    attn = attn_ref[...]
    grad = og_ref[...]
    resid = x_ref[...].astype(F32) + dot(attn, pu_ref[:, :width])
    xhat, rstd = normalize(resid)
    gain = norms_ref[2:3, :]
    normed = (xhat * gain + norms_ref[3:4, :]).astype(BF)
    attnt_scr[:, rows] = attn.T
    n2t_scr[:, rows] = normed.T
    ogt_scr[:, rows] = grad.T
    for at in range(0, hidden, chunk):
        pre = dot(normed, pu_ref[:, width + at : width + at + chunk])
        act_grad = dot_nt(grad, down_ref[at : at + chunk, :])
        value, slope = gelu_parts(pre)
        activ = value.astype(BF)
        pre_grad = (act_grad * slope).astype(BF)
        activ_scr[rows, at : at + chunk] = activ
        pre_grad_scr[rows, at : at + chunk] = pre_grad
    out_ref[...] = (resid + dot(activ_scr[rows, :], down_ref[...])).astype(BF)
    back = dot_nt(pre_grad_scr[rows, :], pu_ref[:, width:])
    resid_grad = grad.astype(F32) + norm_back(back, gain, xhat, rstd)
    resid_grad_ref[...] = resid_grad
    pig = resid_grad.astype(BF)
    pig_scr[rows, :] = pig
    attn_grad_ref[...] = dot_nt(pig, pu_ref[:, :width]).astype(BF)
    gain_part = jnp.sum(back * xhat, axis=0, keepdims=True)
    shift_part = jnp.sum(back, axis=0, keepdims=True)
    part = jnp.concatenate([gain_part, shift_part], axis=0)

    @pl.when(step == 0)
    def _():
        norm_scr[...] = part

    @pl.when(step > 0)
    def _():
        norm_scr[...] += part

    @pl.when(step == pl.num_programs(0) - 1)
    def _():
        norm_grad_ref[...] = norm_scr[...]
        pu_grad_ref[:, :width] = dot(attnt_scr[...], pig_scr[...]).astype(BF)
        cols = 512

        def one(index, carry):
            c = pl.ds(pl.multiple_of(index * cols, cols), cols)
            out = pl.ds(pl.multiple_of(width + index * cols, cols), cols)
            pu_grad_ref[:, out] = dot(n2t_scr[...], pre_grad_scr[:, c]).astype(BF)
            down_grad_ref[c, :] = dot(ogt_scr[...], activ_scr[:, c]).T.astype(BF)
            return carry

        lax.fori_loop(0, hidden // cols, one, 0)


def final_kernel(
    info_ref, x_ref, back_ref, extra_ref, resid_grad_ref, norms_ref, weight_ref,
    input_grad_ref, qkv_grad_ref, norm_grad_ref, mg_scr, normed_scr,
):
    step = pl.program_id(0)
    tile, width = x_ref.shape
    rows = pl.ds(pl.multiple_of(step * tile, tile), tile)
    length, first_span = info_ref[0], info_ref[1]
    xhat, rstd = normalize(x_ref[...].astype(F32))
    gain = norms_ref[0:1, :]
    normed_scr[rows, :] = (xhat * gain + norms_ref[1:2, :]).astype(BF)
    per = tile // SPAN
    parts = []
    for part in range(per):
        span = step * per + part
        here = back_ref[part * SPAN : (part + 1) * SPAN, width:]
        parts.append(with_extra(here, extra_ref[pl.ds(span, 1), :], length, (first_span + span) * SPAN))
    mg = jnp.concatenate([back_ref[:, :width], jnp.concatenate(parts, axis=0)], axis=1)
    mg_scr[rows, :] = mg
    back = dot_nt(mg, weight_ref[...])
    input_grad_ref[...] = resid_grad_ref[...] + norm_back(back, gain, xhat, rstd)

    @pl.when(step == 0)
    def _():
        norm_grad_ref[...] = jnp.zeros_like(norm_grad_ref)

    norm_grad_ref[0:1, :] += jnp.sum(back * xhat, axis=0, keepdims=True)
    norm_grad_ref[1:2, :] += jnp.sum(back, axis=0, keepdims=True)

    @pl.when(step == pl.num_programs(0) - 1)
    def _():
        cols = 256

        def one(index, carry):
            c = pl.ds(pl.multiple_of(index * cols, cols), cols)
            qkv_grad_ref[:, c] = dot_tn(normed_scr[...], mg_scr[:, c]).astype(BF)
            return carry

        lax.fori_loop(0, qkv_grad_ref.shape[1] // cols, one, 0)


def whole(shape):
    return pl.BlockSpec(shape, lambda i: (0,) * len(shape))


def by_rows(tile, width):
    return pl.BlockSpec((tile, width), lambda i: (i, 0))


SCALARS = pl.BlockSpec(memory_space=pltpu.SMEM)
PARAMS = pltpu.CompilerParams(vmem_limit_bytes=VMEM_LIMIT)


def remote_call(kernel, groups, seqs, name, collective_id, outs, ins, scratch, loads, copies):
    return pl.pallas_call(
        functools.partial(kernel, groups, seqs),
        in_specs=[pl.BlockSpec(memory_space=space) for space in ins],
        out_specs=[pl.BlockSpec(memory_space=space) for space, _, _ in outs],
        out_shape=[jax.ShapeDtypeStruct(shape, kind) for _, shape, kind in outs],
        scratch_shapes=list(scratch) + [pltpu.SemaphoreType.DMA((n,)) for n in (loads, copies, copies)],
        compiler_params=pltpu.CompilerParams(
            vmem_limit_bytes=VMEM_LIMIT, collective_id=collective_id, has_side_effects=True
        ),
        name=name,
    )


def regroup(grad, dim, outer, inner):
    shape = grad.shape
    piece = shape[dim] // (outer * inner)
    split = grad.reshape(shape[:dim] + (outer, inner, piece) + shape[dim + 1 :])
    return jnp.swapaxes(split, dim, dim + 1).reshape(shape)


def gather_plain(state):
    both = ("batch", "seq")
    qkv, proj, up, down = (lax.all_gather(w.astype(BF), both, axis=0, tiled=True) for w in state[:4])
    norms = lax.all_gather(state[4].astype(BF), both, axis=1, tiled=True).astype(F32)
    return qkv, jnp.concatenate([proj, up], axis=1), down, norms


def reduce_plain(qkv_grad, pu_grad, down_grad, norm_grad):
    groups, seqs = lax.axis_size("batch"), lax.axis_size("seq")
    reduced = []
    for grad, dim in ((qkv_grad, 0), (pu_grad, 0), (down_grad, 0)):
        part = lax.psum_scatter(
            regroup(grad.astype(F32), dim, groups, seqs), "seq", scatter_dimension=dim, tiled=True
        )
        reduced.append(lax.psum_scatter(part, "batch", scatter_dimension=dim, tiled=True))
    norm_total = lax.psum(norm_grad, ("batch", "seq"))
    squares = lax.psum(sum(jnp.sum(grad * grad) for grad in reduced), ("batch", "seq"))
    squares = squares + jnp.sum(norm_total * norm_total)
    return (*reduced, norm_total, jnp.zeros((8, LANES), F32).at[0, 0].set(squares))


def mlp_call(x, attn_out, grad_rows, norms, pu_full, down_full):
    sds = jax.ShapeDtypeStruct
    rows, width = x.shape
    hidden = down_full.shape[0]
    tile = min(512, rows)
    steps = rows // tile
    return pl.pallas_call(
        mlp_kernel,
        grid=(steps,),
        in_specs=[by_rows(tile, width)] * 3
        + [whole(norms.shape), whole(pu_full.shape), whole(down_full.shape)],
        out_specs=[by_rows(tile, width)] * 3
        + [whole(pu_full.shape), whole(down_full.shape), whole((2, width))],
        out_shape=[
            sds((rows, width), BF), sds((rows, width), F32), sds((rows, width), BF),
            sds(pu_full.shape, BF), sds(down_full.shape, BF), sds((2, width), F32),
        ],
        scratch_shapes=[
            pltpu.VMEM((rows, hidden), BF), pltpu.VMEM((rows, hidden), BF),
            pltpu.VMEM((width, rows), BF), pltpu.VMEM((width, rows), BF), pltpu.VMEM((width, rows), BF),
            pltpu.VMEM((rows, width), BF), pltpu.VMEM((2, width), F32),
        ],
        compiler_params=PARAMS,
        name="mlp",
    )(x, attn_out, grad_rows, norms, pu_full, down_full)


def direct_body(groups, seqs, inputs, out_grad, lengths, *state):
    rows, width = inputs.shape[1], inputs.shape[2]
    own_rows, down_rows = state[0].shape[0], state[3].shape[0]
    hidden = state[2].shape[1]
    chips = seqs // 2
    grid3 = (groups, chips, 2)
    local = rows // SPAN
    spans = local * seqs
    pairs = width // LANES
    count = rows // TILE
    x, grad_rows = inputs[0], out_grad[0]
    vmem, hbm, smem = pltpu.VMEM, pl.ANY, pltpu.SMEM
    shapes = (
        (*grid3, own_rows, 3 * width), (*grid3, own_rows, width + hidden), (*grid3, down_rows, width),
    )
    tokens = (rows, width)
    (
        qkv_full, pu_full, down_full, norms, mixed, summ, attn_out, probs, activ, resid, slope, down_grad,
    ) = remote_call(
        front_kernel, groups, seqs, "front", 0,
        [
            *((hbm, shape, BF) for shape in shapes), (vmem, (4, width), F32), (hbm, (rows, 3 * width), BF),
            (vmem, (chips, 2, local, 2 * width), BF), (hbm, tokens, BF), (hbm, (rows, 4 * SPAN * pairs), BF),
            (hbm, (rows, hidden), BF), (hbm, tokens, F32), (hbm, (rows, hidden), BF), (hbm, (hidden, width), BF),
        ],
        [smem, hbm, hbm] + [vmem] * 5,
        [
            vmem(tokens, BF), vmem(tokens, BF), *(vmem(shape, BF) for shape in shapes),
            vmem((rows, 3 * width), BF), vmem(tokens, BF), vmem(tokens, F32),
            vmem((rows, hidden), BF), vmem((rows, hidden), BF), vmem((hidden, width), BF),
            vmem((*grid3, 4, LANES), F32), vmem((local, 2 * width), F32), vmem((width, spans), BF),
        ],
        4 + 7 * count + hidden // TILE, 3 * GATHER_COPIES + fast_gather_copies(chips) + 2 * chips,
    )(lengths, x, grad_rows, *state[:5])
    pu_flat, down_flat = pu_full.reshape(width, width + hidden), down_full.reshape(hidden, width)
    resid_grad, attn_grad, pu_grad, down_own, norm_two = remote_call(
        middle_kernel, groups, seqs, "middle", 1,
        [
            (hbm, tokens, F32), (hbm, tokens, BF), (hbm, pu_flat.shape, BF),
            (vmem, (down_rows, width), F32), (vmem, (2, width), F32),
        ],
        [hbm] * 6 + [vmem, hbm],
        [
            vmem(tokens, BF), vmem(tokens, F32), vmem((rows, hidden), BF), vmem(tokens, BF),
            vmem(pu_flat.shape, BF), vmem(down_flat.shape, BF), vmem(tokens, F32), vmem(tokens, BF),
            vmem(pu_flat.shape, BF), vmem((rows, hidden), BF), vmem(tokens, BF), vmem(tokens, BF),
            *scatter_scratch(groups, chips, down_rows // 2, width) * 2,
        ],
        6 + 5 * count + (width + hidden) // TILE, 2 * SCATTER_COPIES,
    )(grad_rows, resid, slope, attn_out, pu_flat, down_flat, norms, down_grad.reshape(shapes[2]))
    half = (width + hidden) // 2
    blocks = ((own_rows, half),) * 2 + ((own_rows, width),) * 3
    summ_block = (local, 2 * width)
    scratch = [
        vmem(tokens, BF), vmem((rows, 3 * width), BF), vmem(tokens, BF), vmem(probs.shape, BF), vmem(tokens, F32),
        vmem((width, 3 * width), BF), vmem(tokens, BF), vmem(tokens, F32), vmem(down_flat.shape, BF), vmem(tokens, BF),
        vmem((rows, 3 * width), BF), vmem(tokens, BF), vmem((width, spans), BF), vmem((spans, 2 * width), F32),
        vmem((chips, *summ_block), F32), vmem((chips - 1, *summ_block), BF),
        vmem((chips - 1, *summ_block), BF), vmem(summ_block, F32),
        *[vmem((*grid3, own_rows, width), BF)] * 3, *[vmem((width, LANES), F32)] * 2,
    ]
    scratch += [buffer for block in blocks for buffer in scatter_scratch(groups, chips, *block)]
    scratch += [
        vmem((4, width), F32), vmem((seqs, 4, width), F32), vmem((groups, 4, width), F32),
        vmem((8, LANES), F32), vmem((seqs, 8, LANES), F32), vmem((groups, 8, LANES), F32),
    ]
    input_grad, outputs, qkv_own, pu_own, norm_total, total = remote_call(
        back_kernel, groups, seqs, "back", 2,
        [
            (hbm, tokens, BF), (hbm, tokens, BF), (vmem, (own_rows, 3 * width), F32),
            (vmem, (own_rows, width + hidden), F32), (vmem, (4, width), F32), (vmem, (8, LANES), F32),
        ],
        [smem, hbm, hbm, hbm, hbm, vmem, hbm, hbm, vmem, vmem, hbm, vmem, hbm, hbm, hbm],
        scratch, 3 * local // 2 + 6 + 5 + 2 * count,
        5 * SCATTER_COPIES + 2 * share_copies(groups, seqs) + 2 * chips,
    )(
        lengths, x, mixed, attn_grad, probs, summ.reshape(spans, 2 * width), pu_grad.reshape(shapes[1]),
        resid_grad, down_own, norms, qkv_full.reshape(width, 3 * width), norm_two, activ, resid, down_flat,
    )
    return outputs, input_grad, (qkv_own, pu_own, down_own), norm_total, total


def plain_body(groups, seqs, inputs, out_grad, lengths, *state):
    sds = jax.ShapeDtypeStruct
    rows, width = inputs.shape[1], inputs.shape[2]
    qkv_full, pu_full, down_full, norms = gather_plain(state[:5])
    local = rows // SPAN
    spans = local * seqs
    info = jnp.stack([lengths[0], (lax.axis_index("seq") * local).astype(jnp.int32)])
    x, grad_rows = inputs[0], out_grad[0]
    tile = 256
    steps = rows // tile
    mixed, own_summ = pl.pallas_call(
        qkv_kernel,
        grid=(steps,),
        in_specs=[SCALARS, by_rows(tile, width), whole(norms.shape), whole(qkv_full.shape)],
        out_specs=[by_rows(tile, 3 * width), whole((local, 2 * width))],
        out_shape=[sds((rows, 3 * width), BF), sds((local, 2 * width), BF)],
        scratch_shapes=[pltpu.VMEM((local, 2 * width), F32)],
        compiler_params=PARAMS,
        name="qkv",
    )(info, x, norms, qkv_full)
    summ = lax.all_gather(own_summ, "seq", axis=0, tiled=True)
    pairs = width // LANES
    lse_spec = pl.BlockSpec((1, pairs, 2 * SPAN), lambda i: (i, 0, 0))
    attn_out, lse = pl.pallas_call(
        attend_kernel,
        grid=(local,),
        in_specs=[SCALARS, by_rows(SPAN, 3 * width), whole(summ.shape)],
        out_specs=[by_rows(SPAN, width), lse_spec],
        out_shape=[sds((rows, width), BF), sds((local, pairs, 2 * SPAN), F32)],
        scratch_shapes=[pltpu.VMEM((width, spans), BF)],
        compiler_params=PARAMS,
        name="attend",
    )(info, mixed, summ)
    outputs, resid_grad, attn_grad, pu_grad, down_grad, norm_two = mlp_call(
        x, attn_out, grad_rows, norms, pu_full, down_full
    )
    back, dsumm = pl.pallas_call(
        attend_back_kernel,
        grid=(local,),
        in_specs=[SCALARS, by_rows(SPAN, 3 * width), by_rows(SPAN, width), lse_spec, whole(summ.shape)],
        out_specs=[by_rows(SPAN, 3 * width), whole((spans, 2 * width))],
        out_shape=[sds((rows, 3 * width), BF), sds((spans, 2 * width), F32)],
        scratch_shapes=[pltpu.VMEM((width, spans), BF)],
        compiler_params=PARAMS,
        name="attend_back",
    )(info, mixed, attn_grad, lse, summ)
    extra = lax.psum_scatter(dsumm, "seq", scatter_dimension=0, tiled=True)
    input_grad, qkv_grad, norm_one = pl.pallas_call(
        final_kernel,
        grid=(steps,),
        in_specs=[
            SCALARS, by_rows(tile, width), by_rows(tile, 3 * width), whole(extra.shape), by_rows(tile, width),
            whole(norms.shape), whole(qkv_full.shape),
        ],
        out_specs=[by_rows(tile, width), whole(qkv_full.shape), whole((2, width))],
        out_shape=[sds((rows, width), F32), sds(qkv_full.shape, BF), sds((2, width), F32)],
        scratch_shapes=[pltpu.VMEM((rows, 3 * width), BF), pltpu.VMEM((rows, width), BF)],
        compiler_params=PARAMS,
        name="final",
    )(info, x, back, extra, resid_grad, norms, qkv_full)
    norm_grad = jnp.concatenate([norm_one, norm_two], axis=0)
    *grads, norm_total, total = reduce_plain(qkv_grad, pu_grad, down_grad, norm_grad)
    return outputs, input_grad, grads, norm_total, total


def body(groups, seqs, *args):
    state = args[3:]
    rows, width = args[0].shape[1:]
    direct = groups == 4 and seqs % 4 == 0 and state[0].shape[0] % 16 == 0 and rows % TILE == 0
    direct = direct and rows // SPAN * seqs == SPAN and state[2].shape[1] == 4 * SPAN * (width // LANES)
    run = direct_body if direct else plain_body
    outputs, input_grad, grads, norm_total, total = run(groups, seqs, *args)
    input_grad = input_grad.astype(BF)
    sds = jax.ShapeDtypeStruct
    vmem, hbm = pltpu.VMEM, pl.ANY
    spec = lambda space: pl.BlockSpec(memory_space=space)
    held = [sds(w.shape, F32) for w in state[:5]]
    parts = 8
    operands = (outputs, input_grad, *grads, *state)
    outputs, input_grad, grad_norm, *fresh, shift_clipped = pl.pallas_call(
        functools.partial(update_kernel, parts),
        in_specs=[spec(vmem)] * 2 + [spec(hbm)] * 20,
        out_specs=[spec(hbm)] * 2 + [spec(vmem)] + [spec(hbm)] * 15 + [spec(vmem)],
        out_shape=[
            sds(outputs.shape, BF), sds(outputs.shape, F32), sds((1, 1), F32), *held * 3,
            sds((1, state[4].shape[1]), F32),
        ],
        scratch_shapes=[vmem(a.shape, a.dtype) for a in operands]
        + [vmem(w.shape, F32) for w in held * 3] + [vmem(outputs.shape, F32), pltpu.SemaphoreType.DMA((4 * parts + 33,))],
        compiler_params=PARAMS,
        name="update",
    )(total, norm_total, *operands)
    return (outputs[None], input_grad[None], grad_norm[0, 0], *fresh, shift_clipped[0])


def solution(mesh):
    tokens = P("batch", "seq", None)
    owned = P(("batch", "seq"), None)
    columns = P(None, ("batch", "seq"))
    state = (owned, owned, owned, owned, columns)
    return jax.shard_map(
        functools.partial(body, mesh.shape["batch"], mesh.shape["seq"]),
        mesh=mesh,
        in_specs=(tokens, tokens, P("batch")) + state * 3,
        out_specs=(tokens, tokens, P()) + state * 3 + (P(("batch", "seq")),),
        check_vma=False,
    )
```
